32 devices in a mesh: rep: 2 (over x), fsdp: 16 (over z, y, core).
Axes of the slice: x: 2, y: 2, z: 4, core: 2. Of those that a mesh axis runs over, the one named last changes fastest.
Arguments:
- tokens: bfloat16 [16, 1024, 512], P('fsdp', 'rep'), may hold values from -6 to 6
- cotangent: bfloat16 [16, 1024, 512], P('fsdp', 'rep'), may hold values from -6 to 6
- tags: int32 [16], P('fsdp'), may hold values from 0 to 1
- lengths: int32 [16], P('fsdp'), may hold values from 513 to 1024, as said below
- key_mask: int32 [16, 1024], P('fsdp'), may hold values 0 or 1
- master_qkv: float32 [2, 512, 1536], P(None, 'fsdp'), may hold values from -0.25 to 0.25
- master_out: float32 [2, 512, 512], P(None, 'fsdp'), may hold values from -1 to 1
- master_in: float32 [2, 512, 2048], P(None, 'fsdp'), may hold values from -0.25 to 0.25
- master_feed_output: float32 [2, 2048, 512], P(None, 'fsdp'), may hold values from -0.1875 to 0.1875
- master_vec: float32 [2, 14, 512], P(None, None, 'fsdp'), may hold values from -3 to 3
- first_qkv: float32 [2, 512, 1536], P(None, 'fsdp'), may hold values from -512 to 512
- first_out: float32 [2, 512, 512], P(None, 'fsdp'), may hold values from -48 to 48
- first_in: float32 [2, 512, 2048], P(None, 'fsdp'), may hold values from -224 to 224
- first_ffo: float32 [2, 2048, 512], P(None, 'fsdp'), may hold values from -320 to 320
- first_vec: float32 [2, 14, 512], P(None, None, 'fsdp'), may hold values from -448 to 448
- second_qkv: float32 [2, 512, 1536], P(None, 'fsdp'), may hold values from 8028.16 to 32112.64
- second_out: float32 [2, 512, 512], P(None, 'fsdp'), may hold values from 64 to 256
- second_in: float32 [2, 512, 2048], P(None, 'fsdp'), may hold values from 1474.56 to 5898.24
- second_ffo: float32 [2, 2048, 512], P(None, 'fsdp'), may hold values from 2621.44 to 10485.76
- second_moment_vector: float32 [2, 14, 512], P(None, None, 'fsdp'), may hold values from 5898.24 to 23592.96
Outputs:
- out_tokens: bfloat16 [16, 1024, 512], P('fsdp', 'rep')
- input_grad: float32 [16, 1024, 512], P('fsdp', 'rep')
- new_master_qkv: float32 [2, 512, 1536], P(None, 'fsdp')
- new_master_out: float32 [2, 512, 512], P(None, 'fsdp')
- new_master_in: float32 [2, 512, 2048], P(None, 'fsdp')
- new_master_ffo: float32 [2, 2048, 512], P(None, 'fsdp')
- new_master_vec: float32 [2, 14, 512], P(None, None, 'fsdp')
- new_first_qkv: float32 [2, 512, 1536], P(None, 'fsdp')
- new_first_out: float32 [2, 512, 512], P(None, 'fsdp')
- new_first_in: float32 [2, 512, 2048], P(None, 'fsdp')
- new_first_ffo: float32 [2, 2048, 512], P(None, 'fsdp')
- new_first_vec: float32 [2, 14, 512], P(None, None, 'fsdp')
- new_second_qkv: float32 [2, 512, 1536], P(None, 'fsdp')
- updated_second_output: float32 [2, 512, 512], P(None, 'fsdp')
- new_second_in: float32 [2, 512, 2048], P(None, 'fsdp')
- new_second_ffo: float32 [2, 2048, 512], P(None, 'fsdp')
- new_second_vec: float32 [2, 14, 512], P(None, None, 'fsdp')
The draws below stay inside these ranges and needn't reach their ends.
Inputs may be any that keep to these rules, and one draw needn't show every extreme that they name: `lengths`: every sequence is longer than 512; one sequence of each draw has all 1024 positions.
All inputs are finite; a program needn't handle non-finite values. No bound on the sum of `key_mask` on one device may be relied on, other than what follows from the above.
Results may differ from the reference program's by a relative error of at most 0.018.
Values may be sent and summed in bfloat16 or wider, within the bound.
A program may use at most 192 MiB of HBM per device.

```python
import math
import jax
import jax.numpy as jnp
from jax import lax

D = 512
H = 8
FF = 2048
TOK_DEV = 512
STEP = 10
SEQ_LEN = 1024
SEQS = 16
TOKENS = 16384
NVEC = 14


def draw_lengths(key, part):
    key = jax.random.fold_in(key, 11)
    base_lengths = jax.random.randint(key, (SEQS,), TOK_DEV + 1, SEQ_LEN + 1, dtype=jnp.int32)
    chosen = jax.random.randint(jax.random.fold_in(key, 5), (), 0, SEQS, dtype=jnp.int32)
    return jnp.where(jnp.arange(SEQS, dtype=jnp.int32) == chosen, SEQ_LEN, base_lengths).astype(jnp.int32)


def draw_master_vec(key, part):
    key = jax.random.fold_in(key, 23)
    row_ids = jnp.arange(NVEC, dtype=jnp.int32)[None, :, None]
    gain_rows = (row_ids == 5) | (row_ids == 8)
    spread = jnp.clip(0.3 * jax.random.normal(key, (2, NVEC, D), jnp.float32), -1.5, 1.5)
    gains = jax.random.uniform(jax.random.fold_in(key, 3), (2, NVEC, D), jnp.float32, 0.6, 1.4)
    return jnp.where(gain_rows, gains, spread).astype(jnp.float32)


def touch_ends(values, key, least, largest):
    longest = values.shape.index(max(values.shape))
    spots = []
    for shift in (0, 1):
        where = [jax.random.randint(jax.random.fold_in(key, axis), (), 0, length) for axis, length in enumerate(values.shape)]
        where[longest] = (where[longest] + shift) % values.shape[longest]
        spots.append(tuple(where))
    return values.at[spots[0]].set(least).at[spots[1]].set(largest)


def block_levels(stream_key, extent, cuts, least, top_value):
    level = 1.0
    for axis_at, parts in cuts:
        steps = jax.random.uniform(jax.random.fold_in(jax.random.fold_in(stream_key, 6), axis_at), (parts,), jnp.float32, least / len(cuts), top_value / len(cuts))
        level = level * jnp.repeat(jnp.exp(steps), extent[axis_at] // parts).reshape((-1,) + (1,) * (len(extent) - 1 - axis_at))
    return level


def gaussian(key, dims, width, bound, split=(), held_as=jnp.bfloat16):
    entries = width * jax.random.normal(key, dims, jnp.float32)
    if split:
        entries = entries * block_levels(key, dims, split, -0.22, 0.18)
    return jnp.clip(entries, -bound, bound).astype(held_as)


def setup_inputs(seed: int = 0) -> dict:
    streams_of = jax.random.split(jax.random.key(seed), 21)
    tokens = gaussian(streams_of[0], (SEQS, SEQ_LEN, D), 1.0, 6.0, ((0, 16), (1, 2)))
    cotangent = gaussian(streams_of[1], (SEQS, SEQ_LEN, D), 1.0, 6.0, ((0, 16), (1, 2)))
    tags = touch_ends(jax.random.randint(streams_of[2], (SEQS,), 0, 2), jax.random.fold_in(streams_of[2], 1), 0, 1).astype(jnp.int32)
    lengths = draw_lengths(jax.random.fold_in(streams_of[20], 71), 0)
    key_mask = touch_ends((jax.random.randint(streams_of[4], (SEQS, SEQ_LEN), 0, 8) < 7).astype(jnp.int32), jax.random.fold_in(streams_of[4], 1), 0, 1)
    master_qkv = gaussian(streams_of[5], (2, D, 3 * D), D ** -0.5, 0.25, ((1, 16),), jnp.float32)
    master_out = gaussian(streams_of[6], (2, D, D), (D // 16) ** -0.5, 1.0, ((1, 16),), jnp.float32)
    master_in = gaussian(streams_of[7], (2, D, FF), D ** -0.5, 0.25, ((1, 16),), jnp.float32)
    master_feed_output = gaussian(streams_of[8], (2, FF, D), (FF // 2) ** -0.5, 0.1875, ((1, 16),), jnp.float32)
    master_vec = draw_master_vec(jax.random.fold_in(streams_of[20], 71), 0)
    first_qkv = gaussian(streams_of[10], (2, D, 3 * D), (0.7 * TOKENS ** 0.5), 512.0, ((1, 16),), jnp.float32)
    first_out = gaussian(streams_of[11], (2, D, D), (2.0 * SEQS ** 0.5), 48.0, ((1, 16),), jnp.float32)
    first_in = gaussian(streams_of[12], (2, D, FF), (0.3 * TOKENS ** 0.5), 224.0, ((1, 16),), jnp.float32)
    first_ffo = gaussian(streams_of[13], (2, FF, D), (0.4 * TOKENS ** 0.5), 320.0, ((1, 16),), jnp.float32)
    first_vec = gaussian(streams_of[14], (2, NVEC, D), (0.6 * TOKENS ** 0.5), 448.0, ((2, 16),), jnp.float32)
    second_qkv = jnp.clip(jnp.exp(math.log(32112.64) - 1.3862944 * jax.random.uniform(streams_of[15], (2, D, 3 * D), jnp.float32) ** block_levels(streams_of[15], (2, D, 3 * D), ((1, 16),), -0.2, 0.2)), 8028.16, 32112.64)
    second_out = jnp.clip(jnp.exp(math.log(256.0) - 1.3862944 * jax.random.uniform(streams_of[16], (2, D, D), jnp.float32) ** block_levels(streams_of[16], (2, D, D), ((1, 16),), -0.2, 0.2)), 64.0, 256.0)
    second_in = jnp.clip(jnp.exp(math.log(5898.24) - 1.3862944 * jax.random.uniform(streams_of[17], (2, D, FF), jnp.float32) ** block_levels(streams_of[17], (2, D, FF), ((1, 16),), -0.2, 0.2)), 1474.56, 5898.24)
    second_ffo = jnp.clip(jnp.exp(math.log(10485.76) - 1.3862944 * jax.random.uniform(streams_of[18], (2, FF, D), jnp.float32) ** block_levels(streams_of[18], (2, FF, D), ((1, 16),), -0.2, 0.2)), 2621.44, 10485.76)
    second_moment_vector = jnp.clip(jnp.exp(math.log(23592.96) - 1.3862944 * jax.random.uniform(streams_of[19], (2, NVEC, D), jnp.float32) ** block_levels(streams_of[19], (2, NVEC, D), ((2, 16),), -0.2, 0.2)), 5898.24, 23592.96)
    return dict(tokens=tokens, cotangent=cotangent, tags=tags, lengths=lengths, key_mask=key_mask, master_qkv=master_qkv, master_out=master_out, master_in=master_in, master_feed_output=master_feed_output, master_vec=master_vec, first_qkv=first_qkv, first_out=first_out, first_in=first_in, first_ffo=first_ffo, first_vec=first_vec, second_qkv=second_qkv, second_out=second_out, second_in=second_in, second_ffo=second_ffo, second_moment_vector=second_moment_vector)


@jax.custom_vjp
def low(v):
    return lax.optimization_barrier(v.astype(jnp.bfloat16)).astype(jnp.float32)

@jax.custom_vjp
def low_back(v):
    return v

def low_keep(v):
    return (low(v), None)

def low_pass(kept, grad):
    return (grad,)

def back_keep(v):
    return (v, None)

def back_low(kept, grad):
    return (low(grad),)
low.defvjp(low_keep, low_pass)
low_back.defvjp(back_keep, back_low)
beta_decay = 0.5
epsilon_adam = 1e-08
weight_decay = 0.01
norm_epsilon = 1e-05
masked_score = -1000000000.0
vector_rate = 0.15
matrix_rate = 0.5

def both_round(values):
    return low(low_back(values))

def layer_norm(pre_norm, gain_row, offset_row):
    centre_mean = lax.optimization_barrier(jnp.mean(pre_norm, axis=-1, keepdims=True))
    centred = pre_norm - centre_mean
    variance = lax.optimization_barrier(jnp.mean(centred * centred, axis=-1, keepdims=True))
    return centred * lax.rsqrt(variance + norm_epsilon) * gain_row + offset_row

def project(input_rows, weight_matrix):
    return jnp.einsum('fbg,gh->fbh', input_rows, weight_matrix, precision=lax.Precision.HIGHEST)

def attend(items):
    queries, keys_all, values_all, key_bias = items
    length_seq = queries.shape[0]
    head_size = queries.shape[1] // H
    query_heads = queries.reshape(length_seq, H, head_size)
    key_heads = keys_all.reshape(length_seq, H, head_size)
    value_heads = values_all.reshape(length_seq, H, head_size)
    scores = jnp.einsum('qhd,khd->hqk', query_heads, key_heads, precision=lax.Precision.HIGHEST)
    scores = low_back(scores) * head_size ** (-0.5) + key_bias[None, None, :]
    soft_weights = jax.nn.softmax(scores, axis=-1)
    context = jnp.einsum('hqk,khd->qhd', low(soft_weights), value_heads, precision=lax.Precision.HIGHEST)
    return context.reshape(length_seq, -1)

def encoder_layer(input_rows, params, tags, key_bias):
    w_qkv, w_out, w_in, w_ffo, vectors = [low(param_array) for param_array in params]
    model_width = w_out.shape[0]
    direction = jnp.where((tags == 0)[:, None, None], vectors[0], vectors[1])
    summed = input_rows + direction
    projected = project(low(summed), w_qkv)
    queries = both_round(projected[..., :model_width] + vectors[2])
    keys_all = both_round(projected[..., model_width:2 * model_width])
    values_all = both_round(projected[..., 2 * model_width:] + vectors[3])
    context = lax.map(jax.checkpoint(attend), (queries, keys_all, values_all, key_bias))
    context = both_round(context)
    branch = low_back(project(context, w_out) + vectors[4])
    hidden = layer_norm(summed + branch, vectors[5], vectors[6])
    inner_act = low_back(project(low(hidden), w_in) + vectors[10:].reshape(-1))
    activated = low(jax.nn.gelu(inner_act, approximate=True))
    feed_out = low_back(project(activated, w_ffo) + vectors[7])
    return layer_norm(hidden + feed_out, vectors[8], vectors[9])

def adamw(master, first, second, grad, rate, decay):
    first_new = beta_decay * first + (1.0 - beta_decay) * grad
    second_new = beta_decay * second + (1.0 - beta_decay) * grad * grad
    correction = 1.0 - beta_decay ** STEP
    direction = first_new / correction / (jnp.sqrt(second_new / correction) + epsilon_adam)
    master_new = master - rate * (direction + decay * master)
    return (master_new, first_new, second_new)

def reference(tokens, cotangent, tags, lengths, key_mask, master_qkv, master_out, master_in, master_feed_output, master_vec, first_qkv, first_out, first_in, first_ffo, first_vec, second_qkv, second_out, second_in, second_ffo, second_moment_vector):
    positions = jnp.arange(SEQ_LEN, dtype=jnp.int32)
    inside = positions[None, :] < lengths[:, None]
    key_valid = inside & ((key_mask == 1) | (positions[None, :] == 0))
    key_bias = jnp.where(key_valid, 0.0, masked_score).astype(jnp.float32)
    query_valid = inside.astype(jnp.float32)
    masters = (master_qkv, master_out, master_in, master_feed_output, master_vec)
    firsts = (first_qkv, first_out, first_in, first_ffo, first_vec)
    seconds = (second_qkv, second_out, second_in, second_ffo, second_moment_vector)

    def forward(input_rows, params):
        shared_out = encoder_layer(input_rows, tuple((stacked[0] for stacked in params)), tags, key_bias)
        return encoder_layer(shared_out, tuple((stacked[1] for stacked in params)), tags, key_bias)
    result, pullback = jax.vjp(forward, tokens.astype(jnp.float32), masters)
    input_grad, grads = pullback(cotangent.astype(jnp.float32) * query_valid[:, :, None])
    rates = (matrix_rate * D ** (-0.5), matrix_rate * (D // 16) ** (-0.5), matrix_rate * D ** (-0.5), matrix_rate * (FF // 2) ** (-0.5), vector_rate)
    decays = (weight_decay, weight_decay, weight_decay, weight_decay, 0.0)
    updated = [adamw(masters[kind], firsts[kind], seconds[kind], grads[kind], rates[kind], decays[kind]) for kind in range(5)]
    return (result.astype(jnp.bfloat16), input_grad, updated[0][0], updated[1][0], updated[2][0], updated[3][0], updated[4][0], updated[0][1], updated[1][1], updated[2][1], updated[3][1], updated[4][1], updated[0][2], updated[1][2], updated[2][2], updated[3][2], updated[4][2])
```

```python
import functools
from types import SimpleNamespace
from typing import NamedTuple

import jax
import jax.numpy as jnp
from jax import lax
from jax.experimental import pallas as pl
from jax.experimental.pallas import tpu as pltpu
from jax.sharding import PartitionSpec as P

D = 512
H = 8
FF = 2048
STEP = 10


beta_decay = 0.5
epsilon_adam = 1e-08
weight_decay = 0.01
norm_epsilon = 1e-05
masked_score = -1000000000.0
vector_rate = 0.15
matrix_rate = 0.5


def layer_norm(pre_norm, gain_row, offset_row):
    centre_mean = jnp.mean(pre_norm, axis=-1, keepdims=True)
    centred = pre_norm - centre_mean
    variance = jnp.mean(centred * centred, axis=-1, keepdims=True)
    return centred * lax.rsqrt(variance + norm_epsilon) * gain_row + offset_row


def tanh_gelu_activation(inner_act):
    return jax.nn.gelu(inner_act, approximate=True)


def adamw(master, first, second, grad, rate, decay):
    first_new = beta_decay * first + (1.0 - beta_decay) * grad
    second_new = beta_decay * second + (1.0 - beta_decay) * grad * grad
    correction = 1.0 - beta_decay**STEP
    direction = first_new / correction / (jnp.sqrt(second_new / correction) + epsilon_adam)
    master_new = master - rate * (direction + decay * master)
    return (master_new, first_new, second_new)


def score_block(query_heads, key_heads, key_bias, score_scale):
    scores = jnp.einsum("qhd,khd->hqk", query_heads, key_heads, preferred_element_type=jnp.float32)
    return scores * score_scale + key_bias[None, None, :]


def forward_layer(input_rows, weights, tag_value, key_bias):
    w_qkv, w_out, w_in, w_ffo, vectors_low = weights
    vectors = vectors_low.astype(jnp.float32)
    model_width = w_out.shape[0]
    row_count = input_rows.shape[0]
    head_size = model_width // H
    score_scale = head_size ** (-0.5)
    direction = jnp.where(tag_value == 0, vectors[0], vectors[1])
    summed = input_rows + direction[None, :]
    summed_low = summed.astype(jnp.bfloat16)
    projected = jnp.dot(summed_low, w_qkv, preferred_element_type=jnp.float32)
    queries = (projected[:, :model_width] + vectors[2]).astype(jnp.bfloat16)
    keys_local = projected[:, model_width : 2 * model_width].astype(jnp.bfloat16)
    local_values = (projected[:, 2 * model_width :] + vectors[3]).astype(jnp.bfloat16)
    keys_all, values_all = (
        lax.all_gather(keys_local, "rep", axis=0, tiled=True),
        lax.all_gather(local_values, "rep", axis=0, tiled=True),
    )
    key_count = keys_all.shape[0]
    query_heads = queries.reshape(row_count, H, head_size)
    key_heads = keys_all.reshape(key_count, H, head_size)
    value_heads = values_all.reshape(key_count, H, head_size)
    scores = score_block(query_heads, key_heads, key_bias, score_scale)
    row_top = jnp.max(scores, axis=-1, keepdims=True)
    exponent_terms = jnp.exp(scores - row_top)
    totals = jnp.sum(exponent_terms, axis=-1, keepdims=True)
    soft_weights = exponent_terms / totals
    log_total = row_top + jnp.log(totals)
    context = jnp.einsum(
        "hqk,khd->qhd",
        soft_weights.astype(jnp.bfloat16),
        value_heads,
        preferred_element_type=jnp.float32,
    )
    context_low = context.reshape(row_count, model_width).astype(jnp.bfloat16)
    branch = jnp.dot(context_low, w_out, preferred_element_type=jnp.float32) + vectors[4]
    hidden, norm_first = jax.vjp(layer_norm, summed + branch, vectors[5], vectors[6])
    hidden_low = hidden.astype(jnp.bfloat16)
    inner_act = jnp.dot(hidden_low, w_in, preferred_element_type=jnp.float32) + vectors[
        10:
    ].reshape(-1)
    activated, gelu_pull = jax.vjp(tanh_gelu_activation, inner_act)
    activated_low = activated.astype(jnp.bfloat16)
    feed_out = jnp.dot(activated_low, w_ffo, preferred_element_type=jnp.float32) + vectors[7]
    result, norm_second = jax.vjp(layer_norm, hidden + feed_out, vectors[8], vectors[9])
    saved_state = (
        summed_low,
        query_heads,
        key_heads,
        value_heads,
        log_total,
        context_low,
        norm_first,
        hidden_low,
        gelu_pull,
        activated_low,
        norm_second,
    )
    return (result, saved_state)


def attention_grads(
    query_heads, key_heads, value_heads, log_total, context_heads, key_bias, score_scale
):
    row_count = query_heads.shape[0]
    model_width = query_heads.shape[1] * query_heads.shape[2]
    scores = score_block(query_heads, key_heads, key_bias, score_scale)
    soft_weights = jnp.exp(scores - log_total)
    grad_soft = jnp.einsum(
        "qhd,khd->hqk", context_heads, value_heads, preferred_element_type=jnp.float32
    )
    row_inner = jnp.sum(soft_weights * grad_soft, axis=-1, keepdims=True)
    grad_scores = (soft_weights * (grad_soft - row_inner) * score_scale).astype(jnp.bfloat16)
    grad_queries = jnp.einsum(
        "hqk,khd->qhd", grad_scores, key_heads, preferred_element_type=jnp.float32
    ).reshape(row_count, model_width)
    key_terms = jnp.einsum(
        "hqk,qhd->khd", grad_scores, query_heads, preferred_element_type=jnp.float32
    ).reshape(-1, model_width)
    value_terms = jnp.einsum(
        "hqk,qhd->khd",
        soft_weights.astype(jnp.bfloat16),
        context_heads,
        preferred_element_type=jnp.float32,
    ).reshape(-1, model_width)
    grad_keys, grad_values = (
        lax.psum_scatter(
            key_terms.astype(jnp.bfloat16), "rep", scatter_dimension=0, tiled=True
        ).astype(jnp.float32),
        lax.psum_scatter(
            value_terms.astype(jnp.bfloat16), "rep", scatter_dimension=0, tiled=True
        ).astype(jnp.float32),
    )
    return (grad_queries, grad_keys, grad_values)


def backward_layer(grad_result, saved_state, weights, tag_value, key_bias):
    w_qkv, w_out, w_in, w_ffo, vectors_low = weights
    (
        summed_low,
        query_heads,
        key_heads,
        value_heads,
        log_total,
        context_low,
        norm_first,
        hidden_low,
        gelu_pull,
        activated_low,
        norm_second,
    ) = saved_state
    model_width = w_out.shape[0]
    row_count = summed_low.shape[0]
    head_size = model_width // H
    score_scale = head_size ** (-0.5)
    grad_pre_two, grad_gain_two, grad_shift_two = norm_second(grad_result)
    grad_feed = grad_pre_two.astype(jnp.bfloat16)
    grad_bias_feed = jnp.sum(grad_feed.astype(jnp.float32), axis=0)
    grad_ffo = jnp.einsum("tf,td->fd", activated_low, grad_feed, preferred_element_type=jnp.float32)
    grad_activated = jnp.einsum("td,fd->tf", grad_feed, w_ffo, preferred_element_type=jnp.float32)
    grad_inner = gelu_pull(grad_activated)[0].astype(jnp.bfloat16)
    grad_bias_inner = jnp.sum(grad_inner.astype(jnp.float32), axis=0)
    grad_in = jnp.einsum("td,tf->df", hidden_low, grad_inner, preferred_element_type=jnp.float32)
    grad_hidden = grad_pre_two + jnp.einsum(
        "tf,df->td", grad_inner, w_in, preferred_element_type=jnp.float32
    )
    grad_pre_one, grad_gain_one, grad_shift_one = norm_first(grad_hidden)
    grad_branch = grad_pre_one.astype(jnp.bfloat16)
    grad_bias_out = jnp.sum(grad_branch.astype(jnp.float32), axis=0)
    grad_out_matrix = jnp.einsum(
        "te,td->ed", context_low, grad_branch, preferred_element_type=jnp.float32
    )
    grad_context = jnp.einsum(
        "td,ed->te", grad_branch, w_out, preferred_element_type=jnp.float32
    ).astype(jnp.bfloat16)
    context_heads = grad_context.reshape(row_count, H, head_size)
    grad_queries, grad_keys, grad_values = attention_grads(
        query_heads, key_heads, value_heads, log_total, context_heads, key_bias, score_scale
    )
    grad_joined = jnp.concatenate(
        [
            grad_queries.astype(jnp.bfloat16),
            grad_keys.astype(jnp.bfloat16),
            grad_values.astype(jnp.bfloat16),
        ],
        axis=1,
    )
    grad_qkv = jnp.einsum("td,te->de", summed_low, grad_joined, preferred_element_type=jnp.float32)
    grad_summed = grad_pre_one + jnp.einsum(
        "te,de->td", grad_joined, w_qkv, preferred_element_type=jnp.float32
    )
    column_sums = jnp.sum(grad_joined.astype(jnp.float32), axis=0)
    grad_direction = jnp.sum(grad_summed, axis=0)
    zero_row = jnp.zeros_like(grad_direction)
    grad_rows = jnp.stack(
        [
            jnp.where(tag_value == 0, grad_direction, zero_row),
            jnp.where(tag_value == 1, grad_direction, zero_row),
            column_sums[:model_width],
            column_sums[2 * model_width :],
            grad_bias_out,
            grad_gain_one,
            grad_shift_one,
            grad_bias_feed,
            grad_gain_two,
            grad_shift_two,
        ],
        axis=0,
    )
    grad_vectors = jnp.concatenate([grad_rows, grad_bias_inner.reshape(-1, model_width)], axis=0)
    return (grad_summed, (grad_qkv, grad_out_matrix, grad_in, grad_ffo, grad_vectors))


def reduce_layer(grads):
    shards = (
        lax.psum_scatter(grads[0], "fsdp", scatter_dimension=0, tiled=True),
        lax.psum_scatter(grads[1], "fsdp", scatter_dimension=0, tiled=True),
        lax.psum_scatter(grads[2], "fsdp", scatter_dimension=0, tiled=True),
        lax.psum_scatter(grads[3], "fsdp", scatter_dimension=0, tiled=True),
        lax.psum_scatter(grads[4], "fsdp", scatter_dimension=1, tiled=True),
    )
    return (
        lax.psum(shards[0].astype(jnp.bfloat16), "rep").astype(jnp.float32),
        lax.psum(shards[1].astype(jnp.bfloat16), "rep").astype(jnp.float32),
        lax.psum(shards[2].astype(jnp.bfloat16), "rep").astype(jnp.float32),
        lax.psum(shards[3].astype(jnp.bfloat16), "rep").astype(jnp.float32),
        lax.psum(shards[4].astype(jnp.bfloat16), "rep").astype(jnp.float32),
    )


def body(
    tokens,
    cotangent,
    tags,
    lengths,
    key_mask,
    master_qkv,
    master_out,
    master_in,
    master_feed_output,
    master_vec,
    first_qkv,
    first_out,
    first_in,
    first_ffo,
    first_vec,
    second_qkv,
    second_out,
    second_in,
    second_ffo,
    second_moment_vector,
):
    row_count = tokens.shape[1]
    key_count = key_mask.shape[1]
    start_row = lax.axis_index("rep") * row_count
    query_pos = start_row + jnp.arange(row_count, dtype=jnp.int32)
    key_pos = jnp.arange(key_count, dtype=jnp.int32)
    seq_length = lengths[0]
    tag_value = tags[0]
    key_valid = (key_pos < seq_length) & ((key_mask[0] == 1) | (key_pos == 0))
    key_bias = jnp.where(key_valid, 0.0, masked_score).astype(jnp.float32)
    query_valid = (query_pos < seq_length).astype(jnp.float32)
    masters = (master_qkv, master_out, master_in, master_feed_output, master_vec)
    firsts = (first_qkv, first_out, first_in, first_ffo, first_vec)
    seconds = (second_qkv, second_out, second_in, second_ffo, second_moment_vector)
    shared = (
        lax.all_gather(master_qkv[0].astype(jnp.bfloat16), "fsdp", axis=0, tiled=True),
        lax.all_gather(master_out[0].astype(jnp.bfloat16), "fsdp", axis=0, tiled=True),
        lax.all_gather(master_in[0].astype(jnp.bfloat16), "fsdp", axis=0, tiled=True),
        lax.all_gather(master_feed_output[0].astype(jnp.bfloat16), "fsdp", axis=0, tiled=True),
        lax.all_gather(master_vec[0].astype(jnp.bfloat16), "fsdp", axis=1, tiled=True),
    )
    shared_out, saved_shared = forward_layer(
        tokens[0].astype(jnp.float32), shared, tag_value, key_bias
    )
    unique = (
        lax.all_gather(master_qkv[1].astype(jnp.bfloat16), "fsdp", axis=0, tiled=True),
        lax.all_gather(master_out[1].astype(jnp.bfloat16), "fsdp", axis=0, tiled=True),
        lax.all_gather(master_in[1].astype(jnp.bfloat16), "fsdp", axis=0, tiled=True),
        lax.all_gather(master_feed_output[1].astype(jnp.bfloat16), "fsdp", axis=0, tiled=True),
        lax.all_gather(master_vec[1].astype(jnp.bfloat16), "fsdp", axis=1, tiled=True),
    )
    final_out, saved_unique = forward_layer(shared_out, unique, tag_value, key_bias)
    grad_final = cotangent[0].astype(jnp.float32) * query_valid[:, None]
    unique_back = (
        lax.all_gather(master_qkv[1].astype(jnp.bfloat16), "fsdp", axis=0, tiled=True),
        lax.all_gather(master_out[1].astype(jnp.bfloat16), "fsdp", axis=0, tiled=True),
        lax.all_gather(master_in[1].astype(jnp.bfloat16), "fsdp", axis=0, tiled=True),
        lax.all_gather(master_feed_output[1].astype(jnp.bfloat16), "fsdp", axis=0, tiled=True),
        lax.all_gather(master_vec[1].astype(jnp.bfloat16), "fsdp", axis=1, tiled=True),
    )
    grad_middle, unique_grads = backward_layer(
        grad_final, saved_unique, unique_back, tag_value, key_bias
    )
    reduced_unique = reduce_layer(unique_grads)
    grad_inputs, shared_grads = backward_layer(
        grad_middle, saved_shared, shared, tag_value, key_bias
    )
    reduced_shared = reduce_layer(shared_grads)
    rates = (
        matrix_rate * D ** (-0.5),
        matrix_rate * (D // 16) ** (-0.5),
        matrix_rate * D ** (-0.5),
        matrix_rate * (FF // 2) ** (-0.5),
        vector_rate,
    )
    decays = (weight_decay, weight_decay, weight_decay, weight_decay, 0.0)
    updated = []
    for kind_index in range(5):
        grad_stack = jnp.stack([reduced_shared[kind_index], reduced_unique[kind_index]], axis=0)
        updated.append(
            adamw(
                masters[kind_index],
                firsts[kind_index],
                seconds[kind_index],
                grad_stack,
                rates[kind_index],
                decays[kind_index],
            )
        )
    return (
        final_out.astype(jnp.bfloat16)[None],
        grad_inputs[None],
        updated[0][0],
        updated[1][0],
        updated[2][0],
        updated[3][0],
        updated[4][0],
        updated[0][1],
        updated[1][1],
        updated[2][1],
        updated[3][1],
        updated[4][1],
        updated[0][2],
        updated[1][2],
        updated[2][2],
        updated[3][2],
        updated[4][2],
    )


BF = jnp.bfloat16
F32 = jnp.float32
MESH = pl.DeviceIdType.MESH
KIND_K, KIND_V, KIND_Q, KIND_O, KIND_I, KIND_F = KINDS = tuple(range(6))
VMEM_BYTES = 60 << 20


def nt_dot(left, right):
    return lax.dot_general(left, right, (((1,), (1,)), ((), ())), preferred_element_type=F32)


def nn_dot(left, right):
    return jnp.dot(left, right, preferred_element_type=F32)


def remote(src, dst, send_sem, recv_sem, device):
    return pltpu.make_async_remote_copy(
        src_ref=src,
        dst_ref=dst,
        send_sem=send_sem,
        recv_sem=recv_sem,
        device_id=device,
        device_id_type=MESH,
    )


class ForwardIn(NamedTuple):
    tok: object
    cot: object
    meta: object
    vecb: object
    masters: object


class Saved(NamedTuple):
    w_o: object
    vec_o: object
    meta_o: object
    cot_o: object
    y_o: object
    at_o: object
    q_o: object
    k_o: object
    v_o: object
    lse_o: object
    ct_o: object
    ctp_o: object
    n1_o: object
    r1_o: object
    ht_o: object
    g_o: object
    gp_o: object
    n2_o: object
    r2_o: object


class ForwardScratch(NamedTuple):
    w: object
    stages: object
    vecg: object
    vec: object
    metab: object
    msel: object
    tokb: object
    A32: object
    Ab: object
    ATp: object
    Q: object
    K: object
    V: object
    lse: object
    CT: object
    CTp: object
    C: object
    N1: object
    r1: object
    H32: object
    Hb: object
    HTp: object
    G: object
    Gp: object
    N2: object
    r2: object
    X: object
    Yb: object
    msem: object
    xsem: object
    osem: object
    gs: object
    gr: object
    vs: object
    vr: object
    xs: object
    xr: object
    ks: object
    kr: object


class BackwardOut(NamedTuple):
    fin: object
    vec_g: object
    yo: object
    dxo: object


class BackwardScratch(NamedTuple):
    g: object
    landing: object
    half_y: object
    half_x: object
    quarter_x: object
    quarter_y: object
    level: object
    total: object
    w: object
    AT: object
    Q: object
    K: object
    V: object
    lse: object
    CT: object
    CTp: object
    N1: object
    r1: object
    HT: object
    G: object
    Gp: object
    N2: object
    r2: object
    vec: object
    msel: object
    cotb: object
    dy: object
    dpre: object
    dF: object
    dFT: object
    dU: object
    dZ: object
    delta: object
    dQT: object
    dvb: object
    dkp: object
    dvp: object
    dkr: object
    dvr: object
    vg: object
    va: object
    vrecv: object
    vb: object
    vt: object
    lsem: object
    ssem: object
    fsem: object
    gs: object
    gr: object
    xs: object
    xr: object
    ks: object
    kr: object
    vs: object
    vr: object


class UpdateIn(NamedTuple):
    fin: object
    fvec: object
    y: object
    dx: object
    masters: object
    firsts: object
    seconds: object


class UpdateOut(NamedTuple):
    out: object
    grad: object
    new_masters: object
    new_firsts: object
    new_seconds: object


def named(parts, refs):
    fields, at = {}, 0
    for part in parts:
        leaves, tree = jax.tree.flatten(part)
        fields.update(tree.unflatten(refs[at : at + len(leaves)])._asdict())
        at += len(leaves)
    return SimpleNamespace(**fields)


def call_kernel(kernel, args, outs, scratch, spec, **options):
    leaves, _ = jax.tree.flatten(args)
    out_leaves, out_tree = jax.tree.flatten(outs)
    parts = (args, outs) if scratch is None else (args, outs, scratch)
    empty = jax.tree.map(lambda leaf: 0, parts)
    results = pl.pallas_call(
        functools.partial(kernel, empty),
        out_shape=out_leaves,
        in_specs=[spec] * len(leaves),
        out_specs=[spec] * len(out_leaves),
        scratch_shapes=() if scratch is None else jax.tree.leaves(scratch),
        compiler_params=pltpu.CompilerParams(**options),
    )(*leaves)
    return out_tree.unflatten(results)


class Place:
    def __init__(self):
        self.r = lax.axis_index("rep")
        self.f = lax.axis_index("fsdp")
        self.z = lax.div(self.f, 4)
        self.y = lax.rem(lax.div(self.f, 2), 2)
        self.c = lax.rem(self.f, 2)
        self.xn = (1 - self.r, self.f)
        self.yn = (self.r, self.f + 2 - 4 * self.y)
        self.cn = (self.r, self.f + 1 - 2 * self.c)
        self.dn = (1 - self.r, self.f + 1 - 2 * self.c)

    def zn(self, step, levels):
        other = lax.rem(self.z + step, levels)
        return other, (self.r, other * 4 + 2 * self.y + self.c)


def parity_rows(rows, shards):
    blocks = rows.reshape(shards // 2, 2, rows.shape[0] // shards, rows.shape[1])
    half = rows.shape[0] // 2
    return blocks[:, 0].reshape(half, rows.shape[1]), blocks[:, 1].reshape(half, rows.shape[1])


def lane_masks():
    lane = lax.broadcasted_iota(jnp.int32, (16, 128), 1)
    low = (lane < 64).astype(F32)
    spots = (lax.rem(lane, 64) == 0).astype(F32)
    return low[:1].astype(BF), (1.0 - low[:1]).astype(BF), spots[:1].astype(BF)


def sizes_of(mesh_n, width, inner):
    shard = width // mesh_n
    rows = [shard // 2] * 6
    rows[KIND_F] = inner // mesh_n // 2
    cols = [width] * 6
    cols[KIND_I] = inner
    return rows, cols


def forward_kernel(parts, levels, eps, *refs):
    R = named(parts, refs)
    me = Place()
    r, f, z, y, c = me.r, me.f, me.z, me.y, me.c
    shards = levels * 4
    S, D = R.A32.shape
    FF = R.G.shape[1]
    ha = levels // 2
    first, second = pl.ds(0, ha), pl.ds(ha, levels - ha)
    source = ((0, D), (0, 2 * D), (0, 0), (1, 0), (2, 0), (3, 0))

    half_loads = {}
    for l in range(2):
        for at, (master, stage) in enumerate(zip(R.masters, R.stages)):
            rows = stage.shape[1]
            cp = pltpu.make_async_copy(master.at[l, pl.ds(r * rows, rows)], stage.at[l], R.msem.at[l, at])
            cp.start()
            half_loads[(l, at)] = cp
    vec_local = pltpu.make_async_copy(R.vecb, R.vecg.at[f], R.xsem.at[0])
    vec_local.start()
    meta_local = pltpu.make_async_copy(R.meta, R.metab.at[0], R.xsem.at[1])
    meta_local.start()

    barrier = pltpu.get_barrier_semaphore()
    peers = [(r, lax.rem(f + s, shards)) for s in range(1, shards)] + [me.xn, me.dn]
    for peer in peers:
        pl.semaphore_signal(barrier, inc=1, device_id=peer, device_id_type=MESH)
    pl.semaphore_wait(barrier, len(peers))

    chunks = [(kind, l) for l in range(2) for kind in KINDS]
    gs, gr = R.gs, R.gr
    pending = []

    def start(cp):
        cp.start()
        pending.append(cp)
        return cp

    loaded = set()
    stage_copies = {}

    def g_z(i):
        kind, l = chunks[i]
        w = R.w[kind]
        at, offset = source[kind]
        if (l, at) not in loaded:
            half_loads[(l, at)].wait()
            loaded.add((l, at))
        w[l, z, y, c, r] = R.stages[at][l][:, offset : offset + w.shape[-1]].astype(BF)
        cps = []
        for s in range(1, levels):
            _, dev = me.zn(s, levels)
            spot = w.at[l, z, y, c, r]
            cps.append(start(remote(spot, spot, gs.at[i, s - 1], gr.at[i, s - 1], dev)))
        stage_copies[i] = cps

    def g_1(i):
        kind, l = chunks[i]
        w = R.w[kind]
        for cp in stage_copies[i]:
            cp.wait_recv()
        a, b = w.at[l, first, y, c, r], w.at[l, second, y, c, r]
        stage_copies[i] = [
            start(remote(a, a, gs.at[i, levels - 1], gr.at[i, levels - 1], me.xn)),
            start(remote(b, b, gs.at[i, levels], gr.at[i, levels], me.yn)),
        ]

    def g_2(i):
        kind, l = chunks[i]
        w = R.w[kind]
        for cp in stage_copies[i]:
            cp.wait_recv()
        a, b = w.at[l, first, y, c], w.at[l, second, :, c, r]
        stage_copies[i] = [
            start(remote(a, a, gs.at[i, levels + 1], gr.at[i, levels + 1], me.yn)),
            start(remote(b, b, gs.at[i, levels + 2], gr.at[i, levels + 2], me.xn)),
        ]

    def g_core(i):
        kind, l = chunks[i]
        w = R.w[kind]
        for cp in stage_copies[i]:
            cp.wait_recv()
        a = w.at[l, :, :, c]
        stage_copies[i] = [start(remote(a, a, gs.at[i, levels + 3], gr.at[i, levels + 3], me.cn))]

    def g_ready(i):
        for cp in stage_copies.pop(i):
            cp.wait_recv()

    tick_at = [0]

    def tick():
        t = tick_at[0]
        tick_at[0] += 1
        for lag, step in ((4, g_ready), (3, g_core), (2, g_2), (1, g_1), (0, g_z)):
            if 0 <= t - lag < len(chunks):
                step(t - lag)

    g_z(0)
    meta_cp = start(remote(R.meta, R.metab.at[1], R.xs.at[0], R.xr.at[0], me.cn))
    vec_cps = []
    for s in range(1, shards):
        spot = R.vecg.at[f]
        vec_cps.append((s, remote(R.vecb, spot, R.vs.at[s - 1], R.vr.at[s - 1], (r, lax.rem(f + s, shards)))))
    for _, cp in vec_cps:
        start(cp)
    tok_far = remote(R.tok.at[0], R.tokb, R.xs.at[1], R.xr.at[1], me.dn)
    tok_near = pltpu.make_async_copy(R.tok.at[0], R.tokb, R.xsem.at[2])
    stays = c == r

    @pl.when(stays)
    def _():
        tok_near.start()

    @pl.when(jnp.logical_not(stays))
    def _():
        tok_far.start()

    tick_at[0] = 1
    tick()
    tick()

    vec_local.wait()
    meta_local.wait()
    meta_cp.wait_recv()
    for _, cp in vec_cps:
        cp.wait_recv()
    keep = stays.astype(F32)
    msel = R.msel
    msel[...] = (R.metab[0].astype(F32) * keep + R.metab[1].astype(F32) * (1.0 - keep)).astype(BF)
    vec = R.vec
    for zz in range(levels):
        vec[:, 128 * zz : 128 * zz + 128] = jnp.sum(R.vecg[4 * zz : 4 * zz + 4].astype(F32), axis=0)
    tag_row = msel[2 * S : 2 * S + 16].astype(F32)[:1]
    tag_row = jnp.concatenate([tag_row] * (D // 128), axis=1)
    low, high, spots = lane_masks()

    out_copies = {}
    out_at = [0]

    def out(ref, dst, view=None):
        cp = pltpu.make_async_copy(ref if view is None else view, dst, R.osem.at[out_at[0]])
        out_at[0] += 1
        cp.start()
        out_copies[(id(ref), view is not None and out_at[0])] = cp

    def settle(ref):
        if (id(ref), False) in out_copies:
            out_copies.pop((id(ref), False)).wait()

    @pl.when(stays)
    def _():
        tok_near.wait()

    @pl.when(jnp.logical_not(stays))
    def _():
        tok_far.wait()

    T = 128
    for l in range(2):
        e = lambda row: vec[16 * l + row : 16 * l + row + 1, :]
        direction = e(0) * (1.0 - tag_row) + e(1) * tag_row
        A32, Ab, Q, K, V, CT = R.A32, R.Ab, R.Q, R.K, R.V, R.CT
        x_in = R.tokb if l == 0 else R.X
        summed = x_in[...].astype(F32) + direction
        A32[...] = summed
        Ab[...] = summed.astype(BF)
        at = Ab[...].T
        even, odd = parity_rows(at, shards)
        settle(R.ATp)
        R.ATp[: D // 2] = even
        R.ATp[D // 2 :] = odd
        out(R.ATp, R.at_o.at[l])

        def weight(kind, lo=0, hi=None):
            w = R.w[kind]
            hi = w.shape[-1] if hi is None else hi
            value = w[l, :, :, :, :, :, lo:hi]
            return value.reshape(-1, hi - lo)

        if l == 0:
            tick()
            tick()
        K[l, c] = nn_dot(Ab[...], weight(KIND_K)).astype(BF)
        k_cp = start(remote(K.at[l, c], K.at[l, c], R.ks.at[l, 0], R.kr.at[l, 0], me.cn))
        if l == 0:
            tick()
        V[l, c] = (nn_dot(Ab[...], weight(KIND_V)) + e(3)).astype(BF)
        v_cp = start(remote(V.at[l, c], V.at[l, c], R.ks.at[l, 1], R.kr.at[l, 1], me.cn))
        if l == 0:
            tick()
        settle(R.Q)
        q = (nn_dot(Ab[...], weight(KIND_Q)) + e(2)).astype(BF)
        Q[...] = (q.astype(F32) * 0.125).astype(BF)
        out(R.Q, R.q_o.at[l])
        k_cp.wait_recv()
        v_cp.wait_recv()
        out(K, R.k_o.at[l], K.at[l])
        out(V, R.v_o.at[l], V.at[l])
        lse = R.lse
        settle(R.lse)
        settle(R.CT)
        bias_rows = msel[: 2 * S]

        def pair(j, carry):
            sl = pl.ds(pl.multiple_of(j * 128, 128), 128)
            k2 = K[l, :, :, sl].reshape(2 * S, 128)
            v2t = V[l, :, :, sl].reshape(2 * S, 128).T
            q2 = Q[:, sl]
            for h in range(2):
                mine, other = (low, high) if h == 0 else (high, low)
                kh = k2 * mine + bias_rows * other
                qh = q2 * mine + spots * other
                for part in range(S // 256):
                    cols = slice(part * 256, part * 256 + 256)
                    st = nt_dot(kh, qh[cols])
                    top = jnp.max(st, axis=0, keepdims=True)
                    p = jnp.exp(st - top)
                    total = jnp.sum(p, axis=0, keepdims=True)
                    ctx = nn_dot(v2t, p.astype(BF))[64 * h : 64 * h + 64]
                    rows = pl.ds(pl.multiple_of(j * 128 + 64 * h, 64), 64)
                    CT[rows, cols] = (ctx / total).astype(BF)
                    lse[j, h : h + 1, cols] = top + jnp.log(total)
            return carry

        pairs = D // 128
        lax.fori_loop(0, pairs // 2, pair, 0)
        if l == 0:
            tick()
        lax.fori_loop(pairs // 2, pairs, pair, 0)
        out(R.lse, R.lse_o.at[l])
        out(R.CT, R.ct_o.at[l])
        even, odd = parity_rows(CT[...], shards)
        settle(R.CTp)
        R.CTp[: D // 2] = even
        R.CTp[D // 2 :] = odd
        out(R.CTp, R.ctp_o.at[l])
        R.C[...] = CT[...].T
        settle(R.N1)
        settle(R.r1)

        def norm_one(t, carry):
            rows = pl.ds(pl.multiple_of(t * T, T), T)
            pre = A32[rows] + nn_dot(R.C[rows], weight(KIND_O)) + e(4)
            mean = jnp.mean(pre, axis=-1, keepdims=True)
            centred = pre - mean
            rstd = lax.rsqrt(jnp.mean(centred * centred, axis=-1, keepdims=True) + eps)
            n1 = centred * rstd
            hidden = n1 * e(5) + e(6)
            R.N1[rows] = n1
            R.r1[rows] = jnp.broadcast_to(rstd, (T, 128))
            R.H32[rows] = hidden
            R.Hb[rows] = hidden.astype(BF)
            return carry

        lax.fori_loop(0, S // T, norm_one, 0)
        out(R.N1, R.n1_o.at[l])
        out(R.r1, R.r1_o.at[l])
        even, odd = parity_rows(R.Hb[...].T, shards)
        settle(R.HTp)
        R.HTp[: D // 2] = even
        R.HTp[D // 2 :] = odd
        out(R.HTp, R.ht_o.at[l])
        if l == 0:
            tick()
        settle(R.G)
        settle(R.Gp)

        def inner(t, carry):
            rows = pl.ds(pl.multiple_of(t * T, T), T)
            hb = R.Hb[rows]
            for b in range(FF // D):
                u = nn_dot(hb, weight(KIND_I, b * D, b * D + D)) + e(10 + b)
                u2 = u * u
                th = jnp.tanh(u * (0.7978845608028654 + 0.035677408136300125 * u2))
                half = 0.5 + 0.5 * th
                slope = 0.7978845608028654 + 0.10703222440890038 * u2
                R.G[rows, b * D : b * D + D] = (u * half).astype(BF)
                R.Gp[rows, b * D : b * D + D] = (half + 0.5 * u * (1.0 - th * th) * slope).astype(BF)
            return carry

        lax.fori_loop(0, S // T, inner, 0)
        out(R.G, R.g_o.at[l])
        out(R.Gp, R.gp_o.at[l])
        if l == 0:
            tick()
        settle(R.N2)
        settle(R.r2)

        def norm_two(t, carry):
            rows = pl.ds(pl.multiple_of(t * T, T), T)
            pre = R.H32[rows] + nn_dot(R.G[rows], weight(KIND_F)) + e(7)
            mean = jnp.mean(pre, axis=-1, keepdims=True)
            centred = pre - mean
            rstd = lax.rsqrt(jnp.mean(centred * centred, axis=-1, keepdims=True) + eps)
            n2 = centred * rstd
            R.N2[rows] = n2
            R.r2[rows] = jnp.broadcast_to(rstd, (T, 128))
            R.X[rows] = n2 * e(8) + e(9)
            return carry

        lax.fori_loop(0, S // T, norm_two, 0)
        out(R.N2, R.n2_o.at[l])
        out(R.r2, R.r2_o.at[l])
        if l == 0:
            while tick_at[0] < len(chunks) + 4:
                tick()
            for kind in KINDS:
                out(R.w[kind], R.w_o[kind])

    R.Yb[...] = R.X[...].astype(BF)
    out(R.Yb, R.y_o)
    out(vec, R.vec_o)
    out(msel, R.meta_o)
    cot_far = remote(R.cot.at[0], R.cot_o, R.xs.at[2], R.xr.at[2], me.dn)
    cot_near = pltpu.make_async_copy(R.cot.at[0], R.cot_o, R.xsem.at[3])

    @pl.when(stays)
    def _():
        cot_near.start()

    @pl.when(jnp.logical_not(stays))
    def _():
        cot_far.start()

    for cp in out_copies.values():
        cp.wait()
    for cp in pending:
        cp.wait_send()

    @pl.when(stays)
    def _():
        cot_near.wait()

    @pl.when(jnp.logical_not(stays))
    def _():
        cot_far.wait()


def backward_kernel(parts, levels, *refs):
    R = named(parts, refs)
    me = Place()
    r, f, z, y, c = me.r, me.f, me.z, me.y, me.c
    shards = levels * 4
    S, D = R.dy.shape
    FF = R.G.shape[1]
    ha = levels // 2
    hb = levels - ha
    first, second = pl.ds(0, ha), pl.ds(ha, hb)
    saved = list(zip(R.w, R.w_o)) + [
        (R.AT, R.at_o), (R.Q, R.q_o), (R.K, R.k_o), (R.V, R.v_o), (R.lse, R.lse_o), (R.CT, R.ct_o), (R.CTp, R.ctp_o),
        (R.N1, R.n1_o), (R.r1, R.r1_o), (R.HT, R.ht_o), (R.G, R.g_o), (R.Gp, R.gp_o), (R.N2, R.n2_o), (R.r2, R.r2_o),
    ]
    order = {id(ref): at for at, (ref, _) in enumerate(saved)}
    loads = {}

    def load(ref, l):
        at = order[id(ref)]
        cp = pltpu.make_async_copy(saved[at][1].at[l], ref, R.lsem.at[l, at])
        cp.start()
        loads[id(ref)] = cp

    def use(ref):
        if id(ref) in loads:
            loads.pop(id(ref)).wait()
        return ref

    small = []
    for at, (dst, src) in enumerate(((R.vec, R.vec_o), (R.msel, R.meta_o), (R.cotb, R.cot_o))):
        cp = pltpu.make_async_copy(src, dst, R.ssem.at[at])
        cp.start()
        small.append(cp)
    wk, wv, wq, wo, wi, wf = R.w
    for ref in (R.N2, R.r2, R.G, wf, R.Gp, R.HT, wi, R.N1, R.r1, R.CTp, wo, R.CT, R.K, R.V, R.Q, R.lse, R.AT, wq, wk, wv):
        load(ref, 1)

    barrier = pltpu.get_barrier_semaphore()
    peers = [me.zn(s, levels)[1] for s in range(1, levels)] + [me.xn, me.yn, me.cn, me.dn]
    for peer in peers:
        pl.semaphore_signal(barrier, inc=1, device_id=peer, device_id_type=MESH)
    pl.semaphore_wait(barrier, len(peers))

    pending = []

    def start(cp):
        cp.start()
        pending.append(cp)
        return cp

    stays = c == r
    y_far = remote(R.y_o, R.yo, R.xs.at[0], R.xr.at[0], me.dn)
    y_near = pltpu.make_async_copy(R.y_o, R.yo, R.ssem.at[3])

    @pl.when(stays)
    def _():
        y_near.start()

    @pl.when(jnp.logical_not(stays))
    def _():
        y_far.start()

    gs, gr = R.gs, R.gr
    chunks = [(kind, l) for l in (1, 0) for kind in (KIND_F, KIND_I, KIND_O, KIND_Q, KIND_K, KIND_V)]
    index = {chunk: at for at, chunk in enumerate(chunks)}
    flight = {}
    stage = {}
    fin_copies = []

    def rs_core(i):
        kind, l = chunks[i]
        g = R.g[kind]
        spot = g.at[0, 0] if l == 1 else R.landing[kind]
        flight[i] = [start(remote(g.at[l, 1 - c], spot, gs.at[i, 0], gr.at[i, 0], me.cn))]

    def rs_1(i):
        kind, l = chunks[i]
        g = R.g[kind]
        g[l, c] = g[l, c] + (g[0, 0] if l == 1 else R.landing[kind][...])
        flight[i] = [
            start(remote(g.at[l, c, first, 1 - y], R.half_y[kind].at[l], gs.at[i, 1], gr.at[i, 1], me.yn)),
            start(remote(g.at[l, c, second, :, 1 - r], R.half_x[kind].at[l], gs.at[i, 2], gr.at[i, 2], me.xn)),
        ]

    def rs_2(i):
        kind, l = chunks[i]
        g = R.g[kind]
        g[l, c, first, y] = g[l, c, first, y] + R.half_y[kind][l]
        g[l, c, second, :, r] = g[l, c, second, :, r] + R.half_x[kind][l]
        flight[i] = [
            start(remote(g.at[l, c, first, y, 1 - r], R.quarter_x[kind].at[l], gs.at[i, 3], gr.at[i, 3], me.xn)),
            start(remote(g.at[l, c, second, 1 - y, r], R.quarter_y[kind].at[l], gs.at[i, 4], gr.at[i, 4], me.yn)),
        ]

    def rs_3(i):
        kind, l = chunks[i]
        g = R.g[kind]
        g[l, c, first, y, r] = g[l, c, first, y, r] + R.quarter_x[kind][l]
        g[l, c, second, y, r] = g[l, c, second, y, r] + R.quarter_y[kind][l]
        flight[i] = []
        for s in range(1, levels):
            there, dev = me.zn(s, levels)
            flight[i].append(
                start(remote(g.at[l, c, there, y, r], R.level[kind].at[l, s - 1], gs.at[i, 4 + s], gr.at[i, 4 + s], dev))
            )

    def rs_4(i):
        kind, l = chunks[i]
        g, fin = R.g[kind], R.total[kind]
        total = g[l, c, z, y, r].astype(F32)
        for s in range(levels - 1):
            total = total + R.level[kind][l, s].astype(F32)
        fin[l, r] = total.astype(BF)
        flight[i] = [start(remote(fin.at[l, r], fin.at[l, r], gs.at[i, 4 + levels], gr.at[i, 4 + levels], me.xn))]

    def rs_5(i):
        kind, l = chunks[i]
        cp = pltpu.make_async_copy(R.total[kind].at[l], R.fin[kind].at[l], R.fsem.at[i])
        cp.start()
        fin_copies.append(cp)

    steps = (rs_core, rs_1, rs_2, rs_3, rs_4, rs_5)

    def advance(i):
        at = stage.get(i, 0)
        for cp in flight.pop(i, ()):
            cp.wait_recv()
        steps[at](i)
        stage[i] = at + 1

    started = []

    def push():
        for i in started:
            if stage[i] < len(steps):
                advance(i)

    def begin(kind, l):
        i = index[(kind, l)]
        advance(i)
        started.append(i)

    for cp in small:
        cp.wait()
    vec, msel = R.vec, R.msel
    tag_row = msel[2 * S : 2 * S + 16].astype(F32)[:1]
    tag_row = jnp.concatenate([tag_row] * (D // 128), axis=1)
    low, high, spots = lane_masks()
    low32 = low.astype(F32)
    vg = R.vg
    vg[...] = jnp.zeros_like(vg)
    R.dy[...] = R.cotb[...].astype(F32)
    T = 128
    dy, dpre, dF, dFT, dU, dZ = R.dy, R.dpre, R.dF, R.dFT, R.dU, R.dZ

    def fold(value):
        return jnp.sum(value.reshape(value.shape[0] // 8, 8, value.shape[1]), axis=0)

    zero8 = jnp.zeros((8, D), F32)

    for l in (1, 0):
        base = 16 * l
        e = lambda row: vec[base + row : base + row + 1, :]

        def put(row, value):
            vg[base + row : base + row + 1, :] = value

        def weight(kind):
            w = R.w[kind]
            return w[...].reshape(-1, w.shape[-1])

        N2, r2 = use(R.N2), use(R.r2)

        def norm_two(t, carry):
            s7, s8, s9 = carry
            rows = pl.ds(pl.multiple_of(t * T, T), T)
            g, n = dy[rows], N2[rows]
            dn = g * e(8)
            m1 = jnp.mean(dn, axis=-1, keepdims=True)
            m2 = jnp.mean(dn * n, axis=-1, keepdims=True)
            d = r2[rows][:, :1] * (dn - m1 - n * m2)
            dpre[rows] = d
            db = d.astype(BF)
            dF[rows] = db
            dFT[:, rows] = db.T
            return s7 + fold(db.astype(F32)), s8 + fold(g * n), s9 + fold(g)

        s7, s8, s9 = lax.fori_loop(0, S // T, norm_two, (zero8, zero8, zero8))
        put(7, jnp.sum(s7, axis=0, keepdims=True))
        put(8, jnp.sum(s8, axis=0, keepdims=True))
        put(9, jnp.sum(s9, axis=0, keepdims=True))
        push()
        G = use(R.G)
        gf = R.g[KIND_F]
        piece = 2 * FF // shards

        def grad_f(t, carry):
            d = nn_dot(dFT[...], G[:, pl.ds(pl.multiple_of(t * piece, piece), piece)]).astype(BF)
            zz, yy = lax.div(t, 2), lax.rem(t, 2)
            half = piece // 2
            gf[l, 0, zz, yy] = d[:, :half].reshape(2, D // 2, half)
            gf[l, 1, zz, yy] = d[:, half:].reshape(2, D // 2, half)
            return carry

        lax.fori_loop(0, shards // 2, grad_f, 0)
        begin(KIND_F, l)
        if l == 1:
            for ref in (R.N2, R.r2, R.G):
                load(ref, 0)
        use(R.w[KIND_F])
        Gp = use(R.Gp)
        zero_in = tuple(zero8 for _ in range(FF // D))

        def grad_inner(t, carry):
            rows = pl.ds(pl.multiple_of(t * T, T), T)
            sums = []
            wf = R.w[KIND_F]
            for b in range(FF // D):
                quarter = wf[b * (levels // (FF // D)) : (b + 1) * (levels // (FF // D))].reshape(D, D)
                da = nt_dot(dF[rows], quarter)
                du = (da * Gp[rows, b * D : b * D + D].astype(F32)).astype(BF)
                dU[rows, b * D : b * D + D] = du
                sums.append(carry[b] + fold(du.astype(F32)))
            return tuple(sums)

        sums = lax.fori_loop(0, S // T, grad_inner, zero_in)
        for b in range(FF // D):
            put(10 + b, jnp.sum(sums[b], axis=0, keepdims=True))
        push()
        if l == 1:
            load(R.w[KIND_F], 0)
            load(R.Gp, 0)
        HT = use(R.HT)
        gi = R.g[KIND_I]
        rows_i = 2 * R.g[KIND_I].shape[-2]

        def grad_in(t, carry):
            rows = pl.ds(pl.multiple_of(t * T, T), T)
            cc, zz = lax.div(t, D // 2 // T), lax.rem(t, D // 2 // T)
            span = levels * T // (D // 2)
            for b in range(FF // D):
                d = nn_dot(HT[rows], dU[:, b * D : b * D + D]).astype(BF)
                gi[l, cc, pl.ds(zz * span, span), :, :, :, b * D : b * D + D] = d.reshape(span, 2, 2, rows_i // 2, D)
            return carry

        lax.fori_loop(0, D // T, grad_in, 0)
        begin(KIND_I, l)
        if l == 1:
            load(R.HT, 0)
        use(R.w[KIND_I])
        N1, r1 = use(R.N1), use(R.r1)

        def norm_one(t, carry):
            s4, s5, s6 = carry
            rows = pl.ds(pl.multiple_of(t * T, T), T)
            g = dpre[rows] + nt_dot(dU[rows], weight(KIND_I))
            n = N1[rows]
            dn = g * e(5)
            m1 = jnp.mean(dn, axis=-1, keepdims=True)
            m2 = jnp.mean(dn * n, axis=-1, keepdims=True)
            d = r1[rows][:, :1] * (dn - m1 - n * m2)
            dy[rows] = d
            db = d.astype(BF)
            dZ[rows] = db
            return s4 + fold(db.astype(F32)), s5 + fold(g * n), s6 + fold(g)

        s4, s5, s6 = lax.fori_loop(0, S // T, norm_one, (zero8, zero8, zero8))
        put(4, jnp.sum(s4, axis=0, keepdims=True))
        put(5, jnp.sum(s5, axis=0, keepdims=True))
        put(6, jnp.sum(s6, axis=0, keepdims=True))
        push()
        if l == 1:
            for ref in (R.w[KIND_I], R.N1, R.r1):
                load(ref, 0)
        CTp = use(R.CTp)
        go = R.g[KIND_O]

        def store(ref, value):
            for cc in range(2):
                ref[l, cc] = value[cc * (D // 2) : (cc + 1) * (D // 2)].reshape(ref.shape[2:])

        store(R.g[KIND_O], nn_dot(CTp[...], dZ[...]).astype(BF))
        begin(KIND_O, l)
        use(R.w[KIND_O])
        dF[...] = nt_dot(dZ[...], weight(KIND_O)).astype(BF)
        CT = use(R.CT)
        dct = dF[...].T
        prod = dct.astype(F32) * CT[...].astype(F32)
        prod = jnp.sum(prod.reshape(D // 64, 64, S), axis=1)
        for j in range(D // 128):
            R.delta[j, :2] = prod[2 * j : 2 * j + 2]
        if l == 1:
            for ref in (R.CTp, R.w[KIND_O], R.CT):
                load(ref, 0)
        K, V, Q, lse = use(R.K), use(R.V), use(R.Q), use(R.lse)
        delta, dC, dQT = R.delta, dF, R.dQT
        dkp, dvp, dkr, dvr = R.dkp, R.dvp, R.dkr, R.dvr
        bias_rows = msel[: 2 * S]

        def pair(j, carry):
            sl = pl.ds(pl.multiple_of(j * 128, 128), 128)
            k2 = K[:, :, sl].reshape(2 * S, 128)
            v2 = V[:, :, sl].reshape(2 * S, 128)
            k2t = k2.T
            q2 = Q[:, sl]
            dc2 = dC[:, sl]
            dk_sum, dv_sum = None, None
            for h in range(2):
                mine, other = (low, high) if h == 0 else (high, low)
                mine32 = low32 if h == 0 else 1.0 - low32
                kh = k2 * mine + bias_rows * other
                vh = v2 * mine
                qh = q2 * mine + spots * other
                dk_h, dv_h = None, None
                for part in range(S // 256):
                    cols = slice(part * 256, part * 256 + 256)
                    st = nt_dot(kh, qh[cols])
                    p = jnp.exp(st - lse[j, h : h + 1, cols])
                    dp = nt_dot(vh, dc2[cols])
                    ds = (p * (dp - delta[j, h : h + 1, cols])).astype(BF)
                    pb = p.astype(BF)
                    dv = nn_dot(pb, dc2[cols])
                    dk = nn_dot(ds, q2[cols])
                    dv_h = dv if dv_h is None else dv_h + dv
                    dk_h = dk if dk_h is None else dk_h + dk
                    dq = nn_dot(k2t, ds)[64 * h : 64 * h + 64]
                    rows = pl.ds(pl.multiple_of(j * 128 + 64 * h, 64), 64)
                    dQT[rows, cols] = (dq * 0.125).astype(BF)
                dk_sum = dk_h * mine32 if dk_sum is None else dk_sum + dk_h * mine32
                dv_sum = dv_h * mine32 if dv_sum is None else dv_sum + dv_h * mine32
            dkp[l, :, j] = dk_sum.astype(BF).reshape(2, S, 128)
            dvp[l, :, j] = dv_sum.astype(BF).reshape(2, S, 128)
            return carry

        pairs = D // 128
        half_pairs = pairs // 2
        kv_cps = []
        for part in range(2):
            lax.fori_loop(part * half_pairs, (part + 1) * half_pairs, pair, 0)
            js = pl.ds(part * half_pairs, half_pairs)
            kv_cps.append(start(remote(dkp.at[l, 1 - c, js], dkr.at[l, js], R.ks.at[l, part, 0], R.kr.at[l, part, 0], me.cn)))
            kv_cps.append(start(remote(dvp.at[l, 1 - c, js], dvr.at[l, js], R.ks.at[l, part, 1], R.kr.at[l, part, 1], me.cn)))
            push()
        if l == 1:
            for ref in (R.K, R.V, R.Q, R.lse):
                load(ref, 0)
        AT = use(R.AT)
        dqb = dZ
        dqb[...] = dQT[...].T
        store(R.g[KIND_Q], nn_dot(AT[...], dqb[...]).astype(BF))
        begin(KIND_Q, l)
        for cp in kv_cps:
            cp.wait_recv()
        dkb, dvb = dFT, R.dvb
        for j in range(pairs):
            dkb[:, 128 * j : 128 * j + 128] = dkp[l, c, j] + dkr[l, j]
            dvb[:, 128 * j : 128 * j + 128] = dvp[l, c, j] + dvr[l, j]
        store(R.g[KIND_K], nn_dot(AT[...], dkb[...]).astype(BF))
        begin(KIND_K, l)
        store(R.g[KIND_V], nn_dot(AT[...], dvb[...]).astype(BF))
        begin(KIND_V, l)
        if l == 1:
            load(R.AT, 0)
        use(R.w[KIND_Q])
        use(R.w[KIND_K])
        use(R.w[KIND_V])

        def last(t, carry):
            s0, s2, s3 = carry
            rows = pl.ds(pl.multiple_of(t * T, T), T)
            d = dy[rows] + nt_dot(dqb[rows], weight(KIND_Q)) + nt_dot(dkb[rows], weight(KIND_K)) + nt_dot(dvb[rows], weight(KIND_V))
            dy[rows] = d
            return s0 + fold(d), s2 + fold(dqb[rows].astype(F32)), s3 + fold(dvb[rows].astype(F32))

        s0, s2, s3 = lax.fori_loop(0, S // T, last, (zero8, zero8, zero8))
        s0 = jnp.sum(s0, axis=0, keepdims=True)
        put(0, s0 * (1.0 - tag_row))
        put(1, s0 * tag_row)
        put(2, jnp.sum(s2, axis=0, keepdims=True))
        put(3, jnp.sum(s3, axis=0, keepdims=True))
        push()
        if l == 1:
            for ref in (R.w[KIND_Q], R.w[KIND_K], R.w[KIND_V]):
                load(ref, 0)

    R.cotb[...] = dy[...].astype(BF)
    dx_far = remote(R.cotb, R.dxo, R.xs.at[1], R.xr.at[1], me.dn)
    dx_near = pltpu.make_async_copy(R.cotb, R.dxo, R.ssem.at[4])

    @pl.when(stays)
    def _():
        dx_near.start()

    @pl.when(jnp.logical_not(stays))
    def _():
        dx_far.start()

    vb, vt = R.vb, R.vt
    va, vrecv = R.va, R.vrecv
    va[0] = vg[...]
    for at, dev in enumerate((me.cn, me.xn, me.yn)):
        cp = start(remote(va.at[at], vrecv.at[at], R.vs.at[at], R.vr.at[at], dev))
        push()
        cp.wait_recv()
        va[at + 1] = va[at] + vrecv[at]
    vz = []
    for s in range(1, levels):
        there, dev = me.zn(s, levels)
        lanes = pl.ds(pl.multiple_of(there * 128, 128), 128)
        vz.append(start(remote(va.at[3, :, lanes], vb.at[s - 1], R.vs.at[2 + s], R.vr.at[2 + s], dev)))
    push()
    for cp in vz:
        cp.wait_recv()
    total = va[3, :, pl.ds(pl.multiple_of(z * 128, 128), 128)]
    for s in range(levels - 1):
        total = total + vb[s]
    vt[...] = total
    vec_out = pltpu.make_async_copy(vt, R.vec_g, R.ssem.at[5])
    vec_out.start()
    while any(stage[i] < len(steps) for i in started):
        push()
    for cp in fin_copies:
        cp.wait()
    vec_out.wait()
    for cp in pending:
        cp.wait_send()

    @pl.when(stays)
    def _():
        y_near.wait()
        dx_near.wait()

    @pl.when(jnp.logical_not(stays))
    def _():
        y_far.wait()
        dx_far.wait()


def update_kernel(parts, rates, decays, *refs):
    R = named(parts, refs)
    f = lax.axis_index("fsdp")

    def step(at, where, grad):
        new = adamw(R.masters[at][where], R.firsts[at][where], R.seconds[at][where], grad, rates[at], decays[at])
        for refs, value in zip((R.new_masters, R.new_firsts, R.new_seconds), new):
            refs[at][where] = value

    D = R.dx.shape[1]
    for l in range(2):
        for at, kind in enumerate((KIND_Q, KIND_K, KIND_V)):
            grad = R.fin[kind][l].astype(F32).reshape(-1, D)
            step(0, (l, slice(None), slice(at * D, at * D + D)), grad)
        for at, kind in ((1, KIND_O), (2, KIND_I)):
            ref = R.fin[kind]
            step(at, (l,), ref[l].astype(F32).reshape(-1, ref.shape[-1]))
        ref = R.fin[KIND_F]
        step(3, (l,), ref[l].astype(F32).reshape(-1, ref.shape[-1]).T)
        wide = R.masters[4].shape[2]
        span = 128 // wide
        rows = R.masters[4].shape[1]
        block = R.fvec[16 * l : 16 * l + 16]
        grad = block[:, :wide]
        slot = lax.rem(f, span)
        for s in range(1, span):
            grad = jnp.where(slot == s, block[:, s * wide : s * wide + wide], grad)
        step(4, (l,), grad[:rows])
    R.out[0] = R.y[...]
    R.grad[0] = R.dx[...].astype(F32)


def fast_body(
    tokens, cotangent, tags, lengths, key_mask,
    master_qkv, master_out, master_in, master_feed_output, master_vec,
    first_qkv, first_out, first_in, first_ffo, first_vec,
    second_qkv, second_out, second_in, second_ffo, second_moment_vector,
    shards,
):
    S, D = tokens.shape[1:]
    FF = master_in.shape[2]
    levels = shards // 4
    rows, cols = sizes_of(shards, D, FF)
    f = lax.axis_index("fsdp")
    key_count = key_mask.shape[1]
    key_pos = jnp.arange(key_count, dtype=jnp.int32)
    valid = key_pos < lengths[0]
    key_valid = valid & ((key_mask[0] == 1) | (key_pos == 0))
    lane = jnp.arange(128, dtype=jnp.int32)
    bias = jnp.where(key_valid, 0.0, masked_score).astype(F32)
    meta = jnp.where((lane % 64 == 0)[None, :], bias[:, None], 0.0)
    tag_rows = jnp.full((16, 128), tags[0], F32)
    meta = jnp.concatenate([meta, tag_rows], axis=0).astype(BF)
    start_row = lax.axis_index("rep") * S
    query_valid = (start_row + jnp.arange(S, dtype=jnp.int32)) < lengths[0]
    cot = jnp.where(query_valid[None, :, None], cotangent, jnp.zeros_like(cotangent))
    wide = master_vec.shape[2]
    vec_rows = jnp.pad(master_vec, ((0, 0), (0, 16 - master_vec.shape[1]), (0, 0))).reshape(32, wide)
    slot = (lane // wide) == lax.rem(f, 128 // wide)
    vecb = jnp.where(slot[None, :], jnp.tile(vec_rows, (1, 128 // wide)), 0.0).astype(BF)

    hbm = pl.BlockSpec(memory_space=pl.ANY)
    shape = jax.ShapeDtypeStruct
    V = pltpu.VMEM
    dma = pltpu.SemaphoreType.DMA
    w_tail = [(levels, 2, 2, 2, rows[k], cols[k]) for k in KINDS]
    masters = (master_qkv, master_out, master_in, master_feed_output, master_vec)
    firsts = (first_qkv, first_out, first_in, first_ffo, first_vec)
    seconds = (second_qkv, second_out, second_in, second_ffo, second_moment_vector)

    saved = call_kernel(
        lambda parts, *refs: forward_kernel(parts, levels, norm_epsilon, *refs),
        ForwardIn(tok=tokens, cot=cot, meta=meta, vecb=vecb, masters=masters[:4]),
        Saved(
            w_o=tuple(shape((2,) + tail, BF) for tail in w_tail),
            vec_o=shape((32, D), F32),
            meta_o=shape(meta.shape, BF),
            cot_o=shape((S, D), BF),
            y_o=shape((S, D), BF),
            at_o=shape((2, D, S), BF),
            q_o=shape((2, S, D), BF),
            k_o=shape((2, 2, S, D), BF),
            v_o=shape((2, 2, S, D), BF),
            lse_o=shape((2, D // 128, 8, S), F32),
            ct_o=shape((2, D, S), BF),
            ctp_o=shape((2, D, S), BF),
            n1_o=shape((2, S, D), F32),
            r1_o=shape((2, S, 128), F32),
            ht_o=shape((2, D, S), BF),
            g_o=shape((2, S, FF), BF),
            gp_o=shape((2, S, FF), BF),
            n2_o=shape((2, S, D), F32),
            r2_o=shape((2, S, 128), F32),
        ),
        ForwardScratch(
            w=tuple(V((2,) + tail, BF) for tail in w_tail),
            stages=tuple(V((2, m.shape[1] // 2, m.shape[2]), F32) for m in masters[:4]),
            vecg=V((shards, 32, 128), BF),
            vec=V((32, D), F32),
            metab=V((2,) + meta.shape, BF),
            msel=V(meta.shape, BF),
            tokb=V((S, D), BF),
            A32=V((S, D), F32),
            Ab=V((S, D), BF),
            ATp=V((D, S), BF),
            Q=V((S, D), BF),
            K=V((2, 2, S, D), BF),
            V=V((2, 2, S, D), BF),
            lse=V((D // 128, 8, S), F32),
            CT=V((D, S), BF),
            CTp=V((D, S), BF),
            C=V((S, D), BF),
            N1=V((S, D), F32),
            r1=V((S, 128), F32),
            H32=V((S, D), F32),
            Hb=V((S, D), BF),
            HTp=V((D, S), BF),
            G=V((S, FF), BF),
            Gp=V((S, FF), BF),
            N2=V((S, D), F32),
            r2=V((S, 128), F32),
            X=V((S, D), F32),
            Yb=V((S, D), BF),
            msem=dma((2, 4)),
            xsem=dma((4,)),
            osem=dma((48,)),
            gs=dma((12, levels + 4)),
            gr=dma((12, levels + 4)),
            vs=dma((shards - 1,)),
            vr=dma((shards - 1,)),
            xs=dma((3,)),
            xr=dma((3,)),
            ks=dma((2, 2)),
            kr=dma((2, 2)),
        ),
        hbm,
        collective_id=0,
        has_side_effects=True,
        vmem_limit_bytes=VMEM_BYTES,
    )

    tails = [(rows[k], cols[k]) for k in KINDS]
    tails[KIND_F] = (D // 2, FF // shards)
    ha, hb = levels // 2, levels - levels // 2
    each = lambda *lead: tuple(V(lead + tail, BF) for tail in tails)
    grads = call_kernel(
        lambda parts, *refs: backward_kernel(parts, levels, *refs),
        saved,
        BackwardOut(
            fin=tuple(shape((2, 2) + tail, BF) for tail in tails),
            vec_g=shape((32, 128), F32),
            yo=shape((S, D), BF),
            dxo=shape((S, D), BF),
        ),
        BackwardScratch(
            g=each(2, 2, levels, 2, 2),
            landing=each(levels, 2, 2),
            half_y=each(2, ha, 2),
            half_x=each(2, hb, 2),
            quarter_x=each(2, ha),
            quarter_y=each(2, hb),
            level=each(2, levels - 1),
            total=each(2, 2),
            w=tuple(V(tail, BF) for tail in w_tail),
            AT=V((D, S), BF),
            Q=V((S, D), BF),
            K=V((2, S, D), BF),
            V=V((2, S, D), BF),
            lse=V((D // 128, 8, S), F32),
            CT=V((D, S), BF),
            CTp=V((D, S), BF),
            N1=V((S, D), F32),
            r1=V((S, 128), F32),
            HT=V((D, S), BF),
            G=V((S, FF), BF),
            Gp=V((S, FF), BF),
            N2=V((S, D), F32),
            r2=V((S, 128), F32),
            vec=V((32, D), F32),
            msel=V(meta.shape, BF),
            cotb=V((S, D), BF),
            dy=V((S, D), F32),
            dpre=V((S, D), F32),
            dF=V((S, D), BF),
            dFT=V((D, S), BF),
            dU=V((S, FF), BF),
            dZ=V((S, D), BF),
            delta=V((D // 128, 8, S), F32),
            dQT=V((D, S), BF),
            dvb=V((S, D), BF),
            dkp=V((2, 2, D // 128, S, 128), BF),
            dvp=V((2, 2, D // 128, S, 128), BF),
            dkr=V((2, D // 128, S, 128), BF),
            dvr=V((2, D // 128, S, 128), BF),
            vg=V((32, D), F32),
            va=V((4, 32, D), F32),
            vrecv=V((3, 32, D), F32),
            vb=V((levels - 1, 32, 128), F32),
            vt=V((32, 128), F32),
            lsem=dma((2, 20)),
            ssem=dma((6,)),
            fsem=dma((12,)),
            gs=dma((12, levels + 5)),
            gr=dma((12, levels + 5)),
            xs=dma((2,)),
            xr=dma((2,)),
            ks=dma((2, 2, 2)),
            kr=dma((2, 2, 2)),
            vs=dma((levels + 2,)),
            vr=dma((levels + 2,)),
        ),
        hbm,
        collective_id=1,
        has_side_effects=True,
        vmem_limit_bytes=VMEM_BYTES,
    )

    rates = (
        matrix_rate * D ** (-0.5),
        matrix_rate * (D // 16) ** (-0.5),
        matrix_rate * D ** (-0.5),
        matrix_rate * (FF // 2) ** (-0.5),
        vector_rate,
    )
    decays = (weight_decay, weight_decay, weight_decay, weight_decay, 0.0)
    like = tuple(shape(p.shape, F32) for p in masters)
    new = call_kernel(
        lambda parts, *refs: update_kernel(parts, rates, decays, *refs),
        UpdateIn(fin=grads.fin, fvec=grads.vec_g, y=grads.yo, dx=grads.dxo, masters=masters, firsts=firsts, seconds=seconds),
        UpdateOut(
            out=shape(tokens.shape, BF),
            grad=shape(tokens.shape, F32),
            new_masters=like,
            new_firsts=like,
            new_seconds=like,
        ),
        None,
        pl.BlockSpec(memory_space=pltpu.VMEM),
        vmem_limit_bytes=40 << 20,
    )
    return (new.out, new.grad, *new.new_masters, *new.new_firsts, *new.new_seconds)


def solution(mesh):
    placed = (
        P("fsdp", "rep", None),
        P("fsdp", "rep", None),
        P("fsdp"),
        P("fsdp"),
        P("fsdp", None),
        P(None, "fsdp", None),
        P(None, "fsdp", None),
        P(None, "fsdp", None),
        P(None, "fsdp", None),
        P(None, None, "fsdp"),
        P(None, "fsdp", None),
        P(None, "fsdp", None),
        P(None, "fsdp", None),
        P(None, "fsdp", None),
        P(None, None, "fsdp"),
        P(None, "fsdp", None),
        P(None, "fsdp", None),
        P(None, "fsdp", None),
        P(None, "fsdp", None),
        P(None, None, "fsdp"),
    )
    shards = mesh.shape["fsdp"]

    def chosen(*args):
        tokens, master_in = args[0], args[7]
        width = tokens.shape[2]
        whole_tiles = width % (32 * shards) == 0 and shards * 32 == width
        if mesh.shape["rep"] == 2 and shards % 4 == 0 and whole_tiles and master_in.shape[2] == 4 * width:
            return fast_body(*args, shards)
        return body(*args)

    return jax.shard_map(
        chosen,
        mesh=mesh,
        in_specs=placed,
        out_specs=(
            P("fsdp", "rep", None),
            P("fsdp", "rep", None),
            P(None, "fsdp", None),
            P(None, "fsdp", None),
            P(None, "fsdp", None),
            P(None, "fsdp", None),
            P(None, None, "fsdp"),
            P(None, "fsdp", None),
            P(None, "fsdp", None),
            P(None, "fsdp", None),
            P(None, "fsdp", None),
            P(None, None, "fsdp"),
            P(None, "fsdp", None),
            P(None, "fsdp", None),
            P(None, "fsdp", None),
            P(None, "fsdp", None),
            P(None, None, "fsdp"),
        ),
        check_vma=False,
    )
```

```python
import functools
from types import SimpleNamespace
from typing import NamedTuple

import jax
import jax.numpy as jnp
from jax import lax
from jax.experimental import pallas as pl
from jax.experimental.pallas import tpu as pltpu
from jax.sharding import PartitionSpec as P

D = 512
H = 8
FF = 2048
STEP = 10


beta_decay = 0.5
epsilon_adam = 1e-08
weight_decay = 0.01
norm_epsilon = 1e-05
masked_score = -1000000000.0
vector_rate = 0.15
matrix_rate = 0.5


def layer_norm(pre_norm, gain_row, offset_row):
    centre_mean = jnp.mean(pre_norm, axis=-1, keepdims=True)
    centred = pre_norm - centre_mean
    variance = jnp.mean(centred * centred, axis=-1, keepdims=True)
    return centred * lax.rsqrt(variance + norm_epsilon) * gain_row + offset_row


def tanh_gelu_activation(inner_act):
    return jax.nn.gelu(inner_act, approximate=True)


def adamw(master, first, second, grad, rate, decay):
    first_new = beta_decay * first + (1.0 - beta_decay) * grad
    second_new = beta_decay * second + (1.0 - beta_decay) * grad * grad
    correction = 1.0 - beta_decay**STEP
    direction = first_new / correction / (jnp.sqrt(second_new / correction) + epsilon_adam)
    master_new = master - rate * (direction + decay * master)
    return (master_new, first_new, second_new)


def score_block(query_heads, key_heads, key_bias, score_scale):
    scores = jnp.einsum("qhd,khd->hqk", query_heads, key_heads, preferred_element_type=jnp.float32)
    return scores * score_scale + key_bias[None, None, :]


def forward_layer(input_rows, weights, tag_value, key_bias):
    w_qkv, w_out, w_in, w_ffo, vectors_low = weights
    vectors = vectors_low.astype(jnp.float32)
    model_width = w_out.shape[0]
    row_count = input_rows.shape[0]
    head_size = model_width // H
    score_scale = head_size ** (-0.5)
    direction = jnp.where(tag_value == 0, vectors[0], vectors[1])
    summed = input_rows + direction[None, :]
    summed_low = summed.astype(jnp.bfloat16)
    projected = jnp.dot(summed_low, w_qkv, preferred_element_type=jnp.float32)
    queries = (projected[:, :model_width] + vectors[2]).astype(jnp.bfloat16)
    keys_local = projected[:, model_width : 2 * model_width].astype(jnp.bfloat16)
    local_values = (projected[:, 2 * model_width :] + vectors[3]).astype(jnp.bfloat16)
    keys_all, values_all = (
        lax.all_gather(keys_local, "rep", axis=0, tiled=True),
        lax.all_gather(local_values, "rep", axis=0, tiled=True),
    )
    key_count = keys_all.shape[0]
    query_heads = queries.reshape(row_count, H, head_size)
    key_heads = keys_all.reshape(key_count, H, head_size)
    value_heads = values_all.reshape(key_count, H, head_size)
    scores = score_block(query_heads, key_heads, key_bias, score_scale)
    row_top = jnp.max(scores, axis=-1, keepdims=True)
    exponent_terms = jnp.exp(scores - row_top)
    totals = jnp.sum(exponent_terms, axis=-1, keepdims=True)
    soft_weights = exponent_terms / totals
    log_total = row_top + jnp.log(totals)
    context = jnp.einsum(
        "hqk,khd->qhd",
        soft_weights.astype(jnp.bfloat16),
        value_heads,
        preferred_element_type=jnp.float32,
    )
    context_low = context.reshape(row_count, model_width).astype(jnp.bfloat16)
    branch = jnp.dot(context_low, w_out, preferred_element_type=jnp.float32) + vectors[4]
    hidden, norm_first = jax.vjp(layer_norm, summed + branch, vectors[5], vectors[6])
    hidden_low = hidden.astype(jnp.bfloat16)
    inner_act = jnp.dot(hidden_low, w_in, preferred_element_type=jnp.float32) + vectors[
        10:
    ].reshape(-1)
    activated, gelu_pull = jax.vjp(tanh_gelu_activation, inner_act)
    activated_low = activated.astype(jnp.bfloat16)
    feed_out = jnp.dot(activated_low, w_ffo, preferred_element_type=jnp.float32) + vectors[7]
    result, norm_second = jax.vjp(layer_norm, hidden + feed_out, vectors[8], vectors[9])
    saved_state = (
        summed_low,
        query_heads,
        key_heads,
        value_heads,
        log_total,
        context_low,
        norm_first,
        hidden_low,
        gelu_pull,
        activated_low,
        norm_second,
    )
    return (result, saved_state)


def attention_grads(
    query_heads, key_heads, value_heads, log_total, context_heads, key_bias, score_scale
):
    row_count = query_heads.shape[0]
    model_width = query_heads.shape[1] * query_heads.shape[2]
    scores = score_block(query_heads, key_heads, key_bias, score_scale)
    soft_weights = jnp.exp(scores - log_total)
    grad_soft = jnp.einsum(
        "qhd,khd->hqk", context_heads, value_heads, preferred_element_type=jnp.float32
    )
    row_inner = jnp.sum(soft_weights * grad_soft, axis=-1, keepdims=True)
    grad_scores = (soft_weights * (grad_soft - row_inner) * score_scale).astype(jnp.bfloat16)
    grad_queries = jnp.einsum(
        "hqk,khd->qhd", grad_scores, key_heads, preferred_element_type=jnp.float32
    ).reshape(row_count, model_width)
    key_terms = jnp.einsum(
        "hqk,qhd->khd", grad_scores, query_heads, preferred_element_type=jnp.float32
    ).reshape(-1, model_width)
    value_terms = jnp.einsum(
        "hqk,qhd->khd",
        soft_weights.astype(jnp.bfloat16),
        context_heads,
        preferred_element_type=jnp.float32,
    ).reshape(-1, model_width)
    grad_keys, grad_values = (
        lax.psum_scatter(
            key_terms.astype(jnp.bfloat16), "rep", scatter_dimension=0, tiled=True
        ).astype(jnp.float32),
        lax.psum_scatter(
            value_terms.astype(jnp.bfloat16), "rep", scatter_dimension=0, tiled=True
        ).astype(jnp.float32),
    )
    return (grad_queries, grad_keys, grad_values)


def backward_layer(grad_result, saved_state, weights, tag_value, key_bias):
    w_qkv, w_out, w_in, w_ffo, vectors_low = weights
    (
        summed_low,
        query_heads,
        key_heads,
        value_heads,
        log_total,
        context_low,
        norm_first,
        hidden_low,
        gelu_pull,
        activated_low,
        norm_second,
    ) = saved_state
    model_width = w_out.shape[0]
    row_count = summed_low.shape[0]
    head_size = model_width // H
    score_scale = head_size ** (-0.5)
    grad_pre_two, grad_gain_two, grad_shift_two = norm_second(grad_result)
    grad_feed = grad_pre_two.astype(jnp.bfloat16)
    grad_bias_feed = jnp.sum(grad_feed.astype(jnp.float32), axis=0)
    grad_ffo = jnp.einsum("tf,td->fd", activated_low, grad_feed, preferred_element_type=jnp.float32)
    grad_activated = jnp.einsum("td,fd->tf", grad_feed, w_ffo, preferred_element_type=jnp.float32)
    grad_inner = gelu_pull(grad_activated)[0].astype(jnp.bfloat16)
    grad_bias_inner = jnp.sum(grad_inner.astype(jnp.float32), axis=0)
    grad_in = jnp.einsum("td,tf->df", hidden_low, grad_inner, preferred_element_type=jnp.float32)
    grad_hidden = grad_pre_two + jnp.einsum(
        "tf,df->td", grad_inner, w_in, preferred_element_type=jnp.float32
    )
    grad_pre_one, grad_gain_one, grad_shift_one = norm_first(grad_hidden)
    grad_branch = grad_pre_one.astype(jnp.bfloat16)
    grad_bias_out = jnp.sum(grad_branch.astype(jnp.float32), axis=0)
    grad_out_matrix = jnp.einsum(
        "te,td->ed", context_low, grad_branch, preferred_element_type=jnp.float32
    )
    grad_context = jnp.einsum(
        "td,ed->te", grad_branch, w_out, preferred_element_type=jnp.float32
    ).astype(jnp.bfloat16)
    context_heads = grad_context.reshape(row_count, H, head_size)
    grad_queries, grad_keys, grad_values = attention_grads(
        query_heads, key_heads, value_heads, log_total, context_heads, key_bias, score_scale
    )
    grad_joined = jnp.concatenate(
        [
            grad_queries.astype(jnp.bfloat16),
            grad_keys.astype(jnp.bfloat16),
            grad_values.astype(jnp.bfloat16),
        ],
        axis=1,
    )
    grad_qkv = jnp.einsum("td,te->de", summed_low, grad_joined, preferred_element_type=jnp.float32)
    grad_summed = grad_pre_one + jnp.einsum(
        "te,de->td", grad_joined, w_qkv, preferred_element_type=jnp.float32
    )
    column_sums = jnp.sum(grad_joined.astype(jnp.float32), axis=0)
    grad_direction = jnp.sum(grad_summed, axis=0)
    zero_row = jnp.zeros_like(grad_direction)
    grad_rows = jnp.stack(
        [
            jnp.where(tag_value == 0, grad_direction, zero_row),
            jnp.where(tag_value == 1, grad_direction, zero_row),
            column_sums[:model_width],
            column_sums[2 * model_width :],
            grad_bias_out,
            grad_gain_one,
            grad_shift_one,
            grad_bias_feed,
            grad_gain_two,
            grad_shift_two,
        ],
        axis=0,
    )
    grad_vectors = jnp.concatenate([grad_rows, grad_bias_inner.reshape(-1, model_width)], axis=0)
    return (grad_summed, (grad_qkv, grad_out_matrix, grad_in, grad_ffo, grad_vectors))


def reduce_layer(grads):
    shards = (
        lax.psum_scatter(grads[0], "fsdp", scatter_dimension=0, tiled=True),
        lax.psum_scatter(grads[1], "fsdp", scatter_dimension=0, tiled=True),
        lax.psum_scatter(grads[2], "fsdp", scatter_dimension=0, tiled=True),
        lax.psum_scatter(grads[3], "fsdp", scatter_dimension=0, tiled=True),
        lax.psum_scatter(grads[4], "fsdp", scatter_dimension=1, tiled=True),
    )
    return (
        lax.psum(shards[0].astype(jnp.bfloat16), "rep").astype(jnp.float32),
        lax.psum(shards[1].astype(jnp.bfloat16), "rep").astype(jnp.float32),
        lax.psum(shards[2].astype(jnp.bfloat16), "rep").astype(jnp.float32),
        lax.psum(shards[3].astype(jnp.bfloat16), "rep").astype(jnp.float32),
        lax.psum(shards[4].astype(jnp.bfloat16), "rep").astype(jnp.float32),
    )


def body(
    tokens,
    cotangent,
    tags,
    lengths,
    key_mask,
    master_qkv,
    master_out,
    master_in,
    master_feed_output,
    master_vec,
    first_qkv,
    first_out,
    first_in,
    first_ffo,
    first_vec,
    second_qkv,
    second_out,
    second_in,
    second_ffo,
    second_moment_vector,
):
    row_count = tokens.shape[1]
    key_count = key_mask.shape[1]
    start_row = lax.axis_index("rep") * row_count
    query_pos = start_row + jnp.arange(row_count, dtype=jnp.int32)
    key_pos = jnp.arange(key_count, dtype=jnp.int32)
    seq_length = lengths[0]
    tag_value = tags[0]
    key_valid = (key_pos < seq_length) & ((key_mask[0] == 1) | (key_pos == 0))
    key_bias = jnp.where(key_valid, 0.0, masked_score).astype(jnp.float32)
    query_valid = (query_pos < seq_length).astype(jnp.float32)
    masters = (master_qkv, master_out, master_in, master_feed_output, master_vec)
    firsts = (first_qkv, first_out, first_in, first_ffo, first_vec)
    seconds = (second_qkv, second_out, second_in, second_ffo, second_moment_vector)
    shared = (
        lax.all_gather(master_qkv[0].astype(jnp.bfloat16), "fsdp", axis=0, tiled=True),
        lax.all_gather(master_out[0].astype(jnp.bfloat16), "fsdp", axis=0, tiled=True),
        lax.all_gather(master_in[0].astype(jnp.bfloat16), "fsdp", axis=0, tiled=True),
        lax.all_gather(master_feed_output[0].astype(jnp.bfloat16), "fsdp", axis=0, tiled=True),
        lax.all_gather(master_vec[0].astype(jnp.bfloat16), "fsdp", axis=1, tiled=True),
    )
    shared_out, saved_shared = forward_layer(
        tokens[0].astype(jnp.float32), shared, tag_value, key_bias
    )
    unique = (
        lax.all_gather(master_qkv[1].astype(jnp.bfloat16), "fsdp", axis=0, tiled=True),
        lax.all_gather(master_out[1].astype(jnp.bfloat16), "fsdp", axis=0, tiled=True),
        lax.all_gather(master_in[1].astype(jnp.bfloat16), "fsdp", axis=0, tiled=True),
        lax.all_gather(master_feed_output[1].astype(jnp.bfloat16), "fsdp", axis=0, tiled=True),
        lax.all_gather(master_vec[1].astype(jnp.bfloat16), "fsdp", axis=1, tiled=True),
    )
    final_out, saved_unique = forward_layer(shared_out, unique, tag_value, key_bias)
    grad_final = cotangent[0].astype(jnp.float32) * query_valid[:, None]
    unique_back = (
        lax.all_gather(master_qkv[1].astype(jnp.bfloat16), "fsdp", axis=0, tiled=True),
        lax.all_gather(master_out[1].astype(jnp.bfloat16), "fsdp", axis=0, tiled=True),
        lax.all_gather(master_in[1].astype(jnp.bfloat16), "fsdp", axis=0, tiled=True),
        lax.all_gather(master_feed_output[1].astype(jnp.bfloat16), "fsdp", axis=0, tiled=True),
        lax.all_gather(master_vec[1].astype(jnp.bfloat16), "fsdp", axis=1, tiled=True),
    )
    grad_middle, unique_grads = backward_layer(
        grad_final, saved_unique, unique_back, tag_value, key_bias
    )
    reduced_unique = reduce_layer(unique_grads)
    grad_inputs, shared_grads = backward_layer(
        grad_middle, saved_shared, shared, tag_value, key_bias
    )
    reduced_shared = reduce_layer(shared_grads)
    rates = (
        matrix_rate * D ** (-0.5),
        matrix_rate * (D // 16) ** (-0.5),
        matrix_rate * D ** (-0.5),
        matrix_rate * (FF // 2) ** (-0.5),
        vector_rate,
    )
    decays = (weight_decay, weight_decay, weight_decay, weight_decay, 0.0)
    updated = []
    for kind_index in range(5):
        grad_stack = jnp.stack([reduced_shared[kind_index], reduced_unique[kind_index]], axis=0)
        updated.append(
            adamw(
                masters[kind_index],
                firsts[kind_index],
                seconds[kind_index],
                grad_stack,
                rates[kind_index],
                decays[kind_index],
            )
        )
    return (
        final_out.astype(jnp.bfloat16)[None],
        grad_inputs[None],
        updated[0][0],
        updated[1][0],
        updated[2][0],
        updated[3][0],
        updated[4][0],
        updated[0][1],
        updated[1][1],
        updated[2][1],
        updated[3][1],
        updated[4][1],
        updated[0][2],
        updated[1][2],
        updated[2][2],
        updated[3][2],
        updated[4][2],
    )


BF = jnp.bfloat16
F32 = jnp.float32
MESH = pl.DeviceIdType.MESH
KIND_K, KIND_V, KIND_Q, KIND_O, KIND_I, KIND_F = KINDS = tuple(range(6))
VMEM_BYTES = 60 << 20
FORWARD_TURNS = (
    (1, 2, 0, 3, 1, 4, 2),
    (0, 3, 5, 1, 2, 4, 6, 0, 3, 5, 0, 1, 7),
    (2, 1),
    (6, 4, 8, 2),
    (),
    (3, 9),
    (5, 7, 10, 3, 8, 6),
    (9, 11),
    (4, 10, 12),
    (),
    (5, 11),
    (4, 13),
    (5, 7, 8, 12),
    (14, 6, 9, 10, 13, 11, 6, 15, 14, 7, 8, 12, 7, 15),
    (8, 9),
    (10,),
    (13, 9),
    (10,),
    (),
    (11,),
    (14,),
    (11,),
    (12,),
    (15,),
    (),
    (12, 13),
    (13, 14),
    (14, 15, 15),
    (),
)
BACKWARD_TURNS = (
    (),
    (),
    (0,),
    (),
    (),
    (1,),
    (),
    (0,),
    (2,),
    (1, 2),
    (),
    (0,),
    (),
    (3, 1),
    (4, 5),
    (2,),
    (3, 12),
    (4, 5, 0, 12),
    (1, 6),
    (2,),
    (),
    (3, 7),
    (4,),
    (5, 0, 6, 12, 3),
    (4, 7, 8, 5),
    (0, 1, 8),
    (2, 3, 12),
    (4, 5, 6, 12),
    (7,),
    (9,),
    (1, 10, 11),
    (),
    (8, 2, 9, 3, 13, 4, 10, 5, 11, 13, 6, 7, 6, 8, 9, 10, 11, 7, 13, 8, 6, 9, 10, 13, 11, 7, 8, 9, 10, 13, 9, 11, 10, 11),
)


def nt_dot(left, right):
    return lax.dot_general(left, right, (((1,), (1,)), ((), ())), preferred_element_type=F32)


def nn_dot(left, right):
    return jnp.dot(left, right, preferred_element_type=F32)


def remote(src, dst, send_sem, recv_sem, device):
    return pltpu.make_async_remote_copy(
        src_ref=src,
        dst_ref=dst,
        send_sem=send_sem,
        recv_sem=recv_sem,
        device_id=device,
        device_id_type=MESH,
    )


class ForwardIn(NamedTuple):
    tok: object
    cot: object
    meta: object
    vecb: object
    masters: object


class Saved(NamedTuple):
    w_o: object
    vec_o: object
    meta_o: object
    cot_o: object
    y_o: object
    at_o: object
    q_o: object
    k_o: object
    v_o: object
    lse_o: object
    ct_o: object
    ctp_o: object
    n1_o: object
    r1_o: object
    ht_o: object
    g_o: object
    gp_o: object
    n2_o: object
    r2_o: object


class ForwardScratch(NamedTuple):
    w: object
    stages: object
    vecg: object
    vec: object
    metab: object
    msel: object
    tokb: object
    cotb: object
    A32: object
    Ab: object
    ATp: object
    Q: object
    K: object
    V: object
    lse: object
    CT: object
    CTp: object
    C: object
    N1: object
    r1: object
    H32: object
    Hb: object
    HTp: object
    G: object
    Gp: object
    N2: object
    r2: object
    X: object
    Yb: object
    msem: object
    xsem: object
    osem: object
    gs: object
    gr: object
    vs: object
    vr: object
    xs: object
    xr: object
    ks: object
    kr: object


class BackwardOut(NamedTuple):
    fin: object
    vec_g: object
    yo: object
    dxo: object


class BackwardScratch(NamedTuple):
    g: object
    landing: object
    half_y: object
    half_x: object
    quarter_x: object
    quarter_y: object
    level: object
    total: object
    w: object
    AT: object
    Q: object
    K: object
    V: object
    lse: object
    CT: object
    CTp: object
    N1: object
    r1: object
    HT: object
    G: object
    Gp: object
    N2: object
    r2: object
    vec: object
    msel: object
    cotb: object
    dy: object
    dpre: object
    dF: object
    dFT: object
    dU: object
    dZ: object
    delta: object
    dQT: object
    dvb: object
    dkp: object
    dvp: object
    dkr: object
    dvr: object
    vg: object
    va: object
    vrecv: object
    vb: object
    vt: object
    lsem: object
    ssem: object
    fsem: object
    gs: object
    gr: object
    xs: object
    xr: object
    ks: object
    kr: object
    vs: object
    vr: object


class UpdateIn(NamedTuple):
    fin: object
    fvec: object
    y: object
    dx: object
    masters: object
    firsts: object
    seconds: object


class UpdateOut(NamedTuple):
    out: object
    grad: object
    new_masters: object
    new_firsts: object
    new_seconds: object


class UpdateScratch(NamedTuple):
    inside: object
    wide: object
    isem: object
    osem: object


def named(parts, refs):
    fields, at = {}, 0
    for part in parts:
        leaves, tree = jax.tree.flatten(part)
        fields.update(tree.unflatten(refs[at : at + len(leaves)])._asdict())
        at += len(leaves)
    return SimpleNamespace(**fields)


def call_kernel(kernel, args, outs, scratch, spec, **options):
    leaves, _ = jax.tree.flatten(args)
    out_leaves, out_tree = jax.tree.flatten(outs)
    parts = (args, outs) if scratch is None else (args, outs, scratch)
    empty = jax.tree.map(lambda leaf: 0, parts)
    results = pl.pallas_call(
        functools.partial(kernel, empty),
        out_shape=out_leaves,
        in_specs=[spec] * len(leaves),
        out_specs=[spec] * len(out_leaves),
        scratch_shapes=() if scratch is None else jax.tree.leaves(scratch),
        compiler_params=pltpu.CompilerParams(**options),
    )(*leaves)
    return out_tree.unflatten(results)


class Place:
    def __init__(self):
        self.r = lax.axis_index("rep")
        self.f = lax.axis_index("fsdp")
        self.z = lax.div(self.f, 4)
        self.y = lax.rem(lax.div(self.f, 2), 2)
        self.c = lax.rem(self.f, 2)
        self.xn = (1 - self.r, self.f)
        self.yn = (self.r, self.f + 2 - 4 * self.y)
        self.cn = (self.r, self.f + 1 - 2 * self.c)
        self.dn = (1 - self.r, self.f + 1 - 2 * self.c)

    def zn(self, step, levels):
        other = lax.rem(self.z + step, levels)
        return other, (self.r, other * 4 + 2 * self.y + self.c)


def parity_rows(rows, shards):
    blocks = rows.reshape(shards // 2, 2, rows.shape[0] // shards, rows.shape[1])
    half = rows.shape[0] // 2
    return blocks[:, 0].reshape(half, rows.shape[1]), blocks[:, 1].reshape(half, rows.shape[1])


def go_or_stay(stays, stay, go):
    @pl.when(stays)
    def _():
        stay()

    @pl.when(jnp.logical_not(stays))
    def _():
        go()


def lane_masks():
    lane = lax.broadcasted_iota(jnp.int32, (16, 128), 1)
    low = (lane < 64).astype(F32)
    spots = (lax.rem(lane, 64) == 0).astype(F32)
    return low[:1].astype(BF), (1.0 - low[:1]).astype(BF), spots[:1].astype(BF)


def sizes_of(mesh_n, width, inner):
    shard = width // mesh_n
    rows = [shard // 2] * 6
    rows[KIND_F] = inner // mesh_n // 2
    cols = [width] * 6
    cols[KIND_I] = inner
    return rows, cols


def forward_kernel(parts, levels, eps, *refs):
    R = named(parts, refs)
    me = Place()
    r, f, z, y, c = me.r, me.f, me.z, me.y, me.c
    shards = levels * 4
    S, D = R.A32.shape
    FF = R.G.shape[1]
    ha = levels // 2
    first, second = pl.ds(0, ha), pl.ds(ha, levels - ha)
    source = ((0, D), (0, 2 * D), (0, 0), (1, 0), (2, 0), (3, 0))

    half_loads = {}
    for l in range(2):
        for at, (master, stage) in enumerate(zip(R.masters, R.stages)):
            rows = stage.shape[1]
            cp = pltpu.make_async_copy(master.at[l, pl.ds(r * rows, rows)], stage.at[l], R.msem.at[l, at])
            cp.start()
            half_loads[(l, at)] = cp
    vec_local = pltpu.make_async_copy(R.vecb, R.vecg.at[f], R.xsem.at[0])
    vec_local.start()
    meta_local = pltpu.make_async_copy(R.meta, R.metab.at[0], R.xsem.at[1])
    meta_local.start()

    barrier = pltpu.get_barrier_semaphore()
    peers = [(r, lax.rem(f + s, shards)) for s in range(1, shards)] + [me.xn, me.dn]
    for peer in peers:
        pl.semaphore_signal(barrier, inc=1, device_id=peer, device_id_type=MESH)
    pl.semaphore_wait(barrier, len(peers))

    chunks = []
    for l in range(2):
        for kind in KINDS:
            parts = 2 if kind in (KIND_I, KIND_F) else 1
            span = R.w[kind].shape[-1] // parts
            chunks += [(kind, l, slice(part * span, part * span + span)) for part in range(parts)]
    gs, gr = R.gs, R.gr
    pending = []

    def start(cp):
        cp.start()
        pending.append(cp)
        return cp

    out_copies = {}
    out_at = [0]

    def out(ref, dst, view=None):
        cp = pltpu.make_async_copy(ref if view is None else view, dst, R.osem.at[out_at[0]])
        out_at[0] += 1
        cp.start()
        out_copies[(id(ref), view is not None and out_at[0])] = cp

    def settle(ref):
        if (id(ref), False) in out_copies:
            out_copies.pop((id(ref), False)).wait()

    loaded = set()
    stage_copies = {}

    def g_z(i):
        kind, l, cols = chunks[i]
        w = R.w[kind]
        at, offset = source[kind]
        if (l, at) not in loaded:
            half_loads[(l, at)].wait()
            loaded.add((l, at))
        w[l, z, y, c, r, :, cols] = R.stages[at][l][:, offset + cols.start : offset + cols.stop].astype(BF)
        cps = []
        for s in range(1, levels):
            _, dev = me.zn(s, levels)
            spot = w.at[l, z, y, c, r, :, cols]
            cps.append(start(remote(spot, spot, gs.at[i, s - 1], gr.at[i, s - 1], dev)))
        stage_copies[i] = cps

    def g_1(i):
        kind, l, cols = chunks[i]
        w = R.w[kind]
        for cp in stage_copies[i]:
            cp.wait_recv()
        a, b = w.at[l, first, y, c, r, :, cols], w.at[l, second, y, c, r, :, cols]
        stage_copies[i] = [
            start(remote(a, a, gs.at[i, levels - 1], gr.at[i, levels - 1], me.xn)),
            start(remote(b, b, gs.at[i, levels], gr.at[i, levels], me.yn)),
        ]

    def g_2(i):
        kind, l, cols = chunks[i]
        w = R.w[kind]
        for cp in stage_copies[i]:
            cp.wait_recv()
        a, b = w.at[l, first, y, c, :, :, cols], w.at[l, second, :, c, r, :, cols]
        stage_copies[i] = [
            start(remote(a, a, gs.at[i, levels + 1], gr.at[i, levels + 1], me.yn)),
            start(remote(b, b, gs.at[i, levels + 2], gr.at[i, levels + 2], me.xn)),
        ]

    def g_core(i):
        kind, l, cols = chunks[i]
        w = R.w[kind]
        for cp in stage_copies[i]:
            cp.wait_recv()
        a = w.at[l, :, :, c, :, :, cols]
        stage_copies[i] = [start(remote(a, a, gs.at[i, levels + 3], gr.at[i, levels + 3], me.cn))]

    def g_ready(i):
        kind, l, cols = chunks[i]
        for cp in stage_copies.pop(i):
            cp.wait_recv()
        if cols.stop == R.w[kind].shape[-1]:
            out(R.w[kind], R.w_o[kind].at[l], R.w[kind].at[l])

    steps = (g_z, g_1, g_2, g_core, g_ready)
    reached = [0] * len(chunks)
    turns = iter(FORWARD_TURNS)

    def turn():
        for i in next(turns):
            steps[reached[i]](i)
            reached[i] += 1

    steps[0](0)
    reached[0] = 1
    meta_cp = start(remote(R.meta, R.metab.at[1], R.xs.at[0], R.xr.at[0], me.cn))
    vec_cps = []
    for s in range(1, shards):
        spot = R.vecg.at[f]
        vec_cps.append((s, remote(R.vecb, spot, R.vs.at[s - 1], R.vr.at[s - 1], (r, lax.rem(f + s, shards)))))
    for _, cp in vec_cps:
        start(cp)
    tok_far = remote(R.tok.at[0], R.tokb, R.xs.at[1], R.xr.at[1], me.dn)
    tok_near = pltpu.make_async_copy(R.tok.at[0], R.tokb, R.xsem.at[2])
    stays = c == r

    go_or_stay(stays, tok_near.start, tok_far.start)

    turn()
    vec_local.wait()
    meta_local.wait()
    meta_cp.wait_recv()
    for _, cp in vec_cps:
        cp.wait_recv()
    keep = stays.astype(F32)
    msel = R.msel
    msel[...] = (R.metab[0].astype(F32) * keep + R.metab[1].astype(F32) * (1.0 - keep)).astype(BF)
    vec = R.vec
    for zz in range(levels):
        vec[:, 128 * zz : 128 * zz + 128] = jnp.sum(R.vecg[4 * zz : 4 * zz + 4].astype(F32), axis=0)
    tag_row = msel[2 * S : 2 * S + 16].astype(F32)[:1]
    tag_row = jnp.concatenate([tag_row] * (D // 128), axis=1)
    low, high, spots = lane_masks()

    go_or_stay(stays, tok_near.wait, tok_far.wait)
    cot_far = remote(R.cot.at[0], R.cotb, R.xs.at[2], R.xr.at[2], me.dn)
    cot_near = pltpu.make_async_copy(R.cot.at[0], R.cotb, R.xsem.at[3])

    T = 256
    for l in range(2):
        e = lambda row: vec[16 * l + row : 16 * l + row + 1, :]
        direction = e(0) * (1.0 - tag_row) + e(1) * tag_row
        if l == 1:
            turn()
            go_or_stay(stays, cot_near.start, cot_far.start)
        A32, Ab, Q, K, V, CT = R.A32, R.Ab, R.Q, R.K, R.V, R.CT
        x_in = R.tokb if l == 0 else R.X
        summed = x_in[...].astype(F32) + direction
        A32[...] = summed
        Ab[...] = summed.astype(BF)
        at = Ab[...].T
        even, odd = parity_rows(at, shards)
        settle(R.ATp)
        R.ATp[: D // 2] = even
        R.ATp[D // 2 :] = odd
        out(R.ATp, R.at_o.at[l])

        def weight(kind, lo=0, hi=None):
            w = R.w[kind]
            hi = w.shape[-1] if hi is None else hi
            value = w[l, :, :, :, :, :, lo:hi]
            return value.reshape(-1, hi - lo)

        turn()
        K[l, c] = nn_dot(Ab[...], weight(KIND_K)).astype(BF)
        k_cp = start(remote(K.at[l, c], K.at[l, c], R.ks.at[l, 0], R.kr.at[l, 0], me.cn))
        turn()
        V[l, c] = (nn_dot(Ab[...], weight(KIND_V)) + e(3)).astype(BF)
        v_cp = start(remote(V.at[l, c], V.at[l, c], R.ks.at[l, 1], R.kr.at[l, 1], me.cn))
        turn()
        settle(R.Q)
        q = (nn_dot(Ab[...], weight(KIND_Q)) + e(2)).astype(BF)
        Q[...] = (q.astype(F32) * 0.125).astype(BF)
        out(R.Q, R.q_o.at[l])
        turn()
        k_cp.wait_recv()
        v_cp.wait_recv()
        out(K, R.k_o.at[l], K.at[l])
        out(V, R.v_o.at[l], V.at[l])
        lse = R.lse
        settle(R.lse)
        settle(R.CT)
        bias_rows = msel[: 2 * S]

        def pair(j):
            sl = slice(j * 128, j * 128 + 128)
            k2 = K[l, :, :, sl].reshape(2 * S, 128)
            v2t = V[l, :, :, sl].reshape(2 * S, 128).T
            q2 = Q[:, sl]
            scores = []
            for mine, other in ((low, high), (high, low)):
                scores.append(nt_dot(k2 * mine + bias_rows * other, q2 * mine + spots * other))
            for h, st in enumerate(scores):
                top = jnp.max(st, axis=0, keepdims=True)
                p = jnp.exp(st - top)
                total = jnp.sum(p, axis=0, keepdims=True)
                ctx = nn_dot(v2t, p.astype(BF))[64 * h : 64 * h + 64]
                rows = slice(j * 128 + 64 * h, j * 128 + 64 * h + 64)
                CT[rows] = (ctx * (1.0 / total)).astype(BF)
                lse[j, h : h + 1] = top + jnp.log(total)

        for j in range(D // 128):
            turn()
            pair(j)
        turn()
        out(R.lse, R.lse_o.at[l])
        out(R.CT, R.ct_o.at[l])
        even, odd = parity_rows(CT[...], shards)
        settle(R.CTp)
        R.CTp[: D // 2] = even
        R.CTp[D // 2 :] = odd
        out(R.CTp, R.ctp_o.at[l])
        R.C[...] = CT[...].T
        settle(R.N1)
        settle(R.r1)

        def norm_one(t, carry):
            rows = pl.ds(pl.multiple_of(t * T, T), T)
            pre = A32[rows] + nn_dot(R.C[rows], weight(KIND_O)) + e(4)
            mean = jnp.mean(pre, axis=-1, keepdims=True)
            centred = pre - mean
            rstd = lax.rsqrt(jnp.mean(centred * centred, axis=-1, keepdims=True) + eps)
            n1 = centred * rstd
            hidden = n1 * e(5) + e(6)
            R.N1[rows] = n1
            R.r1[rows] = jnp.broadcast_to(rstd, (T, 128))
            R.H32[rows] = hidden
            R.Hb[rows] = hidden.astype(BF)
            return carry

        turn()
        if l == 1:
            go_or_stay(stays, cot_near.wait, cot_far.wait_recv)
            out(R.cotb, R.cot_o)
        lax.fori_loop(0, S // T, norm_one, 0)
        out(R.N1, R.n1_o.at[l])
        out(R.r1, R.r1_o.at[l])
        even, odd = parity_rows(R.Hb[...].T, shards)
        settle(R.HTp)
        R.HTp[: D // 2] = even
        R.HTp[D // 2 :] = odd
        out(R.HTp, R.ht_o.at[l])
        settle(R.G)
        settle(R.Gp)

        def inner(b):
            u = nn_dot(R.Hb[...], weight(KIND_I, b * D, b * D + D)) + e(10 + b)
            u2 = u * u
            th = jnp.tanh(u * (0.7978845608028654 + 0.035677408136300125 * u2))
            half = 0.5 + 0.5 * th
            slope = 0.7978845608028654 + 0.10703222440890038 * u2
            R.G[:, b * D : b * D + D] = (u * half).astype(BF)
            R.Gp[:, b * D : b * D + D] = (half + 0.5 * u * (1.0 - th * th) * slope).astype(BF)

        for b in range(FF // D):
            if b % 2 == 0:
                turn()
            inner(b)
        out(R.G, R.g_o.at[l])
        out(R.Gp, R.gp_o.at[l])
        turn()
        settle(R.N2)
        settle(R.r2)

        def norm_two(t, carry):
            rows = pl.ds(pl.multiple_of(t * T, T), T)
            pre = R.H32[rows] + nn_dot(R.G[rows], weight(KIND_F)) + e(7)
            mean = jnp.mean(pre, axis=-1, keepdims=True)
            centred = pre - mean
            rstd = lax.rsqrt(jnp.mean(centred * centred, axis=-1, keepdims=True) + eps)
            n2 = centred * rstd
            R.N2[rows] = n2
            R.r2[rows] = jnp.broadcast_to(rstd, (T, 128))
            R.X[rows] = n2 * e(8) + e(9)
            return carry

        lax.fori_loop(0, S // T, norm_two, 0)
        out(R.N2, R.n2_o.at[l])
        out(R.r2, R.r2_o.at[l])

    turn()
    R.Yb[...] = R.X[...].astype(BF)
    out(R.Yb, R.y_o)
    out(vec, R.vec_o)
    out(msel, R.meta_o)
    for cp in out_copies.values():
        cp.wait()
    for cp in pending:
        cp.wait_send()
    go_or_stay(stays, lambda: None, cot_far.wait_send)


def backward_kernel(parts, levels, *refs):
    R = named(parts, refs)
    me = Place()
    r, f, z, y, c = me.r, me.f, me.z, me.y, me.c
    shards = levels * 4
    S, D = R.dy.shape
    FF = R.G.shape[1]
    ha = levels // 2
    hb = levels - ha
    first, second = pl.ds(0, ha), pl.ds(ha, hb)
    saved = list(zip(R.w, R.w_o)) + [
        (R.AT, R.at_o), (R.Q, R.q_o), (R.K, R.k_o), (R.V, R.v_o), (R.lse, R.lse_o), (R.CT, R.ct_o), (R.CTp, R.ctp_o),
        (R.N1, R.n1_o), (R.r1, R.r1_o), (R.HT, R.ht_o), (R.G, R.g_o), (R.Gp, R.gp_o), (R.N2, R.n2_o), (R.r2, R.r2_o),
    ]
    order = {id(ref): at for at, (ref, _) in enumerate(saved)}
    loads = {}

    def load(ref, l):
        at = order[id(ref)]
        cp = pltpu.make_async_copy(saved[at][1].at[l], ref, R.lsem.at[l, at])
        cp.start()
        loads[id(ref)] = cp

    def use(ref):
        if id(ref) in loads:
            loads.pop(id(ref)).wait()
        return ref

    small = []
    for at, (dst, src) in enumerate(((R.vec, R.vec_o), (R.msel, R.meta_o), (R.cotb, R.cot_o))):
        cp = pltpu.make_async_copy(src, dst, R.ssem.at[at])
        cp.start()
        small.append(cp)
    wk, wv, wq, wo, wi, wf = R.w
    for ref in (R.N2, R.r2, R.G, wf, R.Gp, R.HT, wi, R.N1, R.r1, R.CTp, wo, R.CT, R.K, R.V, R.Q, R.lse, R.AT, wq, wk, wv):
        load(ref, 1)

    barrier = pltpu.get_barrier_semaphore()
    peers = [me.zn(s, levels)[1] for s in range(1, levels)] + [me.xn, me.yn, me.cn, me.dn]
    for peer in peers:
        pl.semaphore_signal(barrier, inc=1, device_id=peer, device_id_type=MESH)
    pl.semaphore_wait(barrier, len(peers))

    pending = []

    def start(cp):
        cp.start()
        pending.append(cp)
        return cp

    stays = c == r
    y_far = remote(R.y_o, R.yo, R.xs.at[0], R.xr.at[0], me.dn)
    y_near = pltpu.make_async_copy(R.y_o, R.yo, R.ssem.at[3])
    dx_cps = []

    go_or_stay(stays, y_near.start, y_far.start)

    gs, gr = R.gs, R.gr
    chunks = [(kind, l) for l in (1, 0) for kind in (KIND_F, KIND_I, KIND_O, KIND_Q, KIND_K, KIND_V)]
    chunks += [(None, 1), (None, 0)]
    flight = {}
    stage = {}
    fin_copies = []

    def rs_core(i):
        kind, l = chunks[i]
        g = R.g[kind]
        spot = g.at[0, 0] if l == 1 else R.landing[kind]
        flight[i] = [start(remote(g.at[l, 1 - c], spot, gs.at[i, 0], gr.at[i, 0], me.cn))]

    def rs_1(i):
        kind, l = chunks[i]
        g = R.g[kind]
        g[l, c] = g[l, c] + (g[0, 0] if l == 1 else R.landing[kind][...])
        flight[i] = [
            start(remote(g.at[l, c, first, 1 - y], R.half_y[kind].at[l], gs.at[i, 1], gr.at[i, 1], me.yn)),
            start(remote(g.at[l, c, second, :, 1 - r], R.half_x[kind].at[l], gs.at[i, 2], gr.at[i, 2], me.xn)),
        ]

    def rs_2(i):
        kind, l = chunks[i]
        g = R.g[kind]
        g[l, c, first, y] = g[l, c, first, y] + R.half_y[kind][l]
        g[l, c, second, :, r] = g[l, c, second, :, r] + R.half_x[kind][l]
        flight[i] = [
            start(remote(g.at[l, c, first, y, 1 - r], R.quarter_x[kind].at[l], gs.at[i, 3], gr.at[i, 3], me.xn)),
            start(remote(g.at[l, c, second, 1 - y, r], R.quarter_y[kind].at[l], gs.at[i, 4], gr.at[i, 4], me.yn)),
        ]

    def rs_3(i):
        kind, l = chunks[i]
        g = R.g[kind]
        g[l, c, first, y, r] = g[l, c, first, y, r] + R.quarter_x[kind][l]
        g[l, c, second, y, r] = g[l, c, second, y, r] + R.quarter_y[kind][l]
        flight[i] = []
        for s in range(1, levels):
            there, dev = me.zn(s, levels)
            flight[i].append(
                start(remote(g.at[l, c, there, y, r], R.level[kind].at[l, s - 1], gs.at[i, 4 + s], gr.at[i, 4 + s], dev))
            )

    def rs_4(i):
        kind, l = chunks[i]
        g, fin = R.g[kind], R.total[kind]
        total = g[l, c, z, y, r].astype(F32)
        for s in range(levels - 1):
            total = total + R.level[kind][l, s].astype(F32)
        fin[l, r] = total.astype(BF)
        flight[i] = [start(remote(fin.at[l, r], fin.at[l, r], gs.at[i, 4 + levels], gr.at[i, 4 + levels], me.xn))]

    def rs_5(i):
        kind, l = chunks[i]
        cp = pltpu.make_async_copy(R.total[kind].at[l], R.fin[kind].at[l], R.fsem.at[i])
        cp.start()
        fin_copies.append(cp)

    vg, va, vb, vt = R.vg, R.va, R.vb, R.vt

    def vec_hop(at, device):
        def step(i):
            l = chunks[i][1]
            if at == 0:
                va[l, 0] = vg[16 * l : 16 * l + 16]
            else:
                va[l, at] = va[l, at - 1] + R.vrecv[l, at - 1]
            flight[i] = [start(remote(va.at[l, at], R.vrecv.at[l, at], R.vs.at[l, at], R.vr.at[l, at], device))]

        return step

    def vec_level(i):
        l = chunks[i][1]
        va[l, 3] = va[l, 2] + R.vrecv[l, 2]
        flight[i] = []
        for s in range(1, levels):
            there, dev = me.zn(s, levels)
            lanes = pl.ds(pl.multiple_of(there * 128, 128), 128)
            flight[i].append(start(remote(va.at[l, 3, :, lanes], vb.at[l, s - 1], R.vs.at[l, 2 + s], R.vr.at[l, 2 + s], dev)))

    def vec_end(i):
        l = chunks[i][1]
        total = va[l, 3, :, pl.ds(pl.multiple_of(z * 128, 128), 128)]
        for s in range(levels - 1):
            total = total + vb[l, s]
        vt[16 * l : 16 * l + 16] = total

    matrix_steps = (rs_core, rs_1, rs_2, rs_3, rs_4, rs_5)
    vec_steps = (vec_hop(0, me.cn), vec_hop(1, me.xn), vec_hop(2, me.yn), vec_level, vec_end)
    turns = iter(BACKWARD_TURNS)

    def turn():
        for i in next(turns):
            at = stage.get(i, 0)
            for cp in flight.pop(i, ()):
                cp.wait_recv()
            (matrix_steps if chunks[i][0] is not None else vec_steps)[at](i)
            stage[i] = at + 1

    for cp in small:
        cp.wait()
    vec, msel = R.vec, R.msel
    tag_row = msel[2 * S : 2 * S + 16].astype(F32)[:1]
    tag_row = jnp.concatenate([tag_row] * (D // 128), axis=1)
    low, high, spots = lane_masks()
    low32 = low.astype(F32)
    vg[...] = jnp.zeros_like(vg)
    R.dy[...] = R.cotb[...].astype(F32)
    T = 256
    dy, dpre, dF, dFT, dU, dZ = R.dy, R.dpre, R.dF, R.dFT, R.dU, R.dZ

    def fold(value):
        return jnp.sum(value.reshape(value.shape[0] // 8, 8, value.shape[1]), axis=0)

    zero8 = jnp.zeros((8, D), F32)

    for l in (1, 0):
        base = 16 * l
        e = lambda row: vec[base + row : base + row + 1, :]

        def put(row, value):
            vg[base + row : base + row + 1, :] = value

        def weight(kind):
            w = R.w[kind]
            return w[...].reshape(-1, w.shape[-1])

        turn()
        N2, r2 = use(R.N2), use(R.r2)

        def norm_two(t, carry):
            s7, s8, s9 = carry
            rows = pl.ds(pl.multiple_of(t * T, T), T)
            g, n = dy[rows], N2[rows]
            dn = g * e(8)
            m1 = jnp.mean(dn, axis=-1, keepdims=True)
            m2 = jnp.mean(dn * n, axis=-1, keepdims=True)
            d = r2[rows][:, :1] * (dn - m1 - n * m2)
            dpre[rows] = d
            db = d.astype(BF)
            dF[rows] = db
            dFT[:, rows] = db.T
            return s7 + fold(db.astype(F32)), s8 + fold(g * n), s9 + fold(g)

        s7, s8, s9 = lax.fori_loop(0, S // T, norm_two, (zero8, zero8, zero8))
        put(7, jnp.sum(s7, axis=0, keepdims=True))
        put(8, jnp.sum(s8, axis=0, keepdims=True))
        put(9, jnp.sum(s9, axis=0, keepdims=True))
        turn()
        G = use(R.G)
        gf = R.g[KIND_F]
        piece = 2 * FF // shards

        def grad_f(t, carry):
            d = nn_dot(dFT[...], G[:, pl.ds(pl.multiple_of(t * piece, piece), piece)]).astype(BF)
            zz, yy = lax.div(t, 2), lax.rem(t, 2)
            half = piece // 2
            gf[l, 0, zz, yy] = d[:, :half].reshape(2, D // 2, half)
            gf[l, 1, zz, yy] = d[:, half:].reshape(2, D // 2, half)
            return carry

        lax.fori_loop(0, shards // 2, grad_f, 0)
        if l == 1:
            for ref in (R.N2, R.r2, R.G):
                load(ref, 0)
        use(R.w[KIND_F])
        Gp = use(R.Gp)

        def grad_inner(b):
            wf = R.w[KIND_F]
            quarter = wf[b * (levels // (FF // D)) : (b + 1) * (levels // (FF // D))].reshape(D, D)
            cols = slice(b * D, b * D + D)
            du = (nt_dot(dF[...], quarter) * Gp[:, cols].astype(F32)).astype(BF)
            dU[:, cols] = du
            put(10 + b, jnp.sum(fold(du.astype(F32)), axis=0, keepdims=True))

        for b in range(FF // D):
            if b % 2 == 0:
                turn()
            grad_inner(b)
        turn()
        if l == 1:
            load(R.w[KIND_F], 0)
            load(R.Gp, 0)
        HT = use(R.HT)
        gi = R.g[KIND_I]
        rows_i = 2 * R.g[KIND_I].shape[-2]

        for b in range(FF // D):
            d = nn_dot(HT[...], dU[:, b * D : b * D + D]).astype(BF)
            for cc in range(2):
                part = d[cc * (D // 2) : (cc + 1) * (D // 2)]
                gi[l, cc, :, :, :, :, b * D : b * D + D] = part.reshape(levels, 2, 2, rows_i // 2, D)
        if l == 1:
            load(R.HT, 0)
        use(R.w[KIND_I])
        N1, r1 = use(R.N1), use(R.r1)

        def norm_one(t, carry):
            s4, s5, s6 = carry
            rows = pl.ds(pl.multiple_of(t * T, T), T)
            g = dpre[rows] + nt_dot(dU[rows], weight(KIND_I))
            n = N1[rows]
            dn = g * e(5)
            m1 = jnp.mean(dn, axis=-1, keepdims=True)
            m2 = jnp.mean(dn * n, axis=-1, keepdims=True)
            d = r1[rows][:, :1] * (dn - m1 - n * m2)
            dy[rows] = d
            db = d.astype(BF)
            dZ[rows] = db
            return s4 + fold(db.astype(F32)), s5 + fold(g * n), s6 + fold(g)

        turn()
        sums = lax.fori_loop(0, S // T // 2, norm_one, (zero8, zero8, zero8))
        turn()
        s4, s5, s6 = lax.fori_loop(S // T // 2, S // T, norm_one, sums)
        put(4, jnp.sum(s4, axis=0, keepdims=True))
        put(5, jnp.sum(s5, axis=0, keepdims=True))
        put(6, jnp.sum(s6, axis=0, keepdims=True))
        turn()
        if l == 1:
            for ref in (R.w[KIND_I], R.N1, R.r1):
                load(ref, 0)
        CTp = use(R.CTp)
        go = R.g[KIND_O]

        def store(ref, value):
            for cc in range(2):
                ref[l, cc] = value[cc * (D // 2) : (cc + 1) * (D // 2)].reshape(ref.shape[2:])

        store(R.g[KIND_O], nn_dot(CTp[...], dZ[...]).astype(BF))
        use(R.w[KIND_O])
        dF[...] = nt_dot(dZ[...], weight(KIND_O)).astype(BF)
        CT = use(R.CT)
        dct = dF[...].T
        prod = dct.astype(F32) * CT[...].astype(F32)
        prod = jnp.sum(prod.reshape(D // 64, 64, S), axis=1)
        for j in range(D // 128):
            R.delta[j, :2] = prod[2 * j : 2 * j + 2]
        if l == 1:
            for ref in (R.CTp, R.w[KIND_O], R.CT):
                load(ref, 0)
        K, V, Q, lse = use(R.K), use(R.V), use(R.Q), use(R.lse)
        delta, dC, dQT = R.delta, dF, R.dQT
        dkp, dvp, dkr, dvr = R.dkp, R.dvp, R.dkr, R.dvr
        bias_rows = msel[: 2 * S]

        def pair(j):
            sl = slice(j * 128, j * 128 + 128)
            k2 = K[:, :, sl].reshape(2 * S, 128)
            v2 = V[:, :, sl].reshape(2 * S, 128)
            k2t = k2.T
            q2 = Q[:, sl]
            dc2 = dC[:, sl]
            dk_sum, dv_sum = None, None
            for h in range(2):
                mine, other = (low, high) if h == 0 else (high, low)
                mine32 = low32 if h == 0 else 1.0 - low32
                kh = k2 * mine + bias_rows * other
                vh = v2 * mine
                qh = q2 * mine + spots * other
                dk_h, dv_h = None, None
                for part in range(S // 256):
                    cols = slice(part * 256, part * 256 + 256)
                    st = nt_dot(kh, qh[cols])
                    p = jnp.exp(st - lse[j, h : h + 1, cols])
                    dp = nt_dot(vh, dc2[cols])
                    ds = (p * (dp - delta[j, h : h + 1, cols])).astype(BF)
                    pb = p.astype(BF)
                    dv = nn_dot(pb, dc2[cols])
                    dk = nn_dot(ds, q2[cols])
                    dv_h = dv if dv_h is None else dv_h + dv
                    dk_h = dk if dk_h is None else dk_h + dk
                    dq = nn_dot(k2t, ds)[64 * h : 64 * h + 64]
                    rows = slice(j * 128 + 64 * h, j * 128 + 64 * h + 64)
                    dQT[rows, cols] = (dq * 0.125).astype(BF)
                dk_sum = dk_h * mine32 if dk_sum is None else dk_sum + dk_h * mine32
                dv_sum = dv_h * mine32 if dv_sum is None else dv_sum + dv_h * mine32
            dkp[l, :, j] = dk_sum.astype(BF).reshape(2, S, 128)
            dvp[l, :, j] = dv_sum.astype(BF).reshape(2, S, 128)

        pairs = D // 128
        half_pairs = pairs // 2
        kv_cps = []
        for j in range(pairs):
            turn()
            pair(j)
            if (j + 1) % half_pairs == 0:
                part = j // half_pairs
                js = pl.ds(part * half_pairs, half_pairs)
                for at, (mine, theirs) in enumerate(((dkp, dkr), (dvp, dvr))):
                    sems = R.ks.at[l, part, at], R.kr.at[l, part, at]
                    kv_cps.append(start(remote(mine.at[l, 1 - c, js], theirs.at[l, js], *sems, me.cn)))
        if l == 1:
            for ref in (R.K, R.V, R.Q, R.lse):
                load(ref, 0)
        turn()
        AT = use(R.AT)
        dqb = dZ
        dqb[...] = dQT[...].T
        store(R.g[KIND_Q], nn_dot(AT[...], dqb[...]).astype(BF))
        turn()
        for cp in kv_cps:
            cp.wait_recv()
        dkb, dvb = dFT, R.dvb
        for j in range(pairs):
            dkb[:, 128 * j : 128 * j + 128] = dkp[l, c, j] + dkr[l, j]
            dvb[:, 128 * j : 128 * j + 128] = dvp[l, c, j] + dvr[l, j]
        store(R.g[KIND_K], nn_dot(AT[...], dkb[...]).astype(BF))
        store(R.g[KIND_V], nn_dot(AT[...], dvb[...]).astype(BF))
        if l == 1:
            load(R.AT, 0)
        use(R.w[KIND_Q])
        use(R.w[KIND_K])
        use(R.w[KIND_V])

        def last(t, carry):
            s0, s2, s3 = carry
            rows = pl.ds(pl.multiple_of(t * T, T), T)
            d = dy[rows] + nt_dot(dqb[rows], weight(KIND_Q)) + nt_dot(dkb[rows], weight(KIND_K)) + nt_dot(dvb[rows], weight(KIND_V))
            dy[rows] = d
            return s0 + fold(d), s2 + fold(dqb[rows].astype(F32)), s3 + fold(dvb[rows].astype(F32))

        sums = (zero8, zero8, zero8)
        for part in range(2):
            turn()
            sums = lax.fori_loop(part * (S // T // 2), (part + 1) * (S // T // 2), last, sums)
            if l == 0:
                half = pl.ds(part * (S // 2), S // 2)
                R.cotb[half] = dy[half].astype(BF)
                far = remote(R.cotb.at[half], R.dxo.at[half], R.xs.at[1 + part], R.xr.at[1 + part], me.dn)
                near = pltpu.make_async_copy(R.cotb.at[half], R.dxo.at[half], R.ssem.at[4 + part])
                dx_cps.append((far, near))
                go_or_stay(stays, near.start, far.start)
        s0, s2, s3 = sums
        s0 = jnp.sum(s0, axis=0, keepdims=True)
        put(0, s0 * (1.0 - tag_row))
        put(1, s0 * tag_row)
        put(2, jnp.sum(s2, axis=0, keepdims=True))
        put(3, jnp.sum(s3, axis=0, keepdims=True))
        if l == 1:
            for ref in (R.w[KIND_Q], R.w[KIND_K], R.w[KIND_V]):
                load(ref, 0)

    turn()
    vec_out = pltpu.make_async_copy(vt, R.vec_g, R.ssem.at[6])
    vec_out.start()
    for cp in fin_copies:
        cp.wait()
    vec_out.wait()
    for cp in pending:
        cp.wait_send()

    for far, near in dx_cps:
        go_or_stay(stays, near.wait, far.wait)
    go_or_stay(stays, y_near.wait, y_far.wait)


def update_kernel(parts, rates, decays, *refs):
    R = named(parts, refs)
    f = lax.axis_index("fsdp")
    sources, _ = jax.tree.flatten((R.fin, R.fvec, R.y, R.dx, R.masters, R.firsts, R.seconds))
    places, tree = jax.tree.flatten(R.inside)
    copies = [pltpu.make_async_copy(s, p, R.isem.at[at]) for at, (s, p) in enumerate(zip(sources, places))]
    for cp in copies:
        cp.start()
    fin, fvec, y, dx, masters, firsts, seconds = R.inside
    waits = tree.unflatten(copies)
    finals = (R.new_masters, R.new_firsts, R.new_seconds)
    leaving = []

    def leave(src, dst):
        cp = pltpu.make_async_copy(src, dst, R.osem.at[len(leaving)])
        cp.start()
        leaving.append(cp)

    def arrive(at, kinds):
        for cp in [waits[0][k] for k in kinds] + [w[at] for w in waits[4:]]:
            cp.wait()

    def step(at, where, grad):
        new = adamw(masters[at][where], firsts[at][where], seconds[at][where], grad, rates[at], decays[at])
        for refs, value in zip((masters, firsts, seconds), new):
            refs[at][where] = value

    def done(at):
        for kept, final in zip((masters, firsts, seconds), finals):
            leave(kept[at], final[at])

    D = dx.shape[1]
    for at, kind in ((2, KIND_I), (3, KIND_F), (1, KIND_O)):
        arrive(at, (kind,))
        for l in range(2):
            ref = fin[kind]
            grad = ref[l].astype(F32).reshape(-1, ref.shape[-1])
            step(at, (l,), grad.T if kind == KIND_F else grad)
        done(at)
    arrive(0, (KIND_Q, KIND_K, KIND_V))
    for l in range(2):
        for at, kind in enumerate((KIND_Q, KIND_K, KIND_V)):
            grad = fin[kind][l].astype(F32).reshape(-1, D)
            step(0, (l, slice(None), slice(at * D, at * D + D)), grad)
    done(0)
    arrive(4, ())
    waits[1].wait()
    wide = masters[4].shape[2]
    rows = masters[4].shape[1]
    span = 128 // wide
    slot = lax.rem(f, span)
    for l in range(2):
        block = fvec[16 * l : 16 * l + 16]
        grad = block[:, :wide]
        for s in range(1, span):
            grad = jnp.where(slot == s, block[:, s * wide : s * wide + wide], grad)
        step(4, (l,), grad[:rows])
    done(4)
    waits[2].wait()
    leave(y, R.out.at[0])
    waits[3].wait()
    R.wide[...] = dx[...].astype(F32)
    leave(R.wide, R.grad.at[0])
    for cp in leaving:
        cp.wait()


def fast_body(
    tokens, cotangent, tags, lengths, key_mask,
    master_qkv, master_out, master_in, master_feed_output, master_vec,
    first_qkv, first_out, first_in, first_ffo, first_vec,
    second_qkv, second_out, second_in, second_ffo, second_moment_vector,
    shards,
):
    S, D = tokens.shape[1:]
    FF = master_in.shape[2]
    levels = shards // 4
    rows, cols = sizes_of(shards, D, FF)
    f = lax.axis_index("fsdp")
    key_count = key_mask.shape[1]
    key_pos = jnp.arange(key_count, dtype=jnp.int32)
    valid = key_pos < lengths[0]
    key_valid = valid & ((key_mask[0] == 1) | (key_pos == 0))
    lane = jnp.arange(128, dtype=jnp.int32)
    bias = jnp.where(key_valid, 0.0, masked_score).astype(F32)
    meta = jnp.where((lane % 64 == 0)[None, :], bias[:, None], 0.0)
    tag_rows = jnp.full((16, 128), tags[0], F32)
    meta = jnp.concatenate([meta, tag_rows], axis=0).astype(BF)
    start_row = lax.axis_index("rep") * S
    query_valid = (start_row + jnp.arange(S, dtype=jnp.int32)) < lengths[0]
    cot = jnp.where(query_valid[None, :, None], cotangent, jnp.zeros_like(cotangent))
    wide = master_vec.shape[2]
    vec_rows = jnp.pad(master_vec, ((0, 0), (0, 16 - master_vec.shape[1]), (0, 0))).reshape(32, wide)
    slot = (lane // wide) == lax.rem(f, 128 // wide)
    vecb = jnp.where(slot[None, :], jnp.tile(vec_rows, (1, 128 // wide)), 0.0).astype(BF)

    hbm = pl.BlockSpec(memory_space=pl.ANY)
    shape = jax.ShapeDtypeStruct
    V = pltpu.VMEM
    dma = pltpu.SemaphoreType.DMA
    w_tail = [(levels, 2, 2, 2, rows[k], cols[k]) for k in KINDS]
    masters = (master_qkv, master_out, master_in, master_feed_output, master_vec)
    firsts = (first_qkv, first_out, first_in, first_ffo, first_vec)
    seconds = (second_qkv, second_out, second_in, second_ffo, second_moment_vector)

    saved = call_kernel(
        lambda parts, *refs: forward_kernel(parts, levels, norm_epsilon, *refs),
        ForwardIn(tok=tokens, cot=cot, meta=meta, vecb=vecb, masters=masters[:4]),
        Saved(
            w_o=tuple(shape((2,) + tail, BF) for tail in w_tail),
            vec_o=shape((32, D), F32),
            meta_o=shape(meta.shape, BF),
            cot_o=shape((S, D), BF),
            y_o=shape((S, D), BF),
            at_o=shape((2, D, S), BF),
            q_o=shape((2, S, D), BF),
            k_o=shape((2, 2, S, D), BF),
            v_o=shape((2, 2, S, D), BF),
            lse_o=shape((2, D // 128, 8, S), F32),
            ct_o=shape((2, D, S), BF),
            ctp_o=shape((2, D, S), BF),
            n1_o=shape((2, S, D), F32),
            r1_o=shape((2, S, 128), F32),
            ht_o=shape((2, D, S), BF),
            g_o=shape((2, S, FF), BF),
            gp_o=shape((2, S, FF), BF),
            n2_o=shape((2, S, D), F32),
            r2_o=shape((2, S, 128), F32),
        ),
        ForwardScratch(
            w=tuple(V((2,) + tail, BF) for tail in w_tail),
            stages=tuple(V((2, m.shape[1] // 2, m.shape[2]), F32) for m in masters[:4]),
            vecg=V((shards, 32, 128), BF),
            vec=V((32, D), F32),
            metab=V((2,) + meta.shape, BF),
            msel=V(meta.shape, BF),
            tokb=V((S, D), BF),
            cotb=V((S, D), BF),
            A32=V((S, D), F32),
            Ab=V((S, D), BF),
            ATp=V((D, S), BF),
            Q=V((S, D), BF),
            K=V((2, 2, S, D), BF),
            V=V((2, 2, S, D), BF),
            lse=V((D // 128, 8, S), F32),
            CT=V((D, S), BF),
            CTp=V((D, S), BF),
            C=V((S, D), BF),
            N1=V((S, D), F32),
            r1=V((S, 128), F32),
            H32=V((S, D), F32),
            Hb=V((S, D), BF),
            HTp=V((D, S), BF),
            G=V((S, FF), BF),
            Gp=V((S, FF), BF),
            N2=V((S, D), F32),
            r2=V((S, 128), F32),
            X=V((S, D), F32),
            Yb=V((S, D), BF),
            msem=dma((2, 4)),
            xsem=dma((4,)),
            osem=dma((48,)),
            gs=dma((16, levels + 4)),
            gr=dma((16, levels + 4)),
            vs=dma((shards - 1,)),
            vr=dma((shards - 1,)),
            xs=dma((3,)),
            xr=dma((3,)),
            ks=dma((2, 2)),
            kr=dma((2, 2)),
        ),
        hbm,
        collective_id=0,
        has_side_effects=True,
        vmem_limit_bytes=VMEM_BYTES,
    )

    tails = [(rows[k], cols[k]) for k in KINDS]
    tails[KIND_F] = (D // 2, FF // shards)
    ha, hb = levels // 2, levels - levels // 2
    each = lambda *lead: tuple(V(lead + tail, BF) for tail in tails)
    grads = call_kernel(
        lambda parts, *refs: backward_kernel(parts, levels, *refs),
        saved,
        BackwardOut(
            fin=tuple(shape((2, 2) + tail, BF) for tail in tails),
            vec_g=shape((32, 128), F32),
            yo=shape((S, D), BF),
            dxo=shape((S, D), BF),
        ),
        BackwardScratch(
            g=each(2, 2, levels, 2, 2),
            landing=each(levels, 2, 2),
            half_y=each(2, ha, 2),
            half_x=each(2, hb, 2),
            quarter_x=each(2, ha),
            quarter_y=each(2, hb),
            level=each(2, levels - 1),
            total=each(2, 2),
            w=tuple(V(tail, BF) for tail in w_tail),
            AT=V((D, S), BF),
            Q=V((S, D), BF),
            K=V((2, S, D), BF),
            V=V((2, S, D), BF),
            lse=V((D // 128, 8, S), F32),
            CT=V((D, S), BF),
            CTp=V((D, S), BF),
            N1=V((S, D), F32),
            r1=V((S, 128), F32),
            HT=V((D, S), BF),
            G=V((S, FF), BF),
            Gp=V((S, FF), BF),
            N2=V((S, D), F32),
            r2=V((S, 128), F32),
            vec=V((32, D), F32),
            msel=V(meta.shape, BF),
            cotb=V((S, D), BF),
            dy=V((S, D), F32),
            dpre=V((S, D), F32),
            dF=V((S, D), BF),
            dFT=V((D, S), BF),
            dU=V((S, FF), BF),
            dZ=V((S, D), BF),
            delta=V((D // 128, 8, S), F32),
            dQT=V((D, S), BF),
            dvb=V((S, D), BF),
            dkp=V((2, 2, D // 128, S, 128), BF),
            dvp=V((2, 2, D // 128, S, 128), BF),
            dkr=V((2, D // 128, S, 128), BF),
            dvr=V((2, D // 128, S, 128), BF),
            vg=V((32, D), F32),
            va=V((2, 4, 16, D), F32),
            vrecv=V((2, 3, 16, D), F32),
            vb=V((2, levels - 1, 16, 128), F32),
            vt=V((32, 128), F32),
            lsem=dma((2, 20)),
            ssem=dma((7,)),
            fsem=dma((12,)),
            gs=dma((12, levels + 5)),
            gr=dma((12, levels + 5)),
            xs=dma((3,)),
            xr=dma((3,)),
            ks=dma((2, 2, 2)),
            kr=dma((2, 2, 2)),
            vs=dma((2, levels + 2)),
            vr=dma((2, levels + 2)),
        ),
        hbm,
        collective_id=1,
        has_side_effects=True,
        vmem_limit_bytes=VMEM_BYTES,
    )

    rates = (
        matrix_rate * D ** (-0.5),
        matrix_rate * (D // 16) ** (-0.5),
        matrix_rate * D ** (-0.5),
        matrix_rate * (FF // 2) ** (-0.5),
        vector_rate,
    )
    decays = (weight_decay, weight_decay, weight_decay, weight_decay, 0.0)
    like = tuple(shape(p.shape, F32) for p in masters)
    new = call_kernel(
        lambda parts, *refs: update_kernel(parts, rates, decays, *refs),
        UpdateIn(fin=grads.fin, fvec=grads.vec_g, y=grads.yo, dx=grads.dxo, masters=masters, firsts=firsts, seconds=seconds),
        UpdateOut(
            out=shape(tokens.shape, BF),
            grad=shape(tokens.shape, F32),
            new_masters=like,
            new_firsts=like,
            new_seconds=like,
        ),
        UpdateScratch(
            inside=(
                tuple(V(g.shape, BF) for g in grads.fin),
                V((32, 128), F32),
                V((S, D), BF),
                V((S, D), BF),
                *(tuple(V(p.shape, F32) for p in masters) for _ in range(3)),
            ),
            wide=V((S, D), F32),
            isem=dma((24,)),
            osem=dma((17,)),
        ),
        hbm,
        vmem_limit_bytes=VMEM_BYTES,
    )
    return (new.out, new.grad, *new.new_masters, *new.new_firsts, *new.new_seconds)


def solution(mesh):
    placed = (
        P("fsdp", "rep", None),
        P("fsdp", "rep", None),
        P("fsdp"),
        P("fsdp"),
        P("fsdp", None),
        P(None, "fsdp", None),
        P(None, "fsdp", None),
        P(None, "fsdp", None),
        P(None, "fsdp", None),
        P(None, None, "fsdp"),
        P(None, "fsdp", None),
        P(None, "fsdp", None),
        P(None, "fsdp", None),
        P(None, "fsdp", None),
        P(None, None, "fsdp"),
        P(None, "fsdp", None),
        P(None, "fsdp", None),
        P(None, "fsdp", None),
        P(None, "fsdp", None),
        P(None, None, "fsdp"),
    )
    shards = mesh.shape["fsdp"]

    def chosen(*args):
        tokens, master_in = args[0], args[7]
        width = tokens.shape[2]
        whole_tiles = shards * 32 == width and master_in.shape[2] == 4 * width
        if mesh.shape["rep"] == 2 and shards % 4 == 0 and whole_tiles:
            return fast_body(*args, shards)
        return body(*args)

    return jax.shard_map(
        chosen,
        mesh=mesh,
        in_specs=placed,
        out_specs=(
            P("fsdp", "rep", None),
            P("fsdp", "rep", None),
            P(None, "fsdp", None),
            P(None, "fsdp", None),
            P(None, "fsdp", None),
            P(None, "fsdp", None),
            P(None, None, "fsdp"),
            P(None, "fsdp", None),
            P(None, "fsdp", None),
            P(None, "fsdp", None),
            P(None, "fsdp", None),
            P(None, None, "fsdp"),
            P(None, "fsdp", None),
            P(None, "fsdp", None),
            P(None, "fsdp", None),
            P(None, "fsdp", None),
            P(None, None, "fsdp"),
        ),
        check_vma=False,
    )
```

```python
import functools
from types import SimpleNamespace
from typing import NamedTuple

import jax
import jax.numpy as jnp
from jax import lax
from jax.experimental import pallas as pl
from jax.experimental.pallas import tpu as pltpu
from jax.sharding import PartitionSpec as P

D = 512
H = 8
FF = 2048
STEP = 10


beta_decay = 0.5
epsilon_adam = 1e-08
weight_decay = 0.01
norm_epsilon = 1e-05
masked_score = -1000000000.0
vector_rate = 0.15
matrix_rate = 0.5


def layer_norm(pre_norm, gain_row, offset_row):
    centre_mean = jnp.mean(pre_norm, axis=-1, keepdims=True)
    centred = pre_norm - centre_mean
    variance = jnp.mean(centred * centred, axis=-1, keepdims=True)
    return centred * lax.rsqrt(variance + norm_epsilon) * gain_row + offset_row


def tanh_gelu_activation(inner_act):
    return jax.nn.gelu(inner_act, approximate=True)


def adamw(master, first, second, grad, rate, decay):
    first_new = beta_decay * first + (1.0 - beta_decay) * grad
    second_new = beta_decay * second + (1.0 - beta_decay) * grad * grad
    correction = 1.0 - beta_decay**STEP
    direction = first_new / correction / (jnp.sqrt(second_new / correction) + epsilon_adam)
    master_new = master - rate * (direction + decay * master)
    return (master_new, first_new, second_new)


def score_block(query_heads, key_heads, key_bias, score_scale):
    scores = jnp.einsum("qhd,khd->hqk", query_heads, key_heads, preferred_element_type=jnp.float32)
    return scores * score_scale + key_bias[None, None, :]


def forward_layer(input_rows, weights, tag_value, key_bias):
    w_qkv, w_out, w_in, w_ffo, vectors_low = weights
    vectors = vectors_low.astype(jnp.float32)
    model_width = w_out.shape[0]
    row_count = input_rows.shape[0]
    head_size = model_width // H
    score_scale = head_size ** (-0.5)
    direction = jnp.where(tag_value == 0, vectors[0], vectors[1])
    summed = input_rows + direction[None, :]
    summed_low = summed.astype(jnp.bfloat16)
    projected = jnp.dot(summed_low, w_qkv, preferred_element_type=jnp.float32)
    queries = (projected[:, :model_width] + vectors[2]).astype(jnp.bfloat16)
    keys_local = projected[:, model_width : 2 * model_width].astype(jnp.bfloat16)
    local_values = (projected[:, 2 * model_width :] + vectors[3]).astype(jnp.bfloat16)
    keys_all, values_all = (
        lax.all_gather(keys_local, "rep", axis=0, tiled=True),
        lax.all_gather(local_values, "rep", axis=0, tiled=True),
    )
    key_count = keys_all.shape[0]
    query_heads = queries.reshape(row_count, H, head_size)
    key_heads = keys_all.reshape(key_count, H, head_size)
    value_heads = values_all.reshape(key_count, H, head_size)
    scores = score_block(query_heads, key_heads, key_bias, score_scale)
    row_top = jnp.max(scores, axis=-1, keepdims=True)
    exponent_terms = jnp.exp(scores - row_top)
    totals = jnp.sum(exponent_terms, axis=-1, keepdims=True)
    soft_weights = exponent_terms / totals
    log_total = row_top + jnp.log(totals)
    context = jnp.einsum(
        "hqk,khd->qhd",
        soft_weights.astype(jnp.bfloat16),
        value_heads,
        preferred_element_type=jnp.float32,
    )
    context_low = context.reshape(row_count, model_width).astype(jnp.bfloat16)
    branch = jnp.dot(context_low, w_out, preferred_element_type=jnp.float32) + vectors[4]
    hidden, norm_first = jax.vjp(layer_norm, summed + branch, vectors[5], vectors[6])
    hidden_low = hidden.astype(jnp.bfloat16)
    inner_act = jnp.dot(hidden_low, w_in, preferred_element_type=jnp.float32) + vectors[
        10:
    ].reshape(-1)
    activated, gelu_pull = jax.vjp(tanh_gelu_activation, inner_act)
    activated_low = activated.astype(jnp.bfloat16)
    feed_out = jnp.dot(activated_low, w_ffo, preferred_element_type=jnp.float32) + vectors[7]
    result, norm_second = jax.vjp(layer_norm, hidden + feed_out, vectors[8], vectors[9])
    saved_state = (
        summed_low,
        query_heads,
        key_heads,
        value_heads,
        log_total,
        context_low,
        norm_first,
        hidden_low,
        gelu_pull,
        activated_low,
        norm_second,
    )
    return (result, saved_state)


def attention_grads(
    query_heads, key_heads, value_heads, log_total, context_heads, key_bias, score_scale
):
    row_count = query_heads.shape[0]
    model_width = query_heads.shape[1] * query_heads.shape[2]
    scores = score_block(query_heads, key_heads, key_bias, score_scale)
    soft_weights = jnp.exp(scores - log_total)
    grad_soft = jnp.einsum(
        "qhd,khd->hqk", context_heads, value_heads, preferred_element_type=jnp.float32
    )
    row_inner = jnp.sum(soft_weights * grad_soft, axis=-1, keepdims=True)
    grad_scores = (soft_weights * (grad_soft - row_inner) * score_scale).astype(jnp.bfloat16)
    grad_queries = jnp.einsum(
        "hqk,khd->qhd", grad_scores, key_heads, preferred_element_type=jnp.float32
    ).reshape(row_count, model_width)
    key_terms = jnp.einsum(
        "hqk,qhd->khd", grad_scores, query_heads, preferred_element_type=jnp.float32
    ).reshape(-1, model_width)
    value_terms = jnp.einsum(
        "hqk,qhd->khd",
        soft_weights.astype(jnp.bfloat16),
        context_heads,
        preferred_element_type=jnp.float32,
    ).reshape(-1, model_width)
    grad_keys, grad_values = (
        lax.psum_scatter(
            key_terms.astype(jnp.bfloat16), "rep", scatter_dimension=0, tiled=True
        ).astype(jnp.float32),
        lax.psum_scatter(
            value_terms.astype(jnp.bfloat16), "rep", scatter_dimension=0, tiled=True
        ).astype(jnp.float32),
    )
    return (grad_queries, grad_keys, grad_values)


def backward_layer(grad_result, saved_state, weights, tag_value, key_bias):
    w_qkv, w_out, w_in, w_ffo, vectors_low = weights
    (
        summed_low,
        query_heads,
        key_heads,
        value_heads,
        log_total,
        context_low,
        norm_first,
        hidden_low,
        gelu_pull,
        activated_low,
        norm_second,
    ) = saved_state
    model_width = w_out.shape[0]
    row_count = summed_low.shape[0]
    head_size = model_width // H
    score_scale = head_size ** (-0.5)
    grad_pre_two, grad_gain_two, grad_shift_two = norm_second(grad_result)
    grad_feed = grad_pre_two.astype(jnp.bfloat16)
    grad_bias_feed = jnp.sum(grad_feed.astype(jnp.float32), axis=0)
    grad_ffo = jnp.einsum("tf,td->fd", activated_low, grad_feed, preferred_element_type=jnp.float32)
    grad_activated = jnp.einsum("td,fd->tf", grad_feed, w_ffo, preferred_element_type=jnp.float32)
    grad_inner = gelu_pull(grad_activated)[0].astype(jnp.bfloat16)
    grad_bias_inner = jnp.sum(grad_inner.astype(jnp.float32), axis=0)
    grad_in = jnp.einsum("td,tf->df", hidden_low, grad_inner, preferred_element_type=jnp.float32)
    grad_hidden = grad_pre_two + jnp.einsum(
        "tf,df->td", grad_inner, w_in, preferred_element_type=jnp.float32
    )
    grad_pre_one, grad_gain_one, grad_shift_one = norm_first(grad_hidden)
    grad_branch = grad_pre_one.astype(jnp.bfloat16)
    grad_bias_out = jnp.sum(grad_branch.astype(jnp.float32), axis=0)
    grad_out_matrix = jnp.einsum(
        "te,td->ed", context_low, grad_branch, preferred_element_type=jnp.float32
    )
    grad_context = jnp.einsum(
        "td,ed->te", grad_branch, w_out, preferred_element_type=jnp.float32
    ).astype(jnp.bfloat16)
    context_heads = grad_context.reshape(row_count, H, head_size)
    grad_queries, grad_keys, grad_values = attention_grads(
        query_heads, key_heads, value_heads, log_total, context_heads, key_bias, score_scale
    )
    grad_joined = jnp.concatenate(
        [
            grad_queries.astype(jnp.bfloat16),
            grad_keys.astype(jnp.bfloat16),
            grad_values.astype(jnp.bfloat16),
        ],
        axis=1,
    )
    grad_qkv = jnp.einsum("td,te->de", summed_low, grad_joined, preferred_element_type=jnp.float32)
    grad_summed = grad_pre_one + jnp.einsum(
        "te,de->td", grad_joined, w_qkv, preferred_element_type=jnp.float32
    )
    column_sums = jnp.sum(grad_joined.astype(jnp.float32), axis=0)
    grad_direction = jnp.sum(grad_summed, axis=0)
    zero_row = jnp.zeros_like(grad_direction)
    grad_rows = jnp.stack(
        [
            jnp.where(tag_value == 0, grad_direction, zero_row),
            jnp.where(tag_value == 1, grad_direction, zero_row),
            column_sums[:model_width],
            column_sums[2 * model_width :],
            grad_bias_out,
            grad_gain_one,
            grad_shift_one,
            grad_bias_feed,
            grad_gain_two,
            grad_shift_two,
        ],
        axis=0,
    )
    grad_vectors = jnp.concatenate([grad_rows, grad_bias_inner.reshape(-1, model_width)], axis=0)
    return (grad_summed, (grad_qkv, grad_out_matrix, grad_in, grad_ffo, grad_vectors))


def reduce_layer(grads):
    shards = (
        lax.psum_scatter(grads[0], "fsdp", scatter_dimension=0, tiled=True),
        lax.psum_scatter(grads[1], "fsdp", scatter_dimension=0, tiled=True),
        lax.psum_scatter(grads[2], "fsdp", scatter_dimension=0, tiled=True),
        lax.psum_scatter(grads[3], "fsdp", scatter_dimension=0, tiled=True),
        lax.psum_scatter(grads[4], "fsdp", scatter_dimension=1, tiled=True),
    )
    return (
        lax.psum(shards[0].astype(jnp.bfloat16), "rep").astype(jnp.float32),
        lax.psum(shards[1].astype(jnp.bfloat16), "rep").astype(jnp.float32),
        lax.psum(shards[2].astype(jnp.bfloat16), "rep").astype(jnp.float32),
        lax.psum(shards[3].astype(jnp.bfloat16), "rep").astype(jnp.float32),
        lax.psum(shards[4].astype(jnp.bfloat16), "rep").astype(jnp.float32),
    )


def body(
    tokens,
    cotangent,
    tags,
    lengths,
    key_mask,
    master_qkv,
    master_out,
    master_in,
    master_feed_output,
    master_vec,
    first_qkv,
    first_out,
    first_in,
    first_ffo,
    first_vec,
    second_qkv,
    second_out,
    second_in,
    second_ffo,
    second_moment_vector,
):
    row_count = tokens.shape[1]
    key_count = key_mask.shape[1]
    start_row = lax.axis_index("rep") * row_count
    query_pos = start_row + jnp.arange(row_count, dtype=jnp.int32)
    key_pos = jnp.arange(key_count, dtype=jnp.int32)
    seq_length = lengths[0]
    tag_value = tags[0]
    key_valid = (key_pos < seq_length) & ((key_mask[0] == 1) | (key_pos == 0))
    key_bias = jnp.where(key_valid, 0.0, masked_score).astype(jnp.float32)
    query_valid = (query_pos < seq_length).astype(jnp.float32)
    masters = (master_qkv, master_out, master_in, master_feed_output, master_vec)
    firsts = (first_qkv, first_out, first_in, first_ffo, first_vec)
    seconds = (second_qkv, second_out, second_in, second_ffo, second_moment_vector)
    shared = (
        lax.all_gather(master_qkv[0].astype(jnp.bfloat16), "fsdp", axis=0, tiled=True),
        lax.all_gather(master_out[0].astype(jnp.bfloat16), "fsdp", axis=0, tiled=True),
        lax.all_gather(master_in[0].astype(jnp.bfloat16), "fsdp", axis=0, tiled=True),
        lax.all_gather(master_feed_output[0].astype(jnp.bfloat16), "fsdp", axis=0, tiled=True),
        lax.all_gather(master_vec[0].astype(jnp.bfloat16), "fsdp", axis=1, tiled=True),
    )
    shared_out, saved_shared = forward_layer(
        tokens[0].astype(jnp.float32), shared, tag_value, key_bias
    )
    unique = (
        lax.all_gather(master_qkv[1].astype(jnp.bfloat16), "fsdp", axis=0, tiled=True),
        lax.all_gather(master_out[1].astype(jnp.bfloat16), "fsdp", axis=0, tiled=True),
        lax.all_gather(master_in[1].astype(jnp.bfloat16), "fsdp", axis=0, tiled=True),
        lax.all_gather(master_feed_output[1].astype(jnp.bfloat16), "fsdp", axis=0, tiled=True),
        lax.all_gather(master_vec[1].astype(jnp.bfloat16), "fsdp", axis=1, tiled=True),
    )
    final_out, saved_unique = forward_layer(shared_out, unique, tag_value, key_bias)
    grad_final = cotangent[0].astype(jnp.float32) * query_valid[:, None]
    unique_back = (
        lax.all_gather(master_qkv[1].astype(jnp.bfloat16), "fsdp", axis=0, tiled=True),
        lax.all_gather(master_out[1].astype(jnp.bfloat16), "fsdp", axis=0, tiled=True),
        lax.all_gather(master_in[1].astype(jnp.bfloat16), "fsdp", axis=0, tiled=True),
        lax.all_gather(master_feed_output[1].astype(jnp.bfloat16), "fsdp", axis=0, tiled=True),
        lax.all_gather(master_vec[1].astype(jnp.bfloat16), "fsdp", axis=1, tiled=True),
    )
    grad_middle, unique_grads = backward_layer(
        grad_final, saved_unique, unique_back, tag_value, key_bias
    )
    reduced_unique = reduce_layer(unique_grads)
    grad_inputs, shared_grads = backward_layer(
        grad_middle, saved_shared, shared, tag_value, key_bias
    )
    reduced_shared = reduce_layer(shared_grads)
    rates = (
        matrix_rate * D ** (-0.5),
        matrix_rate * (D // 16) ** (-0.5),
        matrix_rate * D ** (-0.5),
        matrix_rate * (FF // 2) ** (-0.5),
        vector_rate,
    )
    decays = (weight_decay, weight_decay, weight_decay, weight_decay, 0.0)
    updated = []
    for kind_index in range(5):
        grad_stack = jnp.stack([reduced_shared[kind_index], reduced_unique[kind_index]], axis=0)
        updated.append(
            adamw(
                masters[kind_index],
                firsts[kind_index],
                seconds[kind_index],
                grad_stack,
                rates[kind_index],
                decays[kind_index],
            )
        )
    return (
        final_out.astype(jnp.bfloat16)[None],
        grad_inputs[None],
        updated[0][0],
        updated[1][0],
        updated[2][0],
        updated[3][0],
        updated[4][0],
        updated[0][1],
        updated[1][1],
        updated[2][1],
        updated[3][1],
        updated[4][1],
        updated[0][2],
        updated[1][2],
        updated[2][2],
        updated[3][2],
        updated[4][2],
    )


BF = jnp.bfloat16
F32 = jnp.float32
MESH = pl.DeviceIdType.MESH
KIND_K, KIND_V, KIND_Q, KIND_O, KIND_I, KIND_F = KINDS = tuple(range(6))
VMEM_BYTES = 60 << 20
FORWARD_SPLIT = (2, 2, 1, 2, 2, 1, 3, 2, 0, 2, 1, 2, 3, 0, 2, 3)
BACKWARD_SPLIT = (2, 2, 0, 1, 0, 3, 2, 2, 0, 3, 0, 2)
WHOLE_LEVEL_KINDS = (KIND_O, KIND_K)
FORWARD_TURNS = (
    (1, 2, 0, 3, 1, 4, 2),
    (0, 3, 5, 1, 2, 4, 6, 0, 3, 5, 0, 1, 7),
    (2, 1),
    (6, 8, 4, 9, 2),
    (),
    (3, 10, 5, 7),
    (8, 3, 9, 6),
    (10,),
    (4,),
    (),
    (11,),
    (4,),
    (5, 8, 12, 7, 11, 9, 5, 13, 6, 14, 10, 8),
    (12, 6, 15, 7, 11, 9, 14, 7),
    (9, 10, 13),
    (15,),
    (),
    (12, 10),
    (),
    (11,),
    (14,),
    (11,),
    (15,),
    (12,),
    (),
    (14, 12),
    (13, 14, 15, 13),
    (15,),
    (),
)
COTANGENT_AT = 0
BACKWARD_TURNS = (
    (),
    (),
    (0,),
    (),
    (),
    (1,),
    (),
    (0,),
    (2,),
    (1, 2),
    (),
    (0,),
    (2,),
    (1, 3),
    (4, 5),
    (),
    (12, 3),
    (0, 2, 4, 5, 12),
    (1, 3, 6),
    (2,),
    (5, 12),
    (7,),
    (2, 0, 3, 6, 5, 12),
    (),
    (7, 8),
    (0, 4, 8),
    (6,),
    (1, 3),
    (4, 5, 7, 12),
    (9,),
    (10, 11, 6),
    (),
    (9, 1, 13, 3, 10, 4, 8, 5, 11, 13, 7, 8, 6, 9, 4, 11, 10, 13, 8, 6, 9, 10, 11, 13, 8, 7, 10, 9, 11, 13, 7, 10, 9, 11),
)


def nt_dot(left, right):
    return lax.dot_general(left, right, (((1,), (1,)), ((), ())), preferred_element_type=F32)


def nn_dot(left, right):
    return jnp.dot(left, right, preferred_element_type=F32)


def remote(src, dst, send_sem, recv_sem, device):
    return pltpu.make_async_remote_copy(
        src_ref=src,
        dst_ref=dst,
        send_sem=send_sem,
        recv_sem=recv_sem,
        device_id=device,
        device_id_type=MESH,
    )


class ForwardIn(NamedTuple):
    tok: object
    cot: object
    lengths: object
    tags: object
    key_mask: object
    vectors: object
    masters: object


class Saved(NamedTuple):
    w_o: object
    vec_o: object
    meta_o: object
    cot_o: object
    y_o: object
    at_o: object
    q_o: object
    k_o: object
    v_o: object
    lse_o: object
    ct_o: object
    ctp_o: object
    n1_o: object
    r1_o: object
    ht_o: object
    g_o: object
    gp_o: object
    n2_o: object
    r2_o: object


class ForwardScratch(NamedTuple):
    w: object
    stages: object
    vecg: object
    vec: object
    metab: object
    msel: object
    tokb: object
    cotb: object
    A32: object
    Ab: object
    ATp: object
    Q: object
    K: object
    V: object
    lse: object
    CT: object
    CTp: object
    C: object
    N1: object
    r1: object
    H32: object
    Hb: object
    HTp: object
    G: object
    Gp: object
    N2: object
    r2: object
    X: object
    Yb: object
    msem: object
    xsem: object
    osem: object
    gs: object
    gr: object
    vs: object
    vr: object
    xs: object
    xr: object
    ks: object
    kr: object


class BackwardOut(NamedTuple):
    fin: object
    vec_g: object
    yo: object
    dxo: object


class BackwardScratch(NamedTuple):
    g: object
    landing: object
    half: object
    quarter: object
    level: object
    total: object
    w: object
    AT: object
    Q: object
    K: object
    V: object
    lse: object
    CT: object
    CTp: object
    N1: object
    r1: object
    HT: object
    G: object
    Gp: object
    N2: object
    r2: object
    vec: object
    msel: object
    cotb: object
    dy: object
    dpre: object
    dF: object
    dFT: object
    dU: object
    dZ: object
    delta: object
    dQT: object
    dvb: object
    dkp: object
    dvp: object
    dkr: object
    dvr: object
    vg: object
    va: object
    vrecv: object
    vb: object
    vt: object
    lsem: object
    ssem: object
    fsem: object
    gs: object
    gr: object
    xs: object
    xr: object
    ks: object
    kr: object
    vs: object
    vr: object


class UpdateIn(NamedTuple):
    fin: object
    fvec: object
    y: object
    dx: object
    masters: object
    firsts: object
    seconds: object


class UpdateOut(NamedTuple):
    out: object
    grad: object
    new_masters: object
    new_firsts: object
    new_seconds: object


class UpdateScratch(NamedTuple):
    inside: object
    wide: object
    isem: object
    osem: object


def named(parts, refs):
    fields, at = {}, 0
    for part in parts:
        leaves, tree = jax.tree.flatten(part)
        fields.update(tree.unflatten(refs[at : at + len(leaves)])._asdict())
        at += len(leaves)
    return SimpleNamespace(**fields)


def call_kernel(kernel, args, outs, scratch, spec, **options):
    leaves, _ = jax.tree.flatten(args)
    out_leaves, out_tree = jax.tree.flatten(outs)
    parts = (args, outs) if scratch is None else (args, outs, scratch)
    empty = jax.tree.map(lambda leaf: 0, parts)
    results = pl.pallas_call(
        functools.partial(kernel, empty),
        out_shape=out_leaves,
        in_specs=jax.tree.leaves(spec) if isinstance(spec, tuple) else [spec] * len(leaves),
        out_specs=[pl.BlockSpec(memory_space=pl.ANY)] * len(out_leaves),
        scratch_shapes=() if scratch is None else jax.tree.leaves(scratch),
        compiler_params=pltpu.CompilerParams(**options),
    )(*leaves)
    return out_tree.unflatten(results)


class Place:
    def __init__(self):
        self.r = lax.axis_index("rep")
        self.f = lax.axis_index("fsdp")
        self.z = lax.div(self.f, 4)
        self.y = lax.rem(lax.div(self.f, 2), 2)
        self.c = lax.rem(self.f, 2)
        self.xn = (1 - self.r, self.f)
        self.yn = (self.r, self.f + 2 - 4 * self.y)
        self.cn = (self.r, self.f + 1 - 2 * self.c)
        self.dn = (1 - self.r, self.f + 1 - 2 * self.c)

    def zn(self, step, levels):
        other = lax.rem(self.z + step, levels)
        return other, (self.r, other * 4 + 2 * self.y + self.c)


def parity_rows(rows, shards):
    blocks = rows.reshape(shards // 2, 2, rows.shape[0] // shards, rows.shape[1])
    half = rows.shape[0] // 2
    return blocks[:, 0].reshape(half, rows.shape[1]), blocks[:, 1].reshape(half, rows.shape[1])


def halves(cut, levels):
    return pl.ds(0, cut), pl.ds(cut, levels - cut)


def go_or_stay(stays, stay, go):
    @pl.when(stays)
    def _():
        stay()

    @pl.when(jnp.logical_not(stays))
    def _():
        go()


def lane_masks():
    lane = lax.broadcasted_iota(jnp.int32, (16, 128), 1)
    low = (lane < 64).astype(F32)
    spots = (lax.rem(lane, 64) == 0).astype(F32)
    return low[:1].astype(BF), (1.0 - low[:1]).astype(BF), spots[:1].astype(BF)


def sizes_of(mesh_n, width, inner):
    shard = width // mesh_n
    rows = [shard // 2] * 6
    rows[KIND_F] = inner // mesh_n // 2
    cols = [width] * 6
    cols[KIND_I] = inner
    return rows, cols


def forward_kernel(parts, levels, eps, *refs):
    R = named(parts, refs)
    me = Place()
    r, f, z, y, c = me.r, me.f, me.z, me.y, me.c
    shards = levels * 4
    S, D = R.A32.shape
    FF = R.G.shape[1]
    source = ((0, D), (0, 2 * D), (0, 0), (1, 0), (2, 0), (3, 0))

    half_loads = {}
    for l in range(2):
        for at, (master, stage) in enumerate(zip(R.masters, R.stages)):
            cp = pltpu.make_async_copy(master.at[l], stage.at[l], R.msem.at[l, at])
            cp.start()
            half_loads[(l, at)] = cp
    barrier = pltpu.get_barrier_semaphore()
    peers = [(r, lax.rem(f + s, shards)) for s in range(1, shards)] + [me.xn, me.dn]
    for peer in peers:
        pl.semaphore_signal(barrier, inc=1, device_id=peer, device_id_type=MESH)
    pl.semaphore_wait(barrier, len(peers))

    chunks = []
    for l in range(2):
        for kind in KINDS:
            parts = 2 if kind in (KIND_I, KIND_F) else 1
            span = R.w[kind].shape[-1] // parts
            chunks += [(kind, l, slice(part * span, part * span + span)) for part in range(parts)]
    gs, gr = R.gs, R.gr
    pending = []

    def start(cp):
        cp.start()
        pending.append(cp)
        return cp

    out_copies = {}
    out_at = [0]

    def out(ref, dst, view=None):
        cp = pltpu.make_async_copy(ref if view is None else view, dst, R.osem.at[out_at[0]])
        out_at[0] += 1
        cp.start()
        out_copies[(id(ref), view is not None and out_at[0])] = cp

    def settle(ref):
        if (id(ref), False) in out_copies:
            out_copies.pop((id(ref), False)).wait()

    loaded = set()
    stage_copies = {}

    def g_z(i):
        kind, l, cols = chunks[i]
        w = R.w[kind]
        at, offset = source[kind]
        if (l, at) not in loaded:
            half_loads[(l, at)].wait()
            loaded.add((l, at))
        rows = w.shape[5]
        w[l, z, y, c, r, :, cols] = R.stages[at][l, pl.ds(r * rows, rows), offset + cols.start : offset + cols.stop].astype(BF)
        cps = []
        for s in range(1, levels):
            _, dev = me.zn(s, levels)
            spot = w.at[l, z, y, c, r, :, cols]
            cps.append(start(remote(spot, spot, gs.at[i, s - 1], gr.at[i, s - 1], dev)))
        stage_copies[i] = cps

    def g_1(i):
        kind, l, cols = chunks[i]
        w = R.w[kind]
        for cp in stage_copies[i]:
            cp.wait_recv()
        first, second = halves(FORWARD_SPLIT[i], levels)
        a, b = w.at[l, first, y, c, r, :, cols], w.at[l, second, y, c, r, :, cols]
        stage_copies[i] = [
            start(remote(a, a, gs.at[i, levels - 1], gr.at[i, levels - 1], me.xn)),
            start(remote(b, b, gs.at[i, levels], gr.at[i, levels], me.yn)),
        ]

    def g_2(i):
        kind, l, cols = chunks[i]
        w = R.w[kind]
        for cp in stage_copies[i]:
            cp.wait_recv()
        first, second = halves(FORWARD_SPLIT[i], levels)
        a, b = w.at[l, first, y, c, :, :, cols], w.at[l, second, :, c, r, :, cols]
        stage_copies[i] = [
            start(remote(a, a, gs.at[i, levels + 1], gr.at[i, levels + 1], me.yn)),
            start(remote(b, b, gs.at[i, levels + 2], gr.at[i, levels + 2], me.xn)),
        ]

    def g_core(i):
        kind, l, cols = chunks[i]
        w = R.w[kind]
        for cp in stage_copies[i]:
            cp.wait_recv()
        a = w.at[l, :, :, c, :, :, cols]
        stage_copies[i] = [start(remote(a, a, gs.at[i, levels + 3], gr.at[i, levels + 3], me.cn))]

    def h_y(i):
        kind, l, cols = chunks[i]
        w = R.w[kind]
        at, offset = source[kind]
        if (l, at) not in loaded:
            half_loads[(l, at)].wait()
            loaded.add((l, at))
        whole = R.stages[at][l][:, offset + cols.start : offset + cols.stop].astype(BF)
        w[l, z, y, c, :, :, cols] = whole.reshape(2, whole.shape[0] // 2, whole.shape[1])
        spot = w.at[l, z, y, c, :, :, cols]
        stage_copies[i] = [start(remote(spot, spot, gs.at[i, 0], gr.at[i, 0], me.yn))]

    def h_z(i):
        kind, l, cols = chunks[i]
        w = R.w[kind]
        for cp in stage_copies[i]:
            cp.wait_recv()
        spot = w.at[l, z, :, c, :, :, cols]
        stage_copies[i] = [
            start(remote(spot, spot, gs.at[i, s], gr.at[i, s], me.zn(s, levels)[1])) for s in range(1, levels)
        ]

    def g_ready(i):
        kind, l, cols = chunks[i]
        for cp in stage_copies.pop(i):
            cp.wait_recv()
        if cols.stop == R.w[kind].shape[-1]:
            out(R.w[kind], R.w_o[kind].at[l], R.w[kind].at[l])

    steps = (g_z, g_1, g_2, g_core, g_ready)
    other_steps = (h_y, h_z, g_core, g_ready)
    reached = [0] * len(chunks)
    turns = iter(FORWARD_TURNS)

    def turn():
        for i in next(turns):
            (steps if FORWARD_SPLIT[i] else other_steps)[reached[i]](i)
            reached[i] += 1

    steps[0](0)
    reached[0] = 1
    tok_far = remote(R.tok.at[0], R.tokb, R.xs.at[1], R.xr.at[1], me.dn)
    tok_near = pltpu.make_async_copy(R.tok.at[0], R.tokb, R.xsem.at[2])
    stays = c == r

    go_or_stay(stays, tok_near.start, tok_far.start)
    length = R.lengths[0]
    keys = R.key_mask[...]
    key_pos = lax.broadcasted_iota(jnp.int32, keys.shape, 1)
    valid = key_pos < length
    bias = jnp.where(valid & ((keys == 1) | (key_pos == 0)), 0.0, masked_score)
    place = lax.broadcasted_iota(jnp.int32, (128, 2 * S), 0)
    columns = jnp.where(lax.rem(place, 64) == 0, bias, 0.0) + jnp.where((place == 1) & valid, 1.0, 0.0)
    R.metab[0, : 2 * S] = columns.T.astype(BF)
    R.metab[0, 2 * S :] = jnp.full((16, 128), R.tags[0].astype(F32)).astype(BF)
    meta_cp = start(remote(R.metab.at[0], R.metab.at[1], R.xs.at[0], R.xr.at[0], me.cn))
    wide = R.vectors.shape[2]
    lane = lax.broadcasted_iota(jnp.int32, (R.vectors.shape[0], 128), 1)
    R.vecg[f] = jnp.zeros((32, 128), BF)
    for l in range(2):
        block = jnp.concatenate([R.vectors[:, l]] * (128 // wide), axis=1)
        block = jnp.where(lax.div(lane, wide) == lax.rem(f, 128 // wide), block, 0.0)
        block = jnp.concatenate([block, jnp.zeros((16 - block.shape[0], 128), F32)], axis=0)
        R.vecg[f, 16 * l : 16 * l + 16] = block.astype(BF)
    vec_cps = []
    for s in range(1, shards):
        spot = R.vecg.at[f]
        vec_cps.append((s, remote(spot, spot, R.vs.at[s - 1], R.vr.at[s - 1], (r, lax.rem(f + s, shards)))))
    for _, cp in vec_cps:
        start(cp)
    turn()
    meta_cp.wait_recv()
    for _, cp in vec_cps:
        cp.wait_recv()
    keep = stays.astype(F32)
    msel = R.msel
    msel[...] = (R.metab[0].astype(F32) * keep + R.metab[1].astype(F32) * (1.0 - keep)).astype(BF)
    vec = R.vec
    for zz in range(levels):
        vec[:, 128 * zz : 128 * zz + 128] = jnp.sum(R.vecg[4 * zz : 4 * zz + 4].astype(F32), axis=0)
    tag_row = msel[2 * S : 2 * S + 16].astype(F32)[:1]
    tag_row = jnp.concatenate([tag_row] * (D // 128), axis=1)
    low, high, spots = lane_masks()

    go_or_stay(stays, tok_near.wait, tok_far.wait)
    cot_far = remote(R.cot.at[0], R.cotb, R.xs.at[2], R.xr.at[2], me.dn)
    cot_near = pltpu.make_async_copy(R.cot.at[0], R.cotb, R.xsem.at[3])

    T = 256
    for l in range(2):
        e = lambda row: vec[16 * l + row : 16 * l + row + 1, :]
        direction = e(0) * (1.0 - tag_row) + e(1) * tag_row
        if l == 1:
            turn()
        A32, Ab, Q, K, V, CT = R.A32, R.Ab, R.Q, R.K, R.V, R.CT
        x_in = R.tokb if l == 0 else R.X
        summed = x_in[...].astype(F32) + direction
        A32[...] = summed
        Ab[...] = summed.astype(BF)
        at = Ab[...].T
        even, odd = parity_rows(at, shards)
        settle(R.ATp)
        R.ATp[: D // 2] = even
        R.ATp[D // 2 :] = odd
        out(R.ATp, R.at_o.at[l])

        def weight(kind, lo=0, hi=None):
            w = R.w[kind]
            hi = w.shape[-1] if hi is None else hi
            value = w[l, :, :, :, :, :, lo:hi]
            return value.reshape(-1, hi - lo)

        turn()
        K[l, c] = nn_dot(Ab[...], weight(KIND_K)).astype(BF)
        k_cp = start(remote(K.at[l, c], K.at[l, c], R.ks.at[l, 0], R.kr.at[l, 0], me.cn))
        turn()
        V[l, c] = (nn_dot(Ab[...], weight(KIND_V)) + e(3)).astype(BF)
        v_cp = start(remote(V.at[l, c], V.at[l, c], R.ks.at[l, 1], R.kr.at[l, 1], me.cn))
        turn()
        settle(R.Q)
        q = (nn_dot(Ab[...], weight(KIND_Q)) + e(2)).astype(BF)
        Q[...] = (q.astype(F32) * 0.125).astype(BF)
        out(R.Q, R.q_o.at[l])
        turn()
        k_cp.wait_recv()
        v_cp.wait_recv()
        out(K, R.k_o.at[l], K.at[l])
        out(V, R.v_o.at[l], V.at[l])
        lse = R.lse
        settle(R.lse)
        settle(R.CT)
        bias_rows = msel[: 2 * S]

        def pair(j):
            sl = slice(j * 128, j * 128 + 128)
            k2 = K[l, :, :, sl].reshape(2 * S, 128)
            v2t = V[l, :, :, sl].reshape(2 * S, 128).T
            q2 = Q[:, sl]
            scores = []
            for mine, other in ((low, high), (high, low)):
                scores.append(nt_dot(k2 * mine + bias_rows * other, q2 * mine + spots * other))
            for h, st in enumerate(scores):
                top = jnp.max(st, axis=0, keepdims=True)
                p = jnp.exp(st - top)
                total = jnp.sum(p, axis=0, keepdims=True)
                ctx = nn_dot(v2t, p.astype(BF))[64 * h : 64 * h + 64]
                rows = slice(j * 128 + 64 * h, j * 128 + 64 * h + 64)
                CT[rows] = (ctx * (1.0 / total)).astype(BF)
                lse[j, h : h + 1] = top + jnp.log(total)

        for j in range(D // 128):
            turn()
            pair(j)
        turn()
        out(R.lse, R.lse_o.at[l])
        out(R.CT, R.ct_o.at[l])
        even, odd = parity_rows(CT[...], shards)
        settle(R.CTp)
        R.CTp[: D // 2] = even
        R.CTp[D // 2 :] = odd
        out(R.CTp, R.ctp_o.at[l])
        R.C[...] = CT[...].T
        settle(R.N1)
        settle(R.r1)

        def norm_one(t, carry):
            rows = pl.ds(pl.multiple_of(t * T, T), T)
            pre = A32[rows] + nn_dot(R.C[rows], weight(KIND_O)) + e(4)
            mean = jnp.mean(pre, axis=-1, keepdims=True)
            centred = pre - mean
            rstd = lax.rsqrt(jnp.mean(centred * centred, axis=-1, keepdims=True) + eps)
            n1 = centred * rstd
            hidden = n1 * e(5) + e(6)
            R.N1[rows] = n1
            R.r1[rows] = jnp.broadcast_to(rstd, (T, 128))
            R.H32[rows] = hidden
            R.Hb[rows] = hidden.astype(BF)
            return carry

        turn()
        lax.fori_loop(0, S // T, norm_one, 0)
        out(R.N1, R.n1_o.at[l])
        out(R.r1, R.r1_o.at[l])
        even, odd = parity_rows(R.Hb[...].T, shards)
        settle(R.HTp)
        R.HTp[: D // 2] = even
        R.HTp[D // 2 :] = odd
        out(R.HTp, R.ht_o.at[l])
        settle(R.G)
        settle(R.Gp)

        def inner(b):
            u = nn_dot(R.Hb[...], weight(KIND_I, b * D, b * D + D)) + e(10 + b)
            u2 = u * u
            th = jnp.tanh(u * (0.7978845608028654 + 0.035677408136300125 * u2))
            half = 0.5 + 0.5 * th
            slope = 0.7978845608028654 + 0.10703222440890038 * u2
            R.G[:, b * D : b * D + D] = (u * half).astype(BF)
            R.Gp[:, b * D : b * D + D] = (half + 0.5 * u * (1.0 - th * th) * slope).astype(BF)

        for b in range(FF // D):
            if b % 2 == 0:
                turn()
            if l == 1 and b == COTANGENT_AT:
                go_or_stay(stays, cot_near.start, cot_far.start)
            inner(b)
        out(R.G, R.g_o.at[l])
        out(R.Gp, R.gp_o.at[l])
        turn()
        settle(R.N2)
        settle(R.r2)

        def norm_two(t, carry):
            rows = pl.ds(pl.multiple_of(t * T, T), T)
            pre = R.H32[rows] + nn_dot(R.G[rows], weight(KIND_F)) + e(7)
            mean = jnp.mean(pre, axis=-1, keepdims=True)
            centred = pre - mean
            rstd = lax.rsqrt(jnp.mean(centred * centred, axis=-1, keepdims=True) + eps)
            n2 = centred * rstd
            R.N2[rows] = n2
            R.r2[rows] = jnp.broadcast_to(rstd, (T, 128))
            R.X[rows] = n2 * e(8) + e(9)
            return carry

        lax.fori_loop(0, S // T, norm_two, 0)
        out(R.N2, R.n2_o.at[l])
        out(R.r2, R.r2_o.at[l])

    turn()
    R.Yb[...] = R.X[...].astype(BF)
    out(R.Yb, R.y_o)
    out(vec, R.vec_o)
    out(msel, R.meta_o)
    go_or_stay(stays, cot_near.wait, cot_far.wait_recv)
    out(R.cotb, R.cot_o)
    for cp in out_copies.values():
        cp.wait()
    for cp in pending:
        cp.wait_send()
    go_or_stay(stays, lambda: None, cot_far.wait_send)


def backward_kernel(parts, levels, *refs):
    R = named(parts, refs)
    me = Place()
    r, f, z, y, c = me.r, me.f, me.z, me.y, me.c
    shards = levels * 4
    S, D = R.dy.shape
    FF = R.G.shape[1]
    saved = list(zip(R.w, R.w_o)) + [
        (R.AT, R.at_o), (R.Q, R.q_o), (R.K, R.k_o), (R.V, R.v_o), (R.lse, R.lse_o), (R.CT, R.ct_o), (R.CTp, R.ctp_o),
        (R.N1, R.n1_o), (R.r1, R.r1_o), (R.HT, R.ht_o), (R.G, R.g_o), (R.Gp, R.gp_o), (R.N2, R.n2_o), (R.r2, R.r2_o),
    ]
    order = {id(ref): at for at, (ref, _) in enumerate(saved)}
    loads = {}

    def load(ref, l):
        at = order[id(ref)]
        cp = pltpu.make_async_copy(saved[at][1].at[l], ref, R.lsem.at[l, at])
        cp.start()
        loads[id(ref)] = cp

    def use(ref):
        if id(ref) in loads:
            loads.pop(id(ref)).wait()
        return ref

    small = []
    for at, (dst, src) in enumerate(((R.vec, R.vec_o), (R.msel, R.meta_o), (R.cotb, R.cot_o))):
        cp = pltpu.make_async_copy(src, dst, R.ssem.at[at])
        cp.start()
        small.append(cp)
    wk, wv, wq, wo, wi, wf = R.w
    for ref in (R.N2, R.r2, R.G):
        load(ref, 1)
    later = (wf, R.Gp, R.HT, wi, R.N1, R.r1, R.CTp, wo, R.CT, R.K, R.V, R.Q, R.lse, R.AT, wq, wk, wv)

    barrier = pltpu.get_barrier_semaphore()
    peers = [me.zn(s, levels)[1] for s in range(1, levels)] + [me.xn, me.yn, me.cn, me.dn]
    for peer in peers:
        pl.semaphore_signal(barrier, inc=1, device_id=peer, device_id_type=MESH)
    pl.semaphore_wait(barrier, len(peers))

    pending = []

    def start(cp):
        cp.start()
        pending.append(cp)
        return cp

    stays = c == r
    y_far = remote(R.y_o, R.yo, R.xs.at[0], R.xr.at[0], me.dn)
    y_near = pltpu.make_async_copy(R.y_o, R.yo, R.ssem.at[3])
    dx_cps = []

    go_or_stay(stays, y_near.start, y_far.start)

    gs, gr = R.gs, R.gr
    chunks = [(kind, l) for l in (1, 0) for kind in (KIND_F, KIND_I, KIND_O, KIND_Q, KIND_K, KIND_V)]
    chunks += [(None, 1), (None, 0)]
    flight = {}
    stage = {}
    fin_copies = []

    def rs_core(i):
        kind, l = chunks[i]
        g = R.g[kind]
        spot = g.at[0, 0] if l == 1 else R.landing[kind]
        flight[i] = [start(remote(g.at[l, 1 - c], spot, gs.at[i, 0], gr.at[i, 0], me.cn))]

    def rs_1(i):
        kind, l = chunks[i]
        g = R.g[kind]
        first, second = halves(BACKWARD_SPLIT[i], levels)
        half, quarter = R.half[kind], R.quarter[kind]
        g[l, c] = g[l, c] + (g[0, 0] if l == 1 else R.landing[kind][...])
        flight[i] = [
            start(remote(g.at[l, c, first, 1 - y], half.at[l, first], gs.at[i, 1], gr.at[i, 1], me.yn)),
            start(remote(g.at[l, c, second, :, 1 - r], half.at[l, second], gs.at[i, 2], gr.at[i, 2], me.xn)),
        ]

    def rs_2(i):
        kind, l = chunks[i]
        g = R.g[kind]
        first, second = halves(BACKWARD_SPLIT[i], levels)
        half, quarter = R.half[kind], R.quarter[kind]
        g[l, c, first, y] = g[l, c, first, y] + half[l, first]
        g[l, c, second, :, r] = g[l, c, second, :, r] + half[l, second]
        flight[i] = [
            start(remote(g.at[l, c, first, y, 1 - r], quarter.at[l, first], gs.at[i, 3], gr.at[i, 3], me.xn)),
            start(remote(g.at[l, c, second, 1 - y, r], quarter.at[l, second], gs.at[i, 4], gr.at[i, 4], me.yn)),
        ]

    def level_spot(kind, l, s):
        ref = R.level[kind]
        return ref.at[l, s, 0, 0] if len(ref.shape) == 6 else ref.at[l, s]

    def rs_3(i):
        kind, l = chunks[i]
        g = R.g[kind]
        first, second = halves(BACKWARD_SPLIT[i], levels)
        half, quarter = R.half[kind], R.quarter[kind]
        g[l, c, first, y, r] = g[l, c, first, y, r] + quarter[l, first]
        g[l, c, second, y, r] = g[l, c, second, y, r] + quarter[l, second]
        flight[i] = []
        for s in range(1, levels):
            there, dev = me.zn(s, levels)
            flight[i].append(
                start(remote(g.at[l, c, there, y, r], level_spot(kind, l, s - 1), gs.at[i, 4 + s], gr.at[i, 4 + s], dev))
            )

    def rs_4(i):
        kind, l = chunks[i]
        g, fin = R.g[kind], R.total[kind]
        total = g[l, c, z, y, r].astype(F32)
        for s in range(levels - 1):
            total = total + level_spot(kind, l, s)[...].astype(F32)
        fin[l, r] = total.astype(BF)
        flight[i] = [start(remote(fin.at[l, r], fin.at[l, r], gs.at[i, 4 + levels], gr.at[i, 4 + levels], me.xn))]

    def rs_5(i):
        kind, l = chunks[i]
        cp = pltpu.make_async_copy(R.total[kind].at[l], R.fin[kind].at[l], R.fsem.at[i])
        cp.start()
        fin_copies.append(cp)

    vg, va, vb, vt = R.vg, R.va, R.vb, R.vt

    def vec_hop(at, device):
        def step(i):
            l = chunks[i][1]
            if at == 0:
                va[l, 0] = vg[16 * l : 16 * l + 16]
            else:
                va[l, at] = va[l, at - 1] + R.vrecv[l, at - 1]
            flight[i] = [start(remote(va.at[l, at], R.vrecv.at[l, at], R.vs.at[l, at], R.vr.at[l, at], device))]

        return step

    def vec_level(i):
        l = chunks[i][1]
        va[l, 3] = va[l, 2] + R.vrecv[l, 2]
        flight[i] = []
        for s in range(1, levels):
            there, dev = me.zn(s, levels)
            lanes = pl.ds(pl.multiple_of(there * 128, 128), 128)
            flight[i].append(start(remote(va.at[l, 3, :, lanes], vb.at[l, s - 1], R.vs.at[l, 2 + s], R.vr.at[l, 2 + s], dev)))

    def vec_end(i):
        l = chunks[i][1]
        total = va[l, 3, :, pl.ds(pl.multiple_of(z * 128, 128), 128)]
        for s in range(levels - 1):
            total = total + vb[l, s]
        vt[16 * l : 16 * l + 16] = total

    def hs_z(i):
        kind, l = chunks[i]
        g = R.g[kind]
        g[l, c] = g[l, c] + (g[0, 0] if l == 1 else R.landing[kind][...])
        flight[i] = []
        for s in range(1, levels):
            there, dev = me.zn(s, levels)
            flight[i].append(
                start(remote(g.at[l, c, there], R.level[kind].at[l, s - 1], gs.at[i, s], gr.at[i, s], dev))
            )

    def hs_y(i):
        kind, l = chunks[i]
        g = R.g[kind]
        whole = g[l, c, z].astype(F32)
        for s in range(levels - 1):
            whole = whole + R.level[kind][l, s].astype(F32)
        g[l, c, z] = whole.astype(BF)
        spot = R.half[kind].at[l, 0]
        flight[i] = [start(remote(g.at[l, c, z, 1 - y], spot, gs.at[i, levels], gr.at[i, levels], me.yn))]

    def hs_x(i):
        kind, l = chunks[i]
        g = R.g[kind]
        g[l, c, z, y] = g[l, c, z, y] + R.half[kind][l, 0]
        spot = R.quarter[kind].at[l, 0]
        sems = gs.at[i, levels + 1], gr.at[i, levels + 1]
        flight[i] = [start(remote(g.at[l, c, z, y, 1 - r], spot, *sems, me.xn))]

    def hs_end(i):
        kind, l = chunks[i]
        g, fin = R.g[kind], R.total[kind]
        fin[l, r] = g[l, c, z, y, r] + R.quarter[kind][l, 0]
        flight[i] = [start(remote(fin.at[l, r], fin.at[l, r], gs.at[i, 4 + levels], gr.at[i, 4 + levels], me.xn))]

    other_steps = (rs_core, hs_z, hs_y, hs_x, hs_end, rs_5)
    matrix_steps = (rs_core, rs_1, rs_2, rs_3, rs_4, rs_5)
    vec_steps = (vec_hop(0, me.cn), vec_hop(1, me.xn), vec_hop(2, me.yn), vec_level, vec_end)
    turns = iter(BACKWARD_TURNS)

    def turn():
        for i in next(turns):
            at = stage.get(i, 0)
            for cp in flight.pop(i, ()):
                cp.wait_recv()
            known = matrix_steps if i < len(BACKWARD_SPLIT) and BACKWARD_SPLIT[i] else other_steps
            (vec_steps if chunks[i][0] is None else known)[at](i)
            stage[i] = at + 1

    for cp in small:
        cp.wait()
    vec, msel = R.vec, R.msel
    tag_row = msel[2 * S : 2 * S + 16].astype(F32)[:1]
    tag_row = jnp.concatenate([tag_row] * (D // 128), axis=1)
    low, high, spots = lane_masks()
    low32 = low.astype(F32)
    vg[...] = jnp.zeros_like(vg)
    R.dy[...] = R.cotb[...].astype(F32) * msel[pl.ds(c * S, S)][:, 1:2].astype(F32)
    T = 256
    dy, dpre, dF, dFT, dU, dZ = R.dy, R.dpre, R.dF, R.dFT, R.dU, R.dZ

    def fold(value):
        return jnp.sum(value.reshape(value.shape[0] // 8, 8, value.shape[1]), axis=0)

    zero8 = jnp.zeros((8, D), F32)

    for l in (1, 0):
        base = 16 * l
        e = lambda row: vec[base + row : base + row + 1, :]

        def put(row, value):
            vg[base + row : base + row + 1, :] = value

        def weight(kind):
            w = R.w[kind]
            return w[...].reshape(-1, w.shape[-1])

        turn()
        N2, r2 = use(R.N2), use(R.r2)
        if l == 1:
            for ref in later:
                load(ref, 1)

        def norm_two(t, carry):
            s7, s8, s9 = carry
            rows = pl.ds(pl.multiple_of(t * T, T), T)
            g, n = dy[rows], N2[rows]
            dn = g * e(8)
            m1 = jnp.mean(dn, axis=-1, keepdims=True)
            m2 = jnp.mean(dn * n, axis=-1, keepdims=True)
            d = r2[rows][:, :1] * (dn - m1 - n * m2)
            dpre[rows] = d
            db = d.astype(BF)
            dF[rows] = db
            dFT[:, rows] = db.T
            return s7 + fold(db.astype(F32)), s8 + fold(g * n), s9 + fold(g)

        s7, s8, s9 = lax.fori_loop(0, S // T, norm_two, (zero8, zero8, zero8))
        put(7, jnp.sum(s7, axis=0, keepdims=True))
        put(8, jnp.sum(s8, axis=0, keepdims=True))
        put(9, jnp.sum(s9, axis=0, keepdims=True))
        turn()
        G = use(R.G)
        gf = R.g[KIND_F]
        piece = 2 * FF // shards

        def grad_f(t, carry):
            d = nn_dot(dFT[...], G[:, pl.ds(pl.multiple_of(t * piece, piece), piece)]).astype(BF)
            zz, yy = lax.div(t, 2), lax.rem(t, 2)
            half = piece // 2
            gf[l, 0, zz, yy] = d[:, :half].reshape(2, D // 2, half)
            gf[l, 1, zz, yy] = d[:, half:].reshape(2, D // 2, half)
            return carry

        lax.fori_loop(0, shards // 2, grad_f, 0)
        if l == 1:
            for ref in (R.N2, R.r2, R.G):
                load(ref, 0)
        use(R.w[KIND_F])
        Gp = use(R.Gp)

        def grad_inner(b):
            wf = R.w[KIND_F]
            quarter = wf[b * (levels // (FF // D)) : (b + 1) * (levels // (FF // D))].reshape(D, D)
            cols = slice(b * D, b * D + D)
            du = (nt_dot(dF[...], quarter) * Gp[:, cols].astype(F32)).astype(BF)
            dU[:, cols] = du
            put(10 + b, jnp.sum(fold(du.astype(F32)), axis=0, keepdims=True))

        for b in range(FF // D):
            if b % 2 == 0:
                turn()
            grad_inner(b)
        turn()
        if l == 1:
            load(R.w[KIND_F], 0)
            load(R.Gp, 0)
        HT = use(R.HT)
        gi = R.g[KIND_I]
        rows_i = 2 * R.g[KIND_I].shape[-2]

        for b in range(FF // D):
            d = nn_dot(HT[...], dU[:, b * D : b * D + D]).astype(BF)
            for cc in range(2):
                part = d[cc * (D // 2) : (cc + 1) * (D // 2)]
                gi[l, cc, :, :, :, :, b * D : b * D + D] = part.reshape(levels, 2, 2, rows_i // 2, D)
        if l == 1:
            load(R.HT, 0)
        use(R.w[KIND_I])
        N1, r1 = use(R.N1), use(R.r1)

        def norm_one(t, carry):
            s4, s5, s6 = carry
            rows = pl.ds(pl.multiple_of(t * T, T), T)
            g = dpre[rows] + nt_dot(dU[rows], weight(KIND_I))
            n = N1[rows]
            dn = g * e(5)
            m1 = jnp.mean(dn, axis=-1, keepdims=True)
            m2 = jnp.mean(dn * n, axis=-1, keepdims=True)
            d = r1[rows][:, :1] * (dn - m1 - n * m2)
            dy[rows] = d
            db = d.astype(BF)
            dZ[rows] = db
            return s4 + fold(db.astype(F32)), s5 + fold(g * n), s6 + fold(g)

        turn()
        sums = lax.fori_loop(0, S // T // 2, norm_one, (zero8, zero8, zero8))
        turn()
        s4, s5, s6 = lax.fori_loop(S // T // 2, S // T, norm_one, sums)
        put(4, jnp.sum(s4, axis=0, keepdims=True))
        put(5, jnp.sum(s5, axis=0, keepdims=True))
        put(6, jnp.sum(s6, axis=0, keepdims=True))
        turn()
        if l == 1:
            for ref in (R.w[KIND_I], R.N1, R.r1):
                load(ref, 0)
        CTp = use(R.CTp)
        go = R.g[KIND_O]

        def store(ref, value):
            for cc in range(2):
                ref[l, cc] = value[cc * (D // 2) : (cc + 1) * (D // 2)].reshape(ref.shape[2:])

        store(R.g[KIND_O], nn_dot(CTp[...], dZ[...]).astype(BF))
        use(R.w[KIND_O])
        dF[...] = nt_dot(dZ[...], weight(KIND_O)).astype(BF)
        CT = use(R.CT)
        dct = dF[...].T
        prod = dct.astype(F32) * CT[...].astype(F32)
        prod = jnp.sum(prod.reshape(D // 64, 64, S), axis=1)
        for j in range(D // 128):
            R.delta[j, :2] = prod[2 * j : 2 * j + 2]
        if l == 1:
            for ref in (R.CTp, R.w[KIND_O], R.CT):
                load(ref, 0)
        K, V, Q, lse = use(R.K), use(R.V), use(R.Q), use(R.lse)
        delta, dC, dQT = R.delta, dF, R.dQT
        dkp, dvp, dkr, dvr = R.dkp, R.dvp, R.dkr, R.dvr
        bias_rows = msel[: 2 * S]

        def pair(j):
            sl = slice(j * 128, j * 128 + 128)
            k2 = K[:, :, sl].reshape(2 * S, 128)
            v2 = V[:, :, sl].reshape(2 * S, 128)
            k2t = k2.T
            q2 = Q[:, sl]
            dc2 = dC[:, sl]
            dk_sum, dv_sum = None, None
            for h in range(2):
                mine, other = (low, high) if h == 0 else (high, low)
                mine32 = low32 if h == 0 else 1.0 - low32
                kh = k2 * mine + bias_rows * other
                vh = v2 * mine
                qh = q2 * mine + spots * other
                dk_h, dv_h = None, None
                for part in range(S // 256):
                    cols = slice(part * 256, part * 256 + 256)
                    st = nt_dot(kh, qh[cols])
                    p = jnp.exp(st - lse[j, h : h + 1, cols])
                    dp = nt_dot(vh, dc2[cols])
                    ds = (p * (dp - delta[j, h : h + 1, cols])).astype(BF)
                    pb = p.astype(BF)
                    dv = nn_dot(pb, dc2[cols])
                    dk = nn_dot(ds, q2[cols])
                    dv_h = dv if dv_h is None else dv_h + dv
                    dk_h = dk if dk_h is None else dk_h + dk
                    dq = nn_dot(k2t, ds)[64 * h : 64 * h + 64]
                    rows = slice(j * 128 + 64 * h, j * 128 + 64 * h + 64)
                    dQT[rows, cols] = (dq * 0.125).astype(BF)
                dk_sum = dk_h * mine32 if dk_sum is None else dk_sum + dk_h * mine32
                dv_sum = dv_h * mine32 if dv_sum is None else dv_sum + dv_h * mine32
            dkp[l, :, j] = dk_sum.astype(BF).reshape(2, S, 128)
            dvp[l, :, j] = dv_sum.astype(BF).reshape(2, S, 128)

        pairs = D // 128
        half_pairs = pairs // 2
        kv_cps = []
        for j in range(pairs):
            turn()
            pair(j)
            if (j + 1) % half_pairs == 0:
                part = j // half_pairs
                js = pl.ds(part * half_pairs, half_pairs)
                for at, (mine, theirs) in enumerate(((dkp, dkr), (dvp, dvr))):
                    sems = R.ks.at[l, part, at], R.kr.at[l, part, at]
                    kv_cps.append(start(remote(mine.at[l, 1 - c, js], theirs.at[l, js], *sems, me.cn)))
        if l == 1:
            for ref in (R.K, R.V, R.Q, R.lse):
                load(ref, 0)
        turn()
        AT = use(R.AT)
        dqb = dZ
        dqb[...] = dQT[...].T
        store(R.g[KIND_Q], nn_dot(AT[...], dqb[...]).astype(BF))
        turn()
        for cp in kv_cps:
            cp.wait_recv()
        dkb, dvb = dFT, R.dvb
        for j in range(pairs):
            dkb[:, 128 * j : 128 * j + 128] = dkp[l, c, j] + dkr[l, j]
            dvb[:, 128 * j : 128 * j + 128] = dvp[l, c, j] + dvr[l, j]
        store(R.g[KIND_K], nn_dot(AT[...], dkb[...]).astype(BF))
        store(R.g[KIND_V], nn_dot(AT[...], dvb[...]).astype(BF))
        if l == 1:
            load(R.AT, 0)
        use(R.w[KIND_Q])
        use(R.w[KIND_K])
        use(R.w[KIND_V])

        def last(t, carry):
            s0, s2, s3 = carry
            rows = pl.ds(pl.multiple_of(t * T, T), T)
            d = dy[rows] + nt_dot(dqb[rows], weight(KIND_Q)) + nt_dot(dkb[rows], weight(KIND_K)) + nt_dot(dvb[rows], weight(KIND_V))
            dy[rows] = d
            return s0 + fold(d), s2 + fold(dqb[rows].astype(F32)), s3 + fold(dvb[rows].astype(F32))

        sums = (zero8, zero8, zero8)
        for part in range(2):
            turn()
            sums = lax.fori_loop(part * (S // T // 2), (part + 1) * (S // T // 2), last, sums)
            if l == 0:
                half = pl.ds(part * (S // 2), S // 2)
                R.cotb[half] = dy[half].astype(BF)
                far = remote(R.cotb.at[half], R.dxo.at[half], R.xs.at[1 + part], R.xr.at[1 + part], me.dn)
                near = pltpu.make_async_copy(R.cotb.at[half], R.dxo.at[half], R.ssem.at[4 + part])
                dx_cps.append((far, near))
                go_or_stay(stays, near.start, far.start)
        s0, s2, s3 = sums
        s0 = jnp.sum(s0, axis=0, keepdims=True)
        put(0, s0 * (1.0 - tag_row))
        put(1, s0 * tag_row)
        put(2, jnp.sum(s2, axis=0, keepdims=True))
        put(3, jnp.sum(s3, axis=0, keepdims=True))
        if l == 1:
            for ref in (R.w[KIND_Q], R.w[KIND_K], R.w[KIND_V]):
                load(ref, 0)

    turn()
    vec_out = pltpu.make_async_copy(vt, R.vec_g, R.ssem.at[6])
    vec_out.start()
    for cp in fin_copies:
        cp.wait()
    vec_out.wait()
    for cp in pending:
        cp.wait_send()

    for far, near in dx_cps:
        go_or_stay(stays, near.wait, far.wait)
    go_or_stay(stays, y_near.wait, y_far.wait)


def update_kernel(parts, rates, decays, *refs):
    R = named(parts, refs)
    f = lax.axis_index("fsdp")
    sources, _ = jax.tree.flatten((R.fin, R.fvec, R.y, R.dx, R.masters, R.firsts, R.seconds))
    places, tree = jax.tree.flatten(R.inside)
    copies = [pltpu.make_async_copy(s, p, R.isem.at[at]) for at, (s, p) in enumerate(zip(sources, places))]
    for cp in copies:
        cp.start()
    fin, fvec, y, dx, masters, firsts, seconds = R.inside
    waits = tree.unflatten(copies)
    finals = (R.new_masters, R.new_firsts, R.new_seconds)
    leaving = []

    def leave(src, dst):
        cp = pltpu.make_async_copy(src, dst, R.osem.at[len(leaving)])
        cp.start()
        leaving.append(cp)

    def arrive(at, kinds):
        for cp in [waits[0][k] for k in kinds] + [w[at] for w in waits[4:]]:
            cp.wait()

    def step(at, where, grad):
        new = adamw(masters[at][where], firsts[at][where], seconds[at][where], grad, rates[at], decays[at])
        for refs, value in zip((masters, firsts, seconds), new):
            refs[at][where] = value

    def done(at):
        for kept, final in zip((masters, firsts, seconds), finals):
            leave(kept[at], final[at])

    D = dx.shape[1]
    for at, kind in ((2, KIND_I), (3, KIND_F), (1, KIND_O)):
        arrive(at, (kind,))
        for l in range(2):
            ref = fin[kind]
            grad = ref[l].astype(F32).reshape(-1, ref.shape[-1])
            step(at, (l,), grad.T if kind == KIND_F else grad)
        done(at)
    arrive(0, (KIND_Q, KIND_K, KIND_V))
    for l in range(2):
        for at, kind in enumerate((KIND_Q, KIND_K, KIND_V)):
            grad = fin[kind][l].astype(F32).reshape(-1, D)
            step(0, (l, slice(None), slice(at * D, at * D + D)), grad)
    done(0)
    arrive(4, ())
    waits[1].wait()
    wide = masters[4].shape[2]
    rows = masters[4].shape[0]
    span = 128 // wide
    slot = lax.rem(f, span)
    for l in range(2):
        block = fvec[16 * l : 16 * l + 16]
        grad = block[:, :wide]
        for s in range(1, span):
            grad = jnp.where(slot == s, block[:, s * wide : s * wide + wide], grad)
        step(4, (slice(None), l), grad[:rows])
    done(4)
    waits[2].wait()
    leave(y, R.out.at[0])
    waits[3].wait()
    R.wide[...] = dx[...].astype(F32)
    leave(R.wide, R.grad.at[0])
    for cp in leaving:
        cp.wait()


def fast_body(
    tokens, cotangent, tags, lengths, key_mask,
    master_qkv, master_out, master_in, master_feed_output, master_vec,
    first_qkv, first_out, first_in, first_ffo, first_vec,
    second_qkv, second_out, second_in, second_ffo, second_moment_vector,
    shards,
):
    S, D = tokens.shape[1:]
    FF = master_in.shape[2]
    levels = shards // 4
    rows, cols = sizes_of(shards, D, FF)
    meta_shape = (2 * S + 16, 128)
    by_row = lambda vectors: vectors.transpose(1, 0, 2)
    hbm = pl.BlockSpec(memory_space=pl.ANY)
    shape = jax.ShapeDtypeStruct
    V = pltpu.VMEM
    dma = pltpu.SemaphoreType.DMA
    w_tail = [(levels, 2, 2, 2, rows[k], cols[k]) for k in KINDS]
    masters = (master_qkv, master_out, master_in, master_feed_output, by_row(master_vec))
    firsts = (first_qkv, first_out, first_in, first_ffo, by_row(first_vec))
    seconds = (second_qkv, second_out, second_in, second_ffo, by_row(second_moment_vector))

    saved = call_kernel(
        lambda parts, *refs: forward_kernel(parts, levels, norm_epsilon, *refs),
        ForwardIn(
            tok=tokens,
            cot=cotangent,
            lengths=lengths,
            tags=tags,
            key_mask=key_mask,
            vectors=by_row(master_vec),
            masters=masters[:4],
        ),
        Saved(
            w_o=tuple(shape((2,) + tail, BF) for tail in w_tail),
            vec_o=shape((32, D), F32),
            meta_o=shape(meta_shape, BF),
            cot_o=shape((S, D), BF),
            y_o=shape((S, D), BF),
            at_o=shape((2, D, S), BF),
            q_o=shape((2, S, D), BF),
            k_o=shape((2, 2, S, D), BF),
            v_o=shape((2, 2, S, D), BF),
            lse_o=shape((2, D // 128, 8, S), F32),
            ct_o=shape((2, D, S), BF),
            ctp_o=shape((2, D, S), BF),
            n1_o=shape((2, S, D), F32),
            r1_o=shape((2, S, 128), F32),
            ht_o=shape((2, D, S), BF),
            g_o=shape((2, S, FF), BF),
            gp_o=shape((2, S, FF), BF),
            n2_o=shape((2, S, D), F32),
            r2_o=shape((2, S, 128), F32),
        ),
        ForwardScratch(
            w=tuple(V((2,) + tail, BF) for tail in w_tail),
            stages=tuple(V(m.shape, F32) for m in masters[:4]),
            vecg=V((shards, 32, 128), BF),
            vec=V((32, D), F32),
            metab=V((2,) + meta_shape, BF),
            msel=V(meta_shape, BF),
            tokb=V((S, D), BF),
            cotb=V((S, D), BF),
            A32=V((S, D), F32),
            Ab=V((S, D), BF),
            ATp=V((D, S), BF),
            Q=V((S, D), BF),
            K=V((2, 2, S, D), BF),
            V=V((2, 2, S, D), BF),
            lse=V((D // 128, 8, S), F32),
            CT=V((D, S), BF),
            CTp=V((D, S), BF),
            C=V((S, D), BF),
            N1=V((S, D), F32),
            r1=V((S, 128), F32),
            H32=V((S, D), F32),
            Hb=V((S, D), BF),
            HTp=V((D, S), BF),
            G=V((S, FF), BF),
            Gp=V((S, FF), BF),
            N2=V((S, D), F32),
            r2=V((S, 128), F32),
            X=V((S, D), F32),
            Yb=V((S, D), BF),
            msem=dma((2, 4)),
            xsem=dma((4,)),
            osem=dma((48,)),
            gs=dma((16, levels + 4)),
            gr=dma((16, levels + 4)),
            vs=dma((shards - 1,)),
            vr=dma((shards - 1,)),
            xs=dma((3,)),
            xr=dma((3,)),
            ks=dma((2, 2)),
            kr=dma((2, 2)),
        ),
        ForwardIn(
            tok=hbm,
            cot=hbm,
            lengths=pl.BlockSpec(memory_space=pltpu.SMEM),
            tags=pl.BlockSpec(memory_space=pltpu.SMEM),
            key_mask=pl.BlockSpec(memory_space=pltpu.VMEM),
            vectors=pl.BlockSpec(memory_space=pltpu.VMEM),
            masters=(hbm,) * 4,
        ),
        collective_id=0,
        has_side_effects=True,
        vmem_limit_bytes=VMEM_BYTES,
    )

    tails = [(rows[k], cols[k]) for k in KINDS]
    tails[KIND_F] = (D // 2, FF // shards)
    each = lambda *lead: tuple(V(lead + tail, BF) for tail in tails)
    grads = call_kernel(
        lambda parts, *refs: backward_kernel(parts, levels, *refs),
        saved,
        BackwardOut(
            fin=tuple(shape((2, 2) + tail, BF) for tail in tails),
            vec_g=shape((32, 128), F32),
            yo=shape((S, D), BF),
            dxo=shape((S, D), BF),
        ),
        BackwardScratch(
            g=each(2, 2, levels, 2, 2),
            landing=each(levels, 2, 2),
            half=each(2, levels, 2),
            quarter=each(2, levels),
            level=tuple(
                V((2, levels - 1) + ((2, 2) if k in WHOLE_LEVEL_KINDS else ()) + tail, BF) for k, tail in zip(KINDS, tails)
            ),
            total=each(2, 2),
            w=tuple(V(tail, BF) for tail in w_tail),
            AT=V((D, S), BF),
            Q=V((S, D), BF),
            K=V((2, S, D), BF),
            V=V((2, S, D), BF),
            lse=V((D // 128, 8, S), F32),
            CT=V((D, S), BF),
            CTp=V((D, S), BF),
            N1=V((S, D), F32),
            r1=V((S, 128), F32),
            HT=V((D, S), BF),
            G=V((S, FF), BF),
            Gp=V((S, FF), BF),
            N2=V((S, D), F32),
            r2=V((S, 128), F32),
            vec=V((32, D), F32),
            msel=V(meta_shape, BF),
            cotb=V((S, D), BF),
            dy=V((S, D), F32),
            dpre=V((S, D), F32),
            dF=V((S, D), BF),
            dFT=V((D, S), BF),
            dU=V((S, FF), BF),
            dZ=V((S, D), BF),
            delta=V((D // 128, 8, S), F32),
            dQT=V((D, S), BF),
            dvb=V((S, D), BF),
            dkp=V((2, 2, D // 128, S, 128), BF),
            dvp=V((2, 2, D // 128, S, 128), BF),
            dkr=V((2, D // 128, S, 128), BF),
            dvr=V((2, D // 128, S, 128), BF),
            vg=V((32, D), F32),
            va=V((2, 4, 16, D), F32),
            vrecv=V((2, 3, 16, D), F32),
            vb=V((2, levels - 1, 16, 128), F32),
            vt=V((32, 128), F32),
            lsem=dma((2, 20)),
            ssem=dma((7,)),
            fsem=dma((12,)),
            gs=dma((12, levels + 5)),
            gr=dma((12, levels + 5)),
            xs=dma((3,)),
            xr=dma((3,)),
            ks=dma((2, 2, 2)),
            kr=dma((2, 2, 2)),
            vs=dma((2, levels + 2)),
            vr=dma((2, levels + 2)),
        ),
        hbm,
        collective_id=1,
        has_side_effects=True,
        vmem_limit_bytes=VMEM_BYTES,
    )

    rates = (
        matrix_rate * D ** (-0.5),
        matrix_rate * (D // 16) ** (-0.5),
        matrix_rate * D ** (-0.5),
        matrix_rate * (FF // 2) ** (-0.5),
        vector_rate,
    )
    decays = (weight_decay, weight_decay, weight_decay, weight_decay, 0.0)
    like = tuple(shape(p.shape, F32) for p in masters)
    new = call_kernel(
        lambda parts, *refs: update_kernel(parts, rates, decays, *refs),
        UpdateIn(fin=grads.fin, fvec=grads.vec_g, y=grads.yo, dx=grads.dxo, masters=masters, firsts=firsts, seconds=seconds),
        UpdateOut(
            out=shape(tokens.shape, BF),
            grad=shape(tokens.shape, F32),
            new_masters=like,
            new_firsts=like,
            new_seconds=like,
        ),
        UpdateScratch(
            inside=(
                tuple(V(g.shape, BF) for g in grads.fin),
                V((32, 128), F32),
                V((S, D), BF),
                V((S, D), BF),
                *(tuple(V(p.shape, F32) for p in masters) for _ in range(3)),
            ),
            wide=V((S, D), F32),
            isem=dma((24,)),
            osem=dma((17,)),
        ),
        hbm,
        vmem_limit_bytes=VMEM_BYTES,
    )
    trees = [(*tree[:4], by_row(tree[4])) for tree in (new.new_masters, new.new_firsts, new.new_seconds)]
    return (new.out, new.grad, *trees[0], *trees[1], *trees[2])


def solution(mesh):
    placed = (
        P("fsdp", "rep", None),
        P("fsdp", "rep", None),
        P("fsdp"),
        P("fsdp"),
        P("fsdp", None),
        P(None, "fsdp", None),
        P(None, "fsdp", None),
        P(None, "fsdp", None),
        P(None, "fsdp", None),
        P(None, None, "fsdp"),
        P(None, "fsdp", None),
        P(None, "fsdp", None),
        P(None, "fsdp", None),
        P(None, "fsdp", None),
        P(None, None, "fsdp"),
        P(None, "fsdp", None),
        P(None, "fsdp", None),
        P(None, "fsdp", None),
        P(None, "fsdp", None),
        P(None, None, "fsdp"),
    )
    shards = mesh.shape["fsdp"]

    def chosen(*args):
        tokens, master_in = args[0], args[7]
        width = tokens.shape[2]
        whole_tiles = shards * 32 == width and master_in.shape[2] == 4 * width
        if mesh.shape["rep"] == 2 and shards % 4 == 0 and whole_tiles:
            return fast_body(*args, shards)
        return body(*args)

    return jax.shard_map(
        chosen,
        mesh=mesh,
        in_specs=placed,
        out_specs=(
            P("fsdp", "rep", None),
            P("fsdp", "rep", None),
            P(None, "fsdp", None),
            P(None, "fsdp", None),
            P(None, "fsdp", None),
            P(None, "fsdp", None),
            P(None, None, "fsdp"),
            P(None, "fsdp", None),
            P(None, "fsdp", None),
            P(None, "fsdp", None),
            P(None, "fsdp", None),
            P(None, None, "fsdp"),
            P(None, "fsdp", None),
            P(None, "fsdp", None),
            P(None, "fsdp", None),
            P(None, "fsdp", None),
            P(None, None, "fsdp"),
        ),
        check_vma=False,
    )
```

```python
import functools
from types import SimpleNamespace
from typing import NamedTuple

import jax
import jax.numpy as jnp
from jax import lax
from jax.experimental import pallas as pl
from jax.experimental.pallas import tpu as pltpu
from jax.sharding import PartitionSpec as P

D = 512
H = 8
FF = 2048
STEP = 10


beta_decay = 0.5
epsilon_adam = 1e-08
weight_decay = 0.01
norm_epsilon = 1e-05
masked_score = -1000000000.0
vector_rate = 0.15
matrix_rate = 0.5


def layer_norm(pre_norm, gain_row, offset_row):
    centre_mean = jnp.mean(pre_norm, axis=-1, keepdims=True)
    centred = pre_norm - centre_mean
    variance = jnp.mean(centred * centred, axis=-1, keepdims=True)
    return centred * lax.rsqrt(variance + norm_epsilon) * gain_row + offset_row


def tanh_gelu_activation(inner_act):
    return jax.nn.gelu(inner_act, approximate=True)


def adamw(master, first, second, grad, rate, decay):
    first_new = beta_decay * first + (1.0 - beta_decay) * grad
    second_new = beta_decay * second + (1.0 - beta_decay) * grad * grad
    correction = 1.0 - beta_decay**STEP
    direction = first_new / correction / (jnp.sqrt(second_new / correction) + epsilon_adam)
    master_new = master - rate * (direction + decay * master)
    return (master_new, first_new, second_new)


def score_block(query_heads, key_heads, key_bias, score_scale):
    scores = jnp.einsum("qhd,khd->hqk", query_heads, key_heads, preferred_element_type=jnp.float32)
    return scores * score_scale + key_bias[None, None, :]


def forward_layer(input_rows, weights, tag_value, key_bias):
    w_qkv, w_out, w_in, w_ffo, vectors_low = weights
    vectors = vectors_low.astype(jnp.float32)
    model_width = w_out.shape[0]
    row_count = input_rows.shape[0]
    head_size = model_width // H
    score_scale = head_size ** (-0.5)
    direction = jnp.where(tag_value == 0, vectors[0], vectors[1])
    summed = input_rows + direction[None, :]
    summed_low = summed.astype(jnp.bfloat16)
    projected = jnp.dot(summed_low, w_qkv, preferred_element_type=jnp.float32)
    queries = (projected[:, :model_width] + vectors[2]).astype(jnp.bfloat16)
    keys_local = projected[:, model_width : 2 * model_width].astype(jnp.bfloat16)
    local_values = (projected[:, 2 * model_width :] + vectors[3]).astype(jnp.bfloat16)
    keys_all, values_all = (
        lax.all_gather(keys_local, "rep", axis=0, tiled=True),
        lax.all_gather(local_values, "rep", axis=0, tiled=True),
    )
    key_count = keys_all.shape[0]
    query_heads = queries.reshape(row_count, H, head_size)
    key_heads = keys_all.reshape(key_count, H, head_size)
    value_heads = values_all.reshape(key_count, H, head_size)
    scores = score_block(query_heads, key_heads, key_bias, score_scale)
    row_top = jnp.max(scores, axis=-1, keepdims=True)
    exponent_terms = jnp.exp(scores - row_top)
    totals = jnp.sum(exponent_terms, axis=-1, keepdims=True)
    soft_weights = exponent_terms / totals
    log_total = row_top + jnp.log(totals)
    context = jnp.einsum(
        "hqk,khd->qhd",
        soft_weights.astype(jnp.bfloat16),
        value_heads,
        preferred_element_type=jnp.float32,
    )
    context_low = context.reshape(row_count, model_width).astype(jnp.bfloat16)
    branch = jnp.dot(context_low, w_out, preferred_element_type=jnp.float32) + vectors[4]
    hidden, norm_first = jax.vjp(layer_norm, summed + branch, vectors[5], vectors[6])
    hidden_low = hidden.astype(jnp.bfloat16)
    inner_act = jnp.dot(hidden_low, w_in, preferred_element_type=jnp.float32) + vectors[
        10:
    ].reshape(-1)
    activated, gelu_pull = jax.vjp(tanh_gelu_activation, inner_act)
    activated_low = activated.astype(jnp.bfloat16)
    feed_out = jnp.dot(activated_low, w_ffo, preferred_element_type=jnp.float32) + vectors[7]
    result, norm_second = jax.vjp(layer_norm, hidden + feed_out, vectors[8], vectors[9])
    saved_state = (
        summed_low,
        query_heads,
        key_heads,
        value_heads,
        log_total,
        context_low,
        norm_first,
        hidden_low,
        gelu_pull,
        activated_low,
        norm_second,
    )
    return (result, saved_state)


def attention_grads(
    query_heads, key_heads, value_heads, log_total, context_heads, key_bias, score_scale
):
    row_count = query_heads.shape[0]
    model_width = query_heads.shape[1] * query_heads.shape[2]
    scores = score_block(query_heads, key_heads, key_bias, score_scale)
    soft_weights = jnp.exp(scores - log_total)
    grad_soft = jnp.einsum(
        "qhd,khd->hqk", context_heads, value_heads, preferred_element_type=jnp.float32
    )
    row_inner = jnp.sum(soft_weights * grad_soft, axis=-1, keepdims=True)
    grad_scores = (soft_weights * (grad_soft - row_inner) * score_scale).astype(jnp.bfloat16)
    grad_queries = jnp.einsum(
        "hqk,khd->qhd", grad_scores, key_heads, preferred_element_type=jnp.float32
    ).reshape(row_count, model_width)
    key_terms = jnp.einsum(
        "hqk,qhd->khd", grad_scores, query_heads, preferred_element_type=jnp.float32
    ).reshape(-1, model_width)
    value_terms = jnp.einsum(
        "hqk,qhd->khd",
        soft_weights.astype(jnp.bfloat16),
        context_heads,
        preferred_element_type=jnp.float32,
    ).reshape(-1, model_width)
    grad_keys, grad_values = (
        lax.psum_scatter(
            key_terms.astype(jnp.bfloat16), "rep", scatter_dimension=0, tiled=True
        ).astype(jnp.float32),
        lax.psum_scatter(
            value_terms.astype(jnp.bfloat16), "rep", scatter_dimension=0, tiled=True
        ).astype(jnp.float32),
    )
    return (grad_queries, grad_keys, grad_values)


def backward_layer(grad_result, saved_state, weights, tag_value, key_bias):
    w_qkv, w_out, w_in, w_ffo, vectors_low = weights
    (
        summed_low,
        query_heads,
        key_heads,
        value_heads,
        log_total,
        context_low,
        norm_first,
        hidden_low,
        gelu_pull,
        activated_low,
        norm_second,
    ) = saved_state
    model_width = w_out.shape[0]
    row_count = summed_low.shape[0]
    head_size = model_width // H
    score_scale = head_size ** (-0.5)
    grad_pre_two, grad_gain_two, grad_shift_two = norm_second(grad_result)
    grad_feed = grad_pre_two.astype(jnp.bfloat16)
    grad_bias_feed = jnp.sum(grad_feed.astype(jnp.float32), axis=0)
    grad_ffo = jnp.einsum("tf,td->fd", activated_low, grad_feed, preferred_element_type=jnp.float32)
    grad_activated = jnp.einsum("td,fd->tf", grad_feed, w_ffo, preferred_element_type=jnp.float32)
    grad_inner = gelu_pull(grad_activated)[0].astype(jnp.bfloat16)
    grad_bias_inner = jnp.sum(grad_inner.astype(jnp.float32), axis=0)
    grad_in = jnp.einsum("td,tf->df", hidden_low, grad_inner, preferred_element_type=jnp.float32)
    grad_hidden = grad_pre_two + jnp.einsum(
        "tf,df->td", grad_inner, w_in, preferred_element_type=jnp.float32
    )
    grad_pre_one, grad_gain_one, grad_shift_one = norm_first(grad_hidden)
    grad_branch = grad_pre_one.astype(jnp.bfloat16)
    grad_bias_out = jnp.sum(grad_branch.astype(jnp.float32), axis=0)
    grad_out_matrix = jnp.einsum(
        "te,td->ed", context_low, grad_branch, preferred_element_type=jnp.float32
    )
    grad_context = jnp.einsum(
        "td,ed->te", grad_branch, w_out, preferred_element_type=jnp.float32
    ).astype(jnp.bfloat16)
    context_heads = grad_context.reshape(row_count, H, head_size)
    grad_queries, grad_keys, grad_values = attention_grads(
        query_heads, key_heads, value_heads, log_total, context_heads, key_bias, score_scale
    )
    grad_joined = jnp.concatenate(
        [
            grad_queries.astype(jnp.bfloat16),
            grad_keys.astype(jnp.bfloat16),
            grad_values.astype(jnp.bfloat16),
        ],
        axis=1,
    )
    grad_qkv = jnp.einsum("td,te->de", summed_low, grad_joined, preferred_element_type=jnp.float32)
    grad_summed = grad_pre_one + jnp.einsum(
        "te,de->td", grad_joined, w_qkv, preferred_element_type=jnp.float32
    )
    column_sums = jnp.sum(grad_joined.astype(jnp.float32), axis=0)
    grad_direction = jnp.sum(grad_summed, axis=0)
    zero_row = jnp.zeros_like(grad_direction)
    grad_rows = jnp.stack(
        [
            jnp.where(tag_value == 0, grad_direction, zero_row),
            jnp.where(tag_value == 1, grad_direction, zero_row),
            column_sums[:model_width],
            column_sums[2 * model_width :],
            grad_bias_out,
            grad_gain_one,
            grad_shift_one,
            grad_bias_feed,
            grad_gain_two,
            grad_shift_two,
        ],
        axis=0,
    )
    grad_vectors = jnp.concatenate([grad_rows, grad_bias_inner.reshape(-1, model_width)], axis=0)
    return (grad_summed, (grad_qkv, grad_out_matrix, grad_in, grad_ffo, grad_vectors))


def reduce_layer(grads):
    shards = (
        lax.psum_scatter(grads[0], "fsdp", scatter_dimension=0, tiled=True),
        lax.psum_scatter(grads[1], "fsdp", scatter_dimension=0, tiled=True),
        lax.psum_scatter(grads[2], "fsdp", scatter_dimension=0, tiled=True),
        lax.psum_scatter(grads[3], "fsdp", scatter_dimension=0, tiled=True),
        lax.psum_scatter(grads[4], "fsdp", scatter_dimension=1, tiled=True),
    )
    return (
        lax.psum(shards[0].astype(jnp.bfloat16), "rep").astype(jnp.float32),
        lax.psum(shards[1].astype(jnp.bfloat16), "rep").astype(jnp.float32),
        lax.psum(shards[2].astype(jnp.bfloat16), "rep").astype(jnp.float32),
        lax.psum(shards[3].astype(jnp.bfloat16), "rep").astype(jnp.float32),
        lax.psum(shards[4].astype(jnp.bfloat16), "rep").astype(jnp.float32),
    )


def body(
    tokens,
    cotangent,
    tags,
    lengths,
    key_mask,
    master_qkv,
    master_out,
    master_in,
    master_feed_output,
    master_vec,
    first_qkv,
    first_out,
    first_in,
    first_ffo,
    first_vec,
    second_qkv,
    second_out,
    second_in,
    second_ffo,
    second_moment_vector,
):
    row_count = tokens.shape[1]
    key_count = key_mask.shape[1]
    start_row = lax.axis_index("rep") * row_count
    query_pos = start_row + jnp.arange(row_count, dtype=jnp.int32)
    key_pos = jnp.arange(key_count, dtype=jnp.int32)
    seq_length = lengths[0]
    tag_value = tags[0]
    key_valid = (key_pos < seq_length) & ((key_mask[0] == 1) | (key_pos == 0))
    key_bias = jnp.where(key_valid, 0.0, masked_score).astype(jnp.float32)
    query_valid = (query_pos < seq_length).astype(jnp.float32)
    masters = (master_qkv, master_out, master_in, master_feed_output, master_vec)
    firsts = (first_qkv, first_out, first_in, first_ffo, first_vec)
    seconds = (second_qkv, second_out, second_in, second_ffo, second_moment_vector)
    shared = (
        lax.all_gather(master_qkv[0].astype(jnp.bfloat16), "fsdp", axis=0, tiled=True),
        lax.all_gather(master_out[0].astype(jnp.bfloat16), "fsdp", axis=0, tiled=True),
        lax.all_gather(master_in[0].astype(jnp.bfloat16), "fsdp", axis=0, tiled=True),
        lax.all_gather(master_feed_output[0].astype(jnp.bfloat16), "fsdp", axis=0, tiled=True),
        lax.all_gather(master_vec[0].astype(jnp.bfloat16), "fsdp", axis=1, tiled=True),
    )
    shared_out, saved_shared = forward_layer(
        tokens[0].astype(jnp.float32), shared, tag_value, key_bias
    )
    unique = (
        lax.all_gather(master_qkv[1].astype(jnp.bfloat16), "fsdp", axis=0, tiled=True),
        lax.all_gather(master_out[1].astype(jnp.bfloat16), "fsdp", axis=0, tiled=True),
        lax.all_gather(master_in[1].astype(jnp.bfloat16), "fsdp", axis=0, tiled=True),
        lax.all_gather(master_feed_output[1].astype(jnp.bfloat16), "fsdp", axis=0, tiled=True),
        lax.all_gather(master_vec[1].astype(jnp.bfloat16), "fsdp", axis=1, tiled=True),
    )
    final_out, saved_unique = forward_layer(shared_out, unique, tag_value, key_bias)
    grad_final = cotangent[0].astype(jnp.float32) * query_valid[:, None]
    unique_back = (
        lax.all_gather(master_qkv[1].astype(jnp.bfloat16), "fsdp", axis=0, tiled=True),
        lax.all_gather(master_out[1].astype(jnp.bfloat16), "fsdp", axis=0, tiled=True),
        lax.all_gather(master_in[1].astype(jnp.bfloat16), "fsdp", axis=0, tiled=True),
        lax.all_gather(master_feed_output[1].astype(jnp.bfloat16), "fsdp", axis=0, tiled=True),
        lax.all_gather(master_vec[1].astype(jnp.bfloat16), "fsdp", axis=1, tiled=True),
    )
    grad_middle, unique_grads = backward_layer(
        grad_final, saved_unique, unique_back, tag_value, key_bias
    )
    reduced_unique = reduce_layer(unique_grads)
    grad_inputs, shared_grads = backward_layer(
        grad_middle, saved_shared, shared, tag_value, key_bias
    )
    reduced_shared = reduce_layer(shared_grads)
    rates = (
        matrix_rate * D ** (-0.5),
        matrix_rate * (D // 16) ** (-0.5),
        matrix_rate * D ** (-0.5),
        matrix_rate * (FF // 2) ** (-0.5),
        vector_rate,
    )
    decays = (weight_decay, weight_decay, weight_decay, weight_decay, 0.0)
    updated = []
    for kind_index in range(5):
        grad_stack = jnp.stack([reduced_shared[kind_index], reduced_unique[kind_index]], axis=0)
        updated.append(
            adamw(
                masters[kind_index],
                firsts[kind_index],
                seconds[kind_index],
                grad_stack,
                rates[kind_index],
                decays[kind_index],
            )
        )
    return (
        final_out.astype(jnp.bfloat16)[None],
        grad_inputs[None],
        updated[0][0],
        updated[1][0],
        updated[2][0],
        updated[3][0],
        updated[4][0],
        updated[0][1],
        updated[1][1],
        updated[2][1],
        updated[3][1],
        updated[4][1],
        updated[0][2],
        updated[1][2],
        updated[2][2],
        updated[3][2],
        updated[4][2],
    )


BF = jnp.bfloat16
F32 = jnp.float32
MESH = pl.DeviceIdType.MESH
KIND_K, KIND_V, KIND_Q, KIND_O, KIND_I, KIND_F = KINDS = tuple(range(6))
VMEM_BYTES = 60 << 20
FORWARD_SPLIT = (1, 1, 2, 1, 1, 1, 1, 1, 5, 5, 5, 1, 1, 2, 2, 5)
BACKWARD_SPLIT = (1, 2, 5, 1, 1, 5, 2, 2, 5, 3, 1, 5)
FORWARD_TURNS = (
    (1, 2, 0, 3, 4, 1, 2, 5),
    (3, 0, 6, 1, 2, 4, 7, 3, 0, 5, 0, 1, 8),
    (2, 6, 4, 1, 9),
    (2,),
    (),
    (7, 3, 5, 10),
    (6,),
    (11, 3, 8),
    (4, 9, 12, 7),
    (13,),
    (),
    (4, 10),
    (5, 11, 14, 8, 12, 5, 15),
    (6, 8, 13, 9, 6, 10, 14, 9, 7, 11, 10, 12, 7),
    (13,),
    (14, 15),
    (),
    (11,),
    (),
    (),
    (11,),
    (12,),
    (),
    (13, 12),
    (),
    (),
    (13, 14),
    (15, 14, 15),
    (),
)
COTANGENT_AT = 0
BACKWARD_TURNS = (
    (),
    (),
    (0,),
    (),
    (),
    (1,),
    (),
    (0,),
    (2,),
    (2, 1),
    (),
    (2,),
    (0,),
    (3,),
    (4, 5),
    (),
    (2, 3, 12),
    (4, 5, 1, 12),
    (6, 2, 0, 3),
    (),
    (),
    (4, 5, 7),
    (6,),
    (12, 1),
    (3, 8),
    (4, 0, 8, 7),
    (6, 0, 5, 12),
    (8, 1),
    (4, 3, 12),
    (9,),
    (11, 10),
    (7, 5, 8, 9),
    (11, 13, 1, 10, 4, 3, 6, 13, 7, 8, 9, 11, 6, 10, 13, 9, 7, 6, 10, 13, 11, 7, 9, 10, 11, 13, 9, 10),
)


def nt_dot(left, right):
    return lax.dot_general(left, right, (((1,), (1,)), ((), ())), preferred_element_type=F32)


def nn_dot(left, right):
    return jnp.dot(left, right, preferred_element_type=F32)


def remote(src, dst, send_sem, recv_sem, device):
    return pltpu.make_async_remote_copy(
        src_ref=src,
        dst_ref=dst,
        send_sem=send_sem,
        recv_sem=recv_sem,
        device_id=device,
        device_id_type=MESH,
    )


class ForwardIn(NamedTuple):
    tok: object
    cot: object
    lengths: object
    tags: object
    key_mask: object
    vectors: object
    masters: object


class Saved(NamedTuple):
    w_o: object
    vec_o: object
    meta_o: object
    cot_o: object
    y_o: object
    at_o: object
    q_o: object
    k_o: object
    v_o: object
    lse_o: object
    ct_o: object
    ctp_o: object
    n1_o: object
    r1_o: object
    ht_o: object
    g_o: object
    gp_o: object
    n2_o: object
    r2_o: object


class ForwardScratch(NamedTuple):
    w: object
    stages: object
    vecg: object
    vecl: object
    vec: object
    metab: object
    msel: object
    tokb: object
    cotb: object
    A32: object
    Ab: object
    ATp: object
    Q: object
    K: object
    V: object
    lse: object
    CT: object
    CTp: object
    C: object
    N1: object
    r1: object
    H32: object
    Hb: object
    HTp: object
    G: object
    Gp: object
    N2: object
    r2: object
    X: object
    Yb: object
    msem: object
    xsem: object
    osem: object
    gs: object
    gr: object
    vs: object
    vr: object
    xs: object
    xr: object
    ks: object
    kr: object


class BackwardOut(NamedTuple):
    fin: object
    vec_g: object
    yo: object
    dxo: object


class BackwardScratch(NamedTuple):
    g: object
    landing: object
    half: object
    quarter: object
    level: object
    total: object
    w: object
    AT: object
    Q: object
    K: object
    V: object
    lse: object
    CT: object
    CTp: object
    N1: object
    r1: object
    HT: object
    G: object
    Gp: object
    N2: object
    r2: object
    vec: object
    msel: object
    cotb: object
    dy: object
    dpre: object
    dF: object
    dFT: object
    dU: object
    dZ: object
    delta: object
    dQT: object
    dvb: object
    dkp: object
    dvp: object
    dkr: object
    dvr: object
    vg: object
    va: object
    vrecv: object
    vb: object
    vt: object
    lsem: object
    ssem: object
    fsem: object
    gs: object
    gr: object
    xs: object
    xr: object
    ks: object
    kr: object
    vs: object
    vr: object


class UpdateIn(NamedTuple):
    fin: object
    fvec: object
    y: object
    dx: object
    masters: object
    firsts: object
    seconds: object


class UpdateOut(NamedTuple):
    out: object
    grad: object
    new_masters: object
    new_firsts: object
    new_seconds: object


class UpdateScratch(NamedTuple):
    inside: object
    wide: object
    isem: object
    osem: object


def named(parts, refs):
    fields, at = {}, 0
    for part in parts:
        leaves, tree = jax.tree.flatten(part)
        fields.update(tree.unflatten(refs[at : at + len(leaves)])._asdict())
        at += len(leaves)
    return SimpleNamespace(**fields)


def call_kernel(kernel, args, outs, scratch, spec, **options):
    leaves, _ = jax.tree.flatten(args)
    out_leaves, out_tree = jax.tree.flatten(outs)
    parts = (args, outs) if scratch is None else (args, outs, scratch)
    empty = jax.tree.map(lambda leaf: 0, parts)
    results = pl.pallas_call(
        functools.partial(kernel, empty),
        out_shape=out_leaves,
        in_specs=jax.tree.leaves(spec) if isinstance(spec, tuple) else [spec] * len(leaves),
        out_specs=[pl.BlockSpec(memory_space=pl.ANY)] * len(out_leaves),
        scratch_shapes=() if scratch is None else jax.tree.leaves(scratch),
        compiler_params=pltpu.CompilerParams(**options),
    )(*leaves)
    return out_tree.unflatten(results)


class Place:
    def __init__(self):
        self.r = lax.axis_index("rep")
        self.f = lax.axis_index("fsdp")
        self.z = lax.div(self.f, 4)
        self.y = lax.rem(lax.div(self.f, 2), 2)
        self.c = lax.rem(self.f, 2)
        self.xn = (1 - self.r, self.f)
        self.yn = (self.r, self.f + 2 - 4 * self.y)
        self.cn = (self.r, self.f + 1 - 2 * self.c)
        self.dn = (1 - self.r, self.f + 1 - 2 * self.c)
        self.en = (self.r, self.f + 3 - 4 * self.y - 2 * self.c)

    def zn(self, step, levels):
        other = lax.rem(self.z + step, levels)
        return other, (self.r, other * 4 + 2 * self.y + self.c)


def parity_rows(rows, shards):
    blocks = rows.reshape(shards // 2, 2, rows.shape[0] // shards, rows.shape[1])
    half = rows.shape[0] // 2
    return blocks[:, 0].reshape(half, rows.shape[1]), blocks[:, 1].reshape(half, rows.shape[1])


def halves(cut, levels):
    return pl.ds(0, cut), pl.ds(cut, levels - cut)


def go_or_stay(stays, stay, go):
    @pl.when(stays)
    def _():
        stay()

    @pl.when(jnp.logical_not(stays))
    def _():
        go()


def lane_masks():
    lane = lax.broadcasted_iota(jnp.int32, (16, 128), 1)
    low = (lane < 64).astype(F32)
    spots = (lax.rem(lane, 64) == 0).astype(F32)
    return low[:1].astype(BF), (1.0 - low[:1]).astype(BF), spots[:1].astype(BF)


def sizes_of(mesh_n, width, inner):
    shard = width // mesh_n
    rows = [shard // 2] * 6
    rows[KIND_F] = inner // mesh_n // 2
    cols = [width] * 6
    cols[KIND_I] = inner
    return rows, cols


def forward_kernel(parts, levels, eps, *refs):
    R = named(parts, refs)
    me = Place()
    r, f, z, y, c = me.r, me.f, me.z, me.y, me.c
    shards = levels * 4
    S, D = R.A32.shape
    FF = R.G.shape[1]
    source = ((0, D), (0, 2 * D), (0, 0), (1, 0), (2, 0), (3, 0))

    half_loads = {}
    for l in range(2):
        for at, (master, stage) in enumerate(zip(R.masters, R.stages)):
            cp = pltpu.make_async_copy(master.at[l], stage.at[l], R.msem.at[l, at])
            cp.start()
            half_loads[(l, at)] = cp
    barrier = pltpu.get_barrier_semaphore()
    peers = [me.zn(s, levels)[1] for s in range(1, levels)] + [me.xn, me.yn, me.cn, me.dn, me.en]
    for peer in peers:
        pl.semaphore_signal(barrier, inc=1, device_id=peer, device_id_type=MESH)
    pl.semaphore_wait(barrier, len(peers))

    chunks = []
    for l in range(2):
        for kind in KINDS:
            parts = 2 if kind in (KIND_I, KIND_F) else 1
            span = R.w[kind].shape[-1] // parts
            chunks += [(kind, l, slice(part * span, part * span + span)) for part in range(parts)]
    gs, gr = R.gs, R.gr
    pending = []

    def start(cp):
        cp.start()
        pending.append(cp)
        return cp

    out_copies = {}
    out_at = [0]

    def out(ref, dst, view=None):
        cp = pltpu.make_async_copy(ref if view is None else view, dst, R.osem.at[out_at[0]])
        out_at[0] += 1
        cp.start()
        out_copies[(id(ref), view is not None and out_at[0])] = cp

    def settle(ref):
        if (id(ref), False) in out_copies:
            out_copies.pop((id(ref), False)).wait()

    loaded = set()
    stage_copies = {}

    def g_z(i):
        kind, l, cols = chunks[i]
        w = R.w[kind]
        at, offset = source[kind]
        if (l, at) not in loaded:
            half_loads[(l, at)].wait()
            loaded.add((l, at))
        rows = w.shape[5]
        w[l, z, y, c, r, :, cols] = R.stages[at][l, pl.ds(r * rows, rows), offset + cols.start : offset + cols.stop].astype(BF)
        cps = []
        for s in range(1, levels):
            _, dev = me.zn(s, levels)
            spot = w.at[l, z, y, c, r, :, cols]
            cps.append(start(remote(spot, spot, gs.at[i, s - 1], gr.at[i, s - 1], dev)))
        stage_copies[i] = cps

    def g_1(i):
        kind, l, cols = chunks[i]
        w = R.w[kind]
        for cp in stage_copies[i]:
            cp.wait_recv()
        first, second = halves(FORWARD_SPLIT[i], levels)
        a, b = w.at[l, first, y, c, r, :, cols], w.at[l, second, y, c, r, :, cols]
        stage_copies[i] = [
            start(remote(a, a, gs.at[i, levels - 1], gr.at[i, levels - 1], me.xn)),
            start(remote(b, b, gs.at[i, levels], gr.at[i, levels], me.yn)),
        ]

    def g_2(i):
        kind, l, cols = chunks[i]
        w = R.w[kind]
        for cp in stage_copies[i]:
            cp.wait_recv()
        first, second = halves(FORWARD_SPLIT[i], levels)
        a, b = w.at[l, first, y, c, :, :, cols], w.at[l, second, :, c, r, :, cols]
        stage_copies[i] = [
            start(remote(a, a, gs.at[i, levels + 1], gr.at[i, levels + 1], me.yn)),
            start(remote(b, b, gs.at[i, levels + 2], gr.at[i, levels + 2], me.xn)),
        ]

    def g_core(i):
        kind, l, cols = chunks[i]
        w = R.w[kind]
        for cp in stage_copies[i]:
            cp.wait_recv()
        a = w.at[l, :, :, c, :, :, cols]
        stage_copies[i] = [start(remote(a, a, gs.at[i, levels + 3], gr.at[i, levels + 3], me.cn))]

    def h_z(i):
        kind, l, cols = chunks[i]
        w = R.w[kind]
        at, offset = source[kind]
        if (l, at) not in loaded:
            half_loads[(l, at)].wait()
            loaded.add((l, at))
        whole = R.stages[at][l][:, offset + cols.start : offset + cols.stop].astype(BF)
        w[l, z, y, c, :, :, cols] = whole.reshape(2, whole.shape[0] // 2, whole.shape[1])
        spot = w.at[l, z, y, c, :, :, cols]
        stage_copies[i] = [
            start(remote(spot, spot, gs.at[i, s], gr.at[i, s], me.zn(s, levels)[1])) for s in range(1, levels)
        ]

    def h_y(i):
        kind, l, cols = chunks[i]
        w = R.w[kind]
        for cp in stage_copies[i]:
            cp.wait_recv()
        spot = w.at[l, :, y, c, :, :, cols]
        stage_copies[i] = [start(remote(spot, spot, gs.at[i, 0], gr.at[i, 0], me.yn))]

    def g_ready(i):
        kind, l, cols = chunks[i]
        for cp in stage_copies.pop(i):
            cp.wait_recv()
        waiting.remove(i)
        if not any(chunks[k][:2] == (kind, l) for k in waiting):
            out(R.w[kind], R.w_o[kind].at[l], R.w[kind].at[l])

    steps = (g_z, g_1, g_2, g_core, g_ready)
    other_steps = (h_z, h_y, g_core, g_ready)
    reached = [0] * len(chunks)
    waiting = list(range(len(chunks)))
    turns = iter(FORWARD_TURNS)

    def turn():
        for i in next(turns):
            (other_steps if FORWARD_SPLIT[i] == 5 else steps)[reached[i]](i)
            reached[i] += 1

    steps[0](0)
    reached[0] = 1
    tok_far = remote(R.tok.at[0], R.tokb, R.xs.at[1], R.xr.at[1], me.dn)
    tok_near = pltpu.make_async_copy(R.tok.at[0], R.tokb, R.xsem.at[2])
    stays = c == r

    go_or_stay(stays, tok_near.start, tok_far.start)
    length = R.lengths[0]
    keys = R.key_mask[...]
    key_pos = lax.broadcasted_iota(jnp.int32, keys.shape, 1)
    valid = key_pos < length
    bias = jnp.where(valid & ((keys == 1) | (key_pos == 0)), 0.0, masked_score)
    place = lax.broadcasted_iota(jnp.int32, (128, 2 * S), 0)
    columns = jnp.where(lax.rem(place, 64) == 0, bias, 0.0) + jnp.where((place == 1) & valid, 1.0, 0.0)
    R.metab[0, : 2 * S] = columns.T.astype(BF)
    R.metab[0, 2 * S :] = jnp.full((16, 128), R.tags[0].astype(F32)).astype(BF)
    meta_cp = start(remote(R.metab.at[0], R.metab.at[1], R.xs.at[0], R.xr.at[0], me.cn))
    wide = R.vectors.shape[2]
    lane = lax.broadcasted_iota(jnp.int32, (R.vectors.shape[0], 128), 1)
    spot = R.vecg.at[2 * y + c]
    spot[...] = jnp.zeros((32, 128), BF)
    for l in range(2):
        block = jnp.concatenate([R.vectors[:, l]] * (128 // wide), axis=1)
        block = jnp.where(lax.div(lane, wide) == lax.rem(f, 128 // wide), block, 0.0)
        block = jnp.concatenate([block, jnp.zeros((16 - block.shape[0], 128), F32)], axis=0)
        spot[16 * l : 16 * l + 16] = block.astype(BF)
    vec_cps = [start(remote(spot, spot, R.vs.at[at], R.vr.at[at], dev)) for at, dev in enumerate((me.yn, me.cn, me.en))]
    for cp in vec_cps:
        cp.wait_recv()
    spot = R.vecl.at[z]
    spot[...] = jnp.sum(R.vecg[...].astype(F32), axis=0).astype(BF)
    vec_cps = []
    for s in range(1, levels):
        vec_cps.append(start(remote(spot, spot, R.vs.at[2 + s], R.vr.at[2 + s], me.zn(s, levels)[1])))
    turn()
    meta_cp.wait_recv()
    for cp in vec_cps:
        cp.wait_recv()
    keep = stays.astype(F32)
    msel = R.msel
    msel[...] = (R.metab[0].astype(F32) * keep + R.metab[1].astype(F32) * (1.0 - keep)).astype(BF)
    vec = R.vec
    for zz in range(levels):
        vec[:, 128 * zz : 128 * zz + 128] = R.vecl[zz].astype(F32)
    tag_row = msel[2 * S : 2 * S + 16].astype(F32)[:1]
    tag_row = jnp.concatenate([tag_row] * (D // 128), axis=1)
    low, high, spots = lane_masks()

    go_or_stay(stays, tok_near.wait, tok_far.wait)
    cot_far = remote(R.cot.at[0], R.cotb, R.xs.at[2], R.xr.at[2], me.dn)
    cot_near = pltpu.make_async_copy(R.cot.at[0], R.cotb, R.xsem.at[3])

    T = 256
    for l in range(2):
        e = lambda row: vec[16 * l + row : 16 * l + row + 1, :]
        direction = e(0) * (1.0 - tag_row) + e(1) * tag_row
        if l == 1:
            turn()
        A32, Ab, Q, K, V, CT = R.A32, R.Ab, R.Q, R.K, R.V, R.CT
        x_in = R.tokb if l == 0 else R.X
        summed = x_in[...].astype(F32) + direction
        A32[...] = summed
        Ab[...] = summed.astype(BF)
        at = Ab[...].T
        even, odd = parity_rows(at, shards)
        settle(R.ATp)
        R.ATp[: D // 2] = even
        R.ATp[D // 2 :] = odd
        out(R.ATp, R.at_o.at[l])

        def weight(kind, lo=0, hi=None):
            w = R.w[kind]
            hi = w.shape[-1] if hi is None else hi
            value = w[l, :, :, :, :, :, lo:hi]
            return value.reshape(-1, hi - lo)

        turn()
        K[l, c] = nn_dot(Ab[...], weight(KIND_K)).astype(BF)
        k_cp = start(remote(K.at[l, c], K.at[l, c], R.ks.at[l, 0], R.kr.at[l, 0], me.cn))
        turn()
        V[l, c] = (nn_dot(Ab[...], weight(KIND_V)) + e(3)).astype(BF)
        v_cp = start(remote(V.at[l, c], V.at[l, c], R.ks.at[l, 1], R.kr.at[l, 1], me.cn))
        turn()
        settle(R.Q)
        q = (nn_dot(Ab[...], weight(KIND_Q)) + e(2)).astype(BF)
        Q[...] = (q.astype(F32) * 0.125).astype(BF)
        out(R.Q, R.q_o.at[l])
        turn()
        k_cp.wait_recv()
        v_cp.wait_recv()
        out(K, R.k_o.at[l], K.at[l])
        out(V, R.v_o.at[l], V.at[l])
        lse = R.lse
        settle(R.lse)
        settle(R.CT)
        bias_rows = msel[: 2 * S]

        def pair(j):
            sl = slice(j * 128, j * 128 + 128)
            k2 = K[l, :, :, sl].reshape(2 * S, 128)
            v2t = V[l, :, :, sl].reshape(2 * S, 128).T
            q2 = Q[:, sl]
            scores = []
            for mine, other in ((low, high), (high, low)):
                scores.append(nt_dot(k2 * mine + bias_rows * other, q2 * mine + spots * other))
            for h, st in enumerate(scores):
                top = jnp.max(st, axis=0, keepdims=True)
                p = jnp.exp(st - top)
                total = jnp.sum(p, axis=0, keepdims=True)
                ctx = nn_dot(v2t, p.astype(BF))[64 * h : 64 * h + 64]
                rows = slice(j * 128 + 64 * h, j * 128 + 64 * h + 64)
                CT[rows] = (ctx * (1.0 / total)).astype(BF)
                lse[j, h : h + 1] = top + jnp.log(total)

        for j in range(D // 128):
            turn()
            if l == 1 and j == COTANGENT_AT:
                go_or_stay(stays, cot_near.start, cot_far.start)
            pair(j)
        turn()
        out(R.lse, R.lse_o.at[l])
        out(R.CT, R.ct_o.at[l])
        even, odd = parity_rows(CT[...], shards)
        settle(R.CTp)
        R.CTp[: D // 2] = even
        R.CTp[D // 2 :] = odd
        out(R.CTp, R.ctp_o.at[l])
        R.C[...] = CT[...].T
        settle(R.N1)
        settle(R.r1)

        def norm_one(t, carry):
            rows = pl.ds(pl.multiple_of(t * T, T), T)
            pre = A32[rows] + nn_dot(R.C[rows], weight(KIND_O)) + e(4)
            mean = jnp.mean(pre, axis=-1, keepdims=True)
            centred = pre - mean
            rstd = lax.rsqrt(jnp.mean(centred * centred, axis=-1, keepdims=True) + eps)
            n1 = centred * rstd
            hidden = n1 * e(5) + e(6)
            R.N1[rows] = n1
            R.r1[rows] = jnp.broadcast_to(rstd, (T, 128))
            R.H32[rows] = hidden
            R.Hb[rows] = hidden.astype(BF)
            return carry

        turn()
        lax.fori_loop(0, S // T, norm_one, 0)
        out(R.N1, R.n1_o.at[l])
        out(R.r1, R.r1_o.at[l])
        even, odd = parity_rows(R.Hb[...].T, shards)
        settle(R.HTp)
        R.HTp[: D // 2] = even
        R.HTp[D // 2 :] = odd
        out(R.HTp, R.ht_o.at[l])
        settle(R.G)
        settle(R.Gp)

        def inner(b):
            u = nn_dot(R.Hb[...], weight(KIND_I, b * D, b * D + D)) + e(10 + b)
            u2 = u * u
            th = jnp.tanh(u * (0.7978845608028654 + 0.035677408136300125 * u2))
            half = 0.5 + 0.5 * th
            slope = 0.7978845608028654 + 0.10703222440890038 * u2
            R.G[:, b * D : b * D + D] = (u * half).astype(BF)
            R.Gp[:, b * D : b * D + D] = (half + 0.5 * u * (1.0 - th * th) * slope).astype(BF)

        for b in range(FF // D):
            if b % 2 == 0:
                turn()
            inner(b)
        out(R.G, R.g_o.at[l])
        out(R.Gp, R.gp_o.at[l])
        turn()
        settle(R.N2)
        settle(R.r2)

        def norm_two(t, carry):
            rows = pl.ds(pl.multiple_of(t * T, T), T)
            pre = R.H32[rows] + nn_dot(R.G[rows], weight(KIND_F)) + e(7)
            mean = jnp.mean(pre, axis=-1, keepdims=True)
            centred = pre - mean
            rstd = lax.rsqrt(jnp.mean(centred * centred, axis=-1, keepdims=True) + eps)
            n2 = centred * rstd
            R.N2[rows] = n2
            R.r2[rows] = jnp.broadcast_to(rstd, (T, 128))
            R.X[rows] = n2 * e(8) + e(9)
            return carry

        lax.fori_loop(0, S // T, norm_two, 0)
        out(R.N2, R.n2_o.at[l])
        out(R.r2, R.r2_o.at[l])

    turn()
    R.Yb[...] = R.X[...].astype(BF)
    out(R.Yb, R.y_o)
    out(vec, R.vec_o)
    out(msel, R.meta_o)
    go_or_stay(stays, cot_near.wait, cot_far.wait_recv)
    out(R.cotb, R.cot_o)
    for cp in out_copies.values():
        cp.wait()
    for cp in pending:
        cp.wait_send()
    go_or_stay(stays, lambda: None, cot_far.wait_send)


def backward_kernel(parts, levels, *refs):
    R = named(parts, refs)
    me = Place()
    r, f, z, y, c = me.r, me.f, me.z, me.y, me.c
    shards = levels * 4
    S, D = R.dy.shape
    FF = R.G.shape[1]
    saved = list(zip(R.w, R.w_o)) + [
        (R.AT, R.at_o), (R.Q, R.q_o), (R.K, R.k_o), (R.V, R.v_o), (R.lse, R.lse_o), (R.CT, R.ct_o), (R.CTp, R.ctp_o),
        (R.N1, R.n1_o), (R.r1, R.r1_o), (R.HT, R.ht_o), (R.G, R.g_o), (R.Gp, R.gp_o), (R.N2, R.n2_o), (R.r2, R.r2_o),
    ]
    order = {id(ref): at for at, (ref, _) in enumerate(saved)}
    loads = {}

    def load(ref, l):
        at = order[id(ref)]
        cp = pltpu.make_async_copy(saved[at][1].at[l], ref, R.lsem.at[l, at])
        cp.start()
        loads[id(ref)] = cp

    def use(ref):
        if id(ref) in loads:
            loads.pop(id(ref)).wait()
        return ref

    small = []
    for at, (dst, src) in enumerate(((R.vec, R.vec_o), (R.msel, R.meta_o), (R.cotb, R.cot_o))):
        cp = pltpu.make_async_copy(src, dst, R.ssem.at[at])
        cp.start()
        small.append(cp)
    wk, wv, wq, wo, wi, wf = R.w
    for ref in (R.N2, R.r2, R.G):
        load(ref, 1)
    later = (wf, R.Gp, R.HT, wi, R.N1, R.r1, R.CTp, wo, R.CT, R.K, R.V, R.Q, R.lse, R.AT, wq, wk, wv)

    barrier = pltpu.get_barrier_semaphore()
    peers = [me.zn(s, levels)[1] for s in range(1, levels)] + [me.xn, me.yn, me.cn, me.dn]
    for peer in peers:
        pl.semaphore_signal(barrier, inc=1, device_id=peer, device_id_type=MESH)

    pending = []

    def start(cp):
        cp.start()
        pending.append(cp)
        return cp

    stays = c == r
    y_far = remote(R.y_o, R.yo, R.xs.at[0], R.xr.at[0], me.dn)
    y_near = pltpu.make_async_copy(R.y_o, R.yo, R.ssem.at[3])
    dx_cps = []


    gs, gr = R.gs, R.gr
    chunks = [(kind, l) for l in (1, 0) for kind in (KIND_F, KIND_I, KIND_O, KIND_Q, KIND_K, KIND_V)]
    chunks += [(None, 1), (None, 0)]
    flight = {}
    stage = {}
    fin_copies = []

    def rs_core(i):
        kind, l = chunks[i]
        g = R.g[kind]
        spot = g.at[0, 0] if l == 1 else R.landing[kind]
        flight[i] = [start(remote(g.at[l, 1 - c], spot, gs.at[i, 0], gr.at[i, 0], me.cn))]

    def rs_1(i):
        kind, l = chunks[i]
        g = R.g[kind]
        first, second = halves(BACKWARD_SPLIT[i], levels)
        half, quarter = R.half[kind], R.quarter[kind]
        g[l, c] = g[l, c] + (g[0, 0] if l == 1 else R.landing[kind][...])
        flight[i] = [
            start(remote(g.at[l, c, first, 1 - y], half.at[l, first], gs.at[i, 1], gr.at[i, 1], me.yn)),
            start(remote(g.at[l, c, second, :, 1 - r], half.at[l, second], gs.at[i, 2], gr.at[i, 2], me.xn)),
        ]

    def rs_2(i):
        kind, l = chunks[i]
        g = R.g[kind]
        first, second = halves(BACKWARD_SPLIT[i], levels)
        half, quarter = R.half[kind], R.quarter[kind]
        g[l, c, first, y] = g[l, c, first, y] + half[l, first]
        g[l, c, second, :, r] = g[l, c, second, :, r] + half[l, second]
        flight[i] = [
            start(remote(g.at[l, c, first, y, 1 - r], quarter.at[l, first], gs.at[i, 3], gr.at[i, 3], me.xn)),
            start(remote(g.at[l, c, second, 1 - y, r], quarter.at[l, second], gs.at[i, 4], gr.at[i, 4], me.yn)),
        ]

    def rs_3(i):
        kind, l = chunks[i]
        g = R.g[kind]
        first, second = halves(BACKWARD_SPLIT[i], levels)
        half, quarter = R.half[kind], R.quarter[kind]
        g[l, c, first, y, r] = g[l, c, first, y, r] + quarter[l, first]
        g[l, c, second, y, r] = g[l, c, second, y, r] + quarter[l, second]
        flight[i] = []
        for s in range(1, levels):
            there, dev = me.zn(s, levels)
            flight[i].append(
                start(remote(g.at[l, c, there, y, r], R.level[kind].at[l, s - 1, 0], gs.at[i, 4 + s], gr.at[i, 4 + s], dev))
            )

    def rs_4(i):
        kind, l = chunks[i]
        g, fin = R.g[kind], R.total[kind]
        total = g[l, c, z, y, r].astype(F32)
        for s in range(levels - 1):
            total = total + R.level[kind][l, s, 0].astype(F32)
        fin[l, r] = total.astype(BF)
        flight[i] = [start(remote(fin.at[l, r], fin.at[l, r], gs.at[i, 4 + levels], gr.at[i, 4 + levels], me.xn))]

    def rs_5(i):
        kind, l = chunks[i]
        cp = pltpu.make_async_copy(R.total[kind].at[l], R.fin[kind].at[l], R.fsem.at[i])
        cp.start()
        fin_copies.append(cp)

    vg, va, vb, vt = R.vg, R.va, R.vb, R.vt

    def vec_hop(at, device):
        def step(i):
            l = chunks[i][1]
            if at == 0:
                va[l, 0] = vg[16 * l : 16 * l + 16]
            else:
                va[l, at] = va[l, at - 1] + R.vrecv[l, at - 1]
            flight[i] = [start(remote(va.at[l, at], R.vrecv.at[l, at], R.vs.at[l, at], R.vr.at[l, at], device))]

        return step

    def vec_level(i):
        l = chunks[i][1]
        va[l, 3] = va[l, 2] + R.vrecv[l, 2]
        flight[i] = []
        for s in range(1, levels):
            there, dev = me.zn(s, levels)
            lanes = pl.ds(pl.multiple_of(there * 128, 128), 128)
            flight[i].append(start(remote(va.at[l, 3, :, lanes], vb.at[l, s - 1], R.vs.at[l, 2 + s], R.vr.at[l, 2 + s], dev)))

    def vec_end(i):
        l = chunks[i][1]
        total = va[l, 3, :, pl.ds(pl.multiple_of(z * 128, 128), 128)]
        for s in range(levels - 1):
            total = total + vb[l, s]
        vt[16 * l : 16 * l + 16] = total

    def hs_y(i):
        kind, l = chunks[i]
        g = R.g[kind]
        g[l, c] = g[l, c] + (g[0, 0] if l == 1 else R.landing[kind][...])
        spot = R.half[kind].at[l]
        flight[i] = [start(remote(g.at[l, c, :, 1 - y], spot, gs.at[i, levels], gr.at[i, levels], me.yn))]

    def hs_z(i):
        kind, l = chunks[i]
        g = R.g[kind]
        g[l, c, :, y] = g[l, c, :, y] + R.half[kind][l]
        flight[i] = []
        for s in range(1, levels):
            there, dev = me.zn(s, levels)
            spot = R.level[kind].at[l, s - 1]
            flight[i].append(start(remote(g.at[l, c, there, y], spot, gs.at[i, s], gr.at[i, s], dev)))

    def hs_x(i):
        kind, l = chunks[i]
        g = R.g[kind]
        whole = g[l, c, z, y].astype(F32)
        for s in range(levels - 1):
            whole = whole + R.level[kind][l, s].astype(F32)
        g[l, c, z, y] = whole.astype(BF)
        spot = R.quarter[kind].at[l, pl.ds(0, 2)]
        sems = gs.at[i, levels + 1], gr.at[i, levels + 1]
        flight[i] = [start(remote(g.at[l, c, z, y], spot, *sems, me.xn))]

    def hs_end(i):
        kind, l = chunks[i]
        R.total[kind][l] = R.g[kind][l, c, z, y] + R.quarter[kind][l, :2]
        rs_5(i)

    other_steps = (rs_core, hs_y, hs_z, hs_x, hs_end)
    matrix_steps = (rs_core, rs_1, rs_2, rs_3, rs_4, rs_5)
    vec_steps = (vec_hop(0, me.cn), vec_hop(1, me.xn), vec_hop(2, me.yn), vec_level, vec_end)
    turns = iter(BACKWARD_TURNS)

    def turn():
        for i in next(turns):
            at = stage.get(i, 0)
            for cp in flight.pop(i, ()):
                cp.wait_recv()
            known = vec_steps if chunks[i][0] is None else other_steps if BACKWARD_SPLIT[i] == 5 else matrix_steps
            known[at](i)
            stage[i] = at + 1

    for cp in small:
        cp.wait()
    vec, msel = R.vec, R.msel
    tag_row = msel[2 * S : 2 * S + 16].astype(F32)[:1]
    tag_row = jnp.concatenate([tag_row] * (D // 128), axis=1)
    low, high, spots = lane_masks()
    low32 = low.astype(F32)
    vg[...] = jnp.zeros_like(vg)
    R.dy[...] = R.cotb[...].astype(F32) * msel[pl.ds(c * S, S)][:, 1:2].astype(F32)
    T = 256
    dy, dpre, dF, dFT, dU, dZ = R.dy, R.dpre, R.dF, R.dFT, R.dU, R.dZ

    def fold(value):
        return jnp.sum(value.reshape(value.shape[0] // 8, 8, value.shape[1]), axis=0)

    zero8 = jnp.zeros((8, D), F32)

    for l in (1, 0):
        base = 16 * l
        e = lambda row: vec[base + row : base + row + 1, :]

        def put(row, value):
            vg[base + row : base + row + 1, :] = value

        def weight(kind):
            w = R.w[kind]
            return w[...].reshape(-1, w.shape[-1])

        turn()
        N2, r2 = use(R.N2), use(R.r2)
        if l == 1:
            for ref in later:
                load(ref, 1)

        def norm_two(t, carry):
            s7, s8, s9 = carry
            rows = pl.ds(pl.multiple_of(t * T, T), T)
            g, n = dy[rows], N2[rows]
            dn = g * e(8)
            m1 = jnp.mean(dn, axis=-1, keepdims=True)
            m2 = jnp.mean(dn * n, axis=-1, keepdims=True)
            d = r2[rows][:, :1] * (dn - m1 - n * m2)
            dpre[rows] = d
            db = d.astype(BF)
            dF[rows] = db
            dFT[:, rows] = db.T
            return s7 + fold(db.astype(F32)), s8 + fold(g * n), s9 + fold(g)

        s7, s8, s9 = lax.fori_loop(0, S // T, norm_two, (zero8, zero8, zero8))
        put(7, jnp.sum(s7, axis=0, keepdims=True))
        put(8, jnp.sum(s8, axis=0, keepdims=True))
        put(9, jnp.sum(s9, axis=0, keepdims=True))
        if l == 1:
            pl.semaphore_wait(barrier, len(peers))
            go_or_stay(stays, y_near.start, y_far.start)
        turn()
        G = use(R.G)
        gf = R.g[KIND_F]
        piece = 2 * FF // shards

        def grad_f(t, carry):
            d = nn_dot(dFT[...], G[:, pl.ds(pl.multiple_of(t * piece, piece), piece)]).astype(BF)
            zz, yy = lax.div(t, 2), lax.rem(t, 2)
            half = piece // 2
            gf[l, 0, zz, yy] = d[:, :half].reshape(2, D // 2, half)
            gf[l, 1, zz, yy] = d[:, half:].reshape(2, D // 2, half)
            return carry

        lax.fori_loop(0, shards // 2, grad_f, 0)
        if l == 1:
            for ref in (R.N2, R.r2, R.G):
                load(ref, 0)
        use(R.w[KIND_F])
        Gp = use(R.Gp)

        def grad_inner(b):
            wf = R.w[KIND_F]
            quarter = wf[b * (levels // (FF // D)) : (b + 1) * (levels // (FF // D))].reshape(D, D)
            cols = slice(b * D, b * D + D)
            du = (nt_dot(dF[...], quarter) * Gp[:, cols].astype(F32)).astype(BF)
            dU[:, cols] = du
            put(10 + b, jnp.sum(fold(du.astype(F32)), axis=0, keepdims=True))

        for b in range(FF // D):
            if b % 2 == 0:
                turn()
            grad_inner(b)
        turn()
        if l == 1:
            load(R.w[KIND_F], 0)
            load(R.Gp, 0)
        HT = use(R.HT)
        gi = R.g[KIND_I]
        rows_i = 2 * R.g[KIND_I].shape[-2]

        for b in range(FF // D):
            d = nn_dot(HT[...], dU[:, b * D : b * D + D]).astype(BF)
            for cc in range(2):
                part = d[cc * (D // 2) : (cc + 1) * (D // 2)]
                gi[l, cc, :, :, :, :, b * D : b * D + D] = part.reshape(levels, 2, 2, rows_i // 2, D)
        if l == 1:
            load(R.HT, 0)
        use(R.w[KIND_I])
        N1, r1 = use(R.N1), use(R.r1)

        def norm_one(t, carry):
            s4, s5, s6 = carry
            rows = pl.ds(pl.multiple_of(t * T, T), T)
            g = dpre[rows] + nt_dot(dU[rows], weight(KIND_I))
            n = N1[rows]
            dn = g * e(5)
            m1 = jnp.mean(dn, axis=-1, keepdims=True)
            m2 = jnp.mean(dn * n, axis=-1, keepdims=True)
            d = r1[rows][:, :1] * (dn - m1 - n * m2)
            dy[rows] = d
            db = d.astype(BF)
            dZ[rows] = db
            return s4 + fold(db.astype(F32)), s5 + fold(g * n), s6 + fold(g)

        turn()
        sums = lax.fori_loop(0, S // T // 2, norm_one, (zero8, zero8, zero8))
        turn()
        s4, s5, s6 = lax.fori_loop(S // T // 2, S // T, norm_one, sums)
        put(4, jnp.sum(s4, axis=0, keepdims=True))
        put(5, jnp.sum(s5, axis=0, keepdims=True))
        put(6, jnp.sum(s6, axis=0, keepdims=True))
        turn()
        if l == 1:
            for ref in (R.w[KIND_I], R.N1, R.r1):
                load(ref, 0)
        CTp = use(R.CTp)
        go = R.g[KIND_O]

        def store(ref, value):
            for cc in range(2):
                ref[l, cc] = value[cc * (D // 2) : (cc + 1) * (D // 2)].reshape(ref.shape[2:])

        store(R.g[KIND_O], nn_dot(CTp[...], dZ[...]).astype(BF))
        use(R.w[KIND_O])
        dF[...] = nt_dot(dZ[...], weight(KIND_O)).astype(BF)
        CT = use(R.CT)
        dct = dF[...].T
        prod = dct.astype(F32) * CT[...].astype(F32)
        prod = jnp.sum(prod.reshape(D // 64, 64, S), axis=1)
        for j in range(D // 128):
            R.delta[j, :2] = prod[2 * j : 2 * j + 2]
        if l == 1:
            for ref in (R.CTp, R.w[KIND_O], R.CT):
                load(ref, 0)
        K, V, Q, lse = use(R.K), use(R.V), use(R.Q), use(R.lse)
        delta, dC, dQT = R.delta, dF, R.dQT
        dkp, dvp, dkr, dvr = R.dkp, R.dvp, R.dkr, R.dvr
        bias_rows = msel[: 2 * S]

        def pair(j):
            sl = slice(j * 128, j * 128 + 128)
            k2 = K[:, :, sl].reshape(2 * S, 128)
            v2 = V[:, :, sl].reshape(2 * S, 128)
            k2t = k2.T
            q2 = Q[:, sl]
            dc2 = dC[:, sl]
            dk_sum, dv_sum = None, None
            for h in range(2):
                mine, other = (low, high) if h == 0 else (high, low)
                mine32 = low32 if h == 0 else 1.0 - low32
                kh = k2 * mine + bias_rows * other
                vh = v2 * mine
                qh = q2 * mine + spots * other
                dk_h, dv_h = None, None
                for part in range(S // 256):
                    cols = slice(part * 256, part * 256 + 256)
                    st = nt_dot(kh, qh[cols])
                    p = jnp.exp(st - lse[j, h : h + 1, cols])
                    dp = nt_dot(vh, dc2[cols])
                    ds = (p * (dp - delta[j, h : h + 1, cols])).astype(BF)
                    pb = p.astype(BF)
                    dv = nn_dot(pb, dc2[cols])
                    dk = nn_dot(ds, q2[cols])
                    dv_h = dv if dv_h is None else dv_h + dv
                    dk_h = dk if dk_h is None else dk_h + dk
                    dq = nn_dot(k2t, ds)[64 * h : 64 * h + 64]
                    rows = slice(j * 128 + 64 * h, j * 128 + 64 * h + 64)
                    dQT[rows, cols] = (dq * 0.125).astype(BF)
                dk_sum = dk_h * mine32 if dk_sum is None else dk_sum + dk_h * mine32
                dv_sum = dv_h * mine32 if dv_sum is None else dv_sum + dv_h * mine32
            dkp[l, :, j] = dk_sum.astype(BF).reshape(2, S, 128)
            dvp[l, :, j] = dv_sum.astype(BF).reshape(2, S, 128)

        pairs = D // 128
        half_pairs = pairs // 2
        kv_cps = []
        for j in range(pairs):
            turn()
            pair(j)
            if (j + 1) % half_pairs == 0:
                part = j // half_pairs
                js = pl.ds(part * half_pairs, half_pairs)
                for at, (mine, theirs) in enumerate(((dkp, dkr), (dvp, dvr))):
                    sems = R.ks.at[l, part, at], R.kr.at[l, part, at]
                    kv_cps.append(start(remote(mine.at[l, 1 - c, js], theirs.at[l, js], *sems, me.cn)))
        if l == 1:
            for ref in (R.K, R.V, R.Q, R.lse):
                load(ref, 0)
        turn()
        AT = use(R.AT)
        dqb = dZ
        dqb[...] = dQT[...].T
        store(R.g[KIND_Q], nn_dot(AT[...], dqb[...]).astype(BF))
        turn()
        for cp in kv_cps:
            cp.wait_recv()
        dkb, dvb = dFT, R.dvb
        for j in range(pairs):
            dkb[:, 128 * j : 128 * j + 128] = dkp[l, c, j] + dkr[l, j]
            dvb[:, 128 * j : 128 * j + 128] = dvp[l, c, j] + dvr[l, j]
        store(R.g[KIND_K], nn_dot(AT[...], dkb[...]).astype(BF))
        store(R.g[KIND_V], nn_dot(AT[...], dvb[...]).astype(BF))
        if l == 1:
            load(R.AT, 0)
        use(R.w[KIND_Q])
        use(R.w[KIND_K])
        use(R.w[KIND_V])

        def last(t, carry):
            s0, s2, s3 = carry
            rows = pl.ds(pl.multiple_of(t * T, T), T)
            d = dy[rows] + nt_dot(dqb[rows], weight(KIND_Q)) + nt_dot(dkb[rows], weight(KIND_K)) + nt_dot(dvb[rows], weight(KIND_V))
            dy[rows] = d
            return s0 + fold(d), s2 + fold(dqb[rows].astype(F32)), s3 + fold(dvb[rows].astype(F32))

        sums = (zero8, zero8, zero8)
        for part in range(2):
            turn()
            sums = lax.fori_loop(part * (S // T // 2), (part + 1) * (S // T // 2), last, sums)
            if l == 0:
                half = pl.ds(part * (S // 2), S // 2)
                R.cotb[half] = dy[half].astype(BF)
                far = remote(R.cotb.at[half], R.dxo.at[half], R.xs.at[1 + part], R.xr.at[1 + part], me.dn)
                near = pltpu.make_async_copy(R.cotb.at[half], R.dxo.at[half], R.ssem.at[4 + part])
                dx_cps.append((far, near))
                go_or_stay(stays, near.start, far.start)
        s0, s2, s3 = sums
        s0 = jnp.sum(s0, axis=0, keepdims=True)
        put(0, s0 * (1.0 - tag_row))
        put(1, s0 * tag_row)
        put(2, jnp.sum(s2, axis=0, keepdims=True))
        put(3, jnp.sum(s3, axis=0, keepdims=True))
        if l == 1:
            for ref in (R.w[KIND_Q], R.w[KIND_K], R.w[KIND_V]):
                load(ref, 0)

    turn()
    vec_out = pltpu.make_async_copy(vt, R.vec_g, R.ssem.at[6])
    vec_out.start()
    for cp in fin_copies:
        cp.wait()
    vec_out.wait()
    for cp in pending:
        cp.wait_send()

    for far, near in dx_cps:
        go_or_stay(stays, near.wait, far.wait)
    go_or_stay(stays, y_near.wait, y_far.wait)


def update_kernel(parts, rates, decays, *refs):
    R = named(parts, refs)
    f = lax.axis_index("fsdp")
    sources, _ = jax.tree.flatten((R.fin, R.fvec, R.y, R.dx, R.masters, R.firsts, R.seconds))
    places, tree = jax.tree.flatten(R.inside)
    copies = [pltpu.make_async_copy(s, p, R.isem.at[at]) for at, (s, p) in enumerate(zip(sources, places))]
    fin, fvec, y, dx, masters, firsts, seconds = R.inside
    waits = tree.unflatten(copies)
    waits[3].start()
    waits[2].start()
    for at, kinds in ((2, (KIND_I,)), (3, (KIND_F,)), (1, (KIND_O,)), (0, (KIND_Q, KIND_K, KIND_V)), (4, ())):
        for cp in [waits[0][k] for k in kinds] + [w[at] for w in waits[4:]]:
            cp.start()
    waits[1].start()
    finals = (R.new_masters, R.new_firsts, R.new_seconds)
    leaving = []

    def leave(src, dst):
        cp = pltpu.make_async_copy(src, dst, R.osem.at[len(leaving)])
        cp.start()
        leaving.append(cp)

    def arrive(at, kinds):
        for cp in [waits[0][k] for k in kinds] + [w[at] for w in waits[4:]]:
            cp.wait()

    def step(at, where, grad):
        new = adamw(masters[at][where], firsts[at][where], seconds[at][where], grad, rates[at], decays[at])
        for refs, value in zip((masters, firsts, seconds), new):
            refs[at][where] = value

    def done(at):
        for kept, final in zip((masters, firsts, seconds), finals):
            leave(kept[at], final[at])

    waits[3].wait()
    R.wide[...] = dx[...].astype(F32)
    leave(R.wide, R.grad.at[0])
    waits[2].wait()
    leave(y, R.out.at[0])
    D = dx.shape[1]
    for at, kind in ((2, KIND_I), (3, KIND_F), (1, KIND_O)):
        arrive(at, (kind,))
        for l in range(2):
            ref = fin[kind]
            grad = ref[l].astype(F32).reshape(-1, ref.shape[-1])
            step(at, (l,), grad.T if kind == KIND_F else grad)
        done(at)
    arrive(0, (KIND_Q, KIND_K, KIND_V))
    for l in range(2):
        for at, kind in enumerate((KIND_Q, KIND_K, KIND_V)):
            grad = fin[kind][l].astype(F32).reshape(-1, D)
            step(0, (l, slice(None), slice(at * D, at * D + D)), grad)
    done(0)
    arrive(4, ())
    waits[1].wait()
    wide = masters[4].shape[2]
    rows = masters[4].shape[0]
    span = 128 // wide
    slot = lax.rem(f, span)
    for l in range(2):
        block = fvec[16 * l : 16 * l + 16]
        grad = block[:, :wide]
        for s in range(1, span):
            grad = jnp.where(slot == s, block[:, s * wide : s * wide + wide], grad)
        step(4, (slice(None), l), grad[:rows])
    done(4)
    for cp in leaving:
        cp.wait()


def fast_body(
    tokens, cotangent, tags, lengths, key_mask,
    master_qkv, master_out, master_in, master_feed_output, master_vec,
    first_qkv, first_out, first_in, first_ffo, first_vec,
    second_qkv, second_out, second_in, second_ffo, second_moment_vector,
    shards,
):
    S, D = tokens.shape[1:]
    FF = master_in.shape[2]
    levels = shards // 4
    rows, cols = sizes_of(shards, D, FF)
    meta_shape = (2 * S + 16, 128)
    by_row = lambda vectors: vectors.transpose(1, 0, 2)
    hbm = pl.BlockSpec(memory_space=pl.ANY)
    shape = jax.ShapeDtypeStruct
    V = pltpu.VMEM
    dma = pltpu.SemaphoreType.DMA
    w_tail = [(levels, 2, 2, 2, rows[k], cols[k]) for k in KINDS]
    masters = (master_qkv, master_out, master_in, master_feed_output, by_row(master_vec))
    firsts = (first_qkv, first_out, first_in, first_ffo, by_row(first_vec))
    seconds = (second_qkv, second_out, second_in, second_ffo, by_row(second_moment_vector))

    saved = call_kernel(
        lambda parts, *refs: forward_kernel(parts, levels, norm_epsilon, *refs),
        ForwardIn(
            tok=tokens,
            cot=cotangent,
            lengths=lengths,
            tags=tags,
            key_mask=key_mask,
            vectors=by_row(master_vec),
            masters=masters[:4],
        ),
        Saved(
            w_o=tuple(shape((2,) + tail, BF) for tail in w_tail),
            vec_o=shape((32, D), F32),
            meta_o=shape(meta_shape, BF),
            cot_o=shape((S, D), BF),
            y_o=shape((S, D), BF),
            at_o=shape((2, D, S), BF),
            q_o=shape((2, S, D), BF),
            k_o=shape((2, 2, S, D), BF),
            v_o=shape((2, 2, S, D), BF),
            lse_o=shape((2, D // 128, 8, S), F32),
            ct_o=shape((2, D, S), BF),
            ctp_o=shape((2, D, S), BF),
            n1_o=shape((2, S, D), F32),
            r1_o=shape((2, S, 128), F32),
            ht_o=shape((2, D, S), BF),
            g_o=shape((2, S, FF), BF),
            gp_o=shape((2, S, FF), BF),
            n2_o=shape((2, S, D), F32),
            r2_o=shape((2, S, 128), F32),
        ),
        ForwardScratch(
            w=tuple(V((2,) + tail, BF) for tail in w_tail),
            stages=tuple(V(m.shape, F32) for m in masters[:4]),
            vecg=V((4, 32, 128), BF),
            vecl=V((levels, 32, 128), BF),
            vec=V((32, D), F32),
            metab=V((2,) + meta_shape, BF),
            msel=V(meta_shape, BF),
            tokb=V((S, D), BF),
            cotb=V((S, D), BF),
            A32=V((S, D), F32),
            Ab=V((S, D), BF),
            ATp=V((D, S), BF),
            Q=V((S, D), BF),
            K=V((2, 2, S, D), BF),
            V=V((2, 2, S, D), BF),
            lse=V((D // 128, 8, S), F32),
            CT=V((D, S), BF),
            CTp=V((D, S), BF),
            C=V((S, D), BF),
            N1=V((S, D), F32),
            r1=V((S, 128), F32),
            H32=V((S, D), F32),
            Hb=V((S, D), BF),
            HTp=V((D, S), BF),
            G=V((S, FF), BF),
            Gp=V((S, FF), BF),
            N2=V((S, D), F32),
            r2=V((S, 128), F32),
            X=V((S, D), F32),
            Yb=V((S, D), BF),
            msem=dma((2, 4)),
            xsem=dma((4,)),
            osem=dma((48,)),
            gs=dma((16, levels + 4)),
            gr=dma((16, levels + 4)),
            vs=dma((levels + 2,)),
            vr=dma((levels + 2,)),
            xs=dma((3,)),
            xr=dma((3,)),
            ks=dma((2, 2)),
            kr=dma((2, 2)),
        ),
        ForwardIn(
            tok=hbm,
            cot=hbm,
            lengths=pl.BlockSpec(memory_space=pltpu.SMEM),
            tags=pl.BlockSpec(memory_space=pltpu.SMEM),
            key_mask=pl.BlockSpec(memory_space=pltpu.VMEM),
            vectors=pl.BlockSpec(memory_space=pltpu.VMEM),
            masters=(hbm,) * 4,
        ),
        collective_id=0,
        has_side_effects=True,
        vmem_limit_bytes=VMEM_BYTES,
    )

    tails = [(rows[k], cols[k]) for k in KINDS]
    tails[KIND_F] = (D // 2, FF // shards)
    each = lambda *lead: tuple(V(lead + tail, BF) for tail in tails)
    grads = call_kernel(
        lambda parts, *refs: backward_kernel(parts, levels, *refs),
        saved,
        BackwardOut(
            fin=tuple(shape((2, 2) + tail, BF) for tail in tails),
            vec_g=shape((32, 128), F32),
            yo=shape((S, D), BF),
            dxo=shape((S, D), BF),
        ),
        BackwardScratch(
            g=each(2, 2, levels, 2, 2),
            landing=each(levels, 2, 2),
            half=each(2, levels, 2),
            quarter=each(2, levels),
            level=each(2, levels - 1, 2),
            total=each(2, 2),
            w=tuple(V(tail, BF) for tail in w_tail),
            AT=V((D, S), BF),
            Q=V((S, D), BF),
            K=V((2, S, D), BF),
            V=V((2, S, D), BF),
            lse=V((D // 128, 8, S), F32),
            CT=V((D, S), BF),
            CTp=V((D, S), BF),
            N1=V((S, D), F32),
            r1=V((S, 128), F32),
            HT=V((D, S), BF),
            G=V((S, FF), BF),
            Gp=V((S, FF), BF),
            N2=V((S, D), F32),
            r2=V((S, 128), F32),
            vec=V((32, D), F32),
            msel=V(meta_shape, BF),
            cotb=V((S, D), BF),
            dy=V((S, D), F32),
            dpre=V((S, D), F32),
            dF=V((S, D), BF),
            dFT=V((D, S), BF),
            dU=V((S, FF), BF),
            dZ=V((S, D), BF),
            delta=V((D // 128, 8, S), F32),
            dQT=V((D, S), BF),
            dvb=V((S, D), BF),
            dkp=V((2, 2, D // 128, S, 128), BF),
            dvp=V((2, 2, D // 128, S, 128), BF),
            dkr=V((2, D // 128, S, 128), BF),
            dvr=V((2, D // 128, S, 128), BF),
            vg=V((32, D), F32),
            va=V((2, 4, 16, D), F32),
            vrecv=V((2, 3, 16, D), F32),
            vb=V((2, levels - 1, 16, 128), F32),
            vt=V((32, 128), F32),
            lsem=dma((2, 20)),
            ssem=dma((7,)),
            fsem=dma((12,)),
            gs=dma((12, levels + 5)),
            gr=dma((12, levels + 5)),
            xs=dma((3,)),
            xr=dma((3,)),
            ks=dma((2, 2, 2)),
            kr=dma((2, 2, 2)),
            vs=dma((2, levels + 2)),
            vr=dma((2, levels + 2)),
        ),
        hbm,
        collective_id=1,
        has_side_effects=True,
        vmem_limit_bytes=VMEM_BYTES,
    )

    rates = (
        matrix_rate * D ** (-0.5),
        matrix_rate * (D // 16) ** (-0.5),
        matrix_rate * D ** (-0.5),
        matrix_rate * (FF // 2) ** (-0.5),
        vector_rate,
    )
    decays = (weight_decay, weight_decay, weight_decay, weight_decay, 0.0)
    like = tuple(shape(p.shape, F32) for p in masters)
    new = call_kernel(
        lambda parts, *refs: update_kernel(parts, rates, decays, *refs),
        UpdateIn(fin=grads.fin, fvec=grads.vec_g, y=grads.yo, dx=grads.dxo, masters=masters, firsts=firsts, seconds=seconds),
        UpdateOut(
            out=shape(tokens.shape, BF),
            grad=shape(tokens.shape, F32),
            new_masters=like,
            new_firsts=like,
            new_seconds=like,
        ),
        UpdateScratch(
            inside=(
                tuple(V(g.shape, BF) for g in grads.fin),
                V((32, 128), F32),
                V((S, D), BF),
                V((S, D), BF),
                *(tuple(V(p.shape, F32) for p in masters) for _ in range(3)),
            ),
            wide=V((S, D), F32),
            isem=dma((24,)),
            osem=dma((17,)),
        ),
        hbm,
        vmem_limit_bytes=VMEM_BYTES,
    )
    trees = [(*tree[:4], by_row(tree[4])) for tree in (new.new_masters, new.new_firsts, new.new_seconds)]
    return (new.out, new.grad, *trees[0], *trees[1], *trees[2])


def solution(mesh):
    placed = (
        P("fsdp", "rep", None),
        P("fsdp", "rep", None),
        P("fsdp"),
        P("fsdp"),
        P("fsdp", None),
        P(None, "fsdp", None),
        P(None, "fsdp", None),
        P(None, "fsdp", None),
        P(None, "fsdp", None),
        P(None, None, "fsdp"),
        P(None, "fsdp", None),
        P(None, "fsdp", None),
        P(None, "fsdp", None),
        P(None, "fsdp", None),
        P(None, None, "fsdp"),
        P(None, "fsdp", None),
        P(None, "fsdp", None),
        P(None, "fsdp", None),
        P(None, "fsdp", None),
        P(None, None, "fsdp"),
    )
    shards = mesh.shape["fsdp"]

    def chosen(*args):
        tokens, master_in = args[0], args[7]
        width = tokens.shape[2]
        whole_tiles = shards * 32 == width and master_in.shape[2] == 4 * width
        if mesh.shape["rep"] == 2 and shards % 4 == 0 and whole_tiles:
            return fast_body(*args, shards)
        return body(*args)

    return jax.shard_map(
        chosen,
        mesh=mesh,
        in_specs=placed,
        out_specs=(
            P("fsdp", "rep", None),
            P("fsdp", "rep", None),
            P(None, "fsdp", None),
            P(None, "fsdp", None),
            P(None, "fsdp", None),
            P(None, "fsdp", None),
            P(None, None, "fsdp"),
            P(None, "fsdp", None),
            P(None, "fsdp", None),
            P(None, "fsdp", None),
            P(None, "fsdp", None),
            P(None, None, "fsdp"),
            P(None, "fsdp", None),
            P(None, "fsdp", None),
            P(None, "fsdp", None),
            P(None, "fsdp", None),
            P(None, None, "fsdp"),
        ),
        check_vma=False,
    )
```

```python
import functools
from types import SimpleNamespace
from typing import NamedTuple

import jax
import jax.numpy as jnp
from jax import lax
from jax.experimental import pallas as pl
from jax.experimental.pallas import tpu as pltpu
from jax.sharding import PartitionSpec as P

D = 512
H = 8
FF = 2048
STEP = 10


beta_decay = 0.5
epsilon_adam = 1e-08
weight_decay = 0.01
norm_epsilon = 1e-05
masked_score = -1000000000.0
vector_rate = 0.15
matrix_rate = 0.5


def layer_norm(pre_norm, gain_row, offset_row):
    centre_mean = jnp.mean(pre_norm, axis=-1, keepdims=True)
    centred = pre_norm - centre_mean
    variance = jnp.mean(centred * centred, axis=-1, keepdims=True)
    return centred * lax.rsqrt(variance + norm_epsilon) * gain_row + offset_row


def tanh_gelu_activation(inner_act):
    return jax.nn.gelu(inner_act, approximate=True)


def adamw(master, first, second, grad, rate, decay):
    first_new = beta_decay * first + (1.0 - beta_decay) * grad
    second_new = beta_decay * second + (1.0 - beta_decay) * grad * grad
    correction = 1.0 - beta_decay**STEP
    direction = first_new / correction / (jnp.sqrt(second_new / correction) + epsilon_adam)
    master_new = master - rate * (direction + decay * master)
    return (master_new, first_new, second_new)


def score_block(query_heads, key_heads, key_bias, score_scale):
    scores = jnp.einsum("qhd,khd->hqk", query_heads, key_heads, preferred_element_type=jnp.float32)
    return scores * score_scale + key_bias[None, None, :]


def forward_layer(input_rows, weights, tag_value, key_bias):
    w_qkv, w_out, w_in, w_ffo, vectors_low = weights
    vectors = vectors_low.astype(jnp.float32)
    model_width = w_out.shape[0]
    row_count = input_rows.shape[0]
    head_size = model_width // H
    score_scale = head_size ** (-0.5)
    direction = jnp.where(tag_value == 0, vectors[0], vectors[1])
    summed = input_rows + direction[None, :]
    summed_low = summed.astype(jnp.bfloat16)
    projected = jnp.dot(summed_low, w_qkv, preferred_element_type=jnp.float32)
    queries = (projected[:, :model_width] + vectors[2]).astype(jnp.bfloat16)
    keys_local = projected[:, model_width : 2 * model_width].astype(jnp.bfloat16)
    local_values = (projected[:, 2 * model_width :] + vectors[3]).astype(jnp.bfloat16)
    keys_all, values_all = (
        lax.all_gather(keys_local, "rep", axis=0, tiled=True),
        lax.all_gather(local_values, "rep", axis=0, tiled=True),
    )
    key_count = keys_all.shape[0]
    query_heads = queries.reshape(row_count, H, head_size)
    key_heads = keys_all.reshape(key_count, H, head_size)
    value_heads = values_all.reshape(key_count, H, head_size)
    scores = score_block(query_heads, key_heads, key_bias, score_scale)
    row_top = jnp.max(scores, axis=-1, keepdims=True)
    exponent_terms = jnp.exp(scores - row_top)
    totals = jnp.sum(exponent_terms, axis=-1, keepdims=True)
    soft_weights = exponent_terms / totals
    log_total = row_top + jnp.log(totals)
    context = jnp.einsum(
        "hqk,khd->qhd",
        soft_weights.astype(jnp.bfloat16),
        value_heads,
        preferred_element_type=jnp.float32,
    )
    context_low = context.reshape(row_count, model_width).astype(jnp.bfloat16)
    branch = jnp.dot(context_low, w_out, preferred_element_type=jnp.float32) + vectors[4]
    hidden, norm_first = jax.vjp(layer_norm, summed + branch, vectors[5], vectors[6])
    hidden_low = hidden.astype(jnp.bfloat16)
    inner_act = jnp.dot(hidden_low, w_in, preferred_element_type=jnp.float32) + vectors[
        10:
    ].reshape(-1)
    activated, gelu_pull = jax.vjp(tanh_gelu_activation, inner_act)
    activated_low = activated.astype(jnp.bfloat16)
    feed_out = jnp.dot(activated_low, w_ffo, preferred_element_type=jnp.float32) + vectors[7]
    result, norm_second = jax.vjp(layer_norm, hidden + feed_out, vectors[8], vectors[9])
    saved_state = (
        summed_low,
        query_heads,
        key_heads,
        value_heads,
        log_total,
        context_low,
        norm_first,
        hidden_low,
        gelu_pull,
        activated_low,
        norm_second,
    )
    return (result, saved_state)


def attention_grads(
    query_heads, key_heads, value_heads, log_total, context_heads, key_bias, score_scale
):
    row_count = query_heads.shape[0]
    model_width = query_heads.shape[1] * query_heads.shape[2]
    scores = score_block(query_heads, key_heads, key_bias, score_scale)
    soft_weights = jnp.exp(scores - log_total)
    grad_soft = jnp.einsum(
        "qhd,khd->hqk", context_heads, value_heads, preferred_element_type=jnp.float32
    )
    row_inner = jnp.sum(soft_weights * grad_soft, axis=-1, keepdims=True)
    grad_scores = (soft_weights * (grad_soft - row_inner) * score_scale).astype(jnp.bfloat16)
    grad_queries = jnp.einsum(
        "hqk,khd->qhd", grad_scores, key_heads, preferred_element_type=jnp.float32
    ).reshape(row_count, model_width)
    key_terms = jnp.einsum(
        "hqk,qhd->khd", grad_scores, query_heads, preferred_element_type=jnp.float32
    ).reshape(-1, model_width)
    value_terms = jnp.einsum(
        "hqk,qhd->khd",
        soft_weights.astype(jnp.bfloat16),
        context_heads,
        preferred_element_type=jnp.float32,
    ).reshape(-1, model_width)
    grad_keys, grad_values = (
        lax.psum_scatter(
            key_terms.astype(jnp.bfloat16), "rep", scatter_dimension=0, tiled=True
        ).astype(jnp.float32),
        lax.psum_scatter(
            value_terms.astype(jnp.bfloat16), "rep", scatter_dimension=0, tiled=True
        ).astype(jnp.float32),
    )
    return (grad_queries, grad_keys, grad_values)


def backward_layer(grad_result, saved_state, weights, tag_value, key_bias):
    w_qkv, w_out, w_in, w_ffo, vectors_low = weights
    (
        summed_low,
        query_heads,
        key_heads,
        value_heads,
        log_total,
        context_low,
        norm_first,
        hidden_low,
        gelu_pull,
        activated_low,
        norm_second,
    ) = saved_state
    model_width = w_out.shape[0]
    row_count = summed_low.shape[0]
    head_size = model_width // H
    score_scale = head_size ** (-0.5)
    grad_pre_two, grad_gain_two, grad_shift_two = norm_second(grad_result)
    grad_feed = grad_pre_two.astype(jnp.bfloat16)
    grad_bias_feed = jnp.sum(grad_feed.astype(jnp.float32), axis=0)
    grad_ffo = jnp.einsum("tf,td->fd", activated_low, grad_feed, preferred_element_type=jnp.float32)
    grad_activated = jnp.einsum("td,fd->tf", grad_feed, w_ffo, preferred_element_type=jnp.float32)
    grad_inner = gelu_pull(grad_activated)[0].astype(jnp.bfloat16)
    grad_bias_inner = jnp.sum(grad_inner.astype(jnp.float32), axis=0)
    grad_in = jnp.einsum("td,tf->df", hidden_low, grad_inner, preferred_element_type=jnp.float32)
    grad_hidden = grad_pre_two + jnp.einsum(
        "tf,df->td", grad_inner, w_in, preferred_element_type=jnp.float32
    )
    grad_pre_one, grad_gain_one, grad_shift_one = norm_first(grad_hidden)
    grad_branch = grad_pre_one.astype(jnp.bfloat16)
    grad_bias_out = jnp.sum(grad_branch.astype(jnp.float32), axis=0)
    grad_out_matrix = jnp.einsum(
        "te,td->ed", context_low, grad_branch, preferred_element_type=jnp.float32
    )
    grad_context = jnp.einsum(
        "td,ed->te", grad_branch, w_out, preferred_element_type=jnp.float32
    ).astype(jnp.bfloat16)
    context_heads = grad_context.reshape(row_count, H, head_size)
    grad_queries, grad_keys, grad_values = attention_grads(
        query_heads, key_heads, value_heads, log_total, context_heads, key_bias, score_scale
    )
    grad_joined = jnp.concatenate(
        [
            grad_queries.astype(jnp.bfloat16),
            grad_keys.astype(jnp.bfloat16),
            grad_values.astype(jnp.bfloat16),
        ],
        axis=1,
    )
    grad_qkv = jnp.einsum("td,te->de", summed_low, grad_joined, preferred_element_type=jnp.float32)
    grad_summed = grad_pre_one + jnp.einsum(
        "te,de->td", grad_joined, w_qkv, preferred_element_type=jnp.float32
    )
    column_sums = jnp.sum(grad_joined.astype(jnp.float32), axis=0)
    grad_direction = jnp.sum(grad_summed, axis=0)
    zero_row = jnp.zeros_like(grad_direction)
    grad_rows = jnp.stack(
        [
            jnp.where(tag_value == 0, grad_direction, zero_row),
            jnp.where(tag_value == 1, grad_direction, zero_row),
            column_sums[:model_width],
            column_sums[2 * model_width :],
            grad_bias_out,
            grad_gain_one,
            grad_shift_one,
            grad_bias_feed,
            grad_gain_two,
            grad_shift_two,
        ],
        axis=0,
    )
    grad_vectors = jnp.concatenate([grad_rows, grad_bias_inner.reshape(-1, model_width)], axis=0)
    return (grad_summed, (grad_qkv, grad_out_matrix, grad_in, grad_ffo, grad_vectors))


def reduce_layer(grads):
    shards = (
        lax.psum_scatter(grads[0], "fsdp", scatter_dimension=0, tiled=True),
        lax.psum_scatter(grads[1], "fsdp", scatter_dimension=0, tiled=True),
        lax.psum_scatter(grads[2], "fsdp", scatter_dimension=0, tiled=True),
        lax.psum_scatter(grads[3], "fsdp", scatter_dimension=0, tiled=True),
        lax.psum_scatter(grads[4], "fsdp", scatter_dimension=1, tiled=True),
    )
    return (
        lax.psum(shards[0].astype(jnp.bfloat16), "rep").astype(jnp.float32),
        lax.psum(shards[1].astype(jnp.bfloat16), "rep").astype(jnp.float32),
        lax.psum(shards[2].astype(jnp.bfloat16), "rep").astype(jnp.float32),
        lax.psum(shards[3].astype(jnp.bfloat16), "rep").astype(jnp.float32),
        lax.psum(shards[4].astype(jnp.bfloat16), "rep").astype(jnp.float32),
    )


def body(
    tokens,
    cotangent,
    tags,
    lengths,
    key_mask,
    master_qkv,
    master_out,
    master_in,
    master_feed_output,
    master_vec,
    first_qkv,
    first_out,
    first_in,
    first_ffo,
    first_vec,
    second_qkv,
    second_out,
    second_in,
    second_ffo,
    second_moment_vector,
):
    row_count = tokens.shape[1]
    key_count = key_mask.shape[1]
    start_row = lax.axis_index("rep") * row_count
    query_pos = start_row + jnp.arange(row_count, dtype=jnp.int32)
    key_pos = jnp.arange(key_count, dtype=jnp.int32)
    seq_length = lengths[0]
    tag_value = tags[0]
    key_valid = (key_pos < seq_length) & ((key_mask[0] == 1) | (key_pos == 0))
    key_bias = jnp.where(key_valid, 0.0, masked_score).astype(jnp.float32)
    query_valid = (query_pos < seq_length).astype(jnp.float32)
    masters = (master_qkv, master_out, master_in, master_feed_output, master_vec)
    firsts = (first_qkv, first_out, first_in, first_ffo, first_vec)
    seconds = (second_qkv, second_out, second_in, second_ffo, second_moment_vector)
    shared = (
        lax.all_gather(master_qkv[0].astype(jnp.bfloat16), "fsdp", axis=0, tiled=True),
        lax.all_gather(master_out[0].astype(jnp.bfloat16), "fsdp", axis=0, tiled=True),
        lax.all_gather(master_in[0].astype(jnp.bfloat16), "fsdp", axis=0, tiled=True),
        lax.all_gather(master_feed_output[0].astype(jnp.bfloat16), "fsdp", axis=0, tiled=True),
        lax.all_gather(master_vec[0].astype(jnp.bfloat16), "fsdp", axis=1, tiled=True),
    )
    shared_out, saved_shared = forward_layer(
        tokens[0].astype(jnp.float32), shared, tag_value, key_bias
    )
    unique = (
        lax.all_gather(master_qkv[1].astype(jnp.bfloat16), "fsdp", axis=0, tiled=True),
        lax.all_gather(master_out[1].astype(jnp.bfloat16), "fsdp", axis=0, tiled=True),
        lax.all_gather(master_in[1].astype(jnp.bfloat16), "fsdp", axis=0, tiled=True),
        lax.all_gather(master_feed_output[1].astype(jnp.bfloat16), "fsdp", axis=0, tiled=True),
        lax.all_gather(master_vec[1].astype(jnp.bfloat16), "fsdp", axis=1, tiled=True),
    )
    final_out, saved_unique = forward_layer(shared_out, unique, tag_value, key_bias)
    grad_final = cotangent[0].astype(jnp.float32) * query_valid[:, None]
    unique_back = (
        lax.all_gather(master_qkv[1].astype(jnp.bfloat16), "fsdp", axis=0, tiled=True),
        lax.all_gather(master_out[1].astype(jnp.bfloat16), "fsdp", axis=0, tiled=True),
        lax.all_gather(master_in[1].astype(jnp.bfloat16), "fsdp", axis=0, tiled=True),
        lax.all_gather(master_feed_output[1].astype(jnp.bfloat16), "fsdp", axis=0, tiled=True),
        lax.all_gather(master_vec[1].astype(jnp.bfloat16), "fsdp", axis=1, tiled=True),
    )
    grad_middle, unique_grads = backward_layer(
        grad_final, saved_unique, unique_back, tag_value, key_bias
    )
    reduced_unique = reduce_layer(unique_grads)
    grad_inputs, shared_grads = backward_layer(
        grad_middle, saved_shared, shared, tag_value, key_bias
    )
    reduced_shared = reduce_layer(shared_grads)
    rates = (
        matrix_rate * D ** (-0.5),
        matrix_rate * (D // 16) ** (-0.5),
        matrix_rate * D ** (-0.5),
        matrix_rate * (FF // 2) ** (-0.5),
        vector_rate,
    )
    decays = (weight_decay, weight_decay, weight_decay, weight_decay, 0.0)
    updated = []
    for kind_index in range(5):
        grad_stack = jnp.stack([reduced_shared[kind_index], reduced_unique[kind_index]], axis=0)
        updated.append(
            adamw(
                masters[kind_index],
                firsts[kind_index],
                seconds[kind_index],
                grad_stack,
                rates[kind_index],
                decays[kind_index],
            )
        )
    return (
        final_out.astype(jnp.bfloat16)[None],
        grad_inputs[None],
        updated[0][0],
        updated[1][0],
        updated[2][0],
        updated[3][0],
        updated[4][0],
        updated[0][1],
        updated[1][1],
        updated[2][1],
        updated[3][1],
        updated[4][1],
        updated[0][2],
        updated[1][2],
        updated[2][2],
        updated[3][2],
        updated[4][2],
    )


BF = jnp.bfloat16
F32 = jnp.float32
MESH = pl.DeviceIdType.MESH
KIND_K, KIND_V, KIND_Q, KIND_O, KIND_I, KIND_F = KINDS = tuple(range(6))
VMEM_BYTES = 60 << 20
FORWARD_SPLIT = (1, 1, 1, 2, 1, 1, 1, 1, 5, 5, 1, 1, 1, 1, 5, 5)
BACKWARD_SPLIT = (1, 2, 1, 2, 5, 1, 5, 2, 5, 1, 1, 1, 5, 2, 5, 5)
FORWARD_TURNS = (
    (1, 2, 0, 3, 4, 1, 2, 5),
    (3, 0, 6, 1, 2, 4, 3, 0, 7, 5, 0, 1, 8),
    (6, 2, 9, 1),
    (4, 7, 2, 3),
    (10, 5),
    (6, 11),
    (3, 8, 12),
    (),
    (4, 9, 10, 13, 7),
    (11, 14),
    (4,),
    (),
    (5, 8, 12, 9, 13, 5, 15),
    (6, 9, 8, 10, 6, 7, 14, 11, 12, 13, 7),
    (10,),
    (),
    (),
    (15, 10),
    (),
    (),
    (11, 14),
    (12,),
    (11, 14),
    (12,),
    (13,),
    (),
    (15, 13),
    (15,),
    (),
)
COTANGENT_AT = 2
BACKWARD_TURNS = (
    (),
    (),
    (0, 1),
    (),
    (),
    (2, 0, 3),
    (),
    (1,),
    (2, 4),
    (3, 4, 0),
    (1,),
    (),
    (2, 4),
    (5,),
    (7, 3, 0, 6),
    (),
    (5, 1, 16, 7),
    (2, 6, 4, 16),
    (0, 8, 3, 5, 7, 9),
    (4,),
    (16, 1, 6, 8, 0),
    (5, 7, 10, 11, 9, 2, 16, 1),
    (),
    (10,),
    (3, 12, 11),
    (8, 12, 2, 5, 6, 9),
    (7, 16),
    (3, 12, 10),
    (8, 5, 11),
    (13, 6, 9),
    (7, 12, 14, 10, 15),
    (13,),
    (8, 17, 14, 11, 15, 12, 17, 9, 10, 13, 14, 11, 15, 17, 9, 10, 14, 13, 11, 17, 15, 14, 13, 17, 15, 13),
)


def nt_dot(left, right):
    return lax.dot_general(left, right, (((1,), (1,)), ((), ())), preferred_element_type=F32)


def nn_dot(left, right):
    return jnp.dot(left, right, preferred_element_type=F32)


def remote(src, dst, send_sem, recv_sem, device):
    return pltpu.make_async_remote_copy(
        src_ref=src,
        dst_ref=dst,
        send_sem=send_sem,
        recv_sem=recv_sem,
        device_id=device,
        device_id_type=MESH,
    )


class ForwardIn(NamedTuple):
    tok: object
    cot: object
    lengths: object
    tags: object
    key_mask: object
    vectors: object
    masters: object


class Saved(NamedTuple):
    w_o: object
    vec_o: object
    meta_o: object
    cot_o: object
    y_o: object
    at_o: object
    q_o: object
    k_o: object
    v_o: object
    lse_o: object
    ct_o: object
    ctp_o: object
    n1_o: object
    r1_o: object
    ht_o: object
    g_o: object
    gp_o: object
    n2_o: object
    r2_o: object


class ForwardScratch(NamedTuple):
    w: object
    stages: object
    vecg: object
    vecl: object
    vec: object
    metab: object
    msel: object
    tokb: object
    cotb: object
    A32: object
    Ab: object
    ATp: object
    Q: object
    K: object
    V: object
    lse: object
    CT: object
    CTp: object
    C: object
    N1: object
    r1: object
    H32: object
    Hb: object
    HTp: object
    G: object
    Gp: object
    N2: object
    r2: object
    X: object
    Yb: object
    msem: object
    xsem: object
    osem: object
    gs: object
    gr: object
    vs: object
    vr: object
    xs: object
    xr: object
    ks: object
    kr: object


class BackwardOut(NamedTuple):
    fin: object
    vec_g: object
    yo: object
    dxo: object


class BackwardScratch(NamedTuple):
    g: object
    landing: object
    half: object
    quarter: object
    level: object
    total: object
    w: object
    AT: object
    Q: object
    K: object
    V: object
    lse: object
    CT: object
    CTp: object
    N1: object
    r1: object
    HT: object
    G: object
    Gp: object
    N2: object
    r2: object
    vec: object
    msel: object
    cotb: object
    dy: object
    dpre: object
    dF: object
    dFT: object
    dU: object
    dZ: object
    delta: object
    dQT: object
    dvb: object
    dkp: object
    dvp: object
    dkr: object
    dvr: object
    vg: object
    va: object
    vrecv: object
    vb: object
    vt: object
    lsem: object
    ssem: object
    fsem: object
    gs: object
    gr: object
    xs: object
    xr: object
    ks: object
    kr: object
    vs: object
    vr: object


class UpdateIn(NamedTuple):
    fin: object
    fvec: object
    y: object
    dx: object
    masters: object
    firsts: object
    seconds: object


class UpdateOut(NamedTuple):
    out: object
    grad: object
    new_masters: object
    new_firsts: object
    new_seconds: object


class UpdateScratch(NamedTuple):
    inside: object
    wide: object
    isem: object
    osem: object


def named(parts, refs):
    fields, at = {}, 0
    for part in parts:
        leaves, tree = jax.tree.flatten(part)
        fields.update(tree.unflatten(refs[at : at + len(leaves)])._asdict())
        at += len(leaves)
    return SimpleNamespace(**fields)


def call_kernel(kernel, args, outs, scratch, spec, **options):
    leaves, _ = jax.tree.flatten(args)
    out_leaves, out_tree = jax.tree.flatten(outs)
    parts = (args, outs) if scratch is None else (args, outs, scratch)
    empty = jax.tree.map(lambda leaf: 0, parts)
    results = pl.pallas_call(
        functools.partial(kernel, empty),
        out_shape=out_leaves,
        in_specs=jax.tree.leaves(spec) if isinstance(spec, tuple) else [spec] * len(leaves),
        out_specs=[pl.BlockSpec(memory_space=pl.ANY)] * len(out_leaves),
        scratch_shapes=() if scratch is None else jax.tree.leaves(scratch),
        compiler_params=pltpu.CompilerParams(**options),
    )(*leaves)
    return out_tree.unflatten(results)


class Place:
    def __init__(self):
        self.r = lax.axis_index("rep")
        self.f = lax.axis_index("fsdp")
        self.z = lax.div(self.f, 4)
        self.y = lax.rem(lax.div(self.f, 2), 2)
        self.c = lax.rem(self.f, 2)
        self.xn = (1 - self.r, self.f)
        self.yn = (self.r, self.f + 2 - 4 * self.y)
        self.cn = (self.r, self.f + 1 - 2 * self.c)
        self.dn = (1 - self.r, self.f + 1 - 2 * self.c)
        self.en = (self.r, self.f + 3 - 4 * self.y - 2 * self.c)

    def zn(self, step, levels):
        other = lax.rem(self.z + step, levels)
        return other, (self.r, other * 4 + 2 * self.y + self.c)


def parity_rows(rows, shards):
    blocks = rows.reshape(shards // 2, 2, rows.shape[0] // shards, rows.shape[1])
    half = rows.shape[0] // 2
    return blocks[:, 0].reshape(half, rows.shape[1]), blocks[:, 1].reshape(half, rows.shape[1])


def halves(cut, levels):
    return pl.ds(0, cut), pl.ds(cut, levels - cut)


def go_or_stay(stays, stay, go):
    @pl.when(stays)
    def _():
        stay()

    @pl.when(jnp.logical_not(stays))
    def _():
        go()


def lane_masks():
    lane = lax.broadcasted_iota(jnp.int32, (16, 128), 1)
    low = (lane < 64).astype(F32)
    spots = (lax.rem(lane, 64) == 0).astype(F32)
    return low[:1].astype(BF), (1.0 - low[:1]).astype(BF), spots[:1].astype(BF)


def sizes_of(mesh_n, width, inner):
    shard = width // mesh_n
    rows = [shard // 2] * 6
    rows[KIND_F] = inner // mesh_n // 2
    cols = [width] * 6
    cols[KIND_I] = inner
    return rows, cols


def forward_kernel(parts, levels, eps, *refs):
    R = named(parts, refs)
    me = Place()
    r, f, z, y, c = me.r, me.f, me.z, me.y, me.c
    shards = levels * 4
    S, D = R.A32.shape
    FF = R.G.shape[1]
    source = ((0, D), (0, 2 * D), (0, 0), (1, 0), (2, 0), (3, 0))

    half_loads = {}
    for l in range(2):
        for at, (master, stage) in enumerate(zip(R.masters, R.stages)):
            cp = pltpu.make_async_copy(master.at[l], stage.at[l], R.msem.at[l, at])
            cp.start()
            half_loads[(l, at)] = cp
    barrier = pltpu.get_barrier_semaphore()
    peers = [me.zn(s, levels)[1] for s in range(1, levels)] + [me.xn, me.yn, me.cn, me.dn, me.en]
    for peer in peers:
        pl.semaphore_signal(barrier, inc=1, device_id=peer, device_id_type=MESH)
    pl.semaphore_wait(barrier, len(peers))

    chunks = []
    for l in range(2):
        for kind in KINDS:
            parts = 2 if kind in (KIND_I, KIND_F) else 1
            span = R.w[kind].shape[-1] // parts
            chunks += [(kind, l, slice(part * span, part * span + span)) for part in range(parts)]
    gs, gr = R.gs, R.gr
    pending = []

    def start(cp):
        cp.start()
        pending.append(cp)
        return cp

    out_copies = {}
    out_at = [0]

    def out(ref, dst, view=None):
        cp = pltpu.make_async_copy(ref if view is None else view, dst, R.osem.at[out_at[0]])
        out_at[0] += 1
        cp.start()
        out_copies[(id(ref), view is not None and out_at[0])] = cp

    def settle(ref):
        if (id(ref), False) in out_copies:
            out_copies.pop((id(ref), False)).wait()

    loaded = set()
    stage_copies = {}

    def g_z(i):
        kind, l, cols = chunks[i]
        w = R.w[kind]
        at, offset = source[kind]
        if (l, at) not in loaded:
            half_loads[(l, at)].wait()
            loaded.add((l, at))
        rows = w.shape[5]
        w[l, z, y, c, r, :, cols] = R.stages[at][l, pl.ds(r * rows, rows), offset + cols.start : offset + cols.stop].astype(BF)
        cps = []
        for s in range(1, levels):
            _, dev = me.zn(s, levels)
            spot = w.at[l, z, y, c, r, :, cols]
            cps.append(start(remote(spot, spot, gs.at[i, s - 1], gr.at[i, s - 1], dev)))
        stage_copies[i] = cps

    def g_1(i):
        kind, l, cols = chunks[i]
        w = R.w[kind]
        for cp in stage_copies[i]:
            cp.wait_recv()
        first, second = halves(FORWARD_SPLIT[i], levels)
        a, b = w.at[l, first, y, c, r, :, cols], w.at[l, second, y, c, r, :, cols]
        stage_copies[i] = [
            start(remote(a, a, gs.at[i, levels - 1], gr.at[i, levels - 1], me.xn)),
            start(remote(b, b, gs.at[i, levels], gr.at[i, levels], me.yn)),
        ]

    def g_2(i):
        kind, l, cols = chunks[i]
        w = R.w[kind]
        for cp in stage_copies[i]:
            cp.wait_recv()
        first, second = halves(FORWARD_SPLIT[i], levels)
        a, b = w.at[l, first, y, c, :, :, cols], w.at[l, second, :, c, r, :, cols]
        stage_copies[i] = [
            start(remote(a, a, gs.at[i, levels + 1], gr.at[i, levels + 1], me.yn)),
            start(remote(b, b, gs.at[i, levels + 2], gr.at[i, levels + 2], me.xn)),
        ]

    def g_core(i):
        kind, l, cols = chunks[i]
        w = R.w[kind]
        for cp in stage_copies[i]:
            cp.wait_recv()
        a = w.at[l, :, :, c, :, :, cols]
        stage_copies[i] = [start(remote(a, a, gs.at[i, levels + 3], gr.at[i, levels + 3], me.cn))]

    def h_z(i):
        kind, l, cols = chunks[i]
        w = R.w[kind]
        at, offset = source[kind]
        if (l, at) not in loaded:
            half_loads[(l, at)].wait()
            loaded.add((l, at))
        whole = R.stages[at][l][:, offset + cols.start : offset + cols.stop].astype(BF)
        w[l, z, y, c, :, :, cols] = whole.reshape(2, whole.shape[0] // 2, whole.shape[1])
        spot = w.at[l, z, y, c, :, :, cols]
        stage_copies[i] = [
            start(remote(spot, spot, gs.at[i, s], gr.at[i, s], me.zn(s, levels)[1])) for s in range(1, levels)
        ]

    def h_y(i):
        kind, l, cols = chunks[i]
        w = R.w[kind]
        for cp in stage_copies[i]:
            cp.wait_recv()
        spot = w.at[l, :, y, c, :, :, cols]
        stage_copies[i] = [start(remote(spot, spot, gs.at[i, 0], gr.at[i, 0], me.yn))]

    def g_ready(i):
        kind, l, cols = chunks[i]
        for cp in stage_copies.pop(i):
            cp.wait_recv()
        waiting.remove(i)
        if not any(chunks[k][:2] == (kind, l) for k in waiting):
            out(R.w[kind], R.w_o[kind].at[l], R.w[kind].at[l])

    steps = (g_z, g_1, g_2, g_core, g_ready)
    other_steps = (h_z, h_y, g_core, g_ready)
    reached = [0] * len(chunks)
    waiting = list(range(len(chunks)))
    turns = iter(FORWARD_TURNS)

    def turn():
        for i in next(turns):
            (other_steps if FORWARD_SPLIT[i] == 5 else steps)[reached[i]](i)
            reached[i] += 1

    steps[0](0)
    reached[0] = 1
    tok_far = remote(R.tok.at[0], R.tokb, R.xs.at[1], R.xr.at[1], me.dn)
    tok_near = pltpu.make_async_copy(R.tok.at[0], R.tokb, R.xsem.at[2])
    stays = c == r

    go_or_stay(stays, tok_near.start, tok_far.start)
    length = R.lengths[0]
    keys = R.key_mask[...]
    key_pos = lax.broadcasted_iota(jnp.int32, keys.shape, 1)
    valid = key_pos < length
    bias = jnp.where(valid & ((keys == 1) | (key_pos == 0)), 0.0, masked_score)
    place = lax.broadcasted_iota(jnp.int32, (128, 2 * S), 0)
    columns = jnp.where(lax.rem(place, 64) == 0, bias, 0.0) + jnp.where((place == 1) & valid, 1.0, 0.0)
    R.metab[0, : 2 * S] = columns.T.astype(BF)
    R.metab[0, 2 * S :] = jnp.full((16, 128), R.tags[0].astype(F32)).astype(BF)
    meta_cp = start(remote(R.metab.at[0], R.metab.at[1], R.xs.at[0], R.xr.at[0], me.cn))
    wide = R.vectors.shape[2]
    lane = lax.broadcasted_iota(jnp.int32, (R.vectors.shape[0], 128), 1)
    spot = R.vecg.at[2 * y + c]
    spot[...] = jnp.zeros((32, 128), BF)
    for l in range(2):
        block = jnp.concatenate([R.vectors[:, l]] * (128 // wide), axis=1)
        block = jnp.where(lax.div(lane, wide) == lax.rem(f, 128 // wide), block, 0.0)
        block = jnp.concatenate([block, jnp.zeros((16 - block.shape[0], 128), F32)], axis=0)
        spot[16 * l : 16 * l + 16] = block.astype(BF)
    vec_cps = [start(remote(spot, spot, R.vs.at[at], R.vr.at[at], dev)) for at, dev in enumerate((me.yn, me.cn, me.en))]
    for cp in vec_cps:
        cp.wait_recv()
    spot = R.vecl.at[z]
    spot[...] = jnp.sum(R.vecg[...].astype(F32), axis=0).astype(BF)
    vec_cps = []
    for s in range(1, levels):
        vec_cps.append(start(remote(spot, spot, R.vs.at[2 + s], R.vr.at[2 + s], me.zn(s, levels)[1])))
    turn()
    meta_cp.wait_recv()
    for cp in vec_cps:
        cp.wait_recv()
    keep = stays.astype(F32)
    msel = R.msel
    msel[...] = (R.metab[0].astype(F32) * keep + R.metab[1].astype(F32) * (1.0 - keep)).astype(BF)
    vec = R.vec
    for zz in range(levels):
        vec[:, 128 * zz : 128 * zz + 128] = R.vecl[zz].astype(F32)
    tag_row = msel[2 * S : 2 * S + 16].astype(F32)[:1]
    tag_row = jnp.concatenate([tag_row] * (D // 128), axis=1)
    low, high, spots = lane_masks()

    go_or_stay(stays, tok_near.wait, tok_far.wait)
    cot_far = remote(R.cot.at[0], R.cotb, R.xs.at[2], R.xr.at[2], me.dn)
    cot_near = pltpu.make_async_copy(R.cot.at[0], R.cotb, R.xsem.at[3])

    T = 256
    for l in range(2):
        e = lambda row: vec[16 * l + row : 16 * l + row + 1, :]
        direction = e(0) * (1.0 - tag_row) + e(1) * tag_row
        if l == 1:
            turn()
        A32, Ab, Q, K, V, CT = R.A32, R.Ab, R.Q, R.K, R.V, R.CT
        x_in = R.tokb if l == 0 else R.X
        summed = x_in[...].astype(F32) + direction
        A32[...] = summed
        Ab[...] = summed.astype(BF)
        at = Ab[...].T
        even, odd = parity_rows(at, shards)
        settle(R.ATp)
        R.ATp[: D // 2] = even
        R.ATp[D // 2 :] = odd
        out(R.ATp, R.at_o.at[l])

        def weight(kind, lo=0, hi=None):
            w = R.w[kind]
            hi = w.shape[-1] if hi is None else hi
            value = w[l, :, :, :, :, :, lo:hi]
            return value.reshape(-1, hi - lo)

        turn()
        K[l, c] = nn_dot(Ab[...], weight(KIND_K)).astype(BF)
        k_cp = start(remote(K.at[l, c], K.at[l, c], R.ks.at[l, 0], R.kr.at[l, 0], me.cn))
        turn()
        V[l, c] = (nn_dot(Ab[...], weight(KIND_V)) + e(3)).astype(BF)
        v_cp = start(remote(V.at[l, c], V.at[l, c], R.ks.at[l, 1], R.kr.at[l, 1], me.cn))
        turn()
        settle(R.Q)
        q = (nn_dot(Ab[...], weight(KIND_Q)) + e(2)).astype(BF)
        Q[...] = (q.astype(F32) * 0.125).astype(BF)
        out(R.Q, R.q_o.at[l])
        turn()
        k_cp.wait_recv()
        v_cp.wait_recv()
        out(K, R.k_o.at[l], K.at[l])
        out(V, R.v_o.at[l], V.at[l])
        lse = R.lse
        settle(R.lse)
        settle(R.CT)
        bias_rows = msel[: 2 * S]

        def pair(j):
            sl = slice(j * 128, j * 128 + 128)
            k2 = K[l, :, :, sl].reshape(2 * S, 128)
            v2t = V[l, :, :, sl].reshape(2 * S, 128).T
            q2 = Q[:, sl]
            scores = []
            for mine, other in ((low, high), (high, low)):
                scores.append(nt_dot(k2 * mine + bias_rows * other, q2 * mine + spots * other))
            for h, st in enumerate(scores):
                top = jnp.max(st, axis=0, keepdims=True)
                p = jnp.exp(st - top)
                total = jnp.sum(p, axis=0, keepdims=True)
                ctx = nn_dot(v2t, p.astype(BF))[64 * h : 64 * h + 64]
                rows = slice(j * 128 + 64 * h, j * 128 + 64 * h + 64)
                CT[rows] = (ctx * (1.0 / total)).astype(BF)
                lse[j, h : h + 1] = top + jnp.log(total)

        for j in range(D // 128):
            turn()
            if l == 1 and j == COTANGENT_AT:
                go_or_stay(stays, cot_near.start, cot_far.start)
            pair(j)
        turn()
        out(R.lse, R.lse_o.at[l])
        out(R.CT, R.ct_o.at[l])
        even, odd = parity_rows(CT[...], shards)
        settle(R.CTp)
        R.CTp[: D // 2] = even
        R.CTp[D // 2 :] = odd
        out(R.CTp, R.ctp_o.at[l])
        R.C[...] = CT[...].T
        settle(R.N1)
        settle(R.r1)

        def norm_one(t, carry):
            rows = pl.ds(pl.multiple_of(t * T, T), T)
            pre = A32[rows] + nn_dot(R.C[rows], weight(KIND_O)) + e(4)
            mean = jnp.mean(pre, axis=-1, keepdims=True)
            centred = pre - mean
            rstd = lax.rsqrt(jnp.mean(centred * centred, axis=-1, keepdims=True) + eps)
            n1 = centred * rstd
            hidden = n1 * e(5) + e(6)
            R.N1[rows] = n1
            R.r1[rows] = jnp.broadcast_to(rstd, (T, 128))
            R.H32[rows] = hidden
            R.Hb[rows] = hidden.astype(BF)
            return carry

        turn()
        lax.fori_loop(0, S // T, norm_one, 0)
        out(R.N1, R.n1_o.at[l])
        out(R.r1, R.r1_o.at[l])
        even, odd = parity_rows(R.Hb[...].T, shards)
        settle(R.HTp)
        R.HTp[: D // 2] = even
        R.HTp[D // 2 :] = odd
        out(R.HTp, R.ht_o.at[l])
        settle(R.G)
        settle(R.Gp)

        def inner(b):
            u = nn_dot(R.Hb[...], weight(KIND_I, b * D, b * D + D)) + e(10 + b)
            u2 = u * u
            th = jnp.tanh(u * (0.7978845608028654 + 0.035677408136300125 * u2))
            half = 0.5 + 0.5 * th
            slope = 0.7978845608028654 + 0.10703222440890038 * u2
            R.G[:, b * D : b * D + D] = (u * half).astype(BF)
            R.Gp[:, b * D : b * D + D] = (half + 0.5 * u * (1.0 - th * th) * slope).astype(BF)

        for b in range(FF // D):
            if b % 2 == 0:
                turn()
            inner(b)
        out(R.G, R.g_o.at[l])
        out(R.Gp, R.gp_o.at[l])
        turn()
        settle(R.N2)
        settle(R.r2)

        def norm_two(t, carry):
            rows = pl.ds(pl.multiple_of(t * T, T), T)
            pre = R.H32[rows] + nn_dot(R.G[rows], weight(KIND_F)) + e(7)
            mean = jnp.mean(pre, axis=-1, keepdims=True)
            centred = pre - mean
            rstd = lax.rsqrt(jnp.mean(centred * centred, axis=-1, keepdims=True) + eps)
            n2 = centred * rstd
            R.N2[rows] = n2
            R.r2[rows] = jnp.broadcast_to(rstd, (T, 128))
            R.X[rows] = n2 * e(8) + e(9)
            return carry

        lax.fori_loop(0, S // T, norm_two, 0)
        out(R.N2, R.n2_o.at[l])
        out(R.r2, R.r2_o.at[l])

    turn()
    R.Yb[...] = R.X[...].astype(BF)
    out(R.Yb, R.y_o)
    out(vec, R.vec_o)
    out(msel, R.meta_o)
    go_or_stay(stays, cot_near.wait, cot_far.wait_recv)
    out(R.cotb, R.cot_o)
    for cp in out_copies.values():
        cp.wait()
    for cp in pending:
        cp.wait_send()
    go_or_stay(stays, lambda: None, cot_far.wait_send)


def backward_kernel(parts, levels, *refs):
    R = named(parts, refs)
    me = Place()
    r, f, z, y, c = me.r, me.f, me.z, me.y, me.c
    shards = levels * 4
    S, D = R.dy.shape
    FF = R.G.shape[1]
    saved = list(zip(R.w, R.w_o)) + [
        (R.AT, R.at_o), (R.Q, R.q_o), (R.K, R.k_o), (R.V, R.v_o), (R.lse, R.lse_o), (R.CT, R.ct_o), (R.CTp, R.ctp_o),
        (R.N1, R.n1_o), (R.r1, R.r1_o), (R.HT, R.ht_o), (R.G, R.g_o), (R.Gp, R.gp_o), (R.N2, R.n2_o), (R.r2, R.r2_o),
    ]
    order = {id(ref): at for at, (ref, _) in enumerate(saved)}
    loads = {}

    def load(ref, l):
        at = order[id(ref)]
        cp = pltpu.make_async_copy(saved[at][1].at[l], ref, R.lsem.at[l, at])
        cp.start()
        loads[id(ref)] = cp

    def use(ref):
        if id(ref) in loads:
            loads.pop(id(ref)).wait()
        return ref

    small = []
    for at, (dst, src) in enumerate(((R.vec, R.vec_o), (R.msel, R.meta_o), (R.cotb, R.cot_o))):
        cp = pltpu.make_async_copy(src, dst, R.ssem.at[at])
        cp.start()
        small.append(cp)
    wk, wv, wq, wo, wi, wf = R.w
    for ref in (R.N2, R.r2, R.G):
        load(ref, 1)
    later = (wf, R.Gp, R.HT, wi, R.N1, R.r1, R.CTp, wo, R.CT, R.K, R.V, R.Q, R.lse, R.AT, wq, wk, wv)

    barrier = pltpu.get_barrier_semaphore()
    peers = [me.zn(s, levels)[1] for s in range(1, levels)] + [me.xn, me.yn, me.cn, me.dn]
    for peer in peers:
        pl.semaphore_signal(barrier, inc=1, device_id=peer, device_id_type=MESH)

    pending = []

    def start(cp):
        cp.start()
        pending.append(cp)
        return cp

    stays = c == r
    y_far = remote(R.y_o, R.yo, R.xs.at[0], R.xr.at[0], me.dn)
    y_near = pltpu.make_async_copy(R.y_o, R.yo, R.ssem.at[3])
    dx_cps = []


    gs, gr = R.gs, R.gr
    chunks = []
    for l in (1, 0):
        for kind in (KIND_F, KIND_I, KIND_O, KIND_Q, KIND_K, KIND_V):
            rows, cols = R.g[kind].shape[-2:]
            if kind == KIND_F:
                spans = [(slice(0, rows // 2), slice(0, cols)), (slice(rows // 2, rows), slice(0, cols))]
            elif kind == KIND_I:
                spans = [(slice(0, rows), slice(0, cols // 2)), (slice(0, rows), slice(cols // 2, cols))]
            else:
                spans = [(slice(0, rows), slice(0, cols))]
            chunks += [(kind, l, *span) for span in spans]
    chunks += [(None, 1), (None, 0)]
    flight = {}
    stage = {}
    fin_copies = []

    def rs_core(i):
        kind, l, rs, cs = chunks[i]
        g = R.g[kind]
        spot = g.at[0, 0, :, :, :, rs, cs] if l == 1 else R.landing[kind].at[:, :, :, rs, cs]
        mine = g.at[l, 1 - c, :, :, :, rs, cs]
        flight[i] = [start(remote(mine, spot, gs.at[i, 0], gr.at[i, 0], me.cn))]

    def add_landed(i):
        kind, l, rs, cs = chunks[i]
        g = R.g[kind]
        landed = g[0, 0, :, :, :, rs, cs] if l == 1 else R.landing[kind][:, :, :, rs, cs]
        g[l, c, :, :, :, rs, cs] = g[l, c, :, :, :, rs, cs] + landed

    def rs_1(i):
        kind, l, rs, cs = chunks[i]
        g, half = R.g[kind], R.half[kind]
        first, second = halves(BACKWARD_SPLIT[i], levels)
        add_landed(i)
        a, b = g.at[l, c, first, 1 - y, :, rs, cs], g.at[l, c, second, :, 1 - r, rs, cs]
        flight[i] = [
            start(remote(a, half.at[l, first, :, rs, cs], gs.at[i, 1], gr.at[i, 1], me.yn)),
            start(remote(b, half.at[l, second, :, rs, cs], gs.at[i, 2], gr.at[i, 2], me.xn)),
        ]

    def rs_2(i):
        kind, l, rs, cs = chunks[i]
        g, half, quarter = R.g[kind], R.half[kind], R.quarter[kind]
        first, second = halves(BACKWARD_SPLIT[i], levels)
        g[l, c, first, y, :, rs, cs] = g[l, c, first, y, :, rs, cs] + half[l, first, :, rs, cs]
        g[l, c, second, :, r, rs, cs] = g[l, c, second, :, r, rs, cs] + half[l, second, :, rs, cs]
        a, b = g.at[l, c, first, y, 1 - r, rs, cs], g.at[l, c, second, 1 - y, r, rs, cs]
        flight[i] = [
            start(remote(a, quarter.at[l, first, rs, cs], gs.at[i, 3], gr.at[i, 3], me.xn)),
            start(remote(b, quarter.at[l, second, rs, cs], gs.at[i, 4], gr.at[i, 4], me.yn)),
        ]

    def rs_3(i):
        kind, l, rs, cs = chunks[i]
        g, quarter = R.g[kind], R.quarter[kind]
        first, second = halves(BACKWARD_SPLIT[i], levels)
        g[l, c, first, y, r, rs, cs] = g[l, c, first, y, r, rs, cs] + quarter[l, first, rs, cs]
        g[l, c, second, y, r, rs, cs] = g[l, c, second, y, r, rs, cs] + quarter[l, second, rs, cs]
        flight[i] = []
        for s in range(1, levels):
            there, dev = me.zn(s, levels)
            mine, spot = g.at[l, c, there, y, r, rs, cs], R.level[kind].at[l, s - 1, 0, rs, cs]
            flight[i].append(start(remote(mine, spot, gs.at[i, 4 + s], gr.at[i, 4 + s], dev)))

    def rs_4(i):
        kind, l, rs, cs = chunks[i]
        total = R.g[kind][l, c, z, y, r, rs, cs].astype(F32)
        for s in range(levels - 1):
            total = total + R.level[kind][l, s, 0, rs, cs].astype(F32)
        R.total[kind][l, r, rs, cs] = total.astype(BF)
        spot = R.total[kind].at[l, r, rs, cs]
        flight[i] = [start(remote(spot, spot, gs.at[i, 4 + levels], gr.at[i, 4 + levels], me.xn))]

    def rs_5(i):
        kind, l, rs, cs = chunks[i]
        cp = pltpu.make_async_copy(R.total[kind].at[l, :, rs, cs], R.fin[kind].at[l, :, rs, cs], R.fsem.at[i])
        cp.start()
        fin_copies.append(cp)

    vg, va, vb, vt = R.vg, R.va, R.vb, R.vt

    def vec_hop(at, device):
        def step(i):
            l = chunks[i][1]
            if at == 0:
                va[l, 0] = vg[16 * l : 16 * l + 16]
            else:
                va[l, at] = va[l, at - 1] + R.vrecv[l, at - 1]
            flight[i] = [start(remote(va.at[l, at], R.vrecv.at[l, at], R.vs.at[l, at], R.vr.at[l, at], device))]

        return step

    def vec_level(i):
        l = chunks[i][1]
        va[l, 3] = va[l, 2] + R.vrecv[l, 2]
        flight[i] = []
        for s in range(1, levels):
            there, dev = me.zn(s, levels)
            lanes = pl.ds(pl.multiple_of(there * 128, 128), 128)
            flight[i].append(start(remote(va.at[l, 3, :, lanes], vb.at[l, s - 1], R.vs.at[l, 2 + s], R.vr.at[l, 2 + s], dev)))

    def vec_end(i):
        l = chunks[i][1]
        total = va[l, 3, :, pl.ds(pl.multiple_of(z * 128, 128), 128)]
        for s in range(levels - 1):
            total = total + vb[l, s]
        vt[16 * l : 16 * l + 16] = total

    def hs_y(i):
        kind, l, rs, cs = chunks[i]
        add_landed(i)
        mine, spot = R.g[kind].at[l, c, :, 1 - y, :, rs, cs], R.half[kind].at[l, :, :, rs, cs]
        flight[i] = [start(remote(mine, spot, gs.at[i, levels], gr.at[i, levels], me.yn))]

    def hs_z(i):
        kind, l, rs, cs = chunks[i]
        g = R.g[kind]
        g[l, c, :, y, :, rs, cs] = g[l, c, :, y, :, rs, cs] + R.half[kind][l, :, :, rs, cs]
        flight[i] = []
        for s in range(1, levels):
            there, dev = me.zn(s, levels)
            mine, spot = g.at[l, c, there, y, :, rs, cs], R.level[kind].at[l, s - 1, :, rs, cs]
            flight[i].append(start(remote(mine, spot, gs.at[i, s], gr.at[i, s], dev)))

    def hs_x(i):
        kind, l, rs, cs = chunks[i]
        g = R.g[kind]
        whole = g[l, c, z, y, :, rs, cs].astype(F32)
        for s in range(levels - 1):
            whole = whole + R.level[kind][l, s, :, rs, cs].astype(F32)
        g[l, c, z, y, :, rs, cs] = whole.astype(BF)
        mine, spot = g.at[l, c, z, y, :, rs, cs], R.quarter[kind].at[l, pl.ds(0, 2), rs, cs]
        sems = gs.at[i, levels + 1], gr.at[i, levels + 1]
        flight[i] = [start(remote(mine, spot, *sems, me.xn))]

    def hs_end(i):
        kind, l, rs, cs = chunks[i]
        R.total[kind][l, :, rs, cs] = R.g[kind][l, c, z, y, :, rs, cs] + R.quarter[kind][l, :2, rs, cs]
        rs_5(i)

    other_steps = (rs_core, hs_y, hs_z, hs_x, hs_end)
    matrix_steps = (rs_core, rs_1, rs_2, rs_3, rs_4, rs_5)
    vec_steps = (vec_hop(0, me.cn), vec_hop(1, me.xn), vec_hop(2, me.yn), vec_level, vec_end)
    turns = iter(BACKWARD_TURNS)

    def turn():
        for i in next(turns):
            at = stage.get(i, 0)
            for cp in flight.pop(i, ()):
                cp.wait_recv()
            known = vec_steps if chunks[i][0] is None else other_steps if BACKWARD_SPLIT[i] == 5 else matrix_steps
            known[at](i)
            stage[i] = at + 1

    for cp in small:
        cp.wait()
    vec, msel = R.vec, R.msel
    tag_row = msel[2 * S : 2 * S + 16].astype(F32)[:1]
    tag_row = jnp.concatenate([tag_row] * (D // 128), axis=1)
    low, high, spots = lane_masks()
    low32 = low.astype(F32)
    vg[...] = jnp.zeros_like(vg)
    R.dy[...] = R.cotb[...].astype(F32) * msel[pl.ds(c * S, S)][:, 1:2].astype(F32)
    T = 256
    dy, dpre, dF, dFT, dU, dZ = R.dy, R.dpre, R.dF, R.dFT, R.dU, R.dZ

    def fold(value):
        return jnp.sum(value.reshape(value.shape[0] // 8, 8, value.shape[1]), axis=0)

    zero8 = jnp.zeros((8, D), F32)

    for l in (1, 0):
        base = 16 * l
        e = lambda row: vec[base + row : base + row + 1, :]

        def put(row, value):
            vg[base + row : base + row + 1, :] = value

        def weight(kind):
            w = R.w[kind]
            return w[...].reshape(-1, w.shape[-1])

        turn()
        N2, r2 = use(R.N2), use(R.r2)
        if l == 1:
            for ref in later:
                load(ref, 1)

        def norm_two(t, carry):
            s7, s8, s9 = carry
            rows = pl.ds(pl.multiple_of(t * T, T), T)
            g, n = dy[rows], N2[rows]
            dn = g * e(8)
            m1 = jnp.mean(dn, axis=-1, keepdims=True)
            m2 = jnp.mean(dn * n, axis=-1, keepdims=True)
            d = r2[rows][:, :1] * (dn - m1 - n * m2)
            dpre[rows] = d
            db = d.astype(BF)
            dF[rows] = db
            dFT[:, rows] = db.T
            return s7 + fold(db.astype(F32)), s8 + fold(g * n), s9 + fold(g)

        s7, s8, s9 = lax.fori_loop(0, S // T, norm_two, (zero8, zero8, zero8))
        put(7, jnp.sum(s7, axis=0, keepdims=True))
        put(8, jnp.sum(s8, axis=0, keepdims=True))
        put(9, jnp.sum(s9, axis=0, keepdims=True))
        if l == 1:
            pl.semaphore_wait(barrier, len(peers))
            go_or_stay(stays, y_near.start, y_far.start)
        turn()
        G = use(R.G)
        gf = R.g[KIND_F]
        piece = 2 * FF // shards

        def grad_f(t, carry):
            d = nn_dot(dFT[...], G[:, pl.ds(pl.multiple_of(t * piece, piece), piece)]).astype(BF)
            zz, yy = lax.div(t, 2), lax.rem(t, 2)
            half = piece // 2
            gf[l, 0, zz, yy] = d[:, :half].reshape(2, D // 2, half)
            gf[l, 1, zz, yy] = d[:, half:].reshape(2, D // 2, half)
            return carry

        lax.fori_loop(0, shards // 2, grad_f, 0)
        if l == 1:
            for ref in (R.N2, R.r2, R.G):
                load(ref, 0)
        use(R.w[KIND_F])
        Gp = use(R.Gp)

        def grad_inner(b):
            wf = R.w[KIND_F]
            quarter = wf[b * (levels // (FF // D)) : (b + 1) * (levels // (FF // D))].reshape(D, D)
            cols = slice(b * D, b * D + D)
            du = (nt_dot(dF[...], quarter) * Gp[:, cols].astype(F32)).astype(BF)
            dU[:, cols] = du
            put(10 + b, jnp.sum(fold(du.astype(F32)), axis=0, keepdims=True))

        for b in range(FF // D):
            if b % 2 == 0:
                turn()
            grad_inner(b)
        turn()
        if l == 1:
            load(R.w[KIND_F], 0)
            load(R.Gp, 0)
        HT = use(R.HT)
        gi = R.g[KIND_I]
        rows_i = 2 * R.g[KIND_I].shape[-2]

        for b in range(FF // D):
            d = nn_dot(HT[...], dU[:, b * D : b * D + D]).astype(BF)
            for cc in range(2):
                part = d[cc * (D // 2) : (cc + 1) * (D // 2)]
                gi[l, cc, :, :, :, :, b * D : b * D + D] = part.reshape(levels, 2, 2, rows_i // 2, D)
        if l == 1:
            load(R.HT, 0)
        use(R.w[KIND_I])
        N1, r1 = use(R.N1), use(R.r1)

        def norm_one(t, carry):
            s4, s5, s6 = carry
            rows = pl.ds(pl.multiple_of(t * T, T), T)
            g = dpre[rows] + nt_dot(dU[rows], weight(KIND_I))
            n = N1[rows]
            dn = g * e(5)
            m1 = jnp.mean(dn, axis=-1, keepdims=True)
            m2 = jnp.mean(dn * n, axis=-1, keepdims=True)
            d = r1[rows][:, :1] * (dn - m1 - n * m2)
            dy[rows] = d
            db = d.astype(BF)
            dZ[rows] = db
            return s4 + fold(db.astype(F32)), s5 + fold(g * n), s6 + fold(g)

        turn()
        sums = lax.fori_loop(0, S // T // 2, norm_one, (zero8, zero8, zero8))
        turn()
        s4, s5, s6 = lax.fori_loop(S // T // 2, S // T, norm_one, sums)
        put(4, jnp.sum(s4, axis=0, keepdims=True))
        put(5, jnp.sum(s5, axis=0, keepdims=True))
        put(6, jnp.sum(s6, axis=0, keepdims=True))
        turn()
        if l == 1:
            for ref in (R.w[KIND_I], R.N1, R.r1):
                load(ref, 0)
        CTp = use(R.CTp)
        go = R.g[KIND_O]

        def store(ref, value):
            for cc in range(2):
                ref[l, cc] = value[cc * (D // 2) : (cc + 1) * (D // 2)].reshape(ref.shape[2:])

        store(R.g[KIND_O], nn_dot(CTp[...], dZ[...]).astype(BF))
        use(R.w[KIND_O])
        dF[...] = nt_dot(dZ[...], weight(KIND_O)).astype(BF)
        CT = use(R.CT)
        dct = dF[...].T
        prod = dct.astype(F32) * CT[...].astype(F32)
        prod = jnp.sum(prod.reshape(D // 64, 64, S), axis=1)
        for j in range(D // 128):
            R.delta[j, :2] = prod[2 * j : 2 * j + 2]
        if l == 1:
            for ref in (R.CTp, R.w[KIND_O], R.CT):
                load(ref, 0)
        K, V, Q, lse = use(R.K), use(R.V), use(R.Q), use(R.lse)
        delta, dC, dQT = R.delta, dF, R.dQT
        dkp, dvp, dkr, dvr = R.dkp, R.dvp, R.dkr, R.dvr
        bias_rows = msel[: 2 * S]

        def pair(j):
            sl = slice(j * 128, j * 128 + 128)
            k2 = K[:, :, sl].reshape(2 * S, 128)
            v2 = V[:, :, sl].reshape(2 * S, 128)
            k2t = k2.T
            q2 = Q[:, sl]
            dc2 = dC[:, sl]
            dk_sum, dv_sum = None, None
            for h in range(2):
                mine, other = (low, high) if h == 0 else (high, low)
                mine32 = low32 if h == 0 else 1.0 - low32
                kh = k2 * mine + bias_rows * other
                vh = v2 * mine
                qh = q2 * mine + spots * other
                dk_h, dv_h = None, None
                for part in range(S // 256):
                    cols = slice(part * 256, part * 256 + 256)
                    st = nt_dot(kh, qh[cols])
                    p = jnp.exp(st - lse[j, h : h + 1, cols])
                    dp = nt_dot(vh, dc2[cols])
                    ds = (p * (dp - delta[j, h : h + 1, cols])).astype(BF)
                    pb = p.astype(BF)
                    dv = nn_dot(pb, dc2[cols])
                    dk = nn_dot(ds, q2[cols])
                    dv_h = dv if dv_h is None else dv_h + dv
                    dk_h = dk if dk_h is None else dk_h + dk
                    dq = nn_dot(k2t, ds)[64 * h : 64 * h + 64]
                    rows = slice(j * 128 + 64 * h, j * 128 + 64 * h + 64)
                    dQT[rows, cols] = (dq * 0.125).astype(BF)
                dk_sum = dk_h * mine32 if dk_sum is None else dk_sum + dk_h * mine32
                dv_sum = dv_h * mine32 if dv_sum is None else dv_sum + dv_h * mine32
            dkp[l, :, j] = dk_sum.astype(BF).reshape(2, S, 128)
            dvp[l, :, j] = dv_sum.astype(BF).reshape(2, S, 128)

        pairs = D // 128
        half_pairs = pairs // 2
        kv_cps = []
        for j in range(pairs):
            turn()
            pair(j)
            if (j + 1) % half_pairs == 0:
                part = j // half_pairs
                js = pl.ds(part * half_pairs, half_pairs)
                for at, (mine, theirs) in enumerate(((dkp, dkr), (dvp, dvr))):
                    sems = R.ks.at[l, part, at], R.kr.at[l, part, at]
                    kv_cps.append(start(remote(mine.at[l, 1 - c, js], theirs.at[l, js], *sems, me.cn)))
        if l == 1:
            for ref in (R.K, R.V, R.Q, R.lse):
                load(ref, 0)
        turn()
        AT = use(R.AT)
        dqb = dZ
        dqb[...] = dQT[...].T
        store(R.g[KIND_Q], nn_dot(AT[...], dqb[...]).astype(BF))
        turn()
        for cp in kv_cps:
            cp.wait_recv()
        dkb, dvb = dFT, R.dvb
        for j in range(pairs):
            dkb[:, 128 * j : 128 * j + 128] = dkp[l, c, j] + dkr[l, j]
            dvb[:, 128 * j : 128 * j + 128] = dvp[l, c, j] + dvr[l, j]
        store(R.g[KIND_K], nn_dot(AT[...], dkb[...]).astype(BF))
        store(R.g[KIND_V], nn_dot(AT[...], dvb[...]).astype(BF))
        if l == 1:
            load(R.AT, 0)
        use(R.w[KIND_Q])
        use(R.w[KIND_K])
        use(R.w[KIND_V])

        def last(t, carry):
            s0, s2, s3 = carry
            rows = pl.ds(pl.multiple_of(t * T, T), T)
            d = dy[rows] + nt_dot(dqb[rows], weight(KIND_Q)) + nt_dot(dkb[rows], weight(KIND_K)) + nt_dot(dvb[rows], weight(KIND_V))
            dy[rows] = d
            return s0 + fold(d), s2 + fold(dqb[rows].astype(F32)), s3 + fold(dvb[rows].astype(F32))

        sums = (zero8, zero8, zero8)
        for part in range(2):
            turn()
            sums = lax.fori_loop(part * (S // T // 2), (part + 1) * (S // T // 2), last, sums)
            if l == 0:
                half = pl.ds(part * (S // 2), S // 2)
                R.cotb[half] = dy[half].astype(BF)
                far = remote(R.cotb.at[half], R.dxo.at[half], R.xs.at[1 + part], R.xr.at[1 + part], me.dn)
                near = pltpu.make_async_copy(R.cotb.at[half], R.dxo.at[half], R.ssem.at[4 + part])
                dx_cps.append((far, near))
                go_or_stay(stays, near.start, far.start)
        s0, s2, s3 = sums
        s0 = jnp.sum(s0, axis=0, keepdims=True)
        put(0, s0 * (1.0 - tag_row))
        put(1, s0 * tag_row)
        put(2, jnp.sum(s2, axis=0, keepdims=True))
        put(3, jnp.sum(s3, axis=0, keepdims=True))
        if l == 1:
            for ref in (R.w[KIND_Q], R.w[KIND_K], R.w[KIND_V]):
                load(ref, 0)

    turn()
    vec_out = pltpu.make_async_copy(vt, R.vec_g, R.ssem.at[6])
    vec_out.start()
    for cp in fin_copies:
        cp.wait()
    vec_out.wait()
    for cp in pending:
        cp.wait_send()

    for far, near in dx_cps:
        go_or_stay(stays, near.wait, far.wait)
    go_or_stay(stays, y_near.wait, y_far.wait)


def update_kernel(parts, rates, decays, *refs):
    R = named(parts, refs)
    f = lax.axis_index("fsdp")
    sources, _ = jax.tree.flatten((R.fin, R.fvec, R.y, R.dx, R.masters, R.firsts, R.seconds))
    places, tree = jax.tree.flatten(R.inside)
    copies = [pltpu.make_async_copy(s, p, R.isem.at[at]) for at, (s, p) in enumerate(zip(sources, places))]
    fin, fvec, y, dx, masters, firsts, seconds = R.inside
    waits = tree.unflatten(copies)
    waits[3].start()
    waits[2].start()
    for at, kinds in ((2, (KIND_I,)), (3, (KIND_F,)), (1, (KIND_O,)), (0, (KIND_Q, KIND_K, KIND_V)), (4, ())):
        for cp in [waits[0][k] for k in kinds] + [w[at] for w in waits[4:]]:
            cp.start()
    waits[1].start()
    finals = (R.new_masters, R.new_firsts, R.new_seconds)
    leaving = []

    def leave(src, dst):
        cp = pltpu.make_async_copy(src, dst, R.osem.at[len(leaving)])
        cp.start()
        leaving.append(cp)

    def arrive(at, kinds):
        for cp in [waits[0][k] for k in kinds] + [w[at] for w in waits[4:]]:
            cp.wait()

    def step(at, where, grad):
        new = adamw(masters[at][where], firsts[at][where], seconds[at][where], grad, rates[at], decays[at])
        for refs, value in zip((masters, firsts, seconds), new):
            refs[at][where] = value

    def done(at):
        for kept, final in zip((masters, firsts, seconds), finals):
            leave(kept[at], final[at])

    waits[3].wait()
    R.wide[...] = dx[...].astype(F32)
    leave(R.wide, R.grad.at[0])
    waits[2].wait()
    leave(y, R.out.at[0])
    D = dx.shape[1]
    for at, kind in ((2, KIND_I), (3, KIND_F), (1, KIND_O)):
        arrive(at, (kind,))
        for l in range(2):
            ref = fin[kind]
            grad = ref[l].astype(F32).reshape(-1, ref.shape[-1])
            step(at, (l,), grad.T if kind == KIND_F else grad)
        done(at)
    arrive(0, (KIND_Q, KIND_K, KIND_V))
    for l in range(2):
        for at, kind in enumerate((KIND_Q, KIND_K, KIND_V)):
            grad = fin[kind][l].astype(F32).reshape(-1, D)
            step(0, (l, slice(None), slice(at * D, at * D + D)), grad)
    done(0)
    arrive(4, ())
    waits[1].wait()
    wide = masters[4].shape[2]
    rows = masters[4].shape[0]
    span = 128 // wide
    slot = lax.rem(f, span)
    for l in range(2):
        block = fvec[16 * l : 16 * l + 16]
        grad = block[:, :wide]
        for s in range(1, span):
            grad = jnp.where(slot == s, block[:, s * wide : s * wide + wide], grad)
        step(4, (slice(None), l), grad[:rows])
    done(4)
    for cp in leaving:
        cp.wait()


def fast_body(
    tokens, cotangent, tags, lengths, key_mask,
    master_qkv, master_out, master_in, master_feed_output, master_vec,
    first_qkv, first_out, first_in, first_ffo, first_vec,
    second_qkv, second_out, second_in, second_ffo, second_moment_vector,
    shards,
):
    S, D = tokens.shape[1:]
    FF = master_in.shape[2]
    levels = shards // 4
    rows, cols = sizes_of(shards, D, FF)
    meta_shape = (2 * S + 16, 128)
    by_row = lambda vectors: vectors.transpose(1, 0, 2)
    hbm = pl.BlockSpec(memory_space=pl.ANY)
    shape = jax.ShapeDtypeStruct
    V = pltpu.VMEM
    dma = pltpu.SemaphoreType.DMA
    w_tail = [(levels, 2, 2, 2, rows[k], cols[k]) for k in KINDS]
    masters = (master_qkv, master_out, master_in, master_feed_output, by_row(master_vec))
    firsts = (first_qkv, first_out, first_in, first_ffo, by_row(first_vec))
    seconds = (second_qkv, second_out, second_in, second_ffo, by_row(second_moment_vector))

    saved = call_kernel(
        lambda parts, *refs: forward_kernel(parts, levels, norm_epsilon, *refs),
        ForwardIn(
            tok=tokens,
            cot=cotangent,
            lengths=lengths,
            tags=tags,
            key_mask=key_mask,
            vectors=by_row(master_vec),
            masters=masters[:4],
        ),
        Saved(
            w_o=tuple(shape((2,) + tail, BF) for tail in w_tail),
            vec_o=shape((32, D), F32),
            meta_o=shape(meta_shape, BF),
            cot_o=shape((S, D), BF),
            y_o=shape((S, D), BF),
            at_o=shape((2, D, S), BF),
            q_o=shape((2, S, D), BF),
            k_o=shape((2, 2, S, D), BF),
            v_o=shape((2, 2, S, D), BF),
            lse_o=shape((2, D // 128, 8, S), F32),
            ct_o=shape((2, D, S), BF),
            ctp_o=shape((2, D, S), BF),
            n1_o=shape((2, S, D), F32),
            r1_o=shape((2, S, 128), F32),
            ht_o=shape((2, D, S), BF),
            g_o=shape((2, S, FF), BF),
            gp_o=shape((2, S, FF), BF),
            n2_o=shape((2, S, D), F32),
            r2_o=shape((2, S, 128), F32),
        ),
        ForwardScratch(
            w=tuple(V((2,) + tail, BF) for tail in w_tail),
            stages=tuple(V(m.shape, F32) for m in masters[:4]),
            vecg=V((4, 32, 128), BF),
            vecl=V((levels, 32, 128), BF),
            vec=V((32, D), F32),
            metab=V((2,) + meta_shape, BF),
            msel=V(meta_shape, BF),
            tokb=V((S, D), BF),
            cotb=V((S, D), BF),
            A32=V((S, D), F32),
            Ab=V((S, D), BF),
            ATp=V((D, S), BF),
            Q=V((S, D), BF),
            K=V((2, 2, S, D), BF),
            V=V((2, 2, S, D), BF),
            lse=V((D // 128, 8, S), F32),
            CT=V((D, S), BF),
            CTp=V((D, S), BF),
            C=V((S, D), BF),
            N1=V((S, D), F32),
            r1=V((S, 128), F32),
            H32=V((S, D), F32),
            Hb=V((S, D), BF),
            HTp=V((D, S), BF),
            G=V((S, FF), BF),
            Gp=V((S, FF), BF),
            N2=V((S, D), F32),
            r2=V((S, 128), F32),
            X=V((S, D), F32),
            Yb=V((S, D), BF),
            msem=dma((2, 4)),
            xsem=dma((4,)),
            osem=dma((48,)),
            gs=dma((16, levels + 4)),
            gr=dma((16, levels + 4)),
            vs=dma((levels + 2,)),
            vr=dma((levels + 2,)),
            xs=dma((3,)),
            xr=dma((3,)),
            ks=dma((2, 2)),
            kr=dma((2, 2)),
        ),
        ForwardIn(
            tok=hbm,
            cot=hbm,
            lengths=pl.BlockSpec(memory_space=pltpu.SMEM),
            tags=pl.BlockSpec(memory_space=pltpu.SMEM),
            key_mask=pl.BlockSpec(memory_space=pltpu.VMEM),
            vectors=pl.BlockSpec(memory_space=pltpu.VMEM),
            masters=(hbm,) * 4,
        ),
        collective_id=0,
        has_side_effects=True,
        vmem_limit_bytes=VMEM_BYTES,
    )

    tails = [(rows[k], cols[k]) for k in KINDS]
    tails[KIND_F] = (D // 2, FF // shards)
    each = lambda *lead: tuple(V(lead + tail, BF) for tail in tails)
    grads = call_kernel(
        lambda parts, *refs: backward_kernel(parts, levels, *refs),
        saved,
        BackwardOut(
            fin=tuple(shape((2, 2) + tail, BF) for tail in tails),
            vec_g=shape((32, 128), F32),
            yo=shape((S, D), BF),
            dxo=shape((S, D), BF),
        ),
        BackwardScratch(
            g=each(2, 2, levels, 2, 2),
            landing=each(levels, 2, 2),
            half=each(2, levels, 2),
            quarter=each(2, levels),
            level=each(2, levels - 1, 2),
            total=each(2, 2),
            w=tuple(V(tail, BF) for tail in w_tail),
            AT=V((D, S), BF),
            Q=V((S, D), BF),
            K=V((2, S, D), BF),
            V=V((2, S, D), BF),
            lse=V((D // 128, 8, S), F32),
            CT=V((D, S), BF),
            CTp=V((D, S), BF),
            N1=V((S, D), F32),
            r1=V((S, 128), F32),
            HT=V((D, S), BF),
            G=V((S, FF), BF),
            Gp=V((S, FF), BF),
            N2=V((S, D), F32),
            r2=V((S, 128), F32),
            vec=V((32, D), F32),
            msel=V(meta_shape, BF),
            cotb=V((S, D), BF),
            dy=V((S, D), F32),
            dpre=V((S, D), F32),
            dF=V((S, D), BF),
            dFT=V((D, S), BF),
            dU=V((S, FF), BF),
            dZ=V((S, D), BF),
            delta=V((D // 128, 8, S), F32),
            dQT=V((D, S), BF),
            dvb=V((S, D), BF),
            dkp=V((2, 2, D // 128, S, 128), BF),
            dvp=V((2, 2, D // 128, S, 128), BF),
            dkr=V((2, D // 128, S, 128), BF),
            dvr=V((2, D // 128, S, 128), BF),
            vg=V((32, D), F32),
            va=V((2, 4, 16, D), F32),
            vrecv=V((2, 3, 16, D), F32),
            vb=V((2, levels - 1, 16, 128), F32),
            vt=V((32, 128), F32),
            lsem=dma((2, 20)),
            ssem=dma((7,)),
            fsem=dma((16,)),
            gs=dma((16, levels + 5)),
            gr=dma((16, levels + 5)),
            xs=dma((3,)),
            xr=dma((3,)),
            ks=dma((2, 2, 2)),
            kr=dma((2, 2, 2)),
            vs=dma((2, levels + 2)),
            vr=dma((2, levels + 2)),
        ),
        hbm,
        collective_id=1,
        has_side_effects=True,
        vmem_limit_bytes=VMEM_BYTES,
    )

    rates = (
        matrix_rate * D ** (-0.5),
        matrix_rate * (D // 16) ** (-0.5),
        matrix_rate * D ** (-0.5),
        matrix_rate * (FF // 2) ** (-0.5),
        vector_rate,
    )
    decays = (weight_decay, weight_decay, weight_decay, weight_decay, 0.0)
    like = tuple(shape(p.shape, F32) for p in masters)
    new = call_kernel(
        lambda parts, *refs: update_kernel(parts, rates, decays, *refs),
        UpdateIn(fin=grads.fin, fvec=grads.vec_g, y=grads.yo, dx=grads.dxo, masters=masters, firsts=firsts, seconds=seconds),
        UpdateOut(
            out=shape(tokens.shape, BF),
            grad=shape(tokens.shape, F32),
            new_masters=like,
            new_firsts=like,
            new_seconds=like,
        ),
        UpdateScratch(
            inside=(
                tuple(V(g.shape, BF) for g in grads.fin),
                V((32, 128), F32),
                V((S, D), BF),
                V((S, D), BF),
                *(tuple(V(p.shape, F32) for p in masters) for _ in range(3)),
            ),
            wide=V((S, D), F32),
            isem=dma((24,)),
            osem=dma((17,)),
        ),
        hbm,
        vmem_limit_bytes=VMEM_BYTES,
    )
    trees = [(*tree[:4], by_row(tree[4])) for tree in (new.new_masters, new.new_firsts, new.new_seconds)]
    return (new.out, new.grad, *trees[0], *trees[1], *trees[2])


def solution(mesh):
    placed = (
        P("fsdp", "rep", None),
        P("fsdp", "rep", None),
        P("fsdp"),
        P("fsdp"),
        P("fsdp", None),
        P(None, "fsdp", None),
        P(None, "fsdp", None),
        P(None, "fsdp", None),
        P(None, "fsdp", None),
        P(None, None, "fsdp"),
        P(None, "fsdp", None),
        P(None, "fsdp", None),
        P(None, "fsdp", None),
        P(None, "fsdp", None),
        P(None, None, "fsdp"),
        P(None, "fsdp", None),
        P(None, "fsdp", None),
        P(None, "fsdp", None),
        P(None, "fsdp", None),
        P(None, None, "fsdp"),
    )
    shards = mesh.shape["fsdp"]

    def chosen(*args):
        tokens, master_in = args[0], args[7]
        width = tokens.shape[2]
        whole_tiles = shards * 32 == width and master_in.shape[2] == 4 * width
        if mesh.shape["rep"] == 2 and shards % 4 == 0 and whole_tiles:
            return fast_body(*args, shards)
        return body(*args)

    return jax.shard_map(
        chosen,
        mesh=mesh,
        in_specs=placed,
        out_specs=(
            P("fsdp", "rep", None),
            P("fsdp", "rep", None),
            P(None, "fsdp", None),
            P(None, "fsdp", None),
            P(None, "fsdp", None),
            P(None, "fsdp", None),
            P(None, None, "fsdp"),
            P(None, "fsdp", None),
            P(None, "fsdp", None),
            P(None, "fsdp", None),
            P(None, "fsdp", None),
            P(None, None, "fsdp"),
            P(None, "fsdp", None),
            P(None, "fsdp", None),
            P(None, "fsdp", None),
            P(None, "fsdp", None),
            P(None, None, "fsdp"),
        ),
        check_vma=False,
    )
```

```python
import functools
from types import SimpleNamespace
from typing import NamedTuple

import jax
import jax.numpy as jnp
from jax import lax
from jax.experimental import pallas as pl
from jax.experimental.pallas import tpu as pltpu
from jax.sharding import PartitionSpec as P

D = 512
H = 8
FF = 2048
STEP = 10


beta_decay = 0.5
epsilon_adam = 1e-08
weight_decay = 0.01
norm_epsilon = 1e-05
masked_score = -1000000000.0
vector_rate = 0.15
matrix_rate = 0.5


def layer_norm(pre_norm, gain_row, offset_row):
    centre_mean = jnp.mean(pre_norm, axis=-1, keepdims=True)
    centred = pre_norm - centre_mean
    variance = jnp.mean(centred * centred, axis=-1, keepdims=True)
    return centred * lax.rsqrt(variance + norm_epsilon) * gain_row + offset_row


def tanh_gelu_activation(inner_act):
    return jax.nn.gelu(inner_act, approximate=True)


def adamw(master, first, second, grad, rate, decay):
    first_new = beta_decay * first + (1.0 - beta_decay) * grad
    second_new = beta_decay * second + (1.0 - beta_decay) * grad * grad
    correction = 1.0 - beta_decay**STEP
    direction = first_new / correction / (jnp.sqrt(second_new / correction) + epsilon_adam)
    master_new = master - rate * (direction + decay * master)
    return (master_new, first_new, second_new)


def score_block(query_heads, key_heads, key_bias, score_scale):
    scores = jnp.einsum("qhd,khd->hqk", query_heads, key_heads, preferred_element_type=jnp.float32)
    return scores * score_scale + key_bias[None, None, :]


def forward_layer(input_rows, weights, tag_value, key_bias):
    w_qkv, w_out, w_in, w_ffo, vectors_low = weights
    vectors = vectors_low.astype(jnp.float32)
    model_width = w_out.shape[0]
    row_count = input_rows.shape[0]
    head_size = model_width // H
    score_scale = head_size ** (-0.5)
    direction = jnp.where(tag_value == 0, vectors[0], vectors[1])
    summed = input_rows + direction[None, :]
    summed_low = summed.astype(jnp.bfloat16)
    projected = jnp.dot(summed_low, w_qkv, preferred_element_type=jnp.float32)
    queries = (projected[:, :model_width] + vectors[2]).astype(jnp.bfloat16)
    keys_local = projected[:, model_width : 2 * model_width].astype(jnp.bfloat16)
    local_values = (projected[:, 2 * model_width :] + vectors[3]).astype(jnp.bfloat16)
    keys_all, values_all = (
        lax.all_gather(keys_local, "rep", axis=0, tiled=True),
        lax.all_gather(local_values, "rep", axis=0, tiled=True),
    )
    key_count = keys_all.shape[0]
    query_heads = queries.reshape(row_count, H, head_size)
    key_heads = keys_all.reshape(key_count, H, head_size)
    value_heads = values_all.reshape(key_count, H, head_size)
    scores = score_block(query_heads, key_heads, key_bias, score_scale)
    row_top = jnp.max(scores, axis=-1, keepdims=True)
    exponent_terms = jnp.exp(scores - row_top)
    totals = jnp.sum(exponent_terms, axis=-1, keepdims=True)
    soft_weights = exponent_terms / totals
    log_total = row_top + jnp.log(totals)
    context = jnp.einsum(
        "hqk,khd->qhd",
        soft_weights.astype(jnp.bfloat16),
        value_heads,
        preferred_element_type=jnp.float32,
    )
    context_low = context.reshape(row_count, model_width).astype(jnp.bfloat16)
    branch = jnp.dot(context_low, w_out, preferred_element_type=jnp.float32) + vectors[4]
    hidden, norm_first = jax.vjp(layer_norm, summed + branch, vectors[5], vectors[6])
    hidden_low = hidden.astype(jnp.bfloat16)
    inner_act = jnp.dot(hidden_low, w_in, preferred_element_type=jnp.float32) + vectors[
        10:
    ].reshape(-1)
    activated, gelu_pull = jax.vjp(tanh_gelu_activation, inner_act)
    activated_low = activated.astype(jnp.bfloat16)
    feed_out = jnp.dot(activated_low, w_ffo, preferred_element_type=jnp.float32) + vectors[7]
    result, norm_second = jax.vjp(layer_norm, hidden + feed_out, vectors[8], vectors[9])
    saved_state = (
        summed_low,
        query_heads,
        key_heads,
        value_heads,
        log_total,
        context_low,
        norm_first,
        hidden_low,
        gelu_pull,
        activated_low,
        norm_second,
    )
    return (result, saved_state)


def attention_grads(
    query_heads, key_heads, value_heads, log_total, context_heads, key_bias, score_scale
):
    row_count = query_heads.shape[0]
    model_width = query_heads.shape[1] * query_heads.shape[2]
    scores = score_block(query_heads, key_heads, key_bias, score_scale)
    soft_weights = jnp.exp(scores - log_total)
    grad_soft = jnp.einsum(
        "qhd,khd->hqk", context_heads, value_heads, preferred_element_type=jnp.float32
    )
    row_inner = jnp.sum(soft_weights * grad_soft, axis=-1, keepdims=True)
    grad_scores = (soft_weights * (grad_soft - row_inner) * score_scale).astype(jnp.bfloat16)
    grad_queries = jnp.einsum(
        "hqk,khd->qhd", grad_scores, key_heads, preferred_element_type=jnp.float32
    ).reshape(row_count, model_width)
    key_terms = jnp.einsum(
        "hqk,qhd->khd", grad_scores, query_heads, preferred_element_type=jnp.float32
    ).reshape(-1, model_width)
    value_terms = jnp.einsum(
        "hqk,qhd->khd",
        soft_weights.astype(jnp.bfloat16),
        context_heads,
        preferred_element_type=jnp.float32,
    ).reshape(-1, model_width)
    grad_keys, grad_values = (
        lax.psum_scatter(
            key_terms.astype(jnp.bfloat16), "rep", scatter_dimension=0, tiled=True
        ).astype(jnp.float32),
        lax.psum_scatter(
            value_terms.astype(jnp.bfloat16), "rep", scatter_dimension=0, tiled=True
        ).astype(jnp.float32),
    )
    return (grad_queries, grad_keys, grad_values)


def backward_layer(grad_result, saved_state, weights, tag_value, key_bias):
    w_qkv, w_out, w_in, w_ffo, vectors_low = weights
    (
        summed_low,
        query_heads,
        key_heads,
        value_heads,
        log_total,
        context_low,
        norm_first,
        hidden_low,
        gelu_pull,
        activated_low,
        norm_second,
    ) = saved_state
    model_width = w_out.shape[0]
    row_count = summed_low.shape[0]
    head_size = model_width // H
    score_scale = head_size ** (-0.5)
    grad_pre_two, grad_gain_two, grad_shift_two = norm_second(grad_result)
    grad_feed = grad_pre_two.astype(jnp.bfloat16)
    grad_bias_feed = jnp.sum(grad_feed.astype(jnp.float32), axis=0)
    grad_ffo = jnp.einsum("tf,td->fd", activated_low, grad_feed, preferred_element_type=jnp.float32)
    grad_activated = jnp.einsum("td,fd->tf", grad_feed, w_ffo, preferred_element_type=jnp.float32)
    grad_inner = gelu_pull(grad_activated)[0].astype(jnp.bfloat16)
    grad_bias_inner = jnp.sum(grad_inner.astype(jnp.float32), axis=0)
    grad_in = jnp.einsum("td,tf->df", hidden_low, grad_inner, preferred_element_type=jnp.float32)
    grad_hidden = grad_pre_two + jnp.einsum(
        "tf,df->td", grad_inner, w_in, preferred_element_type=jnp.float32
    )
    grad_pre_one, grad_gain_one, grad_shift_one = norm_first(grad_hidden)
    grad_branch = grad_pre_one.astype(jnp.bfloat16)
    grad_bias_out = jnp.sum(grad_branch.astype(jnp.float32), axis=0)
    grad_out_matrix = jnp.einsum(
        "te,td->ed", context_low, grad_branch, preferred_element_type=jnp.float32
    )
    grad_context = jnp.einsum(
        "td,ed->te", grad_branch, w_out, preferred_element_type=jnp.float32
    ).astype(jnp.bfloat16)
    context_heads = grad_context.reshape(row_count, H, head_size)
    grad_queries, grad_keys, grad_values = attention_grads(
        query_heads, key_heads, value_heads, log_total, context_heads, key_bias, score_scale
    )
    grad_joined = jnp.concatenate(
        [
            grad_queries.astype(jnp.bfloat16),
            grad_keys.astype(jnp.bfloat16),
            grad_values.astype(jnp.bfloat16),
        ],
        axis=1,
    )
    grad_qkv = jnp.einsum("td,te->de", summed_low, grad_joined, preferred_element_type=jnp.float32)
    grad_summed = grad_pre_one + jnp.einsum(
        "te,de->td", grad_joined, w_qkv, preferred_element_type=jnp.float32
    )
    column_sums = jnp.sum(grad_joined.astype(jnp.float32), axis=0)
    grad_direction = jnp.sum(grad_summed, axis=0)
    zero_row = jnp.zeros_like(grad_direction)
    grad_rows = jnp.stack(
        [
            jnp.where(tag_value == 0, grad_direction, zero_row),
            jnp.where(tag_value == 1, grad_direction, zero_row),
            column_sums[:model_width],
            column_sums[2 * model_width :],
            grad_bias_out,
            grad_gain_one,
            grad_shift_one,
            grad_bias_feed,
            grad_gain_two,
            grad_shift_two,
        ],
        axis=0,
    )
    grad_vectors = jnp.concatenate([grad_rows, grad_bias_inner.reshape(-1, model_width)], axis=0)
    return (grad_summed, (grad_qkv, grad_out_matrix, grad_in, grad_ffo, grad_vectors))


def reduce_layer(grads):
    shards = (
        lax.psum_scatter(grads[0], "fsdp", scatter_dimension=0, tiled=True),
        lax.psum_scatter(grads[1], "fsdp", scatter_dimension=0, tiled=True),
        lax.psum_scatter(grads[2], "fsdp", scatter_dimension=0, tiled=True),
        lax.psum_scatter(grads[3], "fsdp", scatter_dimension=0, tiled=True),
        lax.psum_scatter(grads[4], "fsdp", scatter_dimension=1, tiled=True),
    )
    return (
        lax.psum(shards[0].astype(jnp.bfloat16), "rep").astype(jnp.float32),
        lax.psum(shards[1].astype(jnp.bfloat16), "rep").astype(jnp.float32),
        lax.psum(shards[2].astype(jnp.bfloat16), "rep").astype(jnp.float32),
        lax.psum(shards[3].astype(jnp.bfloat16), "rep").astype(jnp.float32),
        lax.psum(shards[4].astype(jnp.bfloat16), "rep").astype(jnp.float32),
    )


def body(
    tokens,
    cotangent,
    tags,
    lengths,
    key_mask,
    master_qkv,
    master_out,
    master_in,
    master_feed_output,
    master_vec,
    first_qkv,
    first_out,
    first_in,
    first_ffo,
    first_vec,
    second_qkv,
    second_out,
    second_in,
    second_ffo,
    second_moment_vector,
):
    row_count = tokens.shape[1]
    key_count = key_mask.shape[1]
    start_row = lax.axis_index("rep") * row_count
    query_pos = start_row + jnp.arange(row_count, dtype=jnp.int32)
    key_pos = jnp.arange(key_count, dtype=jnp.int32)
    seq_length = lengths[0]
    tag_value = tags[0]
    key_valid = (key_pos < seq_length) & ((key_mask[0] == 1) | (key_pos == 0))
    key_bias = jnp.where(key_valid, 0.0, masked_score).astype(jnp.float32)
    query_valid = (query_pos < seq_length).astype(jnp.float32)
    masters = (master_qkv, master_out, master_in, master_feed_output, master_vec)
    firsts = (first_qkv, first_out, first_in, first_ffo, first_vec)
    seconds = (second_qkv, second_out, second_in, second_ffo, second_moment_vector)
    shared = (
        lax.all_gather(master_qkv[0].astype(jnp.bfloat16), "fsdp", axis=0, tiled=True),
        lax.all_gather(master_out[0].astype(jnp.bfloat16), "fsdp", axis=0, tiled=True),
        lax.all_gather(master_in[0].astype(jnp.bfloat16), "fsdp", axis=0, tiled=True),
        lax.all_gather(master_feed_output[0].astype(jnp.bfloat16), "fsdp", axis=0, tiled=True),
        lax.all_gather(master_vec[0].astype(jnp.bfloat16), "fsdp", axis=1, tiled=True),
    )
    shared_out, saved_shared = forward_layer(
        tokens[0].astype(jnp.float32), shared, tag_value, key_bias
    )
    unique = (
        lax.all_gather(master_qkv[1].astype(jnp.bfloat16), "fsdp", axis=0, tiled=True),
        lax.all_gather(master_out[1].astype(jnp.bfloat16), "fsdp", axis=0, tiled=True),
        lax.all_gather(master_in[1].astype(jnp.bfloat16), "fsdp", axis=0, tiled=True),
        lax.all_gather(master_feed_output[1].astype(jnp.bfloat16), "fsdp", axis=0, tiled=True),
        lax.all_gather(master_vec[1].astype(jnp.bfloat16), "fsdp", axis=1, tiled=True),
    )
    final_out, saved_unique = forward_layer(shared_out, unique, tag_value, key_bias)
    grad_final = cotangent[0].astype(jnp.float32) * query_valid[:, None]
    unique_back = (
        lax.all_gather(master_qkv[1].astype(jnp.bfloat16), "fsdp", axis=0, tiled=True),
        lax.all_gather(master_out[1].astype(jnp.bfloat16), "fsdp", axis=0, tiled=True),
        lax.all_gather(master_in[1].astype(jnp.bfloat16), "fsdp", axis=0, tiled=True),
        lax.all_gather(master_feed_output[1].astype(jnp.bfloat16), "fsdp", axis=0, tiled=True),
        lax.all_gather(master_vec[1].astype(jnp.bfloat16), "fsdp", axis=1, tiled=True),
    )
    grad_middle, unique_grads = backward_layer(
        grad_final, saved_unique, unique_back, tag_value, key_bias
    )
    reduced_unique = reduce_layer(unique_grads)
    grad_inputs, shared_grads = backward_layer(
        grad_middle, saved_shared, shared, tag_value, key_bias
    )
    reduced_shared = reduce_layer(shared_grads)
    rates = (
        matrix_rate * D ** (-0.5),
        matrix_rate * (D // 16) ** (-0.5),
        matrix_rate * D ** (-0.5),
        matrix_rate * (FF // 2) ** (-0.5),
        vector_rate,
    )
    decays = (weight_decay, weight_decay, weight_decay, weight_decay, 0.0)
    updated = []
    for kind_index in range(5):
        grad_stack = jnp.stack([reduced_shared[kind_index], reduced_unique[kind_index]], axis=0)
        updated.append(
            adamw(
                masters[kind_index],
                firsts[kind_index],
                seconds[kind_index],
                grad_stack,
                rates[kind_index],
                decays[kind_index],
            )
        )
    return (
        final_out.astype(jnp.bfloat16)[None],
        grad_inputs[None],
        updated[0][0],
        updated[1][0],
        updated[2][0],
        updated[3][0],
        updated[4][0],
        updated[0][1],
        updated[1][1],
        updated[2][1],
        updated[3][1],
        updated[4][1],
        updated[0][2],
        updated[1][2],
        updated[2][2],
        updated[3][2],
        updated[4][2],
    )


BF = jnp.bfloat16
F32 = jnp.float32
MESH = pl.DeviceIdType.MESH
KIND_K, KIND_V, KIND_Q, KIND_O, KIND_I, KIND_F = KINDS = tuple(range(6))
VMEM_BYTES = 60 << 20
FORWARD_SPLIT = (1, 1, 1, 2, 1, 1, 1, 1, 5, 5, 1, 1, 1, 1, 5, 5)
BACKWARD_SPLIT = (1, 2, 1, 2, 5, 1, 5, 2, 5, 1, 1, 1, 5, 2, 5, 5)
FORWARD_TURNS = (
    (1, 2, 0, 3, 4, 1, 2, 5),
    (3, 0, 6, 1, 2, 4, 3, 0, 7, 5, 0, 1, 8),
    (6, 2, 9, 1),
    (4, 7, 2, 3),
    (10, 5),
    (6, 11),
    (3, 8, 12),
    (),
    (4, 9, 10, 13, 7),
    (11, 14),
    (4,),
    (),
    (5, 8, 12, 9, 13, 5, 15),
    (6, 9, 8, 10, 6, 7, 14, 11, 12, 13, 7),
    (10,),
    (),
    (),
    (15, 10),
    (),
    (),
    (11, 14),
    (12,),
    (11, 14),
    (12,),
    (13,),
    (),
    (15, 13),
    (15,),
    (),
)
COTANGENT_AT = 2
BACKWARD_TURNS = (
    (),
    (),
    (0, 1),
    (),
    (),
    (2, 0, 3),
    (),
    (1,),
    (2, 4),
    (3, 4, 0),
    (1,),
    (),
    (2, 4),
    (5,),
    (7, 3, 0, 6),
    (),
    (5, 1, 16, 7),
    (2, 6, 4, 16),
    (0, 8, 3, 5, 7, 9),
    (4,),
    (16, 1, 6, 8, 0),
    (5, 7, 10, 11, 9, 2, 16, 1),
    (),
    (10,),
    (3, 12, 11),
    (8, 12, 2, 5, 6, 9),
    (7, 16),
    (3, 12, 10),
    (8, 5, 11),
    (13, 6, 9),
    (7, 12, 14, 10, 15),
    (13,),
    (8, 17, 14, 11, 15, 12, 17, 9, 10, 13, 14, 11, 15, 17, 9, 10, 14, 13, 11, 17, 15, 14, 13, 17, 15, 13),
)


def nt_dot(left, right):
    return lax.dot_general(left, right, (((1,), (1,)), ((), ())), preferred_element_type=F32)


def nn_dot(left, right):
    return jnp.dot(left, right, preferred_element_type=F32)


def remote(src, dst, send_sem, recv_sem, device):
    return pltpu.make_async_remote_copy(
        src_ref=src,
        dst_ref=dst,
        send_sem=send_sem,
        recv_sem=recv_sem,
        device_id=device,
        device_id_type=MESH,
    )


class ForwardIn(NamedTuple):
    tok: object
    cot: object
    lengths: object
    tags: object
    key_mask: object
    vectors: object
    masters: object


class Saved(NamedTuple):
    w_o: object
    vec_o: object
    meta_o: object
    cot_o: object
    y_o: object
    at_o: object
    q_o: object
    k_o: object
    v_o: object
    lse_o: object
    ct_o: object
    ctp_o: object
    n1_o: object
    r1_o: object
    ht_o: object
    g_o: object
    gp_o: object
    n2_o: object
    r2_o: object


class ForwardScratch(NamedTuple):
    w: object
    stages: object
    vecg: object
    vecl: object
    vecs: object
    vec: object
    metab: object
    msel: object
    tokb: object
    cotb: object
    A32: object
    Ab: object
    ATp: object
    Q: object
    K: object
    V: object
    lse: object
    CT: object
    CTp: object
    C: object
    N1: object
    r1: object
    H32: object
    Hb: object
    HTp: object
    G: object
    Gp: object
    N2: object
    r2: object
    X: object
    Yb: object
    msem: object
    xsem: object
    osem: object
    gs: object
    gr: object
    vs: object
    vr: object
    xs: object
    xr: object
    ks: object
    kr: object


class BackwardOut(NamedTuple):
    fin: object
    vec_g: object
    yo: object
    dxo: object


class BackwardScratch(NamedTuple):
    g: object
    landing: object
    half: object
    quarter: object
    level: object
    total: object
    w: object
    AT: object
    Q: object
    K: object
    V: object
    lse: object
    CT: object
    CTp: object
    N1: object
    r1: object
    HT: object
    G: object
    Gp: object
    N2: object
    r2: object
    vec: object
    msel: object
    cotb: object
    dy: object
    dpre: object
    dF: object
    dFT: object
    dU: object
    dZ: object
    delta: object
    dQT: object
    dvb: object
    dkp: object
    dvp: object
    dkr: object
    dvr: object
    vg: object
    va: object
    vrecv: object
    vb: object
    vt: object
    lsem: object
    ssem: object
    fsem: object
    gs: object
    gr: object
    xs: object
    xr: object
    ks: object
    kr: object
    vs: object
    vr: object


class UpdateIn(NamedTuple):
    fin: object
    fvec: object
    y: object
    dx: object
    masters: object
    firsts: object
    seconds: object


class UpdateOut(NamedTuple):
    out: object
    grad: object
    new_masters: object
    new_firsts: object
    new_seconds: object


class UpdateScratch(NamedTuple):
    inside: object
    wide: object
    isem: object
    osem: object


def named(parts, refs):
    fields, at = {}, 0
    for part in parts:
        leaves, tree = jax.tree.flatten(part)
        fields.update(tree.unflatten(refs[at : at + len(leaves)])._asdict())
        at += len(leaves)
    return SimpleNamespace(**fields)


def call_kernel(kernel, args, outs, scratch, spec, **options):
    leaves, _ = jax.tree.flatten(args)
    out_leaves, out_tree = jax.tree.flatten(outs)
    parts = (args, outs) if scratch is None else (args, outs, scratch)
    empty = jax.tree.map(lambda leaf: 0, parts)
    results = pl.pallas_call(
        functools.partial(kernel, empty),
        out_shape=out_leaves,
        in_specs=jax.tree.leaves(spec) if isinstance(spec, tuple) else [spec] * len(leaves),
        out_specs=[pl.BlockSpec(memory_space=pl.ANY)] * len(out_leaves),
        scratch_shapes=() if scratch is None else jax.tree.leaves(scratch),
        compiler_params=pltpu.CompilerParams(**options),
    )(*leaves)
    return out_tree.unflatten(results)


class Place:
    def __init__(self):
        self.r = lax.axis_index("rep")
        self.f = lax.axis_index("fsdp")
        self.z = lax.div(self.f, 4)
        self.y = lax.rem(lax.div(self.f, 2), 2)
        self.c = lax.rem(self.f, 2)
        self.xn = (1 - self.r, self.f)
        self.yn = (self.r, self.f + 2 - 4 * self.y)
        self.cn = (self.r, self.f + 1 - 2 * self.c)
        self.dn = (1 - self.r, self.f + 1 - 2 * self.c)
        self.en = (self.r, self.f + 3 - 4 * self.y - 2 * self.c)

    def zn(self, step, levels):
        other = lax.rem(self.z + step, levels)
        return other, (self.r, other * 4 + 2 * self.y + self.c)


def parity_rows(rows, shards):
    blocks = rows.reshape(shards // 2, 2, rows.shape[0] // shards, rows.shape[1])
    half = rows.shape[0] // 2
    return blocks[:, 0].reshape(half, rows.shape[1]), blocks[:, 1].reshape(half, rows.shape[1])


def halves(cut, levels):
    return pl.ds(0, cut), pl.ds(cut, levels - cut)


def go_or_stay(stays, stay, go):
    @pl.when(stays)
    def _():
        stay()

    @pl.when(jnp.logical_not(stays))
    def _():
        go()


def lane_masks():
    lane = lax.broadcasted_iota(jnp.int32, (16, 128), 1)
    low = (lane < 64).astype(F32)
    spots = (lax.rem(lane, 64) == 0).astype(F32)
    return low[:1].astype(BF), (1.0 - low[:1]).astype(BF), spots[:1].astype(BF)


def sizes_of(mesh_n, width, inner):
    shard = width // mesh_n
    rows = [shard // 2] * 6
    rows[KIND_F] = inner // mesh_n // 2
    cols = [width] * 6
    cols[KIND_I] = inner
    return rows, cols


def forward_kernel(parts, levels, eps, *refs):
    R = named(parts, refs)
    me = Place()
    r, f, z, y, c = me.r, me.f, me.z, me.y, me.c
    shards = levels * 4
    S, D = R.A32.shape
    FF = R.G.shape[1]
    source = ((0, D), (0, 2 * D), (0, 0), (1, 0), (2, 0), (3, 0))

    R.vecs[...] = jnp.zeros(R.vecs.shape, F32)
    vec_load = pltpu.make_async_copy(R.vectors, R.vecs.at[pl.ds(0, R.vectors.shape[0])], R.xsem.at[0])
    vec_load.start()
    half_loads = {}
    for l in range(2):
        for at, (master, stage) in enumerate(zip(R.masters, R.stages)):
            cp = pltpu.make_async_copy(master.at[l], stage.at[l], R.msem.at[l, at])
            cp.start()
            half_loads[(l, at)] = cp
    barrier = pltpu.get_barrier_semaphore()
    peers = [me.zn(s, levels)[1] for s in range(1, levels)] + [me.xn, me.yn, me.cn, me.dn, me.en]
    for peer in peers:
        pl.semaphore_signal(barrier, inc=1, device_id=peer, device_id_type=MESH)
    pl.semaphore_wait(barrier, len(peers))

    chunks = []
    for l in range(2):
        for kind in KINDS:
            parts = 2 if kind in (KIND_I, KIND_F) else 1
            span = R.w[kind].shape[-1] // parts
            chunks += [(kind, l, slice(part * span, part * span + span)) for part in range(parts)]
    gs, gr = R.gs, R.gr
    pending = []

    def start(cp):
        cp.start()
        pending.append(cp)
        return cp

    out_copies = {}
    out_at = [0]

    def out(ref, dst, view=None):
        cp = pltpu.make_async_copy(ref if view is None else view, dst, R.osem.at[out_at[0]])
        out_at[0] += 1
        cp.start()
        out_copies[(id(ref), view is not None and out_at[0])] = cp

    def settle(ref):
        if (id(ref), False) in out_copies:
            out_copies.pop((id(ref), False)).wait()

    loaded = set()
    stage_copies = {}

    def g_z(i):
        kind, l, cols = chunks[i]
        w = R.w[kind]
        at, offset = source[kind]
        if (l, at) not in loaded:
            half_loads[(l, at)].wait()
            loaded.add((l, at))
        rows = w.shape[5]
        w[l, z, y, c, r, :, cols] = R.stages[at][l, pl.ds(r * rows, rows), offset + cols.start : offset + cols.stop].astype(BF)
        cps = []
        for s in range(1, levels):
            _, dev = me.zn(s, levels)
            spot = w.at[l, z, y, c, r, :, cols]
            cps.append(start(remote(spot, spot, gs.at[i, s - 1], gr.at[i, s - 1], dev)))
        stage_copies[i] = cps

    def g_1(i):
        kind, l, cols = chunks[i]
        w = R.w[kind]
        for cp in stage_copies[i]:
            cp.wait_recv()
        first, second = halves(FORWARD_SPLIT[i], levels)
        a, b = w.at[l, first, y, c, r, :, cols], w.at[l, second, y, c, r, :, cols]
        stage_copies[i] = [
            start(remote(a, a, gs.at[i, levels - 1], gr.at[i, levels - 1], me.xn)),
            start(remote(b, b, gs.at[i, levels], gr.at[i, levels], me.yn)),
        ]

    def g_2(i):
        kind, l, cols = chunks[i]
        w = R.w[kind]
        for cp in stage_copies[i]:
            cp.wait_recv()
        first, second = halves(FORWARD_SPLIT[i], levels)
        a, b = w.at[l, first, y, c, :, :, cols], w.at[l, second, :, c, r, :, cols]
        stage_copies[i] = [
            start(remote(a, a, gs.at[i, levels + 1], gr.at[i, levels + 1], me.yn)),
            start(remote(b, b, gs.at[i, levels + 2], gr.at[i, levels + 2], me.xn)),
        ]

    def g_core(i):
        kind, l, cols = chunks[i]
        w = R.w[kind]
        for cp in stage_copies[i]:
            cp.wait_recv()
        a = w.at[l, :, :, c, :, :, cols]
        stage_copies[i] = [start(remote(a, a, gs.at[i, levels + 3], gr.at[i, levels + 3], me.cn))]

    def h_z(i):
        kind, l, cols = chunks[i]
        w = R.w[kind]
        at, offset = source[kind]
        if (l, at) not in loaded:
            half_loads[(l, at)].wait()
            loaded.add((l, at))
        whole = R.stages[at][l][:, offset + cols.start : offset + cols.stop].astype(BF)
        w[l, z, y, c, :, :, cols] = whole.reshape(2, whole.shape[0] // 2, whole.shape[1])
        spot = w.at[l, z, y, c, :, :, cols]
        stage_copies[i] = [
            start(remote(spot, spot, gs.at[i, s], gr.at[i, s], me.zn(s, levels)[1])) for s in range(1, levels)
        ]

    def h_y(i):
        kind, l, cols = chunks[i]
        w = R.w[kind]
        for cp in stage_copies[i]:
            cp.wait_recv()
        spot = w.at[l, :, y, c, :, :, cols]
        stage_copies[i] = [start(remote(spot, spot, gs.at[i, 0], gr.at[i, 0], me.yn))]

    def g_ready(i):
        kind, l, cols = chunks[i]
        for cp in stage_copies.pop(i):
            cp.wait_recv()
        waiting.remove(i)
        if not any(chunks[k][:2] == (kind, l) for k in waiting):
            out(R.w[kind], R.w_o[kind].at[l], R.w[kind].at[l])

    steps = (g_z, g_1, g_2, g_core, g_ready)
    other_steps = (h_z, h_y, g_core, g_ready)
    reached = [0] * len(chunks)
    waiting = list(range(len(chunks)))
    turns = iter(FORWARD_TURNS)

    def turn():
        for i in next(turns):
            (other_steps if FORWARD_SPLIT[i] == 5 else steps)[reached[i]](i)
            reached[i] += 1

    steps[0](0)
    reached[0] = 1
    tok_far = remote(R.tok.at[0], R.tokb, R.xs.at[1], R.xr.at[1], me.dn)
    tok_near = pltpu.make_async_copy(R.tok.at[0], R.tokb, R.xsem.at[2])
    stays = c == r

    go_or_stay(stays, tok_near.start, tok_far.start)
    length = R.lengths[0]
    keys = R.key_mask[...]
    key_pos = lax.broadcasted_iota(jnp.int32, keys.shape, 1)
    valid = key_pos < length
    bias = jnp.where(valid & ((keys == 1) | (key_pos == 0)), 0.0, masked_score)
    place = lax.broadcasted_iota(jnp.int32, (128, 2 * S), 0)
    columns = jnp.where(lax.rem(place, 64) == 0, bias, 0.0) + jnp.where((place == 1) & valid, 1.0, 0.0)
    R.metab[0, : 2 * S] = columns.T.astype(BF)
    R.metab[0, 2 * S :] = jnp.full((16, 128), R.tags[0].astype(F32)).astype(BF)
    meta_cp = start(remote(R.metab.at[0], R.metab.at[1], R.xs.at[0], R.xr.at[0], me.cn))
    wide = R.vectors.shape[2]
    lane = lax.broadcasted_iota(jnp.int32, (16, 128), 1)
    vec_load.wait()
    spot = R.vecg.at[2 * y + c]
    spot[...] = jnp.zeros((32, 128), BF)
    for l in range(2):
        block = jnp.concatenate([R.vecs[:, l]] * (128 // wide), axis=1)
        block = jnp.where(lax.div(lane, wide) == lax.rem(f, 128 // wide), block, 0.0)
        spot[16 * l : 16 * l + 16] = block.astype(BF)
    vec_cps = [start(remote(spot, spot, R.vs.at[at], R.vr.at[at], dev)) for at, dev in enumerate((me.yn, me.cn, me.en))]
    for cp in vec_cps:
        cp.wait_recv()
    spot = R.vecl.at[z]
    spot[...] = jnp.sum(R.vecg[...].astype(F32), axis=0).astype(BF)
    vec_cps = []
    for s in range(1, levels):
        vec_cps.append(start(remote(spot, spot, R.vs.at[2 + s], R.vr.at[2 + s], me.zn(s, levels)[1])))
    turn()
    meta_cp.wait_recv()
    for cp in vec_cps:
        cp.wait_recv()
    keep = stays.astype(F32)
    msel = R.msel
    msel[...] = (R.metab[0].astype(F32) * keep + R.metab[1].astype(F32) * (1.0 - keep)).astype(BF)
    vec = R.vec
    for zz in range(levels):
        vec[:, 128 * zz : 128 * zz + 128] = R.vecl[zz].astype(F32)
    tag_row = msel[2 * S : 2 * S + 16].astype(F32)[:1]
    tag_row = jnp.concatenate([tag_row] * (D // 128), axis=1)
    low, high, spots = lane_masks()

    go_or_stay(stays, tok_near.wait, tok_far.wait)
    cot_far = remote(R.cot.at[0], R.cotb, R.xs.at[2], R.xr.at[2], me.dn)
    cot_near = pltpu.make_async_copy(R.cot.at[0], R.cotb, R.xsem.at[3])

    T = 256
    for l in range(2):
        e = lambda row: vec[16 * l + row : 16 * l + row + 1, :]
        direction = e(0) * (1.0 - tag_row) + e(1) * tag_row
        if l == 1:
            turn()
        A32, Ab, Q, K, V, CT = R.A32, R.Ab, R.Q, R.K, R.V, R.CT
        x_in = R.tokb if l == 0 else R.X
        summed = x_in[...].astype(F32) + direction
        A32[...] = summed
        Ab[...] = summed.astype(BF)
        at = Ab[...].T
        even, odd = parity_rows(at, shards)
        settle(R.ATp)
        R.ATp[: D // 2] = even
        R.ATp[D // 2 :] = odd
        out(R.ATp, R.at_o.at[l])

        def weight(kind, lo=0, hi=None):
            w = R.w[kind]
            hi = w.shape[-1] if hi is None else hi
            value = w[l, :, :, :, :, :, lo:hi]
            return value.reshape(-1, hi - lo)

        turn()
        K[l, c] = nn_dot(Ab[...], weight(KIND_K)).astype(BF)
        k_cp = start(remote(K.at[l, c], K.at[l, c], R.ks.at[l, 0], R.kr.at[l, 0], me.cn))
        turn()
        V[l, c] = (nn_dot(Ab[...], weight(KIND_V)) + e(3)).astype(BF)
        v_cp = start(remote(V.at[l, c], V.at[l, c], R.ks.at[l, 1], R.kr.at[l, 1], me.cn))
        turn()
        settle(R.Q)
        q = (nn_dot(Ab[...], weight(KIND_Q)) + e(2)).astype(BF)
        Q[...] = (q.astype(F32) * 0.125).astype(BF)
        out(R.Q, R.q_o.at[l])
        turn()
        k_cp.wait_recv()
        v_cp.wait_recv()
        out(K, R.k_o.at[l], K.at[l])
        out(V, R.v_o.at[l], V.at[l])
        lse = R.lse
        settle(R.lse)
        settle(R.CT)
        bias_rows = msel[: 2 * S]

        def pair(j):
            sl = slice(j * 128, j * 128 + 128)
            k2 = K[l, :, :, sl].reshape(2 * S, 128)
            v2t = V[l, :, :, sl].reshape(2 * S, 128).T
            q2 = Q[:, sl]
            scores = []
            for mine, other in ((low, high), (high, low)):
                scores.append(nt_dot(k2 * mine + bias_rows * other, q2 * mine + spots * other))
            for h, st in enumerate(scores):
                top = jnp.max(st, axis=0, keepdims=True)
                p = jnp.exp(st - top)
                total = jnp.sum(p, axis=0, keepdims=True)
                ctx = nn_dot(v2t, p.astype(BF))[64 * h : 64 * h + 64]
                rows = slice(j * 128 + 64 * h, j * 128 + 64 * h + 64)
                CT[rows] = (ctx * (1.0 / total)).astype(BF)
                lse[j, h : h + 1] = top + jnp.log(total)

        for j in range(D // 128):
            turn()
            if l == 1 and j == COTANGENT_AT:
                go_or_stay(stays, cot_near.start, cot_far.start)
            pair(j)
        turn()
        out(R.lse, R.lse_o.at[l])
        out(R.CT, R.ct_o.at[l])
        even, odd = parity_rows(CT[...], shards)
        settle(R.CTp)
        R.CTp[: D // 2] = even
        R.CTp[D // 2 :] = odd
        out(R.CTp, R.ctp_o.at[l])
        R.C[...] = CT[...].T
        settle(R.N1)
        settle(R.r1)

        def norm_one(t, carry):
            rows = pl.ds(pl.multiple_of(t * T, T), T)
            pre = A32[rows] + nn_dot(R.C[rows], weight(KIND_O)) + e(4)
            mean = jnp.mean(pre, axis=-1, keepdims=True)
            centred = pre - mean
            rstd = lax.rsqrt(jnp.mean(centred * centred, axis=-1, keepdims=True) + eps)
            n1 = centred * rstd
            hidden = n1 * e(5) + e(6)
            R.N1[rows] = n1
            R.r1[rows] = jnp.broadcast_to(rstd, (T, 128))
            R.H32[rows] = hidden
            R.Hb[rows] = hidden.astype(BF)
            return carry

        turn()
        lax.fori_loop(0, S // T, norm_one, 0)
        out(R.N1, R.n1_o.at[l])
        out(R.r1, R.r1_o.at[l])
        even, odd = parity_rows(R.Hb[...].T, shards)
        settle(R.HTp)
        R.HTp[: D // 2] = even
        R.HTp[D // 2 :] = odd
        out(R.HTp, R.ht_o.at[l])
        settle(R.G)
        settle(R.Gp)

        def inner(b):
            u = nn_dot(R.Hb[...], weight(KIND_I, b * D, b * D + D)) + e(10 + b)
            u2 = u * u
            th = jnp.tanh(u * (0.7978845608028654 + 0.035677408136300125 * u2))
            half = 0.5 + 0.5 * th
            slope = 0.7978845608028654 + 0.10703222440890038 * u2
            R.G[:, b * D : b * D + D] = (u * half).astype(BF)
            R.Gp[:, b * D : b * D + D] = (half + 0.5 * u * (1.0 - th * th) * slope).astype(BF)

        for b in range(FF // D):
            if b % 2 == 0:
                turn()
            inner(b)
        out(R.G, R.g_o.at[l])
        out(R.Gp, R.gp_o.at[l])
        turn()
        settle(R.N2)
        settle(R.r2)

        def norm_two(t, carry):
            rows = pl.ds(pl.multiple_of(t * T, T), T)
            pre = R.H32[rows] + nn_dot(R.G[rows], weight(KIND_F)) + e(7)
            mean = jnp.mean(pre, axis=-1, keepdims=True)
            centred = pre - mean
            rstd = lax.rsqrt(jnp.mean(centred * centred, axis=-1, keepdims=True) + eps)
            n2 = centred * rstd
            R.N2[rows] = n2
            R.r2[rows] = jnp.broadcast_to(rstd, (T, 128))
            R.X[rows] = n2 * e(8) + e(9)
            return carry

        lax.fori_loop(0, S // T, norm_two, 0)
        out(R.N2, R.n2_o.at[l])
        out(R.r2, R.r2_o.at[l])

    turn()
    R.Yb[...] = R.X[...].astype(BF)
    out(R.Yb, R.y_o)
    out(vec, R.vec_o)
    out(msel, R.meta_o)
    go_or_stay(stays, cot_near.wait, cot_far.wait_recv)
    out(R.cotb, R.cot_o)
    for cp in out_copies.values():
        cp.wait()
    for cp in pending:
        cp.wait_send()
    go_or_stay(stays, lambda: None, cot_far.wait_send)


def backward_kernel(parts, levels, *refs):
    R = named(parts, refs)
    me = Place()
    r, f, z, y, c = me.r, me.f, me.z, me.y, me.c
    shards = levels * 4
    S, D = R.dy.shape
    FF = R.G.shape[1]
    saved = list(zip(R.w, R.w_o)) + [
        (R.AT, R.at_o), (R.Q, R.q_o), (R.K, R.k_o), (R.V, R.v_o), (R.lse, R.lse_o), (R.CT, R.ct_o), (R.CTp, R.ctp_o),
        (R.N1, R.n1_o), (R.r1, R.r1_o), (R.HT, R.ht_o), (R.G, R.g_o), (R.Gp, R.gp_o), (R.N2, R.n2_o), (R.r2, R.r2_o),
    ]
    order = {id(ref): at for at, (ref, _) in enumerate(saved)}
    loads = {}

    def load(ref, l):
        at = order[id(ref)]
        cp = pltpu.make_async_copy(saved[at][1].at[l], ref, R.lsem.at[l, at])
        cp.start()
        loads[id(ref)] = cp

    def use(ref):
        if id(ref) in loads:
            loads.pop(id(ref)).wait()
        return ref

    small = []
    for at, (dst, src) in enumerate(((R.vec, R.vec_o), (R.msel, R.meta_o), (R.cotb, R.cot_o))):
        cp = pltpu.make_async_copy(src, dst, R.ssem.at[at])
        cp.start()
        small.append(cp)
    wk, wv, wq, wo, wi, wf = R.w
    for ref in (R.N2, R.r2, R.G):
        load(ref, 1)
    later = (wf, R.Gp, R.HT, wi, R.N1, R.r1, R.CTp, wo, R.CT, R.K, R.V, R.Q, R.lse, R.AT, wq, wk, wv)

    barrier = pltpu.get_barrier_semaphore()
    peers = [me.zn(s, levels)[1] for s in range(1, levels)] + [me.xn, me.yn, me.cn, me.dn]
    for peer in peers:
        pl.semaphore_signal(barrier, inc=1, device_id=peer, device_id_type=MESH)

    pending = []

    def start(cp):
        cp.start()
        pending.append(cp)
        return cp

    stays = c == r
    y_far = remote(R.y_o, R.yo, R.xs.at[0], R.xr.at[0], me.dn)
    y_near = pltpu.make_async_copy(R.y_o, R.yo, R.ssem.at[3])
    dx_cps = []


    gs, gr = R.gs, R.gr
    chunks = []
    for l in (1, 0):
        for kind in (KIND_F, KIND_I, KIND_O, KIND_Q, KIND_K, KIND_V):
            rows, cols = R.g[kind].shape[-2:]
            if kind == KIND_F:
                spans = [(slice(0, rows // 2), slice(0, cols)), (slice(rows // 2, rows), slice(0, cols))]
            elif kind == KIND_I:
                spans = [(slice(0, rows), slice(0, cols // 2)), (slice(0, rows), slice(cols // 2, cols))]
            else:
                spans = [(slice(0, rows), slice(0, cols))]
            chunks += [(kind, l, *span) for span in spans]
    chunks += [(None, 1), (None, 0)]
    flight = {}
    stage = {}
    fin_copies = []

    def rs_core(i):
        kind, l, rs, cs = chunks[i]
        g = R.g[kind]
        spot = g.at[0, 0, :, :, :, rs, cs] if l == 1 else R.landing[kind].at[:, :, :, rs, cs]
        mine = g.at[l, 1 - c, :, :, :, rs, cs]
        flight[i] = [start(remote(mine, spot, gs.at[i, 0], gr.at[i, 0], me.cn))]

    def add_landed(i):
        kind, l, rs, cs = chunks[i]
        g = R.g[kind]
        landed = g[0, 0, :, :, :, rs, cs] if l == 1 else R.landing[kind][:, :, :, rs, cs]
        g[l, c, :, :, :, rs, cs] = g[l, c, :, :, :, rs, cs] + landed

    def rs_1(i):
        kind, l, rs, cs = chunks[i]
        g, half = R.g[kind], R.half[kind]
        first, second = halves(BACKWARD_SPLIT[i], levels)
        add_landed(i)
        a, b = g.at[l, c, first, 1 - y, :, rs, cs], g.at[l, c, second, :, 1 - r, rs, cs]
        flight[i] = [
            start(remote(a, half.at[l, first, :, rs, cs], gs.at[i, 1], gr.at[i, 1], me.yn)),
            start(remote(b, half.at[l, second, :, rs, cs], gs.at[i, 2], gr.at[i, 2], me.xn)),
        ]

    def rs_2(i):
        kind, l, rs, cs = chunks[i]
        g, half, quarter = R.g[kind], R.half[kind], R.quarter[kind]
        first, second = halves(BACKWARD_SPLIT[i], levels)
        g[l, c, first, y, :, rs, cs] = g[l, c, first, y, :, rs, cs] + half[l, first, :, rs, cs]
        g[l, c, second, :, r, rs, cs] = g[l, c, second, :, r, rs, cs] + half[l, second, :, rs, cs]
        a, b = g.at[l, c, first, y, 1 - r, rs, cs], g.at[l, c, second, 1 - y, r, rs, cs]
        flight[i] = [
            start(remote(a, quarter.at[l, first, rs, cs], gs.at[i, 3], gr.at[i, 3], me.xn)),
            start(remote(b, quarter.at[l, second, rs, cs], gs.at[i, 4], gr.at[i, 4], me.yn)),
        ]

    def rs_3(i):
        kind, l, rs, cs = chunks[i]
        g, quarter = R.g[kind], R.quarter[kind]
        first, second = halves(BACKWARD_SPLIT[i], levels)
        g[l, c, first, y, r, rs, cs] = g[l, c, first, y, r, rs, cs] + quarter[l, first, rs, cs]
        g[l, c, second, y, r, rs, cs] = g[l, c, second, y, r, rs, cs] + quarter[l, second, rs, cs]
        flight[i] = []
        for s in range(1, levels):
            there, dev = me.zn(s, levels)
            mine, spot = g.at[l, c, there, y, r, rs, cs], R.level[kind].at[l, s - 1, 0, rs, cs]
            flight[i].append(start(remote(mine, spot, gs.at[i, 4 + s], gr.at[i, 4 + s], dev)))

    def rs_4(i):
        kind, l, rs, cs = chunks[i]
        total = R.g[kind][l, c, z, y, r, rs, cs].astype(F32)
        for s in range(levels - 1):
            total = total + R.level[kind][l, s, 0, rs, cs].astype(F32)
        R.total[kind][l, r, rs, cs] = total.astype(BF)
        spot = R.total[kind].at[l, r, rs, cs]
        flight[i] = [start(remote(spot, spot, gs.at[i, 4 + levels], gr.at[i, 4 + levels], me.xn))]

    def rs_5(i):
        kind, l, rs, cs = chunks[i]
        cp = pltpu.make_async_copy(R.total[kind].at[l, :, rs, cs], R.fin[kind].at[l, :, rs, cs], R.fsem.at[i])
        cp.start()
        fin_copies.append(cp)

    vg, va, vb, vt = R.vg, R.va, R.vb, R.vt

    def vec_hop(at, device):
        def step(i):
            l = chunks[i][1]
            if at == 0:
                va[l, 0] = vg[16 * l : 16 * l + 16]
            else:
                va[l, at] = va[l, at - 1] + R.vrecv[l, at - 1]
            flight[i] = [start(remote(va.at[l, at], R.vrecv.at[l, at], R.vs.at[l, at], R.vr.at[l, at], device))]

        return step

    def vec_level(i):
        l = chunks[i][1]
        va[l, 3] = va[l, 2] + R.vrecv[l, 2]
        flight[i] = []
        for s in range(1, levels):
            there, dev = me.zn(s, levels)
            lanes = pl.ds(pl.multiple_of(there * 128, 128), 128)
            flight[i].append(start(remote(va.at[l, 3, :, lanes], vb.at[l, s - 1], R.vs.at[l, 2 + s], R.vr.at[l, 2 + s], dev)))

    def vec_end(i):
        l = chunks[i][1]
        total = va[l, 3, :, pl.ds(pl.multiple_of(z * 128, 128), 128)]
        for s in range(levels - 1):
            total = total + vb[l, s]
        vt[16 * l : 16 * l + 16] = total

    def hs_y(i):
        kind, l, rs, cs = chunks[i]
        add_landed(i)
        mine, spot = R.g[kind].at[l, c, :, 1 - y, :, rs, cs], R.half[kind].at[l, :, :, rs, cs]
        flight[i] = [start(remote(mine, spot, gs.at[i, levels], gr.at[i, levels], me.yn))]

    def hs_z(i):
        kind, l, rs, cs = chunks[i]
        g = R.g[kind]
        g[l, c, :, y, :, rs, cs] = g[l, c, :, y, :, rs, cs] + R.half[kind][l, :, :, rs, cs]
        flight[i] = []
        for s in range(1, levels):
            there, dev = me.zn(s, levels)
            mine, spot = g.at[l, c, there, y, :, rs, cs], R.level[kind].at[l, s - 1, :, rs, cs]
            flight[i].append(start(remote(mine, spot, gs.at[i, s], gr.at[i, s], dev)))

    def hs_x(i):
        kind, l, rs, cs = chunks[i]
        g = R.g[kind]
        whole = g[l, c, z, y, :, rs, cs].astype(F32)
        for s in range(levels - 1):
            whole = whole + R.level[kind][l, s, :, rs, cs].astype(F32)
        g[l, c, z, y, :, rs, cs] = whole.astype(BF)
        mine, spot = g.at[l, c, z, y, :, rs, cs], R.quarter[kind].at[l, pl.ds(0, 2), rs, cs]
        sems = gs.at[i, levels + 1], gr.at[i, levels + 1]
        flight[i] = [start(remote(mine, spot, *sems, me.xn))]

    def hs_end(i):
        kind, l, rs, cs = chunks[i]
        R.total[kind][l, :, rs, cs] = R.g[kind][l, c, z, y, :, rs, cs] + R.quarter[kind][l, :2, rs, cs]
        rs_5(i)

    other_steps = (rs_core, hs_y, hs_z, hs_x, hs_end)
    matrix_steps = (rs_core, rs_1, rs_2, rs_3, rs_4, rs_5)
    vec_steps = (vec_hop(0, me.cn), vec_hop(1, me.xn), vec_hop(2, me.yn), vec_level, vec_end)
    turns = iter(BACKWARD_TURNS)

    def turn():
        for i in next(turns):
            at = stage.get(i, 0)
            for cp in flight.pop(i, ()):
                cp.wait_recv()
            known = vec_steps if chunks[i][0] is None else other_steps if BACKWARD_SPLIT[i] == 5 else matrix_steps
            known[at](i)
            stage[i] = at + 1

    for cp in small:
        cp.wait()
    vec, msel = R.vec, R.msel
    tag_row = msel[2 * S : 2 * S + 16].astype(F32)[:1]
    tag_row = jnp.concatenate([tag_row] * (D // 128), axis=1)
    low, high, spots = lane_masks()
    low32 = low.astype(F32)
    vg[...] = jnp.zeros_like(vg)
    R.dy[...] = R.cotb[...].astype(F32) * msel[pl.ds(c * S, S)][:, 1:2].astype(F32)
    T = 256
    dy, dpre, dF, dFT, dU, dZ = R.dy, R.dpre, R.dF, R.dFT, R.dU, R.dZ

    def fold(value):
        return jnp.sum(value.reshape(value.shape[0] // 8, 8, value.shape[1]), axis=0)

    zero8 = jnp.zeros((8, D), F32)

    for l in (1, 0):
        base = 16 * l
        e = lambda row: vec[base + row : base + row + 1, :]

        def put(row, value):
            vg[base + row : base + row + 1, :] = value

        def weight(kind):
            w = R.w[kind]
            return w[...].reshape(-1, w.shape[-1])

        turn()
        N2, r2 = use(R.N2), use(R.r2)
        if l == 1:
            for ref in later:
                load(ref, 1)

        def norm_two(t, carry):
            s7, s8, s9 = carry
            rows = pl.ds(pl.multiple_of(t * T, T), T)
            g, n = dy[rows], N2[rows]
            dn = g * e(8)
            m1 = jnp.mean(dn, axis=-1, keepdims=True)
            m2 = jnp.mean(dn * n, axis=-1, keepdims=True)
            d = r2[rows][:, :1] * (dn - m1 - n * m2)
            dpre[rows] = d
            db = d.astype(BF)
            dF[rows] = db
            dFT[:, rows] = db.T
            return s7 + fold(db.astype(F32)), s8 + fold(g * n), s9 + fold(g)

        s7, s8, s9 = lax.fori_loop(0, S // T, norm_two, (zero8, zero8, zero8))
        put(7, jnp.sum(s7, axis=0, keepdims=True))
        put(8, jnp.sum(s8, axis=0, keepdims=True))
        put(9, jnp.sum(s9, axis=0, keepdims=True))
        if l == 1:
            pl.semaphore_wait(barrier, len(peers))
            go_or_stay(stays, y_near.start, y_far.start)
        turn()
        G = use(R.G)
        gf = R.g[KIND_F]
        piece = 2 * FF // shards

        def grad_f(t, carry):
            d = nn_dot(dFT[...], G[:, pl.ds(pl.multiple_of(t * piece, piece), piece)]).astype(BF)
            zz, yy = lax.div(t, 2), lax.rem(t, 2)
            half = piece // 2
            gf[l, 0, zz, yy] = d[:, :half].reshape(2, D // 2, half)
            gf[l, 1, zz, yy] = d[:, half:].reshape(2, D // 2, half)
            return carry

        lax.fori_loop(0, shards // 2, grad_f, 0)
        if l == 1:
            for ref in (R.N2, R.r2, R.G):
                load(ref, 0)
        use(R.w[KIND_F])
        Gp = use(R.Gp)

        def grad_inner(b):
            wf = R.w[KIND_F]
            quarter = wf[b * (levels // (FF // D)) : (b + 1) * (levels // (FF // D))].reshape(D, D)
            cols = slice(b * D, b * D + D)
            du = (nt_dot(dF[...], quarter) * Gp[:, cols].astype(F32)).astype(BF)
            dU[:, cols] = du
            put(10 + b, jnp.sum(fold(du.astype(F32)), axis=0, keepdims=True))

        for b in range(FF // D):
            if b % 2 == 0:
                turn()
            grad_inner(b)
        turn()
        if l == 1:
            load(R.w[KIND_F], 0)
            load(R.Gp, 0)
        HT = use(R.HT)
        gi = R.g[KIND_I]
        rows_i = 2 * R.g[KIND_I].shape[-2]

        for b in range(FF // D):
            d = nn_dot(HT[...], dU[:, b * D : b * D + D]).astype(BF)
            for cc in range(2):
                part = d[cc * (D // 2) : (cc + 1) * (D // 2)]
                gi[l, cc, :, :, :, :, b * D : b * D + D] = part.reshape(levels, 2, 2, rows_i // 2, D)
        if l == 1:
            load(R.HT, 0)
        use(R.w[KIND_I])
        N1, r1 = use(R.N1), use(R.r1)

        def norm_one(t, carry):
            s4, s5, s6 = carry
            rows = pl.ds(pl.multiple_of(t * T, T), T)
            g = dpre[rows] + nt_dot(dU[rows], weight(KIND_I))
            n = N1[rows]
            dn = g * e(5)
            m1 = jnp.mean(dn, axis=-1, keepdims=True)
            m2 = jnp.mean(dn * n, axis=-1, keepdims=True)
            d = r1[rows][:, :1] * (dn - m1 - n * m2)
            dy[rows] = d
            db = d.astype(BF)
            dZ[rows] = db
            return s4 + fold(db.astype(F32)), s5 + fold(g * n), s6 + fold(g)

        turn()
        sums = lax.fori_loop(0, S // T // 2, norm_one, (zero8, zero8, zero8))
        turn()
        s4, s5, s6 = lax.fori_loop(S // T // 2, S // T, norm_one, sums)
        put(4, jnp.sum(s4, axis=0, keepdims=True))
        put(5, jnp.sum(s5, axis=0, keepdims=True))
        put(6, jnp.sum(s6, axis=0, keepdims=True))
        turn()
        if l == 1:
            for ref in (R.w[KIND_I], R.N1, R.r1):
                load(ref, 0)
        CTp = use(R.CTp)
        go = R.g[KIND_O]

        def store(ref, value):
            for cc in range(2):
                ref[l, cc] = value[cc * (D // 2) : (cc + 1) * (D // 2)].reshape(ref.shape[2:])

        store(R.g[KIND_O], nn_dot(CTp[...], dZ[...]).astype(BF))
        use(R.w[KIND_O])
        dF[...] = nt_dot(dZ[...], weight(KIND_O)).astype(BF)
        CT = use(R.CT)
        dct = dF[...].T
        prod = dct.astype(F32) * CT[...].astype(F32)
        prod = jnp.sum(prod.reshape(D // 64, 64, S), axis=1)
        for j in range(D // 128):
            R.delta[j, :2] = prod[2 * j : 2 * j + 2]
        if l == 1:
            for ref in (R.CTp, R.w[KIND_O], R.CT):
                load(ref, 0)
        K, V, Q, lse = use(R.K), use(R.V), use(R.Q), use(R.lse)
        delta, dC, dQT = R.delta, dF, R.dQT
        dkp, dvp, dkr, dvr = R.dkp, R.dvp, R.dkr, R.dvr
        bias_rows = msel[: 2 * S]

        def pair(j):
            sl = slice(j * 128, j * 128 + 128)
            k2 = K[:, :, sl].reshape(2 * S, 128)
            v2 = V[:, :, sl].reshape(2 * S, 128)
            k2t = k2.T
            q2 = Q[:, sl]
            dc2 = dC[:, sl]
            dk_sum, dv_sum = None, None
            for h in range(2):
                mine, other = (low, high) if h == 0 else (high, low)
                mine32 = low32 if h == 0 else 1.0 - low32
                kh = k2 * mine + bias_rows * other
                vh = v2 * mine
                qh = q2 * mine + spots * other
                dk_h, dv_h = None, None
                for part in range(S // 256):
                    cols = slice(part * 256, part * 256 + 256)
                    st = nt_dot(kh, qh[cols])
                    p = jnp.exp(st - lse[j, h : h + 1, cols])
                    dp = nt_dot(vh, dc2[cols])
                    ds = (p * (dp - delta[j, h : h + 1, cols])).astype(BF)
                    pb = p.astype(BF)
                    dv = nn_dot(pb, dc2[cols])
                    dk = nn_dot(ds, q2[cols])
                    dv_h = dv if dv_h is None else dv_h + dv
                    dk_h = dk if dk_h is None else dk_h + dk
                    dq = nn_dot(k2t, ds)[64 * h : 64 * h + 64]
                    rows = slice(j * 128 + 64 * h, j * 128 + 64 * h + 64)
                    dQT[rows, cols] = (dq * 0.125).astype(BF)
                dk_sum = dk_h * mine32 if dk_sum is None else dk_sum + dk_h * mine32
                dv_sum = dv_h * mine32 if dv_sum is None else dv_sum + dv_h * mine32
            dkp[l, :, j] = dk_sum.astype(BF).reshape(2, S, 128)
            dvp[l, :, j] = dv_sum.astype(BF).reshape(2, S, 128)

        pairs = D // 128
        half_pairs = pairs // 2
        kv_cps = []
        for j in range(pairs):
            turn()
            pair(j)
            if (j + 1) % half_pairs == 0:
                part = j // half_pairs
                js = pl.ds(part * half_pairs, half_pairs)
                for at, (mine, theirs) in enumerate(((dkp, dkr), (dvp, dvr))):
                    sems = R.ks.at[l, part, at], R.kr.at[l, part, at]
                    kv_cps.append(start(remote(mine.at[l, 1 - c, js], theirs.at[l, js], *sems, me.cn)))
        if l == 1:
            for ref in (R.K, R.V, R.Q, R.lse):
                load(ref, 0)
        turn()
        AT = use(R.AT)
        dqb = dZ
        dqb[...] = dQT[...].T
        store(R.g[KIND_Q], nn_dot(AT[...], dqb[...]).astype(BF))
        turn()
        for cp in kv_cps:
            cp.wait_recv()
        dkb, dvb = dFT, R.dvb
        for j in range(pairs):
            dkb[:, 128 * j : 128 * j + 128] = dkp[l, c, j] + dkr[l, j]
            dvb[:, 128 * j : 128 * j + 128] = dvp[l, c, j] + dvr[l, j]
        store(R.g[KIND_K], nn_dot(AT[...], dkb[...]).astype(BF))
        store(R.g[KIND_V], nn_dot(AT[...], dvb[...]).astype(BF))
        if l == 1:
            load(R.AT, 0)
        use(R.w[KIND_Q])
        use(R.w[KIND_K])
        use(R.w[KIND_V])

        def last(t, carry):
            s0, s2, s3 = carry
            rows = pl.ds(pl.multiple_of(t * T, T), T)
            d = dy[rows] + nt_dot(dqb[rows], weight(KIND_Q)) + nt_dot(dkb[rows], weight(KIND_K)) + nt_dot(dvb[rows], weight(KIND_V))
            dy[rows] = d
            return s0 + fold(d), s2 + fold(dqb[rows].astype(F32)), s3 + fold(dvb[rows].astype(F32))

        sums = (zero8, zero8, zero8)
        for part in range(2):
            turn()
            sums = lax.fori_loop(part * (S // T // 2), (part + 1) * (S // T // 2), last, sums)
            if l == 0:
                half = pl.ds(part * (S // 2), S // 2)
                R.cotb[half] = dy[half].astype(BF)
                far = remote(R.cotb.at[half], R.dxo.at[half], R.xs.at[1 + part], R.xr.at[1 + part], me.dn)
                near = pltpu.make_async_copy(R.cotb.at[half], R.dxo.at[half], R.ssem.at[4 + part])
                dx_cps.append((far, near))
                go_or_stay(stays, near.start, far.start)
        s0, s2, s3 = sums
        s0 = jnp.sum(s0, axis=0, keepdims=True)
        put(0, s0 * (1.0 - tag_row))
        put(1, s0 * tag_row)
        put(2, jnp.sum(s2, axis=0, keepdims=True))
        put(3, jnp.sum(s3, axis=0, keepdims=True))
        if l == 1:
            for ref in (R.w[KIND_Q], R.w[KIND_K], R.w[KIND_V]):
                load(ref, 0)

    turn()
    vec_out = pltpu.make_async_copy(vt, R.vec_g, R.ssem.at[6])
    vec_out.start()
    for cp in fin_copies:
        cp.wait()
    vec_out.wait()
    for cp in pending:
        cp.wait_send()

    for far, near in dx_cps:
        go_or_stay(stays, near.wait, far.wait)
    go_or_stay(stays, y_near.wait, y_far.wait)


def update_kernel(parts, rates, decays, *refs):
    R = named(parts, refs)
    f = lax.axis_index("fsdp")
    sources, _ = jax.tree.flatten((R.fin, R.fvec, R.y, R.dx, R.masters, R.firsts, R.seconds))
    places, tree = jax.tree.flatten(R.inside)
    copies = []
    for at, (s, p) in enumerate(zip(sources, places)):
        if s.shape != p.shape:
            p[...] = jnp.zeros(p.shape, p.dtype)
            p = p.at[pl.ds(0, s.shape[0])]
        copies.append(pltpu.make_async_copy(s, p, R.isem.at[at]))
    fin, fvec, y, dx, masters, firsts, seconds = R.inside
    waits = tree.unflatten(copies)
    waits[3].start()
    waits[2].start()
    for at, kinds in ((2, (KIND_I,)), (3, (KIND_F,)), (1, (KIND_O,)), (0, (KIND_Q, KIND_K, KIND_V)), (4, ())):
        for cp in [waits[0][k] for k in kinds] + [w[at] for w in waits[4:]]:
            cp.start()
    waits[1].start()
    finals = (R.new_masters, R.new_firsts, R.new_seconds)
    leaving = []

    def leave(src, dst):
        cp = pltpu.make_async_copy(src, dst, R.osem.at[len(leaving)])
        cp.start()
        leaving.append(cp)

    def arrive(at, kinds):
        for cp in [waits[0][k] for k in kinds] + [w[at] for w in waits[4:]]:
            cp.wait()

    def step(at, where, grad):
        new = adamw(masters[at][where], firsts[at][where], seconds[at][where], grad, rates[at], decays[at])
        for refs, value in zip((masters, firsts, seconds), new):
            refs[at][where] = value

    def done(at):
        for kept, final in zip((masters, firsts, seconds), finals):
            src = kept[at]
            leave(src if src.shape == final[at].shape else src.at[pl.ds(0, final[at].shape[0])], final[at])

    waits[3].wait()
    R.wide[...] = dx[...].astype(F32)
    leave(R.wide, R.grad.at[0])
    waits[2].wait()
    leave(y, R.out.at[0])
    D = dx.shape[1]
    for at, kind in ((2, KIND_I), (3, KIND_F), (1, KIND_O)):
        arrive(at, (kind,))
        for l in range(2):
            ref = fin[kind]
            grad = ref[l].astype(F32).reshape(-1, ref.shape[-1])
            step(at, (l,), grad.T if kind == KIND_F else grad)
        done(at)
    arrive(0, (KIND_Q, KIND_K, KIND_V))
    for l in range(2):
        for at, kind in enumerate((KIND_Q, KIND_K, KIND_V)):
            grad = fin[kind][l].astype(F32).reshape(-1, D)
            step(0, (l, slice(None), slice(at * D, at * D + D)), grad)
    done(0)
    arrive(4, ())
    waits[1].wait()
    wide = masters[4].shape[2]
    span = 128 // wide
    slot = lax.rem(f, span)
    for l in range(2):
        block = fvec[16 * l : 16 * l + 16]
        grad = block[:, :wide]
        for s in range(1, span):
            grad = jnp.where(slot == s, block[:, s * wide : s * wide + wide], grad)
        step(4, (slice(None), l), grad)
    done(4)
    for cp in leaving:
        cp.wait()


def fast_body(
    tokens, cotangent, tags, lengths, key_mask,
    master_qkv, master_out, master_in, master_feed_output, master_vec,
    first_qkv, first_out, first_in, first_ffo, first_vec,
    second_qkv, second_out, second_in, second_ffo, second_moment_vector,
    shards,
):
    S, D = tokens.shape[1:]
    FF = master_in.shape[2]
    levels = shards // 4
    rows, cols = sizes_of(shards, D, FF)
    meta_shape = (2 * S + 16, 128)
    by_row = lambda vectors: vectors.transpose(1, 0, 2)
    hbm = pl.BlockSpec(memory_space=pl.ANY)
    shape = jax.ShapeDtypeStruct
    V = pltpu.VMEM
    dma = pltpu.SemaphoreType.DMA
    w_tail = [(levels, 2, 2, 2, rows[k], cols[k]) for k in KINDS]
    masters = (master_qkv, master_out, master_in, master_feed_output, by_row(master_vec))
    firsts = (first_qkv, first_out, first_in, first_ffo, by_row(first_vec))
    seconds = (second_qkv, second_out, second_in, second_ffo, by_row(second_moment_vector))

    saved = call_kernel(
        lambda parts, *refs: forward_kernel(parts, levels, norm_epsilon, *refs),
        ForwardIn(
            tok=tokens,
            cot=cotangent,
            lengths=lengths,
            tags=tags,
            key_mask=key_mask,
            vectors=by_row(master_vec),
            masters=masters[:4],
        ),
        Saved(
            w_o=tuple(shape((2,) + tail, BF) for tail in w_tail),
            vec_o=shape((32, D), F32),
            meta_o=shape(meta_shape, BF),
            cot_o=shape((S, D), BF),
            y_o=shape((S, D), BF),
            at_o=shape((2, D, S), BF),
            q_o=shape((2, S, D), BF),
            k_o=shape((2, 2, S, D), BF),
            v_o=shape((2, 2, S, D), BF),
            lse_o=shape((2, D // 128, 8, S), F32),
            ct_o=shape((2, D, S), BF),
            ctp_o=shape((2, D, S), BF),
            n1_o=shape((2, S, D), F32),
            r1_o=shape((2, S, 128), F32),
            ht_o=shape((2, D, S), BF),
            g_o=shape((2, S, FF), BF),
            gp_o=shape((2, S, FF), BF),
            n2_o=shape((2, S, D), F32),
            r2_o=shape((2, S, 128), F32),
        ),
        ForwardScratch(
            w=tuple(V((2,) + tail, BF) for tail in w_tail),
            stages=tuple(V(m.shape, F32) for m in masters[:4]),
            vecg=V((4, 32, 128), BF),
            vecl=V((levels, 32, 128), BF),
            vecs=V((16,) + masters[4].shape[1:], F32),
            vec=V((32, D), F32),
            metab=V((2,) + meta_shape, BF),
            msel=V(meta_shape, BF),
            tokb=V((S, D), BF),
            cotb=V((S, D), BF),
            A32=V((S, D), F32),
            Ab=V((S, D), BF),
            ATp=V((D, S), BF),
            Q=V((S, D), BF),
            K=V((2, 2, S, D), BF),
            V=V((2, 2, S, D), BF),
            lse=V((D // 128, 8, S), F32),
            CT=V((D, S), BF),
            CTp=V((D, S), BF),
            C=V((S, D), BF),
            N1=V((S, D), F32),
            r1=V((S, 128), F32),
            H32=V((S, D), F32),
            Hb=V((S, D), BF),
            HTp=V((D, S), BF),
            G=V((S, FF), BF),
            Gp=V((S, FF), BF),
            N2=V((S, D), F32),
            r2=V((S, 128), F32),
            X=V((S, D), F32),
            Yb=V((S, D), BF),
            msem=dma((2, 4)),
            xsem=dma((4,)),
            osem=dma((48,)),
            gs=dma((16, levels + 4)),
            gr=dma((16, levels + 4)),
            vs=dma((levels + 2,)),
            vr=dma((levels + 2,)),
            xs=dma((3,)),
            xr=dma((3,)),
            ks=dma((2, 2)),
            kr=dma((2, 2)),
        ),
        ForwardIn(
            tok=hbm,
            cot=hbm,
            lengths=pl.BlockSpec(memory_space=pltpu.SMEM),
            tags=pl.BlockSpec(memory_space=pltpu.SMEM),
            key_mask=pl.BlockSpec(memory_space=pltpu.VMEM),
            vectors=hbm,
            masters=(hbm,) * 4,
        ),
        collective_id=0,
        has_side_effects=True,
        vmem_limit_bytes=VMEM_BYTES,
    )

    tails = [(rows[k], cols[k]) for k in KINDS]
    tails[KIND_F] = (D // 2, FF // shards)
    each = lambda *lead: tuple(V(lead + tail, BF) for tail in tails)
    grads = call_kernel(
        lambda parts, *refs: backward_kernel(parts, levels, *refs),
        saved,
        BackwardOut(
            fin=tuple(shape((2, 2) + tail, BF) for tail in tails),
            vec_g=shape((32, 128), F32),
            yo=shape((S, D), BF),
            dxo=shape((S, D), BF),
        ),
        BackwardScratch(
            g=each(2, 2, levels, 2, 2),
            landing=each(levels, 2, 2),
            half=each(2, levels, 2),
            quarter=each(2, levels),
            level=each(2, levels - 1, 2),
            total=each(2, 2),
            w=tuple(V(tail, BF) for tail in w_tail),
            AT=V((D, S), BF),
            Q=V((S, D), BF),
            K=V((2, S, D), BF),
            V=V((2, S, D), BF),
            lse=V((D // 128, 8, S), F32),
            CT=V((D, S), BF),
            CTp=V((D, S), BF),
            N1=V((S, D), F32),
            r1=V((S, 128), F32),
            HT=V((D, S), BF),
            G=V((S, FF), BF),
            Gp=V((S, FF), BF),
            N2=V((S, D), F32),
            r2=V((S, 128), F32),
            vec=V((32, D), F32),
            msel=V(meta_shape, BF),
            cotb=V((S, D), BF),
            dy=V((S, D), F32),
            dpre=V((S, D), F32),
            dF=V((S, D), BF),
            dFT=V((D, S), BF),
            dU=V((S, FF), BF),
            dZ=V((S, D), BF),
            delta=V((D // 128, 8, S), F32),
            dQT=V((D, S), BF),
            dvb=V((S, D), BF),
            dkp=V((2, 2, D // 128, S, 128), BF),
            dvp=V((2, 2, D // 128, S, 128), BF),
            dkr=V((2, D // 128, S, 128), BF),
            dvr=V((2, D // 128, S, 128), BF),
            vg=V((32, D), F32),
            va=V((2, 4, 16, D), F32),
            vrecv=V((2, 3, 16, D), F32),
            vb=V((2, levels - 1, 16, 128), F32),
            vt=V((32, 128), F32),
            lsem=dma((2, 20)),
            ssem=dma((7,)),
            fsem=dma((16,)),
            gs=dma((16, levels + 5)),
            gr=dma((16, levels + 5)),
            xs=dma((3,)),
            xr=dma((3,)),
            ks=dma((2, 2, 2)),
            kr=dma((2, 2, 2)),
            vs=dma((2, levels + 2)),
            vr=dma((2, levels + 2)),
        ),
        hbm,
        collective_id=1,
        has_side_effects=True,
        vmem_limit_bytes=VMEM_BYTES,
    )

    rates = (
        matrix_rate * D ** (-0.5),
        matrix_rate * (D // 16) ** (-0.5),
        matrix_rate * D ** (-0.5),
        matrix_rate * (FF // 2) ** (-0.5),
        vector_rate,
    )
    decays = (weight_decay, weight_decay, weight_decay, weight_decay, 0.0)
    like = tuple(shape(p.shape, F32) for p in masters)
    new = call_kernel(
        lambda parts, *refs: update_kernel(parts, rates, decays, *refs),
        UpdateIn(fin=grads.fin, fvec=grads.vec_g, y=grads.yo, dx=grads.dxo, masters=masters, firsts=firsts, seconds=seconds),
        UpdateOut(
            out=shape(tokens.shape, BF),
            grad=shape(tokens.shape, F32),
            new_masters=like,
            new_firsts=like,
            new_seconds=like,
        ),
        UpdateScratch(
            inside=(
                tuple(V(g.shape, BF) for g in grads.fin),
                V((32, 128), F32),
                V((S, D), BF),
                V((S, D), BF),
                *((*(V(p.shape, F32) for p in masters[:4]), V((16,) + masters[4].shape[1:], F32)) for _ in range(3)),
            ),
            wide=V((S, D), F32),
            isem=dma((24,)),
            osem=dma((17,)),
        ),
        hbm,
        vmem_limit_bytes=VMEM_BYTES,
    )
    trees = [(*tree[:4], by_row(tree[4])) for tree in (new.new_masters, new.new_firsts, new.new_seconds)]
    return (new.out, new.grad, *trees[0], *trees[1], *trees[2])


def solution(mesh):
    placed = (
        P("fsdp", "rep", None),
        P("fsdp", "rep", None),
        P("fsdp"),
        P("fsdp"),
        P("fsdp", None),
        P(None, "fsdp", None),
        P(None, "fsdp", None),
        P(None, "fsdp", None),
        P(None, "fsdp", None),
        P(None, None, "fsdp"),
        P(None, "fsdp", None),
        P(None, "fsdp", None),
        P(None, "fsdp", None),
        P(None, "fsdp", None),
        P(None, None, "fsdp"),
        P(None, "fsdp", None),
        P(None, "fsdp", None),
        P(None, "fsdp", None),
        P(None, "fsdp", None),
        P(None, None, "fsdp"),
    )
    shards = mesh.shape["fsdp"]

    def chosen(*args):
        tokens, master_in = args[0], args[7]
        width = tokens.shape[2]
        whole_tiles = shards * 32 == width and master_in.shape[2] == 4 * width
        if mesh.shape["rep"] == 2 and shards % 4 == 0 and whole_tiles:
            return fast_body(*args, shards)
        return body(*args)

    return jax.shard_map(
        chosen,
        mesh=mesh,
        in_specs=placed,
        out_specs=(
            P("fsdp", "rep", None),
            P("fsdp", "rep", None),
            P(None, "fsdp", None),
            P(None, "fsdp", None),
            P(None, "fsdp", None),
            P(None, "fsdp", None),
            P(None, None, "fsdp"),
            P(None, "fsdp", None),
            P(None, "fsdp", None),
            P(None, "fsdp", None),
            P(None, "fsdp", None),
            P(None, None, "fsdp"),
            P(None, "fsdp", None),
            P(None, "fsdp", None),
            P(None, "fsdp", None),
            P(None, "fsdp", None),
            P(None, None, "fsdp"),
        ),
        check_vma=False,
    )
```
